32 devices in a mesh: seq: 8 (over z, x), batch: 4 (over y, core).
Axes of the slice: x: 2, y: 2, z: 4, core: 2. Of those that a mesh axis runs over, the one named last changes fastest.
Arguments:
- tokens: bfloat16 [8, 2048, 512], P('batch', 'seq'), may hold values from -7 to 7
- doc_lengths: int32 [8, 16], P('batch'), may hold values from 1 to 1792, as said below
- cotangent: bfloat16 [8, 2048, 512], P('batch', 'seq'), may hold values from -6 to 6
- mixer_weights: float32 [4096, 512], P(('seq', 'batch'))
- mlp_weights: float32 [4096, 512], P(('seq', 'batch'))
- small_params: float32 [3072], P(('seq', 'batch')), may hold values from -16 to 5
- mixer_first: float32 [4096, 512], P(('seq', 'batch'))
- mixer_second: float32 [4096, 512], P(('seq', 'batch'))
- mlp_first: float32 [4096, 512], P(('seq', 'batch'))
- mlp_second: float32 [4096, 512], P(('seq', 'batch'))
- small_first: float32 [3072], P(('seq', 'batch'))
- small_second: float32 [3072], P(('seq', 'batch'))
Outputs:
- output: bfloat16 [8, 2048, 512], P('batch', 'seq')
- input_grad: bfloat16 [8, 2048, 512], P('batch', 'seq')
- mixer_grad: float32 [4096, 512], P(('seq', 'batch'))
- mlp_grad: float32 [4096, 512], P(('seq', 'batch'))
- small_grad: float32 [3072], P(('seq', 'batch'))
- mixer_first_new: float32 [4096, 512], P(('seq', 'batch'))
- mixer_second_new: float32 [4096, 512], P(('seq', 'batch'))
- mlp_first_new: float32 [4096, 512], P(('seq', 'batch'))
- mlp_second_new: float32 [4096, 512], P(('seq', 'batch'))
- small_first_new: float32 [3072], P(('seq', 'batch'))
- small_second_new: float32 [3072], P(('seq', 'batch'))
- mixer_new: float32 [4096, 512], P(('seq', 'batch'))
- mlp_new: float32 [4096, 512], P(('seq', 'batch'))
- small_new: float32 [3072], P(('seq', 'batch'))
- mixer_copy: bfloat16 [4096, 512], P(('seq', 'batch'))
- mlp_copy: bfloat16 [4096, 512], P(('seq', 'batch'))
- small_copy: bfloat16 [3072], P(('seq', 'batch'))
- tensor_norms: float32 [2, 10], replicated
- trust_ratios: float32 [10], replicated
The draws below stay inside these ranges and needn't reach their ends.
Inputs may be any that keep to these rules, and one draw needn't show every extreme that they name: `doc_lengths`: each stream's lengths sum to between 2016 and 2047. In every group of 2 consecutive streams one stream holds a document of exactly 1792 positions, its second, starting within the first 64 positions.
All inputs are finite; a program needn't handle non-finite values.
Results may differ from the reference program's by a relative error of at most 0.012.
Values may be sent and summed in bfloat16 or wider, within the bound.
No kernel may reach another device: no remote copies, remote signals or barrier semaphores. Data moves between devices by JAX's collectives and lax.ppermute only.
A program may use at most 128 MiB of HBM per device.

```python
import math
import jax
import jax.numpy as jnp
from jax import lax

D = 512
H = 1024
FF = 2048
BLOCK = 256
DOCS = 16
STEP = 5
STREAMS_GRP = 2
LENGTH = 2048
STREAMS = 8
SMALL = 3072


def rise_rows(count):
    return (1.0 + 2.0 * jnp.arange(count, dtype=jnp.float32) / (count - 1)) / 2.08


def split_total(totals, weights):
    count = weights.shape[-1]
    cumul = jnp.cumsum(weights, axis=-1).astype(jnp.int32)
    cuts = cumul * (totals[:, None] - count) // cumul[:, -1:]
    first_cut = jnp.zeros_like(cuts[:, :1])
    return (1 + jnp.diff(jnp.concatenate([first_cut, cuts], axis=1), axis=1)).astype(jnp.int32)


def mixer_scale():
    rise = rise_rows(H)
    return math.sqrt(STREAMS * LENGTH) * jnp.concatenate([0.03 * rise, 0.3 * rise, 0.3 * rise, 0.5 * rise])


def mlp_scale():
    rise = rise_rows(FF)
    return math.sqrt(STREAMS * LENGTH) * jnp.concatenate([0.3 * rise, 0.6 * rise])


def small_scale():
    return math.sqrt(STREAMS * LENGTH) * jnp.concatenate([jnp.full((D,), 0.5), jnp.full((D,), 0.6), jnp.full((H,), 0.03), jnp.full((H,), 0.3)])


def draw_tokens(key, part):
    key = jax.random.fold_in(key, 1)
    key_noise, key_offset = jax.random.split(key, 2)
    shape = (STREAMS, LENGTH, D)
    noise = jnp.clip(jax.random.normal(key_noise, shape), -4.0, 4.0)
    offset = 0.7 * jnp.clip(jax.random.normal(key_offset, (STREAMS, 1, D)), -3.0, 3.0)
    return (noise + offset).astype(jnp.bfloat16)


def draw_doc_lengths(key, part):
    key = jax.random.fold_in(key, 2)
    key_pad, key_weight, key_head, key_pick = jax.random.split(key, 4)
    padding = jax.random.randint(key_pad, (STREAMS,), 1, BLOCK // 8 + 1)
    totals = (LENGTH - padding).astype(jnp.int32)
    powers = jax.random.randint(key_weight, (STREAMS, DOCS), 0, 7)
    weights = jnp.left_shift(jnp.ones((STREAMS, DOCS), jnp.int32), powers)
    drawn = split_total(totals, weights)
    head_len = jax.random.randint(key_head, (STREAMS,), 1, BLOCK // 4 + 1).astype(jnp.int32)
    rest = (totals - head_len - (LENGTH - BLOCK)).astype(jnp.int32)
    tail = split_total(rest, weights[:, 2:])
    longest = jnp.concatenate([head_len[:, None], jnp.full((STREAMS, 1), LENGTH - BLOCK, jnp.int32), tail], axis=1)
    chosen = jax.random.randint(key_pick, (STREAMS // STREAMS_GRP,), 0, STREAMS_GRP)
    picked = jnp.repeat(chosen, STREAMS_GRP) == jnp.arange(STREAMS) % STREAMS_GRP
    return jnp.where(picked[:, None], longest, drawn).astype(jnp.int32)


def draw_mixer_weights(key, part):
    key = jax.random.fold_in(key, 3)
    shape = (4 * H, D)
    noise = jnp.clip(jax.random.normal(key, shape), -4.0, 4.0)
    rise = rise_rows(H)
    drawn = jnp.full((H,), 1.0 / math.sqrt(D))
    scale = jnp.concatenate([drawn, drawn, rise / math.sqrt(D), 3.0 * rise / math.sqrt(H)])
    return (noise * scale[:, None]).astype(jnp.float32)


def draw_mlp_weights(key, part):
    key = jax.random.fold_in(key, 4)
    shape = (2 * FF, D)
    noise = jnp.clip(jax.random.normal(key, shape), -4.0, 4.0)
    rise = rise_rows(FF)
    scale = jnp.concatenate([rise / math.sqrt(D), rise / math.sqrt(FF)])
    return (noise * scale[:, None]).astype(jnp.float32)


def draw_small_params(key, part):
    key = jax.random.fold_in(key, 5)
    key_gain, key_forget, key_fast, key_slow, key_quick = jax.random.split(key, 5)
    gains = 1.0 + 0.1 * jnp.clip(jax.random.normal(key_gain, (2 * D,)), -4.0, 4.0)
    share = 0.5
    forget_bias = jax.random.uniform(key_forget, (H,), minval=2.0, maxval=4.0)
    fast = jax.random.uniform(key_fast, (H,)) < share
    slow_bias = jnp.log(jax.random.uniform(key_slow, (H,), minval=0.3, maxval=1.0)) - math.log(LENGTH)
    quick_bias = jax.random.uniform(key_quick, (H,), minval=-4.0, maxval=-3.0)
    input_bias = jnp.where(fast, quick_bias, slow_bias)
    return jnp.concatenate([gains, forget_bias, input_bias]).astype(jnp.float32)


def draw_mixer_first(key, part):
    key = jax.random.fold_in(key, 6)
    shape = (4 * H, D)
    noise = jnp.clip(jax.random.normal(key, shape), -3.0, 3.0)
    return (0.8 * mixer_scale()[:, None] * noise).astype(jnp.float32)


def draw_mixer_second(key, part):
    key = jax.random.fold_in(key, 7)
    shape = (4 * H, D)
    spread = jax.random.uniform(key, shape, minval=math.log(0.5), maxval=math.log(8.0))
    return (mixer_scale()[:, None] ** 2 * jnp.exp(spread)).astype(jnp.float32)


def draw_mlp_first(key, part):
    key = jax.random.fold_in(key, 8)
    shape = (2 * FF, D)
    noise = jnp.clip(jax.random.normal(key, shape), -3.0, 3.0)
    return (0.8 * mlp_scale()[:, None] * noise).astype(jnp.float32)


def draw_mlp_second(key, part):
    key = jax.random.fold_in(key, 9)
    shape = (2 * FF, D)
    spread = jax.random.uniform(key, shape, minval=math.log(0.5), maxval=math.log(8.0))
    return (mlp_scale()[:, None] ** 2 * jnp.exp(spread)).astype(jnp.float32)


def draw_small_first(key, part):
    key = jax.random.fold_in(key, 10)
    noise = jnp.clip(jax.random.normal(key, (SMALL,)), -3.0, 3.0)
    return (0.8 * small_scale() * noise).astype(jnp.float32)


def draw_small_second(key, part):
    key = jax.random.fold_in(key, 11)
    spread = jax.random.uniform(key, (SMALL,), minval=math.log(0.5), maxval=math.log(8.0))
    return (small_scale() ** 2 * jnp.exp(spread)).astype(jnp.float32)


def steps_of(own_key, shape, cuts, smallest, largest):
    def one(axis_at, blocks):
        heights = jax.random.uniform(jax.random.fold_in(jax.random.fold_in(own_key, 6), axis_at), (blocks,), jnp.float32, smallest / len(cuts), largest / len(cuts))
        return jnp.repeat(jnp.exp(heights), shape[axis_at] // blocks).reshape((-1,) + (1,) * (len(shape) - axis_at - 1))

    factor_of = one(*cuts[0])
    for cut in cuts[1:]:
        factor_of = factor_of * one(*cut)
    return factor_of


def scatter_about(own_key, shape, scale, bound, shards=(), held_as=jnp.bfloat16):
    level = steps_of(own_key, shape, shards, -0.22, 0.18) if shards else 1.0
    array = jax.random.normal(own_key, shape, jnp.float32) * scale * level
    return jnp.minimum(jnp.maximum(array, -bound), bound).astype(held_as)


def setup_inputs(seed: int = 0) -> dict:
    splits = jax.random.split(jax.random.key(seed), 13)
    return {
        "tokens": draw_tokens(jax.random.fold_in(splits[12], 71), 0),
        "doc_lengths": draw_doc_lengths(jax.random.fold_in(splits[12], 71), 0),
        "cotangent": scatter_about(splits[2], (STREAMS, LENGTH, D), 1.0, 6.0, ((0, 4), (1, 8))),
        "mixer_weights": draw_mixer_weights(jax.random.fold_in(splits[12], 71), 0),
        "mlp_weights": draw_mlp_weights(jax.random.fold_in(splits[12], 71), 0),
        "small_params": draw_small_params(jax.random.fold_in(splits[12], 71), 0),
        "mixer_first": draw_mixer_first(jax.random.fold_in(splits[12], 71), 0),
        "mixer_second": draw_mixer_second(jax.random.fold_in(splits[12], 71), 0),
        "mlp_first": draw_mlp_first(jax.random.fold_in(splits[12], 71), 0),
        "mlp_second": draw_mlp_second(jax.random.fold_in(splits[12], 71), 0),
        "small_first": draw_small_first(jax.random.fold_in(splits[12], 71), 0),
        "small_second": draw_small_second(jax.random.fold_in(splits[12], 71), 0),
    }


@jax.custom_vjp
def low(v):
    return lax.optimization_barrier(v.astype(jnp.bfloat16)).astype(jnp.float32)

@jax.custom_vjp
def low_back(v):
    return v

def low_keep(v):
    return (low(v), None)

def low_pass(kept, grad):
    return (grad,)

def back_keep(v):
    return (v, None)

def back_low(kept, grad):
    return (low(grad),)
low.defvjp(low_keep, low_pass)
low_back.defvjp(back_keep, back_low)
first_decay = 0.5
second_decay = 0.5
learn_rate = 0.25
matrix_decay = 0.01
moment_eps = 1e-06
highest = lax.Precision.HIGHEST

def rms_scale(values, gain):
    return values * lax.rsqrt(lax.optimization_barrier(jnp.mean(values * values, axis=-1, keepdims=True)) + 1e-05) * gain

def linear_join(earlier, later):
    return (earlier[0] * later[0], later[0] * earlier[1] + later[1])

def spans(lengths_row):
    doc_ends = jnp.cumsum(lengths_row).astype(jnp.int32)
    doc_starts = (doc_ends - lengths_row).astype(jnp.int32)
    position = jnp.arange(LENGTH, dtype=jnp.int32)
    begins = jnp.any(position[:, None] == doc_starts[None, :], axis=1) | (position == doc_ends[-1])
    valid = position < doc_ends[-1]
    return (begins.astype(jnp.float32), valid.astype(jnp.float32))

def one_stream(x_row, begin_row, valid_row, mixer_used, mlp_used, small_used):
    gain_one = small_used[:D]
    gain_two = small_used[D:2 * D]
    forget_bias = small_used[2 * D:2 * D + H]
    input_bias = small_used[2 * D + H:]
    normed = low(rms_scale(x_row, gain_one))
    projected = low_back(jnp.dot(normed, mixer_used[:3 * H].T, precision=highest))
    forget = jax.nn.sigmoid(projected[:, :H] + forget_bias)
    input_gate = jax.nn.sigmoid(projected[:, H:2 * H] + input_bias)
    gate_sum = forget + input_gate
    retain = forget / gate_sum * (1.0 - begin_row)[:, None]
    inflow = input_gate / gate_sum * projected[:, 2 * H:]
    states = lax.associative_scan(linear_join, (retain, inflow), axis=0)[1]
    mixed = low_back(jnp.dot(low(states), mixer_used[3 * H:], precision=highest))
    residual = x_row + mixed
    normed_two = low(rms_scale(residual, gain_two))
    inner_pre = low_back(jnp.dot(normed_two, mlp_used[:FF].T, precision=highest))
    activated = low(jax.nn.gelu(inner_pre))
    outer = low_back(jnp.dot(activated, mlp_used[FF:], precision=highest))
    return (residual + outer) * valid_row[:, None]

def moments(weight, gradient, first_moment, second, decay_rate):
    first_new = first_decay * first_moment + (1.0 - first_decay) * gradient
    second_new = second_decay * second + (1.0 - second_decay) * gradient * gradient
    direction = first_new / (1.0 - first_decay ** STEP) / (jnp.sqrt(second_new / (1.0 - second_decay ** STEP)) + moment_eps) + decay_rate * weight
    return (first_new, second_new, direction)

def tensor_squares(mixer_like, mlp_like, small_like):
    mixer_part = lax.optimization_barrier(jnp.sum((mixer_like * mixer_like).reshape(4, H * D), axis=1))
    mlp_part = lax.optimization_barrier(jnp.sum((mlp_like * mlp_like).reshape(2, FF * D), axis=1))
    small_sq = small_like * small_like
    small_part = jnp.stack([jnp.sum(small_sq[:D]), jnp.sum(small_sq[D:2 * D]), jnp.sum(small_sq[2 * D:2 * D + H]), jnp.sum(small_sq[2 * D + H:])])
    return jnp.concatenate([mixer_part, mlp_part, small_part])

def reference(tokens, doc_lengths, cotangent, mixer_weights, mlp_weights, small_params, mixer_first, mixer_second, mlp_first, mlp_second, small_first, small_second):
    begins, valid = jax.vmap(spans)(doc_lengths)

    def forward(x_all, mixer_master, mlp_master, small_master):
        mixer_used = low(mixer_master)
        mlp_used = low(mlp_master)
        small_used = low(small_master)

        def stream_fn(items):
            return one_stream(items[0], items[1], items[2], mixer_used, mlp_used, small_used)
        return lax.map(jax.checkpoint(stream_fn), (x_all, begins, valid))
    result, pull = jax.vjp(forward, tokens.astype(jnp.float32), mixer_weights, mlp_weights, small_params)
    d_tokens, mixer_grad, mlp_grad, small_grad = pull(cotangent.astype(jnp.float32))
    mixer_first_new, mixer_second_new, mixer_dir = moments(mixer_weights, mixer_grad, mixer_first, mixer_second, matrix_decay)
    mlp_first_new, mlp_second_new, mlp_dir = moments(mlp_weights, mlp_grad, mlp_first, mlp_second, matrix_decay)
    small_first_new, small_second_new, small_dir = moments(small_params, small_grad, small_first, small_second, 0.0)
    weight_norms = jnp.sqrt(tensor_squares(mixer_weights, mlp_weights, small_params))
    step_norms = jnp.sqrt(tensor_squares(mixer_dir, mlp_dir, small_dir))
    trust_ratios = weight_norms / (step_norms + 1e-06)
    mixer_rows = jnp.repeat(trust_ratios[:4], H)[:, None]
    mlp_rows = jnp.repeat(trust_ratios[4:6], FF)[:, None]
    small_rows = jnp.concatenate([jnp.full((D,), trust_ratios[6]), jnp.full((D,), trust_ratios[7]), jnp.full((H,), trust_ratios[8]), jnp.full((H,), trust_ratios[9])])
    mixer_new = mixer_weights - learn_rate * mixer_rows * mixer_dir
    mlp_new = mlp_weights - learn_rate * mlp_rows * mlp_dir
    small_new = small_params - learn_rate * small_rows * small_dir
    tensor_norms = jnp.stack([weight_norms, step_norms])
    return (result.astype(jnp.bfloat16), d_tokens.astype(jnp.bfloat16), mixer_grad, mlp_grad, small_grad, mixer_first_new, mixer_second_new, mlp_first_new, mlp_second_new, small_first_new, small_second_new, mixer_new, mlp_new, small_new, mixer_new.astype(jnp.bfloat16), mlp_new.astype(jnp.bfloat16), small_new.astype(jnp.bfloat16), tensor_norms, trust_ratios)
```

```python
import jax
import jax.numpy as jnp
from jax import lax
from jax.experimental import pallas as pl
from jax.experimental.pallas import tpu as pltpu
from jax.sharding import PartitionSpec as P

D = 512
H = 1024
FF = 2048
STEP = 5
SEG = 8
ROWS = 128
PLANES = 4
ROLES = 4

first_decay = 0.5
second_decay = 0.5
learn_rate = 0.25
matrix_decay = 0.01
moment_eps = 1e-06

f32 = jnp.float32
bf16 = jnp.bfloat16
AXES = ("seq", "batch")


def dot_nt(a, b):
    return lax.dot_general(a, b, (((1,), (1,)), ((), ())), preferred_element_type=f32)


def dot_nn(a, b):
    return lax.dot_general(a, b, (((1,), (0,)), ((), ())), preferred_element_type=f32)


def dot_tn(a, b):
    return lax.dot_general(a, b, (((0,), (0,)), ((), ())), preferred_element_type=f32)


def exchange(value, seq_bits, batch_bits):
    seqs, batches = lax.axis_size("seq"), lax.axis_size("batch")
    pairs = [
        (s * batches + b, (s ^ seq_bits) * batches + (b ^ batch_bits))
        for s in range(seqs)
        for b in range(batches)
    ]
    return lax.ppermute(value, AXES, pairs)


def pick(ref, k):
    return ref[0, pl.ds(k, 1)].reshape(ROWS, D)


def both(own_ref, par_ref, k):
    return jnp.concatenate([pick(own_ref, k), pick(par_ref, k)], axis=0)


def forward_kernel(
    z_ref, tok_ref, rs_ref, gain_ref, fb_ref, ib_ref, own_ref, par_ref,
    normed_ref, forget_ref, enter_ref, cand_ref, retain_ref, acc_ref, tot_ref, sega_ref, segb_ref,
):
    z = z_ref[0]

    @pl.when(pl.program_id(0) == 0)
    def _():
        x = tok_ref[...].astype(f32)
        scale = lax.rsqrt(jnp.mean(x * x, axis=-1, keepdims=True) + 1e-05)
        normed_ref[...] = (x * scale * gain_ref[...]).astype(bf16)

    normed = normed_ref[...]
    forget = jax.nn.sigmoid(dot_nt(normed, both(own_ref, par_ref, z)) + fb_ref[...])
    enter = jax.nn.sigmoid(dot_nt(normed, both(own_ref, par_ref, z ^ 1)) + ib_ref[...])
    cand = dot_nt(normed, both(own_ref, par_ref, z ^ 2))
    inverse = 1.0 / (forget + enter)
    forget_ref[...] = forget
    enter_ref[...] = enter
    cand_ref[...] = cand
    retain_ref[...] = forget * inverse * rs_ref[...]
    acc_ref[...] = enter * inverse * cand
    rows = normed.shape[0] // 2
    for s in range(2):
        seg_a = seg_b = None
        for j in range(rows // SEG):
            at = pl.ds(s * rows + j * SEG, SEG)
            a, b = retain_ref[at, :], acc_ref[at, :]
            if j == 0:
                seg_a, seg_b = a, b
            else:
                seg_a, seg_b = a * seg_a, a * seg_b + b
                acc_ref[at, :] = seg_b
        sega_ref[pl.ds(s * SEG, SEG), :] = seg_a
        segb_ref[pl.ds(s * SEG, SEG), :] = seg_b
        tot_a, tot_b = seg_a[0:1], seg_b[0:1]
        for k in range(1, SEG):
            tot_a, tot_b = seg_a[k : k + 1] * tot_a, seg_a[k : k + 1] * tot_b + seg_b[k : k + 1]
        tot_ref[pl.ds(s, 1), :] = tot_a
        tot_ref[pl.ds(2 + s, 1), :] = tot_b


def states_kernel(
    z_ref, inc_ref, tok_ref, gain_ref, retain_ref, acc_ref, sega_ref, segb_ref, own_ref, par_ref,
    states_ref, resid_ref, normed_ref,
):
    z = z_ref[0]
    step = pl.program_id(0)
    rows = resid_ref.shape[0] // 2

    @pl.when(step == 0)
    def _():
        resid_ref[...] = tok_ref[...].astype(f32)

    for s in range(2):
        seg_a, seg_b = sega_ref[pl.ds(s * SEG, SEG), :], segb_ref[pl.ds(s * SEG, SEG), :]
        at_seg = [inc_ref[pl.ds(s, 1), :]]
        for k in range(SEG - 1):
            at_seg.append(seg_a[k : k + 1] * at_seg[-1] + seg_b[k : k + 1])
        carried = jnp.concatenate(at_seg, axis=0)
        for j in range(rows // SEG):
            at = pl.ds(s * rows + j * SEG, SEG)
            carried = retain_ref[at, :] * carried
            states_ref[at, :] = acc_ref[at, :] + carried
    low = states_ref[...].astype(bf16)
    resid_ref[...] += dot_nn(low, both(own_ref, par_ref, z ^ 3))

    @pl.when(step == pl.num_programs(0) - 1)
    def _():
        r = resid_ref[...]
        scale = lax.rsqrt(jnp.mean(r * r, axis=-1, keepdims=True) + 1e-05)
        normed_ref[...] = (r * scale * gain_ref[...]).astype(bf16)


GELU_A = 0.7978845608028654
GELU_B = 0.044715


def mlp_kernel(
    z_ref, normed_ref, resid_ref, cot_ref, valid_ref, gain_ref, own_ref, par_ref,
    output_ref, dresid_ref, dgain_ref, gown_ref, gpar_ref,
    dout_ref, outer_ref, dnorm_ref,
):
    z = z_ref[0]
    step = pl.program_id(0)
    low = step % 2
    up_at = low ^ z
    down_at = (2 + low) ^ z

    @pl.when(step == 0)
    def _():
        dout_ref[...] = (cot_ref[...].astype(f32) * valid_ref[...]).astype(bf16)
        outer_ref[...] = jnp.zeros_like(outer_ref)
        dnorm_ref[...] = jnp.zeros_like(dnorm_ref)

    normed = normed_ref[...]
    dout = dout_ref[...]
    w_up = both(own_ref, par_ref, up_at)
    w_down = both(own_ref, par_ref, down_at)
    inner = dot_nt(normed, w_up)
    square = inner * inner
    curve = jnp.tanh(GELU_A * inner * (1.0 + GELU_B * square))
    half = 0.5 * (1.0 + curve)
    activated = (inner * half).astype(bf16)
    slope = half + 0.5 * inner * (1.0 - curve * curve) * (GELU_A * (1.0 + 3.0 * GELU_B * square))
    d_inner = (slope * dot_nt(dout, w_down)).astype(bf16)
    outer_ref[...] += dot_nn(activated, w_down)
    dnorm_ref[...] += dot_nn(d_inner, w_up)
    g_up = dot_tn(d_inner, normed).astype(bf16)
    g_down = dot_tn(activated, dout).astype(bf16)
    gown_ref[0, pl.ds(up_at, 1)] = g_up[:ROWS].reshape(1, ROWS, D)
    gpar_ref[0, pl.ds(up_at, 1)] = g_up[ROWS:].reshape(1, ROWS, D)
    gown_ref[0, pl.ds(down_at, 1)] = g_down[:ROWS].reshape(1, ROWS, D)
    gpar_ref[0, pl.ds(down_at, 1)] = g_down[ROWS:].reshape(1, ROWS, D)

    @pl.when(step == pl.num_programs(0) - 1)
    def _():
        r = resid_ref[...]
        output_ref[...] = ((r + outer_ref[...]) * valid_ref[...]).astype(bf16)
        scale = lax.rsqrt(jnp.mean(r * r, axis=-1, keepdims=True) + 1e-05)
        d_normed = dnorm_ref[...]
        unit = r * scale
        dgain_ref[...] = jnp.sum(d_normed * unit, axis=0, keepdims=True)
        d_unit = d_normed * gain_ref[...]
        mean = jnp.mean(d_unit * unit, axis=-1, keepdims=True)
        dresid_ref[...] = dout_ref[...].astype(f32) + scale * (d_unit - unit * mean)


def back_kernel(
    z_ref, dresid_ref, states_ref, retain_ref, sega_ref, own_ref, par_ref,
    acc_ref, tot_ref, segb_ref, gown_ref, gpar_ref,
    dmix_ref,
):
    z = z_ref[0]
    rows = dresid_ref.shape[0] // 2

    @pl.when(pl.program_id(0) == 0)
    def _():
        dmix_ref[...] = dresid_ref[...].astype(bf16)

    dmix = dmix_ref[...]
    acc_ref[...] = dot_nt(dmix, both(own_ref, par_ref, z ^ 3))
    grad = dot_tn(states_ref[...].astype(bf16), dmix).astype(bf16)
    gown_ref[0] = grad[:ROWS]
    gpar_ref[0] = grad[ROWS:]
    for s in range(2):
        back = emitted = None
        for j in reversed(range(rows // SEG)):
            at = pl.ds(s * rows + j * SEG, SEG)
            back = acc_ref[at, :] if back is None else acc_ref[at, :] + emitted
            acc_ref[at, :] = back
            emitted = retain_ref[at, :] * back
        segb_ref[pl.ds(s * SEG, SEG), :] = emitted
        seg_a = sega_ref[pl.ds(s * SEG, SEG), :]
        tot_a, tot_b = seg_a[SEG - 1 :], emitted[SEG - 1 :]
        for k in reversed(range(SEG - 1)):
            tot_a, tot_b = seg_a[k : k + 1] * tot_a, seg_a[k : k + 1] * tot_b + emitted[k : k + 1]
        tot_ref[pl.ds(s, 1), :] = tot_a
        tot_ref[pl.ds(2 + s, 1), :] = tot_b


def gates_kernel(
    z_ref, arr_ref, inc_ref, acc_ref, sega_ref, segb_ref, forget_ref, enter_ref, cand_ref, retain_ref, states_ref,
    rs_ref, normed_ref, tok_ref, gain_ref, dresid_ref, own_ref, par_ref,
    gown_ref, gpar_ref, dfb_ref, dib_ref, dgain_ref, dx_ref,
    pf_ref, pi_ref, pc_ref, dnorm_ref,
):
    z = z_ref[0]
    step = pl.program_id(0)
    rows = dresid_ref.shape[0] // 2
    steps = rows // SEG

    @pl.when(step == 0)
    def _():
        dnorm_ref[...] = jnp.zeros_like(dnorm_ref)

    sum_f = sum_i = 0.0
    for s in range(2):
        seg_a, seg_b = sega_ref[pl.ds(s * SEG, SEG), :], segb_ref[pl.ds(s * SEG, SEG), :]
        at_seg = [arr_ref[pl.ds(s, 1), :]]
        for k in reversed(range(1, SEG)):
            at_seg.append(seg_a[k : k + 1] * at_seg[-1] + seg_b[k : k + 1])
        carried = jnp.concatenate(at_seg[::-1], axis=0)
        for j in reversed(range(steps)):
            at = pl.ds(s * rows + j * SEG, SEG)
            back = acc_ref[at, :] + carried
            carried = carried * retain_ref[at, :]
            if j > 0:
                previous = states_ref[pl.ds(s * rows + (j - 1) * SEG, SEG), :]
            else:
                ends = states_ref[pl.ds(s * rows + (steps - 1) * SEG, SEG), :]
                previous = jnp.concatenate([inc_ref[pl.ds(s, 1), :], ends[: SEG - 1]], axis=0)
            forget, enter, cand = forget_ref[at, :], enter_ref[at, :], cand_ref[at, :]
            inverse = 1.0 / (forget + enter)
            keep, gain = forget * inverse, enter * inverse
            both_ways = back * (previous * rs_ref[at, :] - cand) * (keep * gain)
            d_f = both_ways * (1.0 - forget)
            d_i = both_ways * (enter - 1.0)
            pf_ref[at, :] = d_f
            pi_ref[at, :] = d_i
            pc_ref[at, :] = back * gain
            sum_f = sum_f + d_f
            sum_i = sum_i + d_i
    dfb_ref[...] = jnp.sum(sum_f, axis=0, keepdims=True)
    dib_ref[...] = jnp.sum(sum_i, axis=0, keepdims=True)
    normed = normed_ref[...]
    total = dnorm_ref[...]
    for role, ref in enumerate((pf_ref, pi_ref, pc_ref)):
        d_proj = ref[...].astype(bf16)
        grad = dot_tn(d_proj, normed).astype(bf16)
        gown_ref[0, pl.ds(z ^ role, 1)] = grad[:ROWS].reshape(1, ROWS, D)
        gpar_ref[0, pl.ds(z ^ role, 1)] = grad[ROWS:].reshape(1, ROWS, D)
        total = total + dot_nn(d_proj, both(own_ref, par_ref, z ^ role))
    dnorm_ref[...] = total

    @pl.when(step == pl.num_programs(0) - 1)
    def _():
        x = tok_ref[...].astype(f32)
        scale = lax.rsqrt(jnp.mean(x * x, axis=-1, keepdims=True) + 1e-05)
        d_normed = dnorm_ref[...]
        unit = x * scale
        dgain_ref[...] = jnp.sum(d_normed * unit, axis=0, keepdims=True)
        d_unit = d_normed * gain_ref[...]
        mean = jnp.mean(d_unit * unit, axis=-1, keepdims=True)
        dx_ref[...] = (dresid_ref[...] + scale * (d_unit - unit * mean)).astype(bf16)


def whole(*shape):
    return pl.BlockSpec(shape, lambda i: (0,) * len(shape))


def columns(rows, width):
    return pl.BlockSpec((rows, width), lambda i: (0, i))


def plane(per_plane=1):
    return pl.BlockSpec((1, ROLES, ROWS, D), lambda i: (i // per_plane, 0, 0, 0))


SMEM = pl.BlockSpec(memory_space=pltpu.SMEM)
PARAMS = pltpu.CompilerParams(vmem_limit_bytes=56 * 1024 * 1024)


def shape(*dims, dtype=f32):
    return jax.ShapeDtypeStruct(dims, dtype)


def gather_weights(shard, z_steps):
    slabs = jnp.concatenate([shard] + [exchange(shard, 2 * k, 0) for k in range(1, z_steps)], axis=0)
    own = jnp.stack([slabs, exchange(slabs, 0, 2), exchange(slabs, 1, 0), exchange(slabs, 1, 2)])
    par = exchange(own, 0, 1)
    return own.reshape(PLANES, ROLES, ROWS, D), par.reshape(PLANES, ROLES, ROWS, D)


def reduce_terms(own, par):
    total = (own.astype(f32) + exchange(par, 0, 1).astype(f32)).astype(bf16)
    total = (
        (total[0].astype(f32) + exchange(total[1], 0, 2).astype(f32))
        + (exchange(total[2], 1, 0).astype(f32) + exchange(total[3], 1, 2).astype(f32))
    ).astype(bf16)
    return (total[0].astype(f32) + exchange(total[1], 2, 0).astype(f32)) + (
        exchange(total[2], 4, 0).astype(f32) + exchange(total[3], 6, 0).astype(f32)
    )


def all_sum(value):
    seqs, batches = lax.axis_size("seq"), lax.axis_size("batch")
    bit = 1
    while bit < batches:
        value = value + exchange(value, 0, bit)
        bit *= 2
    bit = 1
    while bit < seqs:
        value = value + exchange(value, bit, 0)
        bit *= 2
    return value


def relay(total, forward, flipped):
    count = lax.axis_size("seq")
    me = lax.axis_index("seq")
    fast, slow = me % 2, me // 2
    other = exchange(total, 1, 0)
    if flipped:
        other = jnp.concatenate([other[:, H // 2 :], other[:, : H // 2]], axis=1)
    late = (fast == 1) if forward else (fast == 0)
    first = jnp.where(late, other, total)
    second = jnp.where(late, total, other)
    pair = jnp.concatenate([first[:2] * second[:2], second[:2] * first[2:] + second[2:]], axis=0)
    got = [pair] + [exchange(pair, 2 * k, 0) for k in range(1, count // 2)]
    state = jnp.zeros_like(pair[:2])
    for place in range(count // 2 - 1):
        source = place if forward else count // 2 - 1 - place
        term = got[0]
        for k in range(1, count // 2):
            term = jnp.where((slow ^ source) == k, got[k], term)
        earlier = (source < slow) if forward else (source > slow)
        state = jnp.where(earlier, term[2:] + term[:2] * state, state)
    return jnp.where(late, first[2:] + first[:2] * state, state)


def flip_by(value, axis, bit):
    return jnp.where(bit == 1, jnp.flip(value, axis), value)


def moments(weight, gradient, first_moment, second, decay_rate):
    first_new = first_decay * first_moment + (1.0 - first_decay) * gradient
    second_new = second_decay * second + (1.0 - second_decay) * gradient * gradient
    direction = (
        first_new
        / (1.0 - first_decay**STEP)
        / (jnp.sqrt(second_new / (1.0 - second_decay**STEP)) + moment_eps)
        + decay_rate * weight
    )
    return (first_new, second_new, direction)


def on_device(
    tokens, doc_lengths, cotangent, mixer_weights, mlp_weights, small_params,
    mixer_first, mixer_second, mlp_first, mlp_second, small_first, small_second,
):
    seqs, batches = lax.axis_size("seq"), lax.axis_size("batch")
    seq_at, batch_at = lax.axis_index("seq"), lax.axis_index("batch")
    device = seq_at * batches + batch_at
    streams, block, _ = tokens.shape
    rows = streams * block
    direct = (seqs, batches) == (8, 4)

    def inward(value):
        return value.reshape(streams, SEG, block // SEG, D).transpose(0, 2, 1, 3).reshape(rows, D)

    def outward(value):
        return value.reshape(streams, block // SEG, SEG, D).transpose(0, 2, 1, 3).reshape(streams, block, D)

    small_low = small_params.astype(bf16).astype(f32)
    if direct:
        z, x = seq_at // 2, seq_at % 2
        y, c = batch_at // 2, batch_at % 2
        piece = jnp.pad(small_low, (0, ROWS - small_low.shape[0]))[None]
        slabs = jnp.concatenate([piece] + [exchange(piece, 2 * k, 0) for k in range(1, 4)], axis=0)
        own = jnp.stack([slabs, exchange(slabs, 0, 2), exchange(slabs, 1, 0), exchange(slabs, 1, 2)])
        every = jnp.stack([own, exchange(own, 0, 1)])
        every = every.reshape(2, 2, 2, 2, 2, ROWS)
        for axis, bit in enumerate((c, x, y, z // 2, z % 2)):
            every = flip_by(every, axis, bit)
        small_used = every.transpose(3, 4, 1, 2, 0, 5)[..., : small_low.shape[0]].reshape(-1)
        mixer_own, mixer_par = gather_weights(mixer_weights.astype(bf16), 4)
        mlp_own, mlp_par = gather_weights(mlp_weights.astype(bf16), 4)
        bits = (x, y, c)
    else:
        z = jnp.zeros((), jnp.int32)
        small_used = lax.all_gather(small_low, AXES, axis=0, tiled=True)

        def gathered(shard):
            full = lax.all_gather(shard.astype(bf16), AXES, axis=0, tiled=True)
            full = full.reshape(ROLES, PLANES, 2, ROWS, D).transpose(2, 1, 0, 3, 4)
            return full[0], full[1]

        mixer_own, mixer_par = gathered(mixer_weights)
        mlp_own, mlp_par = gathered(mlp_weights)
        bits = (0, 0, 0)

    def reorder(value):
        if not direct:
            return value
        value = value.reshape(2, 2, 2, ROWS)
        for axis, bit in enumerate(bits):
            value = flip_by(value, axis, bit)
        return value.reshape(H)

    gain_one = small_used[:D][None]
    gain_two = small_used[D : 2 * D][None]
    forget_bias = reorder(small_used[2 * D : 2 * D + H])[None]
    input_bias = reorder(small_used[2 * D + H :])[None]
    z_arr = z.reshape(1).astype(jnp.int32)

    doc_ends = jnp.cumsum(doc_lengths, axis=1)
    doc_starts = doc_ends - doc_lengths
    place = lax.iota(jnp.int32, block)
    position = seq_at * block + (place % SEG) * (block // SEG) + place // SEG
    begins = jnp.any(position[None, :, None] == doc_starts[:, None, :], axis=2) | (
        position[None, :] == doc_ends[:, -1:]
    )
    valid = (position[None, :] < doc_ends[:, -1:]).astype(f32).reshape(rows, 1)
    restart = (1.0 - begins.astype(f32)).reshape(rows, 1)
    tok = inward(tokens)
    cot = inward(cotangent)

    width = H // PLANES
    wide = shape(rows, H)
    full = whole(rows, D)
    column = columns(rows, width)
    normed, forget, enter, cand, retain, acc, tot, sega, segb = pl.pallas_call(
        forward_kernel,
        grid=(PLANES,),
        in_specs=[SMEM, full, whole(rows, 1), whole(1, D), columns(1, width), columns(1, width), plane(), plane()],
        out_specs=[full, column, column, column, column, column, columns(4, width), columns(2 * SEG, width), columns(2 * SEG, width)],
        out_shape=[shape(rows, D, dtype=bf16), wide, wide, wide, wide, wide, shape(4, H), shape(2 * SEG, H), shape(2 * SEG, H)],
        compiler_params=PARAMS,
        name="gates_scan",
    )(z_arr, tok, restart, gain_one, forget_bias, input_bias, mixer_own, mixer_par)

    incoming = relay(tot, True, direct)

    states, resid, normed_two = pl.pallas_call(
        states_kernel,
        grid=(PLANES,),
        in_specs=[SMEM, columns(2, width), full, whole(1, D), column, column, columns(2 * SEG, width), columns(2 * SEG, width), plane(), plane()],
        out_specs=[column, full, full],
        out_shape=[wide, shape(rows, D), shape(rows, D, dtype=bf16)],
        compiler_params=PARAMS,
        name="states",
    )(z_arr, incoming, tok, gain_two, retain, acc, sega, segb, mixer_own, mixer_par)

    terms = shape(PLANES, ROLES, ROWS, D, dtype=bf16)
    output, d_resid, d_gain_two, mlp_gown, mlp_gpar = pl.pallas_call(
        mlp_kernel,
        grid=(2 * PLANES,),
        in_specs=[SMEM, full, full, full, whole(rows, 1), whole(1, D), plane(2), plane(2)],
        out_specs=[full, full, whole(1, D), plane(2), plane(2)],
        out_shape=[shape(rows, D, dtype=bf16), shape(rows, D), shape(1, D), terms, terms],
        scratch_shapes=[pltpu.VMEM((rows, D), bf16), pltpu.VMEM((rows, D), f32), pltpu.VMEM((rows, D), f32)],
        compiler_params=PARAMS,
        name="mlp",
    )(z_arr, normed_two, resid, cot, valid, gain_two, mlp_own, mlp_par)

    half_terms = shape(PLANES, ROWS, D, dtype=bf16)
    half_plane = pl.BlockSpec((1, ROWS, D), lambda i: (i, 0, 0))
    acc_back, tot_back, segb_back, out_gown, out_gpar = pl.pallas_call(
        back_kernel,
        grid=(PLANES,),
        in_specs=[SMEM, full, column, column, columns(2 * SEG, width), plane(), plane()],
        out_specs=[column, columns(4, width), columns(2 * SEG, width), half_plane, half_plane],
        out_shape=[wide, shape(4, H), shape(2 * SEG, H), half_terms, half_terms],
        scratch_shapes=[pltpu.VMEM((rows, D), bf16)],
        compiler_params=PARAMS,
        name="back_scan",
    )(z_arr, d_resid, states, retain, sega, mixer_own, mixer_par)

    arriving = relay(tot_back, False, direct)

    gate_gown, gate_gpar, d_fb, d_ib, d_gain_one, d_x = pl.pallas_call(
        gates_kernel,
        grid=(PLANES,),
        in_specs=[
            SMEM, columns(2, width), columns(2, width), column, columns(2 * SEG, width), columns(2 * SEG, width),
            column, column, column, column, column, whole(rows, 1), full, full, whole(1, D), full, plane(), plane(),
        ],
        out_specs=[plane(), plane(), columns(1, width), columns(1, width), whole(1, D), full],
        out_shape=[terms, terms, shape(1, H), shape(1, H), shape(1, D), shape(rows, D, dtype=bf16)],
        scratch_shapes=[pltpu.VMEM((rows, width), f32)] * 3 + [pltpu.VMEM((rows, D), f32)],
        compiler_params=PARAMS,
        name="gates_back",
    )(
        z_arr, arriving, incoming, acc_back, sega, segb_back, forget, enter, cand, retain, states,
        restart, normed, tok, gain_one, d_resid, mixer_own, mixer_par,
    )

    small_terms = jnp.concatenate([d_gain_one[0], d_gain_two[0], reorder(d_fb[0]), reorder(d_ib[0])])

    def with_out(gates, out):
        at = lax.broadcasted_iota(jnp.int32, (1, ROLES, 1, 1), 1) == (z ^ 3)
        return jnp.where(at, out[:, None], gates)

    mixer_gown = with_out(gate_gown, out_gown)
    mixer_gpar = with_out(gate_gpar, out_gpar)
    if direct:
        mlp_grad = reduce_terms(mlp_gown, mlp_gpar)
        mixer_grad = reduce_terms(mixer_gown, mixer_gpar)
    else:

        def scattered(own, par):
            full_terms = jnp.stack([own, par]).transpose(2, 1, 0, 3, 4).reshape(-1, D)
            return lax.psum_scatter(full_terms, AXES, scatter_dimension=0, tiled=True).astype(f32)

        mlp_grad = scattered(mlp_gown, mlp_gpar)
        mixer_grad = scattered(mixer_gown, mixer_gpar)
    small_count = small_params.shape[0]
    small_sum = all_sum(small_terms.reshape(-1, 128)).reshape(-1)
    small_grad = lax.dynamic_slice(small_sum, (device * small_count,), (small_count,))

    mixer_first_new, mixer_second_new, mixer_dir = moments(
        mixer_weights, mixer_grad, mixer_first, mixer_second, matrix_decay
    )
    mlp_first_new, mlp_second_new, mlp_dir = moments(
        mlp_weights, mlp_grad, mlp_first, mlp_second, matrix_decay
    )
    small_first_new, small_second_new, small_dir = moments(
        small_params, small_grad, small_first, small_second, 0.0
    )
    mixer_role = device * mixer_weights.shape[0] // H
    mlp_role = device * mlp_weights.shape[0] // FF
    small_at = device * small_count + lax.iota(jnp.int32, small_count)
    small_segment = (
        (small_at >= D).astype(jnp.int32)
        + (small_at >= 2 * D).astype(jnp.int32)
        + (small_at >= 2 * D + H).astype(jnp.int32)
    )
    small_hot = (small_segment[:, None] == lax.iota(jnp.int32, 4)[None, :]).astype(f32)

    def grouped(mixer_like, mlp_like, small_like):
        return jnp.concatenate(
            [
                jnp.where(lax.iota(jnp.int32, 4) == mixer_role, jnp.sum(mixer_like * mixer_like), 0.0),
                jnp.where(lax.iota(jnp.int32, 2) == mlp_role, jnp.sum(mlp_like * mlp_like), 0.0),
                jnp.sum(small_hot * (small_like * small_like)[:, None], axis=0),
            ]
        )

    squares = all_sum(
        jnp.stack(
            [grouped(mixer_weights, mlp_weights, small_params), grouped(mixer_dir, mlp_dir, small_dir)]
        )
    )
    tensor_norms = jnp.sqrt(squares)
    trust_ratios = tensor_norms[0] / (tensor_norms[1] + 1e-06)
    mixer_ratio = jnp.sum(jnp.where(lax.iota(jnp.int32, 4) == mixer_role, trust_ratios[:4], 0.0))
    mlp_ratio = jnp.sum(jnp.where(lax.iota(jnp.int32, 2) == mlp_role, trust_ratios[4:6], 0.0))
    small_rows = jnp.sum(small_hot * trust_ratios[None, 6:], axis=1)
    mixer_new = mixer_weights - learn_rate * mixer_ratio * mixer_dir
    mlp_new = mlp_weights - learn_rate * mlp_ratio * mlp_dir
    small_new = small_params - learn_rate * small_rows * small_dir
    return (
        outward(output),
        outward(d_x),
        mixer_grad,
        mlp_grad,
        small_grad,
        mixer_first_new,
        mixer_second_new,
        mlp_first_new,
        mlp_second_new,
        small_first_new,
        small_second_new,
        mixer_new,
        mlp_new,
        small_new,
        mixer_new.astype(bf16),
        mlp_new.astype(bf16),
        small_new.astype(bf16),
        tensor_norms,
        trust_ratios,
    )


def solution(mesh):
    shard = P(("seq", "batch"), None)
    shard_flat = P(("seq", "batch"))
    stream = P("batch", "seq", None)
    return jax.shard_map(
        on_device,
        mesh=mesh,
        in_specs=(
            stream, P("batch", None), stream, shard, shard, shard_flat,
            shard, shard, shard, shard, shard_flat, shard_flat,
        ),
        out_specs=(
            stream, stream, shard, shard, shard_flat, shard, shard, shard, shard, shard_flat, shard_flat,
            shard, shard, shard_flat, shard, shard, shard_flat, P(), P(),
        ),
        check_vma=False,
    )
```

```python
import functools

import jax
import jax.numpy as jnp
from jax import lax
from jax.experimental import pallas as pl
from jax.experimental.pallas import tpu as pltpu
from jax.sharding import PartitionSpec as P

D = 512
H = 1024
FF = 2048
STEP = 5
SEG = 8
ROWS = 128
PLANES = 4
HALF = PLANES * ROWS
GATES = 3
ROLES = 4
TAIL = 16
SMALL_BLOCKS = 3
Z, X, Y, CORE, SEQ, DEVICE, MIXER_ROLE, MLP_ROLE = range(8)

first_decay = 0.5
second_decay = 0.5
learn_rate = 0.25
matrix_decay = 0.01
moment_eps = 1e-06

f32 = jnp.float32
bf16 = jnp.bfloat16
AXES = ("seq", "batch")

PLANE_BITS = ((0, 0), (0, 2), (1, 0), (1, 2))


def dot_nt(a, b):
    return lax.dot_general(a, b, (((1,), (1,)), ((), ())), preferred_element_type=f32)


def dot_nn(a, b):
    return lax.dot_general(a, b, (((1,), (0,)), ((), ())), preferred_element_type=f32)


def dot_tn(a, b):
    return lax.dot_general(a, b, (((0,), (0,)), ((), ())), preferred_element_type=f32)


def exchange(value, seq_bits, batch_bits, targets=None):
    seqs, batches = lax.axis_size("seq"), lax.axis_size("batch")
    pairs = [
        (s * batches + b, (s ^ seq_bits) * batches + (b ^ batch_bits))
        for s in range(seqs)
        for b in range(batches)
        if targets is None or (s ^ seq_bits) in targets
    ]
    return lax.ppermute(value, AXES, pairs)


def unit(x):
    return lax.rsqrt(jnp.mean(x * x, axis=-1, keepdims=True) + 1e-05)


def rms_back(x, d_normed, gain):
    scale = unit(x)
    normal = x * scale
    d_unit = d_normed * gain
    mean = jnp.mean(d_unit * normal, axis=-1, keepdims=True)
    return jnp.sum(d_normed * normal, axis=0, keepdims=True), scale * (d_unit - normal * mean)


def rows_of(slabs, role):
    return jnp.concatenate([ref[role] for ref in slabs], axis=0)


def group(s, steps, j):
    return pl.ds(pl.multiple_of((s * steps + j) * SEG, SEG), SEG)


def pair(s, steps, j):
    return pl.ds(pl.multiple_of((s * steps + 2 * j) * SEG, 2 * SEG), 2 * SEG)


def segment_order(block):
    row = lax.broadcasted_iota(jnp.int32, (block, block), 0)
    position = lax.broadcasted_iota(jnp.int32, (block, block), 1)
    return jnp.where(position == (row % SEG) * (block // SEG) + row // SEG, 1.0, 0.0).astype(bf16)


def inward(ref):
    order = segment_order(ref.shape[1])
    return jnp.concatenate([dot_nn(order, ref[s]) for s in range(2)], axis=0)


def outward(ref, value):
    block = ref.shape[1]
    order = segment_order(block)
    for s in range(2):
        ref[s] = dot_tn(order, value[s * block : (s + 1) * block]).astype(bf16)


def slab_kernel(ids_ref, p0, p1, p2, p3, *refs):
    z = ids_ref[Z]
    for k, ref in enumerate((p0, p1, p2, p3)):
        refs[-1][pl.ds(z ^ k, 1)] = ref[...].reshape(1, ROWS, D)


def relay_kernel(bit, forward, flipped, ids_ref, group_ref, other_ref, *refs):
    late = ((ids_ref[SEQ] & bit) != 0) == forward
    mine, other = group_ref[...], other_ref[...]
    if flipped:
        quarter = HALF // 2
        at = (quarter, 0, 3 * quarter, 2 * quarter)
        other = jnp.concatenate([other[:, k : k + quarter] for k in at], axis=1)
    if bit == 1:
        decay, state = jnp.ones_like(mine[:2]), jnp.zeros_like(mine[:2])
    else:
        decay, state = refs[0][0:2, :], refs[0][2:4, :]
    state = jnp.where(late, decay * other[2:] + state, state)
    if refs[-1].shape[0] == 2:
        refs[-1][...] = state
        return
    group_out, before_out = refs[-2:]
    before_out[...] = jnp.concatenate([jnp.where(late, decay * other[:2], decay), state], axis=0)
    first, second = jnp.where(late, other, mine), jnp.where(late, mine, other)
    group_out[...] = jnp.concatenate([first[:2] * second[:2], second[:2] * first[2:] + second[2:]], axis=0)


def gate_shares(f, i):
    most = jnp.maximum(jnp.maximum(-f, -i), 0.0)
    one, low_f, low_i = jnp.exp(-most), jnp.exp(-f - most), jnp.exp(-i - most)
    inverse = 1.0 / ((one + low_i) + (one + low_f))
    return (one + low_i) * inverse, (one + low_f) * inverse, low_f * inverse, low_i * inverse


def first_norm(tok_ref, gain_ref):
    x = inward(tok_ref)
    return (x * unit(x) * gain_ref[...]).astype(bf16)


def scan_kernel(first, *refs):
    if first:
        tok_ref, gain_ref, rs_ref, fb_ref, ib_ref, *refs = refs
        slabs, refs = refs[:PLANES], refs[-9:]
        normed_ref, *refs = refs
        normed_ref[...] = first_norm(tok_ref, gain_ref)
    else:
        normed_ref, earlier_ref, rs_ref, fb_ref, ib_ref, *refs = refs
        slabs, refs = refs[:PLANES], refs[-8:]
    retain_ref, acc_ref, tot_ref, sega_ref, segb_ref, f_ref, i_ref, c_ref = refs
    normed = normed_ref[...]
    for role, ref in enumerate((f_ref, i_ref, c_ref)):
        ref[...] = dot_nt(normed, rows_of(slabs, role))
    steps = normed.shape[0] // (2 * SEG)
    f_bias, i_bias = fb_ref[...], ib_ref[...]

    def step(j, carry):
        after = []
        for s in range(2):
            at = group(s, steps, j)
            keep, share, _, _ = gate_shares(f_ref[at, :] + f_bias, i_ref[at, :] + i_bias)
            a = keep * rs_ref[at, :]
            b = a * carry[s][1] + share * c_ref[at, :]
            retain_ref[at, :] = a
            acc_ref[at, :] = b
            after.append((a * carry[s][0], b))
        return tuple(after)

    start = (jnp.ones((SEG, HALF), f32), jnp.zeros((SEG, HALF), f32))
    ends = lax.fori_loop(0, steps, step, (start, start), unroll=2)
    columns = pl.ds(0 if first else HALF, HALF)
    if not first:
        tot_ref[:, pl.ds(0, HALF)] = earlier_ref[...]
    for s, (seg_a, seg_b) in enumerate(ends):
        sega_ref[pl.ds(s * SEG, SEG), :] = seg_a
        segb_ref[pl.ds(s * SEG, SEG), :] = seg_b
        tot_a, tot_b = seg_a[0:1], seg_b[0:1]
        for k in range(1, SEG):
            a = seg_a[k : k + 1]
            tot_a, tot_b = a * tot_a, a * tot_b + seg_b[k : k + 1]
        tot_ref[pl.ds(s, 1), columns] = tot_a
        tot_ref[pl.ds(2 + s, 1), columns] = tot_b


def terms_kernel(first, *refs):
    if first:
        tok_ref, gain_ref, fb_ref, ib_ref, *refs = refs
        slabs, refs = refs[:PLANES], refs[-7:]
        normed_ref, *refs = refs
        normed_ref[...] = first_norm(tok_ref, gain_ref)
    else:
        normed_ref, fb_ref, ib_ref, *refs = refs
        slabs, refs = refs[:PLANES], refs[-6:]
    share_ref, df_ref, di_ref, cand_ref, f_ref, i_ref = refs
    normed = normed_ref[...]
    for role, ref in enumerate((f_ref, i_ref, cand_ref)):
        ref[...] = dot_nt(normed, rows_of(slabs, role))
    f_bias, i_bias = fb_ref[...], ib_ref[...]

    def step(j, carry):
        at = pl.ds(pl.multiple_of(j * 2 * SEG, 2 * SEG), 2 * SEG)
        keep, share, slow_f, slow_i = gate_shares(f_ref[at, :] + f_bias, i_ref[at, :] + i_bias)
        share_ref[at, :] = share
        df_ref[at, :] = keep * slow_f
        di_ref[at, :] = share * slow_i
        return carry

    lax.fori_loop(0, normed.shape[0] // (2 * SEG), step, 0, unroll=2)


def states_kernel(
    inc_ref, tok_ref, gain_ref, retain_o, retain_p, acc_o, acc_p, sega_o, sega_p, segb_o, segb_p, *refs
):
    slabs, refs = refs[: 2 * PLANES], refs[2 * PLANES :]
    states_o, states_p, low_o, low_p, resid_ref, normed_ref = refs
    steps = resid_ref.shape[0] // (2 * SEG)
    halves = (
        (retain_o, acc_o, sega_o, segb_o, states_o, low_o, 0),
        (retain_p, acc_p, sega_p, segb_p, states_p, low_p, HALF),
    )
    start = []
    for _, _, sega, segb, _, _, column in halves:
        for s in range(2):
            seg_a, seg_b = sega[pl.ds(s * SEG, SEG), :], segb[pl.ds(s * SEG, SEG), :]
            at_seg = [inc_ref[pl.ds(s, 1), pl.ds(column, HALF)]]
            for k in range(SEG - 1):
                at_seg.append(seg_a[k : k + 1] * at_seg[-1] + seg_b[k : k + 1])
            start.append(jnp.concatenate(at_seg, axis=0))

    def step(j, carry):
        after = []
        for k, (retain, acc, _, _, states, low, _) in enumerate(halves):
            for s in range(2):
                carried, two = carry[2 * k + s], []
                for q in range(2):
                    at = group(s, steps, 2 * j + q)
                    carried = retain[at, :] * carried
                    two.append(acc[at, :] + carried)
                    states[at, :] = two[-1]
                low[pair(s, steps, j), :] = jnp.concatenate(two, axis=0).astype(bf16)
                after.append(carried)
        return tuple(after)

    lax.fori_loop(0, steps // 2, step, tuple(start))
    r = (
        inward(tok_ref)
        + dot_nn(low_o[...], rows_of(slabs[:PLANES], GATES))
        + dot_nn(low_p[...], rows_of(slabs[PLANES:], GATES))
    )
    resid_ref[...] = r
    normed_ref[...] = (r * unit(r) * gain_ref[...]).astype(bf16)


GELU_A = 0.7978845608028654
GELU_B = 0.044715


def mlp_kernel(normed_ref, resid_ref, cot_ref, valid_ref, gain_ref, *refs):
    slabs, refs = refs[: 2 * PLANES], refs[2 * PLANES :]
    output_ref, dresid_ref, dgain_ref, gown_ref, gpar_ref, held, sems, dout_ref, outer_ref, dnorm_ref = refs
    for k, ref in enumerate(slabs):
        at = (k % PLANES, k // PLANES)
        pltpu.make_async_copy(ref, held.at[at], sems.at[at]).start()
    dout_ref[...] = (inward(cot_ref) * valid_ref[...]).astype(bf16)
    outer_ref[...] = jnp.zeros_like(outer_ref)
    dnorm_ref[...] = jnp.zeros_like(dnorm_ref)

    def step(i, carry):
        at, low = i // 2, i % 2

        @pl.when(low == 0)
        def _():
            for k in range(2):
                pltpu.make_async_copy(slabs[0], held.at[at, k], sems.at[at, k]).wait()

        normed = normed_ref[...]
        dout = dout_ref[...]
        w_up = held[at, :, low].reshape(2 * ROWS, D)
        w_down = held[at, :, low + 2].reshape(2 * ROWS, D)
        inner = dot_nt(normed, w_up)
        square = inner * inner
        curve = jnp.tanh(GELU_A * inner * (1.0 + GELU_B * square))
        half = 0.5 * (1.0 + curve)
        activated = (inner * half).astype(bf16)
        slope = half + 0.5 * inner * (1.0 - curve * curve) * (GELU_A * (1.0 + 3.0 * GELU_B * square))
        d_inner = (slope * dot_nt(dout, w_down)).astype(bf16)
        outer_ref[...] += dot_nn(activated, w_down)
        dnorm_ref[...] += dot_nn(d_inner, w_up)
        g_up = dot_tn(d_inner, normed).astype(bf16).reshape(2, 1, ROWS, D)
        g_down = dot_tn(activated, dout).astype(bf16).reshape(2, 1, ROWS, D)
        for k, ref in enumerate((gown_ref, gpar_ref)):
            ref[at, pl.ds(low, 1)] = g_up[k]
            ref[at, pl.ds(low + 2, 1)] = g_down[k]
        return carry

    lax.fori_loop(0, 2 * PLANES, step, 0)
    r = resid_ref[...]
    outward(output_ref, ((r + outer_ref[...]) * valid_ref[...]).astype(bf16))
    dgain_ref[...], d_r = rms_back(r, dnorm_ref[...], gain_ref[...])
    dresid_ref[...] = dout_ref[...].astype(f32) + d_r


def back_kernel(dresid_ref, low_o, low_p, retain_o, retain_p, sega_o, sega_p, *refs):
    slabs, refs = refs[: 2 * PLANES], refs[2 * PLANES :]
    acc_o, acc_p, tot_ref, segb_o, segb_p, gown_ref, gpar_ref = refs
    steps = dresid_ref.shape[0] // (2 * SEG)
    dmix = dresid_ref[...].astype(bf16)
    acc_o[...] = dot_nt(dmix, rows_of(slabs[:PLANES], GATES))
    acc_p[...] = dot_nt(dmix, rows_of(slabs[PLANES:], GATES))
    halves = ((retain_o, acc_o), (retain_p, acc_p))

    def step(n, carry):
        after = []
        for k, (retain, acc) in enumerate(halves):
            for s in range(2):
                at = group(s, steps, steps - 1 - n)
                back = acc[at, :] + carry[2 * k + s]
                acc[at, :] = back
                after.append(retain[at, :] * back)
        return tuple(after)

    ends = lax.fori_loop(0, steps, step, (jnp.zeros((SEG, HALF), f32),) * 4, unroll=2)
    for k, (sega, segb) in enumerate(((sega_o, segb_o), (sega_p, segb_p))):
        for s in range(2):
            emitted = ends[2 * k + s]
            segb[pl.ds(s * SEG, SEG), :] = emitted
            seg_a = sega[pl.ds(s * SEG, SEG), :]
            tot_a, tot_b = seg_a[SEG - 1 :], emitted[SEG - 1 :]
            for q in reversed(range(SEG - 1)):
                a = seg_a[q : q + 1]
                tot_a, tot_b = a * tot_a, a * tot_b + emitted[q : q + 1]
            tot_ref[pl.ds(s, 1), pl.ds(k * HALF, HALF)] = tot_a
            tot_ref[pl.ds(2 + s, 1), pl.ds(k * HALF, HALF)] = tot_b
    for low, ref in ((low_o, gown_ref), (low_p, gpar_ref)):
        ref[...] = dot_tn(low[...], dmix).astype(bf16).reshape(PLANES, 1, ROWS, D)


def gates_kernel(
    column, arr_ref, inc_ref, acc_ref, sega_ref, segb_ref, share_ref, df_ref, di_ref, cand_ref, retain_ref, states_ref,
    rs_ref, normed_ref, order_ref, grad_ref, pf_ref, pi_ref, pc_ref, dfb_ref, dib_ref,
):
    steps = normed_ref.shape[0] // (2 * SEG)
    start, first = [], []
    for s in range(2):
        seg_a, seg_b = sega_ref[pl.ds(s * SEG, SEG), :], segb_ref[pl.ds(s * SEG, SEG), :]
        at_seg = [arr_ref[pl.ds(s, 1), pl.ds(column, HALF)]]
        for k in reversed(range(1, SEG)):
            at_seg.append(seg_a[k : k + 1] * at_seg[-1] + seg_b[k : k + 1])
        start.append(jnp.concatenate(at_seg[::-1], axis=0))
        ends = states_ref[group(s, steps, steps - 1), :]
        first.append(jnp.concatenate([inc_ref[pl.ds(s, 1), pl.ds(column, HALF)], ends[: SEG - 1]], axis=0))

    def step(n, carry):
        *carried, sum_f, sum_i = carry
        m = steps // 2 - 1 - n
        for s in range(2):
            terms = []
            for q in (1, 0):
                j = 2 * m + q
                at = group(s, steps, j)
                back = acc_ref[at, :] + carried[s]
                carried[s] = carried[s] * retain_ref[at, :]
                previous = states_ref[group(s, steps, jnp.maximum(j - 1, 0)), :]
                if q == 0:
                    previous = jnp.where(m == 0, first[s], previous)
                both_ways = back * (previous * rs_ref[at, :] - cand_ref[at, :])
                d_f = both_ways * df_ref[at, :]
                d_i = both_ways * di_ref[at, :]
                sum_f = sum_f + d_f
                sum_i = sum_i - d_i
                terms.append((d_f, -d_i, back * share_ref[at, :]))
            for late, early, ref in zip(*terms, (pf_ref, pi_ref, pc_ref), strict=True):
                ref[pair(s, steps, m), :] = jnp.concatenate([early, late], axis=0).astype(bf16)
        return (*carried, sum_f, sum_i)

    nothing = jnp.zeros((SEG, HALF), f32)
    *_, sum_f, sum_i = lax.fori_loop(0, steps // 2, step, (*start, nothing, nothing))
    dfb_ref[...] = jnp.sum(sum_f, axis=0, keepdims=True)
    dib_ref[...] = jnp.sum(sum_i, axis=0, keepdims=True)
    normed = normed_ref[...]
    for role, ref in enumerate((pf_ref, pi_ref, pc_ref)):
        grad_ref[:, role] = dot_tn(ref[...], normed).astype(bf16).reshape(PLANES, ROWS, D)


def input_kernel(ids_ref, tok_ref, gain_ref, dresid_ref, dgain_two_ref, dfb_o, dfb_p, dib_o, dib_p, *refs):
    terms, slabs, refs = refs[: 2 * GATES], refs[2 * GATES : 2 * GATES + 2 * PLANES], refs[-3:]
    dx_ref, small_ref, rows_ref = refs
    d_normed = 0.0
    for k in range(2):
        for role in range(GATES):
            weights = rows_of(slabs[k * PLANES : (k + 1) * PLANES], role)
            d_normed = d_normed + dot_nn(terms[k * GATES + role][...], weights)
    d_gain, d_x = rms_back(inward(tok_ref), d_normed, gain_ref[...])
    outward(dx_ref, (dresid_ref[...] + d_x).astype(bf16))
    for k in range(PLANES):
        rows_ref[pl.ds(k, 1), :] = d_gain[:, k * ROWS : (k + 1) * ROWS]
        rows_ref[pl.ds(PLANES + k, 1), :] = dgain_two_ref[:, pl.ds(k * ROWS, ROWS)]
        chip = 4 * (ids_ref[X] ^ (k // 2)) + 2 * (ids_ref[Y] ^ (k % 2))
        for core, (fb, ib) in enumerate(((dfb_o, dib_o), (dfb_p, dib_p))):
            row = 2 * PLANES + chip + (ids_ref[CORE] ^ core)
            rows_ref[pl.ds(row, 1), :] = fb[:, pl.ds(k * ROWS, ROWS)]
            rows_ref[pl.ds(row + 2 * PLANES, 1), :] = ib[:, pl.ds(k * ROWS, ROWS)]
    blocks = [rows_ref[pl.ds(k * SEG, SEG), :] for k in range(SMALL_BLOCKS)] + [jnp.zeros((SEG, ROWS), f32)]
    small_ref[...] = jnp.concatenate([jnp.concatenate(blocks, axis=1), jnp.zeros((SEG, D), f32)], axis=0)


def mlp_pair_kernel(ids_ref, own_ref, got_ref, out_ref, outgot_ref, *refs):
    core = ids_ref[CORE]
    for k in range(PLANES):
        ref = refs[-2 + k // 2]
        ref[k % 2, pl.ds(0, ROLES)] = (own_ref[k].astype(f32) + got_ref[k].astype(f32)).astype(bf16)
        at = pl.ds(jnp.where(core == 0, 3 - k, k) if k in (1, 2) else k, 1)
        ref[k % 2, pl.ds(ROLES, 1)] = (out_ref[at, 0].astype(f32) + outgot_ref[at, 0].astype(f32)).astype(bf16)


def gate_pair_kernel(own_ref, got_ref, small_ref, small_got, *outs):
    small = (small_ref[...] + small_got[...]).astype(bf16)
    for k, ref in enumerate(outs[-PLANES:]):
        total = (own_ref[k].astype(f32) + got_ref[k].astype(f32)).astype(bf16)
        ref[pl.ds(0, GATES * ROWS), :] = total.reshape(GATES * ROWS, D)
        ref[pl.ds(GATES * ROWS, TAIL), :] = small


def half_sum_kernel(own_ref, got_ref, *refs):
    for k, ref in enumerate(refs[-2:]):
        ref[...] = (own_ref[k].astype(f32) + got_ref[k].astype(f32)).astype(bf16)


def mlp_plane_kernel(ids_ref, own_ref, got_ref, keep_ref, send_ref, out_ref):
    z = ids_ref[Z]
    near_bit = jnp.where(ids_ref[CORE] == 0, 1, 2)

    def total(role):
        at = pl.ds(role, 1)
        return (own_ref[at].astype(f32) + got_ref[at].astype(f32)).astype(bf16).reshape(ROWS, D)

    for k, role in enumerate((z, z ^ near_bit ^ 3)):
        keep_ref[k] = total(role)
        send_ref[k] = total(role ^ near_bit)
    out_ref[...] = total(ROLES)


def mlp_far_kernel(keep_ref, got_ref, *refs):
    stay_ref, send_ref = refs[-2:]
    stay_ref[...] = keep_ref[0].astype(f32) + got_ref[0].astype(f32)
    send_ref[...] = (keep_ref[1].astype(f32) + got_ref[1].astype(f32)).astype(bf16)


def gate_plane_kernel(ids_ref, p0, p1, p2, p3, out_ref, *refs):
    z = ids_ref[Z]
    keep_ref, s1_ref, s2_ref, s3_ref = refs[-4:]

    def total(at):
        terms = [ref[at, :].astype(f32) for ref in (p0, p1, p2, p3)]
        return (terms[0] + terms[1]) + (terms[2] + terms[3])

    def of_role(role):
        at = pl.ds(pl.multiple_of(jnp.minimum(role, GATES - 1) * ROWS, ROWS), ROWS)
        return jnp.where(role == GATES, out_ref[...].astype(f32), total(at))

    small = total(pl.ds(GATES * ROWS, TAIL))
    keep_ref[pl.ds(0, ROWS), :] = of_role(z)
    keep_ref[pl.ds(ROWS, TAIL), :] = small
    for k, ref in enumerate((s1_ref, s2_ref, s3_ref)):
        ref[pl.ds(0, ROWS), :] = of_role(z ^ (k + 1)).astype(bf16)
        ref[pl.ds(ROWS, TAIL), :] = small.astype(bf16)


def joined(at, keep_ref, gots):
    total = keep_ref[at, :]
    for ref in gots:
        total = total + ref[at, :].astype(f32)
    return total


def moments_kernel(keep_ref, *refs):
    *gots, weight_ref, first_ref, second_ref, grad_ref, first_out, second_out, dir_ref, wsum_ref, dsum_ref = refs
    weight = weight_ref[...]
    gradient = joined(pl.ds(0, weight.shape[0]), keep_ref, gots)
    grad_ref[...] = gradient
    first_out[...], second_out[...], direction = moments(
        weight, gradient, first_ref[...], second_ref[...], matrix_decay
    )
    dir_ref[...] = direction
    for ref, value in ((wsum_ref, weight), (dsum_ref, direction)):
        square = jnp.sum((value * value).reshape(-1, SEG, D), axis=0)
        ref[...] = (square[:, :128] + square[:, 128:256]) + (square[:, 256:384] + square[:, 384:])


def small_kernel(
    ids_ref, keep_ref, g1_ref, g2_ref, g3_ref, wsum_m, dsum_m, wsum_f, dsum_f, weight_ref, first_ref, second_ref,
    grad_ref, first_out, second_out, dir_ref, squares_ref, rows_ref,
):
    total = joined(pl.ds(keep_ref.shape[0] - TAIL, TAIL), keep_ref, (g1_ref, g2_ref, g3_ref))
    rows_ref[...] = jnp.zeros_like(rows_ref)
    for k in range(SMALL_BLOCKS):
        rows_ref[pl.ds(k * SEG, SEG), :] = total[:SEG, k * ROWS : (k + 1) * ROWS]
    weight = weight_ref[...]
    count = weight.shape[1]
    start = ids_ref[DEVICE] * count
    row, lane = start // ROWS, start % ROWS
    two = jnp.concatenate([rows_ref[pl.ds(row, 1), :], rows_ref[pl.ds(row + 1, 1), :]], axis=1)
    two = jnp.broadcast_to(two, (SEG, 2 * ROWS))
    gradient = pltpu.roll(two, 2 * ROWS - lane, 1)[:1, :count]
    grad_ref[...] = gradient
    first_out[...], second_out[...], direction = moments(weight, gradient, first_ref[...], second_ref[...], 0.0)
    dir_ref[...] = direction
    place = start + lax.broadcasted_iota(jnp.int32, (1, count), 1)
    at = lax.broadcasted_iota(jnp.int32, (1, ROWS), 1)
    bounds = (0, D, 2 * D, 2 * D + H, 2 * D + 2 * H)
    lines = []
    for mixer_sum, mlp_sum, value in ((wsum_m, wsum_f, weight), (dsum_m, dsum_f, direction)):
        line = jnp.where(at == ids_ref[MIXER_ROLE], jnp.sum(mixer_sum[...], keepdims=True), 0.0)
        line = line + jnp.where(at == ROLES + ids_ref[MLP_ROLE], jnp.sum(mlp_sum[...], keepdims=True), 0.0)
        for k in range(4):
            inside = (place >= bounds[k]) & (place < bounds[k + 1])
            part = jnp.sum(jnp.where(inside, value * value, 0.0), axis=1, keepdims=True)
            line = line + jnp.where(at == ROLES + 2 + k, part, 0.0)
        lines.append(line)
    squares_ref[...] = jnp.concatenate(lines + [jnp.zeros((SEG - 2, ROWS), f32)], axis=0)


def update_kernel(
    ids_ref, squares_ref, mixer_ref, mixer_dir, mlp_ref, mlp_dir, small_ref, small_dir,
    mixer_new, mlp_new, small_new, mixer_copy, mlp_copy, small_copy, norms_ref, ratios_ref,
):
    norms = jnp.sqrt(squares_ref[0:2, :])
    ratios = norms[0:1] / (norms[1:2] + 1e-06)
    norms_ref[...] = norms[:, : norms_ref.shape[1]]
    ratios_ref[...] = ratios[:, : ratios_ref.shape[1]]
    at = lax.broadcasted_iota(jnp.int32, (1, ROWS), 1)

    def of(tensor):
        return jnp.sum(jnp.where(at == tensor, ratios, 0.0), axis=1, keepdims=True)

    count = small_ref.shape[1]
    place = ids_ref[DEVICE] * count + lax.broadcasted_iota(jnp.int32, (1, count), 1)
    small_ratio = jnp.where(
        place < 2 * D,
        jnp.where(place < D, of(ROLES + 2), of(ROLES + 3)),
        jnp.where(place < 2 * D + H, of(ROLES + 4), of(ROLES + 5)),
    )
    for ratio, weight, direction, new, copy in (
        (of(ids_ref[MIXER_ROLE]), mixer_ref, mixer_dir, mixer_new, mixer_copy),
        (of(ROLES + ids_ref[MLP_ROLE]), mlp_ref, mlp_dir, mlp_new, mlp_copy),
        (small_ratio, small_ref, small_dir, small_new, small_copy),
    ):
        value = weight[...] - learn_rate * ratio * direction[...]
        new[...] = value
        copy[...] = value.astype(bf16)


SMEM = pl.BlockSpec(memory_space=pltpu.SMEM)
ANY = pl.BlockSpec(memory_space=pl.ANY)
VMEM = pl.BlockSpec(memory_space=pltpu.VMEM)


def shape(*dims, dtype=f32):
    return jax.ShapeDtypeStruct(dims, dtype)


def near(*dims, dtype=f32):
    return pltpu.VMEM(dims, dtype)


def kept(value):
    return pltpu.with_memory_space_constraint(value, pltpu.VMEM)


def call(kernel, name, out_shape, *args, order=(), far=(), scratch=(), mib=8):
    in_specs = [SMEM if arg.dtype == jnp.int32 else VMEM for arg in args] + [ANY] * (len(far) + len(order))
    return pl.pallas_call(
        kernel,
        in_specs=in_specs,
        out_specs=jax.tree.map(lambda _: VMEM, out_shape),
        out_shape=out_shape,
        scratch_shapes=list(scratch),
        compiler_params=pltpu.CompilerParams(vmem_limit_bytes=mib * 1024 * 1024),
        name=name,
    )(*[arg if arg.dtype == jnp.int32 else kept(arg) for arg in args], *far, *order)


def exchange_lane(value, second):
    seqs, batches = lax.axis_size("seq"), lax.axis_size("batch")
    pairs = []
    for s in range(seqs):
        for b in range(batches):
            over_x = (b % 2 == 0) != second
            pairs.append((s * batches + b, (s ^ 1) * batches + b if over_x else s * batches + (b ^ 2)))
    return lax.ppermute(value, AXES, pairs)


def exchange_z_lane(value, second):
    seqs, batches = lax.axis_size("seq"), lax.axis_size("batch")
    pairs = []
    for s in range(seqs):
        for b in range(batches):
            bit = 2 if (b % 2 == 0) != second else 4
            pairs.append((s * batches + b, (s ^ bit) * batches + b))
    return lax.ppermute(value, AXES, pairs)


def after(value, *others):
    return lax.optimization_barrier((value, *others))[0]


def over_z(shard):
    return [shard] + [exchange(shard, 2 * k, 0) for k in range(1, 4)]


def z_terms(sends):
    return [exchange(sent, 2 * (k + 1), 0) for k, sent in enumerate(sends)]


def all_sum(value):
    seqs, batches = lax.axis_size("seq"), lax.axis_size("batch")
    bit = 1
    while bit < batches:
        value = value + exchange(value, 0, bit)
        bit *= 2
    bit = 1
    while bit < seqs:
        value = value + exchange(value, bit, 0)
        bit *= 2
    return value


def relay(ids, total, forward, flipped, beside):
    group, before, bit = total, [], 1
    joint = near(4, H)
    while bit < lax.axis_size("seq"):
        last = 2 * bit == lax.axis_size("seq")
        other = exchange(group, bit, 0)
        order = [beside[bit](group)] if bit in beside else []
        got = call(
            functools.partial(relay_kernel, bit, forward, flipped and bit == 1),
            f"relay_{bit}", near(2, H) if last else [joint, joint],
            ids, group, other, *before, order=order,
        )
        if not last:
            group, before = got[0], [got[1]]
        bit *= 2
    return got


def flip_by(value, axis, bit):
    return jnp.where(bit == 1, jnp.flip(value, axis), value)


def moments(weight, gradient, first_moment, second, decay_rate):
    first_new = first_decay * first_moment + (1.0 - first_decay) * gradient
    second_new = second_decay * second + (1.0 - second_decay) * gradient * gradient
    direction = (
        first_new
        / (1.0 - first_decay**STEP)
        / (jnp.sqrt(second_new / (1.0 - second_decay**STEP)) + moment_eps)
        + decay_rate * weight
    )
    return (first_new, second_new, direction)


def on_device(
    tokens, doc_lengths, cotangent, mixer_weights, mlp_weights, small_params,
    mixer_first, mixer_second, mlp_first, mlp_second, small_first, small_second,
):
    seqs, batches = lax.axis_size("seq"), lax.axis_size("batch")
    seq_at, batch_at = lax.axis_index("seq"), lax.axis_index("batch")
    device = seq_at * batches + batch_at
    streams, block, _ = tokens.shape
    rows = streams * block
    direct = (seqs, batches) == (8, 4)
    if direct:
        z, x, y, c = seq_at // 2, seq_at % 2, batch_at // 2, batch_at % 2
    else:
        z = x = y = c = jnp.zeros((), jnp.int32)
    mixer_role = device * mixer_weights.shape[0] // H
    mlp_role = device * mlp_weights.shape[0] // FF
    ids = jnp.stack([z, x, y, c, seq_at, device, mixer_role, mlp_role]).astype(jnp.int32)

    small_low = small_params.astype(bf16).astype(f32)
    slab = near(ROLES, ROWS, D, dtype=bf16)
    if direct:
        mixer_pieces = over_z(mixer_weights.astype(bf16))
        mixer_slab = call(slab_kernel, "mixer_slab", slab, ids, *mixer_pieces)
        mixer_own = [mixer_slab] + [exchange(mixer_slab, *bits) for bits in PLANE_BITS[1:]]
        mixer_par = [exchange(part, 0, 1) for part in mixer_own]
        small_all = jnp.pad(small_low, (0, ROWS - small_low.shape[0]))[None]
        for bits in ((0, 1), (0, 2), (1, 0), (2, 0), (4, 0)):
            small_all = jnp.concatenate([small_all, exchange(small_all, *bits)], axis=0)
        small_all = small_all.reshape(2, 2, 2, 2, 2, ROWS)
        for axis, bit in enumerate((z // 2, z % 2, x, y, c)):
            small_all = flip_by(small_all, axis, bit)
        small_used = small_all[..., : small_low.shape[0]].reshape(-1)
        mlp_pieces = over_z(after(mlp_weights.astype(bf16), *mixer_pieces[1:]))
        mlp_slab = call(slab_kernel, "mlp_slab", slab, ids, *mlp_pieces, order=mixer_own[1:])
        mlp_near = exchange_lane(mlp_slab, False)
        mlp_order = mlp_slab
    else:
        small_used = lax.all_gather(small_low, AXES, axis=0, tiled=True)

        def gathered(shard):
            full = lax.all_gather(shard.astype(bf16), AXES, axis=0, tiled=True)
            full = full.reshape(ROLES, PLANES, 2, ROWS, D)
            return [[full[:, p, k] for p in range(PLANES)] for k in range(2)]

        mixer_own, mixer_par = gathered(mixer_weights)
        mlp_own, mlp_par = gathered(mlp_weights)
        mlp_order = mlp_own[0]

    def channels_in(value):
        value = value.reshape(2, 2, 2, ROWS)
        if direct:
            for axis, bit in enumerate((x, y, c)):
                value = flip_by(value, axis, bit)
        return value.transpose(2, 0, 1, 3).reshape(2, 1, HALF)

    gain_one = small_used[:D][None]
    gain_two = small_used[D : 2 * D][None]
    forget_bias = channels_in(small_used[2 * D : 2 * D + H])
    input_bias = channels_in(small_used[2 * D + H :])

    doc_ends = jnp.cumsum(doc_lengths, axis=1)
    doc_starts = doc_ends - doc_lengths
    place = lax.iota(jnp.int32, block)
    position = seq_at * block + (place % SEG) * (block // SEG) + place // SEG
    begins = jnp.any(position[None, :, None] == doc_starts[:, None, :], axis=2) | (
        position[None, :] == doc_ends[:, -1:]
    )
    valid = (position[None, :] < doc_ends[:, -1:]).astype(f32).reshape(rows, 1)
    restart = (1.0 - begins.astype(f32)).reshape(rows, 1)

    wide = near(rows, HALF)
    natural = shape(streams, block, D, dtype=bf16)
    low_wide = near(rows, HALF, dtype=bf16)
    low_rows = near(rows, D, dtype=bf16)
    ends = near(2 * SEG, HALF)
    projections = [pltpu.VMEM((rows, HALF), f32)] * 3

    normed, retain_o, acc_o, tot_o, sega_o, segb_o = call(
        lambda *refs: scan_kernel(True, *refs), "scan_own", [low_rows, wide, wide, near(4, HALF), ends, ends],
        tokens, gain_one, restart, forget_bias[0], input_bias[0], *mixer_own,
        order=[mlp_order, valid], scratch=projections,
    )
    retain_p, acc_p, tot, sega_p, segb_p = call(
        lambda *refs: scan_kernel(False, *refs), "scan_other", [wide, wide, near(4, H), ends, ends],
        normed, tot_o, restart, forget_bias[1], input_bias[1], *mixer_par, scratch=projections,
    )

    if direct:
        tot = after(tot, mlp_near)
        mlp_far = [exchange_lane(part, True) for part in after((mlp_slab, mlp_near), tot)]
    incoming = relay(ids, tot, True, direct, {})
    if direct:
        mlp_far = after(tuple(mlp_far), incoming)
        mlp_own = [mlp_slab, mlp_near, *mlp_far]
        mlp_par = [exchange(part, 0, 1) for part in mlp_own]

    states_o, states_p, low_o, low_p, resid, normed_two = call(
        states_kernel, "states", [wide, wide, low_wide, low_wide, near(rows, D), low_rows],
        incoming, tokens, gain_two, retain_o, retain_p, acc_o, acc_p, sega_o, sega_p, segb_o, segb_p,
        *mixer_own, *mixer_par,
    )

    terms = near(PLANES, ROLES, ROWS, D, dtype=bf16)
    output, d_resid, d_gain_two, mlp_gown, mlp_gpar = call(
        mlp_kernel, "mlp", [natural, near(rows, D), near(1, D), terms, terms],
        normed_two, resid, cotangent, valid, gain_two, far=[*mlp_own, *mlp_par], mib=16,
        scratch=[
            pltpu.VMEM((PLANES, 2, ROLES, ROWS, D), bf16), pltpu.SemaphoreType.DMA((PLANES, 2)),
            pltpu.VMEM((rows, D), bf16), pltpu.VMEM((rows, D), f32), pltpu.VMEM((rows, D), f32),
        ],
    )

    half_terms = near(PLANES, 1, ROWS, D, dtype=bf16)
    back_o, back_p, tot_back, bseg_o, bseg_p, out_gown, out_gpar = call(
        back_kernel, "back_scan", [wide, wide, near(4, H), ends, ends, half_terms, half_terms],
        d_resid, low_o, low_p, retain_o, retain_p, sega_o, sega_p, *mixer_own, *mixer_par,
    )

    kept_terms = {}

    def terms_own(ready):
        kept_terms["own"] = call(
            lambda *refs: terms_kernel(True, *refs), "terms_own", [low_rows] + [wide] * 4,
            tokens, gain_one, forget_bias[0], input_bias[0], *mixer_own, order=[ready], scratch=projections[:2],
        )
        return kept_terms["own"][0]

    def terms_other(ready):
        kept_terms["other"] = call(
            lambda *refs: terms_kernel(False, *refs), "terms_other", [wide] * 4,
            kept_terms["own"][0], forget_bias[1], input_bias[1], *mixer_par, order=[ready], scratch=projections[:2],
        )
        return kept_terms["other"][0]

    beside = {1: terms_own, 4: terms_other}
    if direct:
        mlp_got, out_got = exchange(mlp_gpar, 0, 1), exchange(out_gpar, 0, 1)
        two_fives = near(2, ROLES + 1, ROWS, D, dtype=bf16)

        def mlp_pair(ready):
            kept_terms["mlp"] = call(
                mlp_pair_kernel, "mlp_pair_sum", [two_fives] * 2, ids, mlp_gown, mlp_got, out_gown, out_got,
                order=[ready],
            )
            return kept_terms["mlp"][0]

        beside[2] = mlp_pair

    arriving = relay(ids, tot_back, False, direct, beside)
    normed, *terms_o = kept_terms["own"]
    terms_p = kept_terms["other"]
    if direct:
        mlp_keep, mlp_send = kept_terms["mlp"]
        mlp_got = exchange_lane(mlp_send, True)

    def gates_back(column, back, sega, bseg, share, df, di, cand, retain, states, order, name):
        return call(
            lambda *refs: gates_kernel(column, *refs), name,
            [near(PLANES, GATES, ROWS, D, dtype=bf16), low_wide, low_wide, low_wide, near(1, HALF), near(1, HALF)],
            arriving, incoming, back, sega, bseg, share, df, di, cand, retain, states, restart, normed, order=order,
        )

    gate_gpar, pf_p, pi_p, pc_p, dfb_p, dib_p = gates_back(
        HALF, back_p, sega_p, bseg_p, *terms_p, retain_p, states_p, [tot_back], "gates_other"
    )
    gate_gown, pf_o, pi_o, pc_o, dfb_o, dib_o = gates_back(
        0, back_o, sega_o, bseg_o, *terms_o, retain_o, states_o, [dfb_p], "gates_own"
    )

    order = [dfb_o]
    if direct:
        five = near(ROLES + 1, ROWS, D, dtype=bf16)
        mlp_own_sum, mlp_next = call(
            half_sum_kernel, "mlp_half_sum", [five, five], mlp_keep, mlp_got, order=[dfb_o]
        )
        order = [mlp_own_sum]
    d_x, small_terms = call(
        input_kernel, "input_grad", [natural, near(TAIL, D)],
        ids, tokens, gain_one, d_resid, d_gain_two, dfb_o, dfb_p, dib_o, dib_p,
        pf_o, pi_o, pc_o, pf_p, pi_p, pc_p, *mixer_own, *mixer_par, order=order,
        scratch=[pltpu.VMEM((3 * SEG, ROWS), f32)],
    )

    def with_moments(keep, sends, weight, first_moment, second, name):
        count = weight.shape[0]
        return call(
            moments_kernel, name, [shape(count, D)] * 3 + [near(count, D)] + [near(SEG, 128)] * 2,
            keep, *sends, weight, first_moment, second,
        )

    if direct:
        shard, low_shard = near(ROWS, D), near(ROWS, D, dtype=bf16)
        long, low_long = near(ROWS + TAIL, D), near(ROWS + TAIL, D, dtype=bf16)
        gate_parts = call(
            gate_pair_kernel, "gate_pair_sum", [near(GATES * ROWS + TAIL, D, dtype=bf16)] * PLANES,
            gate_gown, exchange(gate_gpar, 0, 1), small_terms, exchange(small_terms, 0, 1), order=[mlp_own_sum],
        )
        gate_round = [gate_parts[0]] + [
            exchange(part, *bits) for part, bits in zip(gate_parts[1:], PLANE_BITS[1:], strict=True)
        ]
        two = near(2, ROWS, D, dtype=bf16)
        mlp_keep, mlp_send, out_sum = call(
            mlp_plane_kernel, "mlp_plane_sum", [two, two, low_shard], ids, mlp_own_sum, exchange_lane(mlp_next, False)
        )
        mlp_stay, mlp_send = call(
            mlp_far_kernel, "mlp_z_sum", [shard, low_shard], mlp_keep, exchange_z_lane(mlp_send, False)
        )
        mlp_done = with_moments(
            mlp_stay, [exchange_z_lane(mlp_send, True)], mlp_weights, mlp_first, mlp_second, "mlp_moments"
        )
        gate_keep, *gate_sends = call(
            gate_plane_kernel, "gate_plane_sum", [long] + [low_long] * 3, ids, *gate_round, out_sum,
        )
        gate_got = z_terms(gate_sends)
    else:

        def scattered(own, par):
            full_terms = jnp.stack([own, par]).transpose(2, 1, 0, 3, 4).reshape(-1, D)
            return lax.psum_scatter(full_terms, AXES, scatter_dimension=0, tiled=True).astype(f32)

        mlp_grad = scattered(mlp_gown, mlp_gpar)
        mixer_grad = scattered(
            jnp.concatenate([gate_gown, out_gown], axis=1), jnp.concatenate([gate_gpar, out_gpar], axis=1)
        )
        none = [jnp.zeros_like(mlp_grad, dtype=bf16)]
        mlp_done = with_moments(mlp_grad, none, mlp_weights, mlp_first, mlp_second, "mlp_moments")
        gate_keep = jnp.concatenate([mixer_grad, lax.psum(small_terms, AXES)], axis=0)
        gate_got = [jnp.zeros_like(gate_keep, dtype=bf16)] * 3
    mixer_done = with_moments(gate_keep, gate_got, mixer_weights, mixer_first, mixer_second, "mixer_moments")
    mlp_grad, mlp_first_new, mlp_second_new, mlp_dir, mlp_wsum, mlp_dsum = mlp_done
    mixer_grad, mixer_first_new, mixer_second_new, mixer_dir, mixer_wsum, mixer_dsum = mixer_done
    count = small_params.shape[0]
    line = shape(1, count)
    small_grad, small_first_new, small_second_new, small_dir, squares = call(
        small_kernel, "small_step", [line, line, line, near(1, count), near(SEG, ROWS)],
        ids, gate_keep, *gate_got, mixer_wsum, mixer_dsum, mlp_wsum, mlp_dsum,
        small_params[None], small_first[None], small_second[None], scratch=[pltpu.VMEM((4 * SEG, ROWS), f32)],
    )
    low_line = shape(1, count, dtype=bf16)
    fresh = [shape(*value.shape) for value in (mixer_weights, mlp_weights)]
    copies = [shape(*value.shape, dtype=bf16) for value in (mixer_weights, mlp_weights)]
    mixer_new, mlp_new, small_new, mixer_copy, mlp_copy, small_copy, tensor_norms, trust_ratios = call(
        update_kernel, "update", [*fresh, line, *copies, low_line, shape(2, 10), shape(1, 10)],
        ids, all_sum(squares), mixer_weights, mixer_dir, mlp_weights, mlp_dir, small_params[None], small_dir,
    )
    return (
        output,
        d_x,
        mixer_grad,
        mlp_grad,
        small_grad[0],
        mixer_first_new,
        mixer_second_new,
        mlp_first_new,
        mlp_second_new,
        small_first_new[0],
        small_second_new[0],
        mixer_new,
        mlp_new,
        small_new[0],
        mixer_copy,
        mlp_copy,
        small_copy[0],
        tensor_norms,
        trust_ratios[0],
    )


def solution(mesh):
    shard = P(("seq", "batch"), None)
    shard_flat = P(("seq", "batch"))
    stream = P("batch", "seq", None)
    return jax.shard_map(
        on_device,
        mesh=mesh,
        in_specs=(
            stream, P("batch", None), stream, shard, shard, shard_flat,
            shard, shard, shard, shard, shard_flat, shard_flat,
        ),
        out_specs=(
            stream, stream, shard, shard, shard_flat, shard, shard, shard, shard, shard_flat, shard_flat,
            shard, shard, shard_flat, shard, shard, shard_flat, P(), P(),
        ),
        check_vma=False,
    )
```

```python
import functools

import jax
import jax.numpy as jnp
from jax import lax
from jax.experimental import pallas as pl
from jax.experimental.pallas import tpu as pltpu
from jax.sharding import PartitionSpec as P

D = 512
H = 1024
FF = 2048
STEP = 5
SEG = 8
ROWS = 128
PLANES = 4
HALF = PLANES * ROWS
GATES = 3
ROLES = 4
TAIL = 16
SMALL_BLOCKS = 3
Z, X, Y, CORE, SEQ, DEVICE, MIXER_ROLE, MLP_ROLE = range(8)

first_decay = 0.5
second_decay = 0.5
learn_rate = 0.25
matrix_decay = 0.01
moment_eps = 1e-06

f32 = jnp.float32
bf16 = jnp.bfloat16
AXES = ("seq", "batch")

PLANE_BITS = ((0, 0), (0, 2), (1, 0), (1, 2))


def dot_nt(a, b):
    return lax.dot_general(a, b, (((1,), (1,)), ((), ())), preferred_element_type=f32)


def dot_nn(a, b):
    return lax.dot_general(a, b, (((1,), (0,)), ((), ())), preferred_element_type=f32)


def dot_tn(a, b):
    return lax.dot_general(a, b, (((0,), (0,)), ((), ())), preferred_element_type=f32)


def exchange(value, seq_bits, batch_bits, targets=None):
    seqs, batches = lax.axis_size("seq"), lax.axis_size("batch")
    pairs = [
        (s * batches + b, (s ^ seq_bits) * batches + (b ^ batch_bits))
        for s in range(seqs)
        for b in range(batches)
        if targets is None or (s ^ seq_bits) in targets
    ]
    return lax.ppermute(value, AXES, pairs)


def unit(x):
    return lax.rsqrt(jnp.mean(x * x, axis=-1, keepdims=True) + 1e-05)


def rms_back(x, d_normed, gain):
    scale = unit(x)
    normal = x * scale
    d_unit = d_normed * gain
    mean = jnp.mean(d_unit * normal, axis=-1, keepdims=True)
    return jnp.sum(d_normed * normal, axis=0, keepdims=True), scale * (d_unit - normal * mean)


def fetch(slabs, roles, held, sems):
    copies = []
    for k, role in enumerate(roles):
        for q, ref in enumerate(slabs):
            place = held.at[k, pl.ds(q * ROWS, ROWS)]
            copies.append(pltpu.make_async_copy(ref.at[pl.ds(role * ROWS, ROWS)], place, sems.at[k, q]))
    for copy in copies:
        copy.start()
    return copies


def arrived(copies, k, count=PLANES):
    for copy in copies[k * count : (k + 1) * count]:
        copy.wait()


def group(s, steps, j):
    return pl.ds(pl.multiple_of((s * steps + j) * SEG, SEG), SEG)


def pair(s, steps, j):
    return pl.ds(pl.multiple_of((s * steps + 2 * j) * SEG, 2 * SEG), 2 * SEG)


def segment_order(block):
    row = lax.broadcasted_iota(jnp.int32, (block, block), 0)
    position = lax.broadcasted_iota(jnp.int32, (block, block), 1)
    return jnp.where(position == (row % SEG) * (block // SEG) + row // SEG, 1.0, 0.0).astype(bf16)


def inward(ref):
    order = segment_order(ref.shape[1])
    return jnp.concatenate([dot_nn(order, ref[s]) for s in range(2)], axis=0)


def outward(ref, value):
    block = ref.shape[1]
    order = segment_order(block)
    for s in range(2):
        ref[s] = dot_tn(order, value[s * block : (s + 1) * block]).astype(bf16)


def z_of(ids_ref, k, core):
    return ids_ref[Z] ^ (jnp.where(core == 0, k, 3 - k) if k in (1, 2) else k)


def pack_kernel(ids_ref, weights_ref, small_ref, got_ref, out_ref):
    out_ref[pl.ds(0, ROWS), :] = weights_ref[...].astype(bf16)
    mine, other = small_ref[...], got_ref[...]
    core = ids_ref[CORE]
    line = jnp.concatenate(
        [jnp.where(core == 0, mine, other), jnp.where(core == 0, other, mine), jnp.zeros((SEG, D - 2 * ROWS), f32)], axis=1
    )
    out_ref[pl.ds(ROWS, TAIL), :] = jnp.concatenate([line, jnp.zeros_like(line)], axis=0).astype(bf16)


def slab_kernel(ids_ref, early_ref, late_ref, *refs):
    slab_ref, lines = refs[-2:]
    lines[...] = jnp.zeros_like(lines)
    for k in range(ROLES):
        part = (early_ref, late_ref)[k // 2].at[k % 2]
        role = z_of(ids_ref, k, ids_ref[CORE])
        slab_ref[pl.ds(pl.multiple_of(role * ROWS, ROWS), ROWS), :] = part[pl.ds(0, ROWS), :]
        lines[pl.ds(role, 1), :] = part[pl.ds(ROWS, TAIL), :].astype(f32)[0:1]
    slab_ref[pl.ds(ROLES * ROWS, TAIL), :] = lines[...].astype(bf16)


def unpack_kernel(count, ids_ref, tok_ref, q0, q1, q2, q3, *refs):
    normed_ref, gain_one_ref, gain_two_ref, fo_ref, fp_ref, io_ref, ip_ref, by_device, flat, sems, held = refs
    copies = [
        pltpu.make_async_copy(ref.at[pl.ds(ROLES * ROWS, TAIL)], held.at[k], sems.at[k])
        for k, ref in enumerate((q0, q1, q2, q3))
    ]
    for copy in copies:
        copy.start()
    chips = [2 * (ids_ref[X] ^ (k // 2)) + (ids_ref[Y] ^ (k % 2)) for k in range(PLANES)]
    for k, copy in enumerate(copies):
        copy.wait()
        lines = held[k].astype(f32)
        for z in range(ROLES):
            for core in range(2):
                row = z * 2 * PLANES + 2 * chips[k] + core
                by_device[pl.ds(row, 1), :] = lines[z : z + 1, core * ROWS : (core + 1) * ROWS]
    parts = [by_device[pl.ds(k, 8, stride=4), :] for k in range(4)]
    for k in range(3):
        cut = ROWS - (k + 1) * (ROWS - count)
        row = jnp.concatenate([parts[k][:, k * (ROWS - count) : count], parts[k + 1][:, : ROWS - cut]], axis=1)
        flat[pl.ds(k, 8, stride=3), :] = row
    rows = [flat[pl.ds(k, 1), :] for k in range(2 * PLANES)]
    gain_one_ref[...] = jnp.concatenate(rows[:PLANES], axis=1)
    gain_two_ref[...] = jnp.concatenate(rows[PLANES:], axis=1)
    for half, (fb, ib) in enumerate(((fo_ref, io_ref), (fp_ref, ip_ref))):
        at = [2 * PLANES + 2 * chips[k] + (ids_ref[CORE] ^ half) for k in range(PLANES)]
        fb[...] = jnp.concatenate([flat[pl.ds(row, 1), :] for row in at], axis=1)
        ib[...] = jnp.concatenate([flat[pl.ds(row + 2 * PLANES, 1), :] for row in at], axis=1)
    normed_ref[...] = first_norm(tok_ref, gain_one_ref)


def stack_kernel(first_ref, second_ref, *refs):
    out_ref = refs[-1]
    if first_ref.shape == out_ref.shape[1:]:
        out_ref[0], out_ref[1] = first_ref[...], second_ref[...]
    else:
        count = first_ref.shape[0]
        out_ref[:count], out_ref[count:] = first_ref[...], second_ref[...]


def normed_kernel(tok_ref, gain_ref, normed_ref):
    normed_ref[...] = first_norm(tok_ref, gain_ref)


def relay_kernel(bit, forward, flipped, ids_ref, group_ref, other_ref, *refs):
    late = ((ids_ref[SEQ] & bit) != 0) == forward
    mine, other = group_ref[...], other_ref[...]
    if flipped:
        quarter = HALF // 2
        at = (quarter, 0, 3 * quarter, 2 * quarter)
        other = jnp.concatenate([other[:, k : k + quarter] for k in at], axis=1)
    if bit == 1:
        decay, state = jnp.ones_like(mine[:2]), jnp.zeros_like(mine[:2])
    else:
        decay, state = refs[0][0:2, :], refs[0][2:4, :]
    state = jnp.where(late, decay * other[2:] + state, state)
    if refs[-1].shape[0] == 2:
        refs[-1][...] = state
        return
    group_out, before_out = refs[-2:]
    before_out[...] = jnp.concatenate([jnp.where(late, decay * other[:2], decay), state], axis=0)
    first, second = jnp.where(late, other, mine), jnp.where(late, mine, other)
    group_out[...] = jnp.concatenate([first[:2] * second[:2], second[:2] * first[2:] + second[2:]], axis=0)


def gate_shares(f, i):
    most = jnp.maximum(jnp.maximum(-f, -i), 0.0)
    one, low_f, low_i = jnp.exp(-most), jnp.exp(-f - most), jnp.exp(-i - most)
    inverse = 1.0 / ((one + low_i) + (one + low_f))
    return (one + low_i) * inverse, (one + low_f) * inverse, low_f * inverse, low_i * inverse


def first_norm(tok_ref, gain_ref):
    x = inward(tok_ref)
    return (x * unit(x) * gain_ref[...]).astype(bf16)


def scan_kernel(first, *refs):
    normed_ref, rs_ref, fb_ref, ib_ref, *refs = refs
    if not first:
        earlier_ref, *refs = refs
    slabs, (held, sems), refs = refs[:PLANES], refs[-2:], refs[-10:-2]
    retain_ref, acc_ref, tot_ref, sega_ref, segb_ref, f_ref, i_ref, c_ref = refs
    copies = fetch(slabs, range(GATES), held, sems)
    normed = normed_ref[...]
    for role, ref in enumerate((f_ref, i_ref, c_ref)):
        arrived(copies, role)
        ref[...] = dot_nt(normed, held[role])
    steps = normed.shape[0] // (2 * SEG)
    f_bias, i_bias = fb_ref[...], ib_ref[...]

    def step(j, carry):
        after = []
        for s in range(2):
            at = group(s, steps, j)
            keep, share, _, _ = gate_shares(f_ref[at, :] + f_bias, i_ref[at, :] + i_bias)
            a = keep * rs_ref[at, :]
            b = a * carry[s][1] + share * c_ref[at, :]
            retain_ref[at, :] = a
            acc_ref[at, :] = b
            after.append((a * carry[s][0], b))
        return tuple(after)

    start = (jnp.ones((SEG, HALF), f32), jnp.zeros((SEG, HALF), f32))
    ends = lax.fori_loop(0, steps, step, (start, start), unroll=2)
    columns = pl.ds(0 if first else HALF, HALF)
    if not first:
        tot_ref[:, pl.ds(0, HALF)] = earlier_ref[...]
    for s, (seg_a, seg_b) in enumerate(ends):
        sega_ref[pl.ds(s * SEG, SEG), :] = seg_a
        segb_ref[pl.ds(s * SEG, SEG), :] = seg_b
        tot_a, tot_b = seg_a[0:1], seg_b[0:1]
        for k in range(1, SEG):
            a = seg_a[k : k + 1]
            tot_a, tot_b = a * tot_a, a * tot_b + seg_b[k : k + 1]
        tot_ref[pl.ds(s, 1), columns] = tot_a
        tot_ref[pl.ds(2 + s, 1), columns] = tot_b


def terms_kernel(first, *refs):
    if first:
        tok_ref, gain_ref, fb_ref, ib_ref, *refs = refs
        slabs, refs = refs[:PLANES], refs[-9:]
        normed_ref, *refs = refs
        normed_ref[...] = first_norm(tok_ref, gain_ref)
    else:
        normed_ref, fb_ref, ib_ref, *refs = refs
        slabs, refs = refs[:PLANES], refs[-8:]
    share_ref, df_ref, di_ref, cand_ref, f_ref, i_ref, held, sems = refs
    copies = fetch(slabs, range(GATES), held, sems)
    normed = normed_ref[...]
    for role, ref in enumerate((f_ref, i_ref, cand_ref)):
        arrived(copies, role)
        ref[...] = dot_nt(normed, held[role])
    f_bias, i_bias = fb_ref[...], ib_ref[...]

    def step(j, carry):
        at = pl.ds(pl.multiple_of(j * 2 * SEG, 2 * SEG), 2 * SEG)
        keep, share, slow_f, slow_i = gate_shares(f_ref[at, :] + f_bias, i_ref[at, :] + i_bias)
        share_ref[at, :] = share
        df_ref[at, :] = keep * slow_f
        di_ref[at, :] = share * slow_i
        return carry

    lax.fori_loop(0, normed.shape[0] // (2 * SEG), step, 0, unroll=2)


def states_kernel(
    inc_ref, tok_ref, gain_ref, retain_o, retain_p, acc_o, acc_p, sega_o, sega_p, segb_o, segb_p, *refs
):
    slabs, refs = refs[: 2 * PLANES], refs[2 * PLANES :]
    states_o, states_p, low_o, low_p, resid_ref, normed_ref, held, sems = refs
    copies = fetch(slabs, [GATES], held, sems)
    steps = resid_ref.shape[0] // (2 * SEG)
    halves = (
        (retain_o, acc_o, sega_o, segb_o, states_o, low_o, 0),
        (retain_p, acc_p, sega_p, segb_p, states_p, low_p, HALF),
    )
    start = []
    for _, _, sega, segb, _, _, column in halves:
        for s in range(2):
            seg_a, seg_b = sega[pl.ds(s * SEG, SEG), :], segb[pl.ds(s * SEG, SEG), :]
            at_seg = [inc_ref[pl.ds(s, 1), pl.ds(column, HALF)]]
            for k in range(SEG - 1):
                at_seg.append(seg_a[k : k + 1] * at_seg[-1] + seg_b[k : k + 1])
            start.append(jnp.concatenate(at_seg, axis=0))

    def step(j, carry):
        after = []
        for k, (retain, acc, _, _, states, low, _) in enumerate(halves):
            for s in range(2):
                carried, two = carry[2 * k + s], []
                for q in range(2):
                    at = group(s, steps, 2 * j + q)
                    carried = retain[at, :] * carried
                    two.append(acc[at, :] + carried)
                    states[at, :] = two[-1]
                low[pair(s, steps, j), :] = jnp.concatenate(two, axis=0).astype(bf16)
                after.append(carried)
        return tuple(after)

    lax.fori_loop(0, steps // 2, step, tuple(start))
    r = inward(tok_ref)
    for low, k in zip((low_o, low_p), range(2), strict=True):
        arrived(copies, k)
        r = r + dot_nn(low[...], held[0, pl.ds(k * HALF, HALF)])
    resid_ref[...] = r
    normed_ref[...] = (r * unit(r) * gain_ref[...]).astype(bf16)


GELU_A = 0.7978845608028654
GELU_B = 0.044715


def mlp_kernel(ids_ref, normed_ref, resid_ref, cot_ref, valid_ref, gain_ref, *refs):
    parts, refs = refs[:4], refs[4:]
    output_ref, dresid_ref, dgain_ref, gown_ref, gpar_ref, held, sems, dout_ref, outer_ref, dnorm_ref = refs

    def bringing(at):
        for half in range(2):
            for k in range(ROLES):
                role = z_of(ids_ref, k, ids_ref[CORE] ^ half)
                source = parts[2 * half + k // 2].at[k % 2, at]
                yield pltpu.make_async_copy(source, held.at[at, half, role], sems.at[at, half, k])

    for copy in bringing(0):
        copy.start()
    dout_ref[...] = (inward(cot_ref) * valid_ref[...]).astype(bf16)
    outer_ref[...] = jnp.zeros_like(outer_ref)
    dnorm_ref[...] = jnp.zeros_like(dnorm_ref)

    def step(i, carry):
        at, low = i // 2, i % 2

        @pl.when(low == 0)
        def _():
            for copy in bringing(at):
                copy.wait()

        @pl.when((low == 0) & (at < PLANES - 1))
        def _():
            for copy in bringing(at + 1):
                copy.start()

        normed = normed_ref[...]
        dout = dout_ref[...]
        w_up = held[at, :, low].reshape(2 * ROWS, D)
        w_down = held[at, :, low + 2].reshape(2 * ROWS, D)
        inner = dot_nt(normed, w_up)
        square = inner * inner
        curve = jnp.tanh(GELU_A * inner * (1.0 + GELU_B * square))
        half = 0.5 * (1.0 + curve)
        activated = (inner * half).astype(bf16)
        slope = half + 0.5 * inner * (1.0 - curve * curve) * (GELU_A * (1.0 + 3.0 * GELU_B * square))
        d_inner = (slope * dot_nt(dout, w_down)).astype(bf16)
        outer_ref[...] += dot_nn(activated, w_down)
        dnorm_ref[...] += dot_nn(d_inner, w_up)
        g_up = dot_tn(d_inner, normed).astype(bf16).reshape(2, 1, ROWS, D)
        g_down = dot_tn(activated, dout).astype(bf16).reshape(2, 1, ROWS, D)
        for k, ref in enumerate((gown_ref, gpar_ref)):
            ref[at, pl.ds(low, 1)] = g_up[k]
            ref[at, pl.ds(low + 2, 1)] = g_down[k]
        return carry

    lax.fori_loop(0, 2 * PLANES, step, 0)
    r = resid_ref[...]
    outward(output_ref, ((r + outer_ref[...]) * valid_ref[...]).astype(bf16))
    dgain_ref[...], d_r = rms_back(r, dnorm_ref[...], gain_ref[...])
    dresid_ref[...] = dout_ref[...].astype(f32) + d_r


def back_kernel(dresid_ref, low_o, low_p, retain_o, retain_p, sega_o, sega_p, *refs):
    slabs, refs = refs[: 2 * PLANES], refs[2 * PLANES :]
    acc_o, acc_p, tot_ref, segb_o, segb_p, gown_ref, gpar_ref, held, sems = refs
    copies = fetch(slabs, [GATES], held, sems)
    steps = dresid_ref.shape[0] // (2 * SEG)
    dmix = dresid_ref[...].astype(bf16)
    for acc, k in zip((acc_o, acc_p), range(2), strict=True):
        arrived(copies, k)
        acc[...] = dot_nt(dmix, held[0, pl.ds(k * HALF, HALF)])
    halves = ((retain_o, acc_o), (retain_p, acc_p))

    def step(n, carry):
        after = []
        for k, (retain, acc) in enumerate(halves):
            for s in range(2):
                at = group(s, steps, steps - 1 - n)
                back = acc[at, :] + carry[2 * k + s]
                acc[at, :] = back
                after.append(retain[at, :] * back)
        return tuple(after)

    ends = lax.fori_loop(0, steps, step, (jnp.zeros((SEG, HALF), f32),) * 4, unroll=2)
    for k, (sega, segb) in enumerate(((sega_o, segb_o), (sega_p, segb_p))):
        for s in range(2):
            emitted = ends[2 * k + s]
            segb[pl.ds(s * SEG, SEG), :] = emitted
            seg_a = sega[pl.ds(s * SEG, SEG), :]
            tot_a, tot_b = seg_a[SEG - 1 :], emitted[SEG - 1 :]
            for q in reversed(range(SEG - 1)):
                a = seg_a[q : q + 1]
                tot_a, tot_b = a * tot_a, a * tot_b + emitted[q : q + 1]
            tot_ref[pl.ds(s, 1), pl.ds(k * HALF, HALF)] = tot_a
            tot_ref[pl.ds(2 + s, 1), pl.ds(k * HALF, HALF)] = tot_b
    for low, ref in ((low_o, gown_ref), (low_p, gpar_ref)):
        ref[...] = dot_tn(low[...], dmix).astype(bf16).reshape(PLANES, 1, ROWS, D)


def gates_kernel(
    column, arr_ref, inc_ref, acc_ref, sega_ref, segb_ref, share_ref, df_ref, di_ref, cand_ref, retain_ref, states_ref,
    rs_ref, normed_ref, order_ref, grad_ref, pf_ref, pi_ref, pc_ref, dfb_ref, dib_ref,
):
    steps = normed_ref.shape[0] // (2 * SEG)
    start, first = [], []
    for s in range(2):
        seg_a, seg_b = sega_ref[pl.ds(s * SEG, SEG), :], segb_ref[pl.ds(s * SEG, SEG), :]
        at_seg = [arr_ref[pl.ds(s, 1), pl.ds(column, HALF)]]
        for k in reversed(range(1, SEG)):
            at_seg.append(seg_a[k : k + 1] * at_seg[-1] + seg_b[k : k + 1])
        start.append(jnp.concatenate(at_seg[::-1], axis=0))
        ends = states_ref[group(s, steps, steps - 1), :]
        first.append(jnp.concatenate([inc_ref[pl.ds(s, 1), pl.ds(column, HALF)], ends[: SEG - 1]], axis=0))

    def step(n, carry):
        *carried, sum_f, sum_i = carry
        m = steps // 2 - 1 - n
        for s in range(2):
            terms = []
            for q in (1, 0):
                j = 2 * m + q
                at = group(s, steps, j)
                back = acc_ref[at, :] + carried[s]
                carried[s] = carried[s] * retain_ref[at, :]
                previous = states_ref[group(s, steps, jnp.maximum(j - 1, 0)), :]
                if q == 0:
                    previous = jnp.where(m == 0, first[s], previous)
                both_ways = back * (previous * rs_ref[at, :] - cand_ref[at, :])
                d_f = both_ways * df_ref[at, :]
                d_i = both_ways * di_ref[at, :]
                sum_f = sum_f + d_f
                sum_i = sum_i - d_i
                terms.append((d_f, -d_i, back * share_ref[at, :]))
            for late, early, ref in zip(*terms, (pf_ref, pi_ref, pc_ref), strict=True):
                ref[pair(s, steps, m), :] = jnp.concatenate([early, late], axis=0).astype(bf16)
        return (*carried, sum_f, sum_i)

    nothing = jnp.zeros((SEG, HALF), f32)
    *_, sum_f, sum_i = lax.fori_loop(0, steps // 2, step, (*start, nothing, nothing))
    dfb_ref[...] = jnp.sum(sum_f, axis=0, keepdims=True)
    dib_ref[...] = jnp.sum(sum_i, axis=0, keepdims=True)
    normed = normed_ref[...]
    for role, ref in enumerate((pf_ref, pi_ref, pc_ref)):
        grad_ref[:, role] = dot_tn(ref[...], normed).astype(bf16).reshape(PLANES, ROWS, D)


def input_terms_kernel(ids_ref, tok_ref, dgain_two_ref, dfb_o, dfb_p, dib_o, dib_p, *refs):
    terms, slabs, refs = refs[: 2 * GATES], refs[2 * GATES : 2 * GATES + 2 * PLANES], refs[-5:]
    dnorm_ref, small_ref, rows_ref, held, sems = refs
    copies = fetch(slabs, range(GATES), held, sems)
    d_normed = 0.0
    for role in range(GATES):
        arrived(copies, role, 2 * PLANES)
        for k in range(2):
            d_normed = d_normed + dot_nn(terms[k * GATES + role][...], held[role, pl.ds(k * HALF, HALF)])
    dnorm_ref[...] = d_normed
    x = inward(tok_ref)
    d_gain = jnp.sum(d_normed * (x * unit(x)), axis=0, keepdims=True)
    for k in range(PLANES):
        rows_ref[pl.ds(k, 1), :] = d_gain[:, k * ROWS : (k + 1) * ROWS]
        rows_ref[pl.ds(PLANES + k, 1), :] = dgain_two_ref[:, pl.ds(k * ROWS, ROWS)]
        chip = 4 * (ids_ref[X] ^ (k // 2)) + 2 * (ids_ref[Y] ^ (k % 2))
        for core, (fb, ib) in enumerate(((dfb_o, dib_o), (dfb_p, dib_p))):
            row = 2 * PLANES + chip + (ids_ref[CORE] ^ core)
            rows_ref[pl.ds(row, 1), :] = fb[:, pl.ds(k * ROWS, ROWS)]
            rows_ref[pl.ds(row + 2 * PLANES, 1), :] = ib[:, pl.ds(k * ROWS, ROWS)]
    blocks = [rows_ref[pl.ds(k * SEG, SEG), :] for k in range(SMALL_BLOCKS)] + [jnp.zeros((SEG, ROWS), f32)]
    small_ref[...] = jnp.concatenate([jnp.concatenate(blocks, axis=1), jnp.zeros((SEG, D), f32)], axis=0)


def input_kernel(tok_ref, gain_ref, dresid_ref, dnorm_ref, order_ref, dx_ref, done_ref):
    done_ref[...] = jnp.zeros_like(done_ref)
    _, d_x = rms_back(inward(tok_ref), dnorm_ref[...], gain_ref[...])
    outward(dx_ref, (dresid_ref[...] + d_x).astype(bf16))


def mlp_pair_kernel(ids_ref, own_ref, got_ref, out_ref, outgot_ref, *refs):
    core = ids_ref[CORE]
    for k in range(PLANES):
        ref = refs[-2 + k // 2]
        ref[k % 2, pl.ds(0, ROLES)] = (own_ref[k].astype(f32) + got_ref[k].astype(f32)).astype(bf16)
        at = pl.ds(jnp.where(core == 0, 3 - k, k) if k in (1, 2) else k, 1)
        ref[k % 2, pl.ds(ROLES, 1)] = (out_ref[at, 0].astype(f32) + outgot_ref[at, 0].astype(f32)).astype(bf16)


def gate_pair_kernel(own_ref, got_ref, small_ref, small_got, *outs):
    small = (small_ref[...] + small_got[...]).astype(bf16)
    for k, ref in enumerate(outs[-PLANES:]):
        total = (own_ref[k].astype(f32) + got_ref[k].astype(f32)).astype(bf16)
        ref[pl.ds(0, GATES * ROWS), :] = total.reshape(GATES * ROWS, D)
        ref[pl.ds(GATES * ROWS, TAIL), :] = small


def half_sum_kernel(own_ref, got_ref, *refs):
    for k, ref in enumerate(refs[-2:]):
        ref[...] = (own_ref[k].astype(f32) + got_ref[k].astype(f32)).astype(bf16)


def mlp_plane_kernel(ids_ref, own_ref, got_ref, keep_ref, send_ref, out_ref):
    z = ids_ref[Z]
    near_bit = jnp.where(ids_ref[CORE] == 0, 1, 2)

    def total(role):
        at = pl.ds(role, 1)
        return (own_ref[at].astype(f32) + got_ref[at].astype(f32)).astype(bf16).reshape(ROWS, D)

    for k, role in enumerate((z, z ^ near_bit ^ 3)):
        keep_ref[k] = total(role)
        send_ref[k] = total(role ^ near_bit)
    out_ref[...] = total(ROLES)


def mlp_far_kernel(keep_ref, got_ref, *refs):
    stay_ref, send_ref = refs[-2:]
    stay_ref[...] = keep_ref[0].astype(f32) + got_ref[0].astype(f32)
    send_ref[...] = (keep_ref[1].astype(f32) + got_ref[1].astype(f32)).astype(bf16)


def gate_plane_kernel(ids_ref, p0, p1, p2, p3, out_ref, *refs):
    z = ids_ref[Z]
    keep_ref, s1_ref, s2_ref, s3_ref = refs[-4:]

    def total(at):
        terms = [ref[at, :].astype(f32) for ref in (p0, p1, p2, p3)]
        return (terms[0] + terms[1]) + (terms[2] + terms[3])

    def of_role(role):
        at = pl.ds(pl.multiple_of(jnp.minimum(role, GATES - 1) * ROWS, ROWS), ROWS)
        return jnp.where(role == GATES, out_ref[...].astype(f32), total(at))

    small = total(pl.ds(GATES * ROWS, TAIL))
    keep_ref[pl.ds(0, ROWS), :] = of_role(z)
    keep_ref[pl.ds(ROWS, TAIL), :] = small
    for k, ref in enumerate((s1_ref, s2_ref, s3_ref)):
        ref[pl.ds(0, ROWS), :] = of_role(z ^ (k + 1)).astype(bf16)
        ref[pl.ds(ROWS, TAIL), :] = small.astype(bf16)


def joined(at, keep_ref, gots):
    total = keep_ref[at, :]
    for ref in gots:
        total = total + ref[at, :].astype(f32)
    return total


def matrix_step(at, keep_ref, gots, weight_ref, first_ref, second_ref, outs):
    grad_ref, first_out, second_out, dir_ref = outs
    weight = weight_ref[...]
    gradient = joined(at, keep_ref, gots)
    grad_ref[...] = gradient
    first_out[...], second_out[...], direction = moments(
        weight, gradient, first_ref[...], second_ref[...], matrix_decay
    )
    dir_ref[...] = direction
    return weight, direction


def square_rows(value):
    square = jnp.sum((value * value).reshape(-1, SEG, D), axis=0)
    return (square[:, :128] + square[:, 128:256]) + (square[:, 256:384] + square[:, 384:])


def moments_kernel(keep_ref, got_ref, weight_ref, first_ref, second_ref, *outs):
    *outs, wsum_ref, dsum_ref = outs
    weight, direction = matrix_step(
        pl.ds(0, weight_ref.shape[0]), keep_ref, [got_ref], weight_ref, first_ref, second_ref, outs
    )
    wsum_ref[...] = square_rows(weight)
    dsum_ref[...] = square_rows(direction)


def finish_kernel(
    ids_ref, keep_ref, g1_ref, g2_ref, g3_ref, wsum_f, dsum_f,
    mixer_ref, mixer_first, mixer_second, weight_ref, first_ref, second_ref,
    mixer_grad, mixer_first_out, mixer_second_out, mixer_dir, grad_ref, first_out, second_out, dir_ref, squares_ref,
    rows_ref,
):
    gots = (g1_ref, g2_ref, g3_ref)
    mixer_rows = mixer_ref.shape[0]
    mixer_values = matrix_step(
        pl.ds(0, mixer_rows), keep_ref, gots, mixer_ref, mixer_first, mixer_second,
        (mixer_grad, mixer_first_out, mixer_second_out, mixer_dir),
    )
    total = joined(pl.ds(mixer_rows, TAIL), keep_ref, gots)
    rows_ref[...] = jnp.zeros_like(rows_ref)
    for k in range(SMALL_BLOCKS):
        rows_ref[pl.ds(k * SEG, SEG), :] = total[:SEG, k * ROWS : (k + 1) * ROWS]
    weight = weight_ref[...]
    count = weight.shape[1]
    start = ids_ref[DEVICE] * count
    row, lane = start // ROWS, start % ROWS
    two = jnp.concatenate([rows_ref[pl.ds(row, 1), :], rows_ref[pl.ds(row + 1, 1), :]], axis=1)
    two = jnp.broadcast_to(two, (SEG, 2 * ROWS))
    gradient = pltpu.roll(two, (2 * ROWS - lane) % (2 * ROWS), 1)[:1, :count]
    grad_ref[...] = gradient
    first_out[...], second_out[...], direction = moments(weight, gradient, first_ref[...], second_ref[...], 0.0)
    dir_ref[...] = direction
    place = start + lax.broadcasted_iota(jnp.int32, (1, count), 1)
    at = lax.broadcasted_iota(jnp.int32, (1, ROWS), 1)
    bounds = (0, D, 2 * D, 2 * D + H, 2 * D + 2 * H)
    lines = []
    for mixer_value, mlp_sum, value in zip(mixer_values, (wsum_f, dsum_f), (weight, direction), strict=True):
        line = jnp.where(at == ids_ref[MIXER_ROLE], jnp.sum(square_rows(mixer_value), keepdims=True), 0.0)
        line = line + jnp.where(at == ROLES + ids_ref[MLP_ROLE], jnp.sum(mlp_sum[...], keepdims=True), 0.0)
        for k in range(4):
            inside = (place >= bounds[k]) & (place < bounds[k + 1])
            part = jnp.sum(jnp.where(inside, value * value, 0.0), axis=1, keepdims=True)
            line = line + jnp.where(at == ROLES + 2 + k, part, 0.0)
        lines.append(line)
    squares_ref[...] = jnp.concatenate(lines + [jnp.zeros((SEG - 2, ROWS), f32)], axis=0)


def ratio_of(squares_ref, tensor):
    norms = jnp.sqrt(squares_ref[0:2, :])
    ratios = norms[0:1] / (norms[1:2] + 1e-06)
    at = lax.broadcasted_iota(jnp.int32, (1, ROWS), 1)
    return jnp.sum(jnp.where(at == tensor, ratios, 0.0), axis=1, keepdims=True)


def new_weights(ratio, weight_ref, dir_ref, new_ref, copy_ref):
    value = weight_ref[...] - learn_rate * ratio * dir_ref[...]
    new_ref[...] = value
    copy_ref[...] = value.astype(bf16)


def matrix_update_kernel(slot, base, ids_ref, squares_ref, weight_ref, dir_ref, new_ref, copy_ref, done_ref):
    done_ref[...] = jnp.zeros_like(done_ref)
    new_weights(ratio_of(squares_ref, base + ids_ref[slot]), weight_ref, dir_ref, new_ref, copy_ref)


def small_update_kernel(
    ids_ref, squares_ref, weight_ref, dir_ref, order_ref, order2_ref, new_ref, copy_ref, norms_ref, ratios_ref
):
    norms = jnp.sqrt(squares_ref[0:2, :])
    ratios = norms[0:1] / (norms[1:2] + 1e-06)
    norms_ref[...] = norms[:, : norms_ref.shape[1]]
    ratios_ref[...] = ratios[:, : ratios_ref.shape[1]]
    count = weight_ref.shape[1]
    place = ids_ref[DEVICE] * count + lax.broadcasted_iota(jnp.int32, (1, count), 1)
    first, second, third, fourth = (ratio_of(squares_ref, ROLES + 2 + k) for k in range(4))
    ratio = jnp.where(
        place < 2 * D, jnp.where(place < D, first, second), jnp.where(place < 2 * D + H, third, fourth)
    )
    new_weights(ratio, weight_ref, dir_ref, new_ref, copy_ref)


SMEM = pl.BlockSpec(memory_space=pltpu.SMEM)
ANY = pl.BlockSpec(memory_space=pl.ANY)
VMEM = pl.BlockSpec(memory_space=pltpu.VMEM)


def shape(*dims, dtype=f32):
    return jax.ShapeDtypeStruct(dims, dtype)


def near(*dims, dtype=f32):
    return pltpu.VMEM(dims, dtype)


def kept(value):
    return pltpu.with_memory_space_constraint(value, pltpu.VMEM)


def away(value):
    return pltpu.with_memory_space_constraint(value, pltpu.HBM)


def weight_scratch(roles, halves):
    return [pltpu.VMEM((roles, halves * HALF, D), bf16), pltpu.SemaphoreType.DMA((roles, halves * PLANES))]


def call(kernel, name, out_shape, *args, order=(), far=(), scratch=(), mib=8):
    in_specs = [SMEM if arg.dtype == jnp.int32 else VMEM for arg in args] + [ANY] * (len(far) + len(order))
    return pl.pallas_call(
        kernel,
        in_specs=in_specs,
        out_specs=jax.tree.map(lambda _: VMEM, out_shape),
        out_shape=out_shape,
        scratch_shapes=list(scratch),
        compiler_params=pltpu.CompilerParams(vmem_limit_bytes=mib * 1024 * 1024),
        name=name,
    )(*[arg if arg.dtype == jnp.int32 else kept(arg) for arg in args], *[away(arg) for arg in far], *order)


def exchange_lane(value, second):
    seqs, batches = lax.axis_size("seq"), lax.axis_size("batch")
    pairs = []
    for s in range(seqs):
        for b in range(batches):
            over_x = (b % 2 == 0) != second
            pairs.append((s * batches + b, (s ^ 1) * batches + b if over_x else s * batches + (b ^ 2)))
    return lax.ppermute(value, AXES, pairs)


def exchange_z_lane(value, second):
    seqs, batches = lax.axis_size("seq"), lax.axis_size("batch")
    pairs = []
    for s in range(seqs):
        for b in range(batches):
            bit = 2 if (b % 2 == 0) != second else 4
            pairs.append((s * batches + b, (s ^ bit) * batches + b))
    return lax.ppermute(value, AXES, pairs)


def after(value, *others):
    return lax.optimization_barrier((value, *others))[0]


def over_z(shard):
    return [shard] + [exchange(shard, 2 * k, 0) for k in range(1, 4)]


def z_terms(sends):
    return [exchange(sent, 2 * (k + 1), 0) for k, sent in enumerate(sends)]


def all_sum(value):
    seqs, batches = lax.axis_size("seq"), lax.axis_size("batch")
    bit = 1
    while bit < batches:
        value = value + exchange(value, 0, bit)
        bit *= 2
    bit = 1
    while bit < seqs:
        value = value + exchange(value, bit, 0)
        bit *= 2
    return value


def relay(ids, total, forward, flipped, beside):
    group, before, bit = total, [], 1
    joint = near(4, H)
    while bit < lax.axis_size("seq"):
        last = 2 * bit == lax.axis_size("seq")
        other = exchange(group, bit, 0)
        order = [beside[bit](group)] if bit in beside else []
        got = call(
            functools.partial(relay_kernel, bit, forward, flipped and bit == 1),
            f"relay_{bit}", near(2, H) if last else [joint, joint],
            ids, group, other, *before, order=order,
        )
        if not last:
            group, before = got[0], [got[1]]
        bit *= 2
    return got


def flip_by(value, axis, bit):
    return jnp.where(bit == 1, jnp.flip(value, axis), value)


def moments(weight, gradient, first_moment, second, decay_rate):
    first_new = first_decay * first_moment + (1.0 - first_decay) * gradient
    second_new = second_decay * second + (1.0 - second_decay) * gradient * gradient
    direction = (
        first_new
        / (1.0 - first_decay**STEP)
        / (jnp.sqrt(second_new / (1.0 - second_decay**STEP)) + moment_eps)
        + decay_rate * weight
    )
    return (first_new, second_new, direction)


def on_device(
    tokens, doc_lengths, cotangent, mixer_weights, mlp_weights, small_params,
    mixer_first, mixer_second, mlp_first, mlp_second, small_first, small_second,
):
    seqs, batches = lax.axis_size("seq"), lax.axis_size("batch")
    seq_at, batch_at = lax.axis_index("seq"), lax.axis_index("batch")
    device = seq_at * batches + batch_at
    streams, block, _ = tokens.shape
    rows = streams * block
    direct = (seqs, batches) == (8, 4)
    if direct:
        z, x, y, c = seq_at // 2, seq_at % 2, batch_at // 2, batch_at % 2
    else:
        z = x = y = c = jnp.zeros((), jnp.int32)
    mixer_role = device * mixer_weights.shape[0] // H
    mlp_role = device * mlp_weights.shape[0] // FF
    ids = jnp.stack([z, x, y, c, seq_at, device, mixer_role, mlp_role]).astype(jnp.int32)

    small_low = small_params.astype(bf16).astype(f32)
    slab = shape(ROLES, ROWS, D, dtype=bf16)
    if direct:
        pair_of = near(2, ROWS, D, dtype=bf16)
        count = small_params.shape[0]
        small_line = jnp.broadcast_to(jnp.pad(small_low, (0, ROWS - count))[None], (SEG, ROWS))
        packed = call(
            pack_kernel, "mixer_pack", near(ROWS + TAIL, D, dtype=bf16),
            ids, mixer_weights, small_line, exchange(small_line, 0, 1),
        )
        mixer_two = call(
            stack_kernel, "mixer_pair", near(2, ROWS + TAIL, D, dtype=bf16), packed, exchange_z_lane(packed, False)
        )
        mixer_far = exchange_z_lane(mixer_two, True)
        mlp_low = after(mlp_weights, packed).astype(bf16)
        mlp_two = call(stack_kernel, "mlp_pair", pair_of, mlp_low, exchange_lane(mlp_low, False))
        mlp_plane = call(stack_kernel, "mlp_plane", slab, mlp_two, exchange_lane(mlp_two, True))
        gate_slab = call(
            slab_kernel, "mixer_slab", shape(ROLES * ROWS + TAIL, D, dtype=bf16),
            ids, mixer_two, mixer_far, order=[mlp_plane], scratch=[pltpu.VMEM((TAIL, D), f32)],
        )
        mixer_own = [gate_slab] + [exchange(gate_slab, *bits) for bits in PLANE_BITS[1:]]
        mlp_plane = after(mlp_plane, gate_slab)
        mlp_early = call(
            stack_kernel, "mlp_early", shape(2, PLANES, ROWS, D, dtype=bf16), mlp_plane, exchange_z_lane(mlp_plane, False)
        )
        mlp_late = exchange_z_lane(mlp_early, True)
    else:
        small_used = lax.all_gather(small_low, AXES, axis=0, tiled=True)

        def gathered(shard):
            full = lax.all_gather(shard.astype(bf16), AXES, axis=0, tiled=True)
            return full.reshape(ROLES, PLANES, 2, ROWS, D)

        full = gathered(mixer_weights)
        mixer_own, mixer_par = [[full[:, p, k].reshape(ROLES * ROWS, D) for p in range(PLANES)] for k in range(2)]
        full = gathered(mlp_weights)
        mlp_parts = [full[roles, :, k] for k in range(2) for roles in (slice(0, 2), slice(2, 4))]

    doc_ends = jnp.cumsum(doc_lengths, axis=1)
    doc_starts = doc_ends - doc_lengths
    place = lax.iota(jnp.int32, block)
    position = seq_at * block + (place % SEG) * (block // SEG) + place // SEG
    begins = jnp.any(position[None, :, None] == doc_starts[:, None, :], axis=2) | (
        position[None, :] == doc_ends[:, -1:]
    )
    valid = (position[None, :] < doc_ends[:, -1:]).astype(f32).reshape(rows, 1)
    restart = (1.0 - begins.astype(f32)).reshape(rows, 1)

    wide = near(rows, HALF)
    natural = shape(streams, block, D, dtype=bf16)
    low_wide = near(rows, HALF, dtype=bf16)
    low_rows = near(rows, D, dtype=bf16)
    ends = near(2 * SEG, HALF)
    projections = [pltpu.VMEM((rows, HALF), f32)] * 3

    if direct:
        mixer_own = [gate_slab, *after(tuple(mixer_own[1:]), mlp_early, restart, valid)]
        mixer_par = [exchange(part, 0, 1) for part in mixer_own]
        normed, gain_one, gain_two, fb_o, fb_p, ib_o, ib_p = call(
            lambda *refs: unpack_kernel(count, *refs), "first_norm", [low_rows] + [near(1, D)] * 2 + [near(1, HALF)] * 4,
            ids, tokens, far=mixer_own,
            scratch=[
                pltpu.VMEM((4 * SEG, ROWS), f32), pltpu.VMEM((3 * SEG, ROWS), f32),
                pltpu.SemaphoreType.DMA((PLANES,)), pltpu.VMEM((PLANES, TAIL, D), bf16),
            ],
        )
        scan_order = []
    else:
        gain_one, gain_two = small_used[:D][None], small_used[D : 2 * D][None]
        biases = small_used[2 * D :].reshape(2, PLANES, 2, ROWS).transpose(0, 2, 1, 3).reshape(4, 1, HALF)
        fb_o, fb_p, ib_o, ib_p = [biases[k] for k in range(4)]
        normed = call(normed_kernel, "first_norm", low_rows, tokens, gain_one)
        scan_order = []
    retain_o, acc_o, tot_o, sega_o, segb_o = call(
        lambda *refs: scan_kernel(True, *refs), "scan_own", [wide, wide, near(4, HALF), ends, ends],
        normed, restart, fb_o, ib_o, far=mixer_own, scratch=projections + weight_scratch(GATES, 1),
    )
    retain_p, acc_p, tot, sega_p, segb_p = call(
        lambda *refs: scan_kernel(False, *refs), "scan_other", [wide, wide, near(4, H), ends, ends],
        normed, restart, fb_p, ib_p, tot_o, far=mixer_par, order=scan_order,
        scratch=projections + weight_scratch(GATES, 1),
    )

    incoming = relay(ids, tot, True, direct, {})
    if direct:
        mlp_late = after(mlp_late, incoming)
        mlp_parts = [mlp_early, mlp_late, exchange(mlp_early, 0, 1), exchange(mlp_late, 0, 1)]

    states_o, states_p, low_o, low_p, resid, normed_two = call(
        states_kernel, "states", [wide, wide, low_wide, low_wide, near(rows, D), low_rows],
        incoming, tokens, gain_two, retain_o, retain_p, acc_o, acc_p, sega_o, sega_p, segb_o, segb_p,
        far=[*mixer_own, *mixer_par], scratch=weight_scratch(1, 2),
    )

    terms = near(PLANES, ROLES, ROWS, D, dtype=bf16)
    output, d_resid, d_gain_two, mlp_gown, mlp_gpar = call(
        mlp_kernel, "mlp", [natural, near(rows, D), near(1, D), terms, terms],
        ids, normed_two, resid, cotangent, valid, gain_two, far=mlp_parts, mib=16,
        scratch=[
            pltpu.VMEM((PLANES, 2, ROLES, ROWS, D), bf16), pltpu.SemaphoreType.DMA((PLANES, 2, ROLES)),
            pltpu.VMEM((rows, D), bf16), pltpu.VMEM((rows, D), f32), pltpu.VMEM((rows, D), f32),
        ],
    )

    half_terms = near(PLANES, 1, ROWS, D, dtype=bf16)
    back_o, back_p, tot_back, bseg_o, bseg_p, out_gown, out_gpar = call(
        back_kernel, "back_scan", [wide, wide, near(4, H), ends, ends, half_terms, half_terms],
        d_resid, low_o, low_p, retain_o, retain_p, sega_o, sega_p, far=[*mixer_own, *mixer_par],
        scratch=weight_scratch(1, 2),
    )

    kept_terms = {}

    def terms_own(ready):
        kept_terms["own"] = call(
            lambda *refs: terms_kernel(True, *refs), "terms_own", [low_rows] + [wide] * 4,
            tokens, gain_one, fb_o, ib_o, far=mixer_own, order=[ready],
            scratch=projections[:2] + weight_scratch(GATES, 1),
        )
        return kept_terms["own"][0]

    def terms_other(ready):
        kept_terms["other"] = call(
            lambda *refs: terms_kernel(False, *refs), "terms_other", [wide] * 4,
            kept_terms["own"][0], fb_p, ib_p, far=mixer_par, order=[ready],
            scratch=projections[:2] + weight_scratch(GATES, 1),
        )
        return kept_terms["other"][0]

    beside = {1: terms_own, 4: terms_other}
    if direct:
        mlp_got, out_got = exchange(mlp_gpar, 0, 1), exchange(out_gpar, 0, 1)
        two_fives = near(2, ROLES + 1, ROWS, D, dtype=bf16)

        def mlp_pair(ready):
            kept_terms["mlp"] = call(
                mlp_pair_kernel, "mlp_pair_sum", [two_fives] * 2, ids, mlp_gown, mlp_got, out_gown, out_got,
                order=[ready],
            )
            return kept_terms["mlp"][0]

        beside[2] = mlp_pair

    arriving = relay(ids, tot_back, False, direct, beside)
    normed, *terms_o = kept_terms["own"]
    terms_p = kept_terms["other"]
    if direct:
        mlp_keep, mlp_send = kept_terms["mlp"]
        mlp_got = exchange_lane(mlp_send, True)

    def gates_back(column, back, sega, bseg, share, df, di, cand, retain, states, order, name):
        return call(
            lambda *refs: gates_kernel(column, *refs), name,
            [near(PLANES, GATES, ROWS, D, dtype=bf16), low_wide, low_wide, low_wide, near(1, HALF), near(1, HALF)],
            arriving, incoming, back, sega, bseg, share, df, di, cand, retain, states, restart, normed, order=order,
        )

    gate_gpar, pf_p, pi_p, pc_p, dfb_p, dib_p = gates_back(
        HALF, back_p, sega_p, bseg_p, *terms_p, retain_p, states_p, [tot_back], "gates_other"
    )
    gate_gown, pf_o, pi_o, pc_o, dfb_o, dib_o = gates_back(
        0, back_o, sega_o, bseg_o, *terms_o, retain_o, states_o, [dfb_p], "gates_own"
    )

    order = [dfb_o]
    if direct:
        five = near(ROLES + 1, ROWS, D, dtype=bf16)
        mlp_own_sum, mlp_next = call(
            half_sum_kernel, "mlp_half_sum", [five, five], mlp_keep, mlp_got, order=[dfb_o]
        )
        order = [mlp_own_sum]
    d_normed, small_terms = call(
        input_terms_kernel, "input_terms", [near(rows, D), near(TAIL, D)],
        ids, tokens, d_gain_two, dfb_o, dfb_p, dib_o, dib_p,
        pf_o, pi_o, pc_o, pf_p, pi_p, pc_p, far=[*mixer_own, *mixer_par], order=order,
        scratch=[pltpu.VMEM((3 * SEG, ROWS), f32)] + weight_scratch(GATES, 2),
    )

    def input_grad(ready):
        return call(input_kernel, "input_grad", [natural, near(SEG, ROWS)], tokens, gain_one, d_resid, d_normed, order=[ready])

    def with_moments(keep, got, weight, first_moment, second, name):
        count = weight.shape[0]
        return call(
            moments_kernel, name, [shape(count, D)] * 3 + [near(count, D)] + [near(SEG, 128)] * 2,
            keep, got, weight, first_moment, second,
        )

    if direct:
        shard, low_shard = near(ROWS, D), near(ROWS, D, dtype=bf16)
        long, low_long = near(ROWS + TAIL, D), near(ROWS + TAIL, D, dtype=bf16)
        gate_parts = call(
            gate_pair_kernel, "gate_pair_sum", [near(GATES * ROWS + TAIL, D, dtype=bf16)] * PLANES,
            gate_gown, exchange(gate_gpar, 0, 1), small_terms, exchange(small_terms, 0, 1), order=[mlp_own_sum],
        )
        gate_round = [gate_parts[0]] + [
            exchange(part, *bits) for part, bits in zip(gate_parts[1:], PLANE_BITS[1:], strict=True)
        ]
        d_x, x_done = input_grad(gate_parts[0])
        two = near(2, ROWS, D, dtype=bf16)
        mlp_keep, mlp_send, out_sum = call(
            mlp_plane_kernel, "mlp_plane_sum", [two, two, low_shard], ids, mlp_own_sum, exchange_lane(mlp_next, False)
        )
        mlp_stay, mlp_send = call(
            mlp_far_kernel, "mlp_z_sum", [shard, low_shard], mlp_keep, exchange_z_lane(mlp_send, False)
        )
        mlp_done = with_moments(
            mlp_stay, exchange_z_lane(mlp_send, True), mlp_weights, mlp_first, mlp_second, "mlp_moments"
        )
        gate_keep, *gate_sends = call(
            gate_plane_kernel, "gate_plane_sum", [long] + [low_long] * 3, ids, *gate_round, out_sum,
            order=[mlp_done[-1], x_done],
        )
        gate_got = z_terms(gate_sends)
    else:

        def scattered(own, par):
            full_terms = jnp.stack([own, par]).transpose(2, 1, 0, 3, 4).reshape(-1, D)
            return lax.psum_scatter(full_terms, AXES, scatter_dimension=0, tiled=True).astype(f32)

        d_x, _ = input_grad(small_terms)
        mlp_grad = scattered(mlp_gown, mlp_gpar)
        mixer_grad = scattered(
            jnp.concatenate([gate_gown, out_gown], axis=1), jnp.concatenate([gate_gpar, out_gpar], axis=1)
        )
        none = jnp.zeros_like(mlp_grad, dtype=bf16)
        mlp_done = with_moments(mlp_grad, none, mlp_weights, mlp_first, mlp_second, "mlp_moments")
        gate_keep = jnp.concatenate([mixer_grad, lax.psum(small_terms, AXES)], axis=0)
        gate_got = [jnp.zeros_like(gate_keep, dtype=bf16)] * 3
    mlp_grad, mlp_first_new, mlp_second_new, mlp_dir, mlp_wsum, mlp_dsum = mlp_done
    count, mixer_count = small_params.shape[0], mixer_weights.shape[0]
    line, matrix = shape(1, count), shape(mixer_count, D)
    mixer_grad, mixer_first_new, mixer_second_new, mixer_dir, small_grad, small_first_new, small_second_new, small_dir, squares = call(
        finish_kernel, "finish", [matrix] * 3 + [near(mixer_count, D)] + [line] * 3 + [near(1, count), near(SEG, ROWS)],
        ids, gate_keep, *gate_got, mlp_wsum, mlp_dsum, mixer_weights, mixer_first, mixer_second,
        small_params[None], small_first[None], small_second[None], scratch=[pltpu.VMEM((4 * SEG, ROWS), f32)],
    )

    def update(sums, slot, base, weight, direction, name):
        return call(
            lambda *refs: matrix_update_kernel(slot, base, *refs), name,
            [shape(*weight.shape), shape(*weight.shape, dtype=bf16), near(SEG, ROWS)], ids, sums, weight, direction,
        )

    if direct:
        sums = squares
        for bits in ((0, 1), (0, 2), (1, 0)):
            sums = sums + exchange(sums, *bits)
        mixer_new, mixer_copy, mixer_updated = update(sums, MIXER_ROLE, 0, mixer_weights, mixer_dir, "mixer_update")
        sums = after(sums + exchange(sums, 2, 0), mixer_updated)
        mlp_new, mlp_copy, mlp_updated = update(sums, MLP_ROLE, ROLES, mlp_weights, mlp_dir, "mlp_update")
        sums = sums + exchange(sums, 4, 0)
    else:
        sums = all_sum(squares)
        mixer_new, mixer_copy, mixer_updated = update(sums, MIXER_ROLE, 0, mixer_weights, mixer_dir, "mixer_update")
        mlp_new, mlp_copy, mlp_updated = update(sums, MLP_ROLE, ROLES, mlp_weights, mlp_dir, "mlp_update")
    small_new, small_copy, tensor_norms, trust_ratios = call(
        small_update_kernel, "small_update", [line, shape(1, count, dtype=bf16), shape(2, 10), shape(1, 10)],
        ids, sums, small_params[None], small_dir, order=[mixer_updated, mlp_updated],
    )
    return (
        output,
        d_x,
        mixer_grad,
        mlp_grad,
        small_grad[0],
        mixer_first_new,
        mixer_second_new,
        mlp_first_new,
        mlp_second_new,
        small_first_new[0],
        small_second_new[0],
        mixer_new,
        mlp_new,
        small_new[0],
        mixer_copy,
        mlp_copy,
        small_copy[0],
        tensor_norms,
        trust_ratios[0],
    )


def solution(mesh):
    shard = P(("seq", "batch"), None)
    shard_flat = P(("seq", "batch"))
    stream = P("batch", "seq", None)
    return jax.shard_map(
        on_device,
        mesh=mesh,
        in_specs=(
            stream, P("batch", None), stream, shard, shard, shard_flat,
            shard, shard, shard, shard, shard_flat, shard_flat,
        ),
        out_specs=(
            stream, stream, shard, shard, shard_flat, shard, shard, shard, shard, shard_flat, shard_flat,
            shard, shard, shard_flat, shard, shard, shard_flat, P(), P(),
        ),
        check_vma=False,
    )
```

```python
import functools

import jax
import jax.numpy as jnp
from jax import lax
from jax.experimental import pallas as pl
from jax.experimental.pallas import tpu as pltpu
from jax.sharding import PartitionSpec as P

D = 512
H = 1024
FF = 2048
STEP = 5
SEG = 8
ROWS = 128
PLANES = 4
HALF = PLANES * ROWS
GATES = 3
ROLES = 4
TAIL = 16
SMALL_BLOCKS = 3
Z, X, Y, CORE, SEQ, DEVICE, MIXER_ROLE, MLP_ROLE = range(8)

first_decay = 0.5
second_decay = 0.5
learn_rate = 0.25
matrix_decay = 0.01
moment_eps = 1e-06

f32 = jnp.float32
bf16 = jnp.bfloat16
AXES = ("seq", "batch")

PLANE_BITS = ((0, 0), (0, 2), (1, 0), (1, 2))


def dot_nt(a, b):
    return lax.dot_general(a, b, (((1,), (1,)), ((), ())), preferred_element_type=f32)


def dot_nn(a, b):
    return lax.dot_general(a, b, (((1,), (0,)), ((), ())), preferred_element_type=f32)


def dot_tn(a, b):
    return lax.dot_general(a, b, (((0,), (0,)), ((), ())), preferred_element_type=f32)


def exchange(value, seq_bits, batch_bits, targets=None):
    seqs, batches = lax.axis_size("seq"), lax.axis_size("batch")
    pairs = [
        (s * batches + b, (s ^ seq_bits) * batches + (b ^ batch_bits))
        for s in range(seqs)
        for b in range(batches)
        if targets is None or (s ^ seq_bits) in targets
    ]
    return lax.ppermute(value, AXES, pairs)


def unit(x):
    return lax.rsqrt(jnp.mean(x * x, axis=-1, keepdims=True) + 1e-05)


def rms_back(x, d_normed, gain):
    scale = unit(x)
    normal = x * scale
    d_unit = d_normed * gain
    mean = jnp.mean(d_unit * normal, axis=-1, keepdims=True)
    return jnp.sum(d_normed * normal, axis=0, keepdims=True), scale * (d_unit - normal * mean)


def gather_roles(slabs, held):
    for role in range(GATES):
        for q, ref in enumerate(slabs):
            held[role, pl.ds(q * ROWS, ROWS)] = ref[pl.ds(role * ROWS, ROWS), :]


def group(s, steps, j):
    return pl.ds(pl.multiple_of((s * steps + j) * SEG, SEG), SEG)


def pair(s, steps, j):
    return pl.ds(pl.multiple_of((s * steps + 2 * j) * SEG, 2 * SEG), 2 * SEG)


def segment_order(block):
    row = lax.broadcasted_iota(jnp.int32, (block, block), 0)
    position = lax.broadcasted_iota(jnp.int32, (block, block), 1)
    return jnp.where(position == (row % SEG) * (block // SEG) + row // SEG, 1.0, 0.0).astype(bf16)


def inward(ref):
    order = segment_order(ref.shape[1])
    return jnp.concatenate([dot_nn(order, ref[s]) for s in range(2)], axis=0)


def outward(ref, value):
    block = ref.shape[1]
    order = segment_order(block)
    for s in range(2):
        ref[s] = dot_tn(order, value[s * block : (s + 1) * block]).astype(bf16)


def z_of(ids_ref, k, core):
    return ids_ref[Z] ^ (jnp.where(core == 0, k, 3 - k) if k in (1, 2) else k)


def pack_kernel(ids_ref, weights_ref, small_ref, got_ref, out_ref):
    out_ref[pl.ds(0, ROWS), :] = weights_ref[...].astype(bf16)
    mine, other = small_ref[...], got_ref[...]
    core = ids_ref[CORE]
    line = jnp.concatenate(
        [jnp.where(core == 0, mine, other), jnp.where(core == 0, other, mine), jnp.zeros((SEG, D - 2 * ROWS), f32)], axis=1
    )
    out_ref[pl.ds(ROWS, TAIL), :] = jnp.concatenate([line, jnp.zeros_like(line)], axis=0).astype(bf16)


def slab_kernel(ids_ref, early_ref, late_ref, *refs):
    slab_ref, lines = refs[-2:]
    lines[...] = jnp.zeros_like(lines)
    for k in range(ROLES):
        part = (early_ref, late_ref)[k // 2].at[k % 2]
        role = z_of(ids_ref, k, ids_ref[CORE])
        slab_ref[pl.ds(pl.multiple_of(role * ROWS, ROWS), ROWS), :] = part[pl.ds(0, ROWS), :]
        lines[pl.ds(role, 1), :] = part[pl.ds(ROWS, TAIL), :].astype(f32)[0:1]
    slab_ref[pl.ds(ROLES * ROWS, TAIL), :] = lines[...].astype(bf16)


def marks_kernel(ids_ref, lengths_ref, restart_ref, valid_ref):
    block = restart_ref.shape[0] // 2
    row = lax.broadcasted_iota(jnp.int32, (block, 1), 0)
    position = ids_ref[SEQ] * block + (row % SEG) * (block // SEG) + row // SEG
    for s in range(2):
        begins = jnp.zeros((block, 1), jnp.bool_)
        end = 0
        for k in range(lengths_ref.shape[1]):
            begins = begins | (position == end)
            end = end + lengths_ref[s, k]
        begins = begins | (position == end)
        restart_ref[pl.ds(s * block, block), :] = jnp.where(begins, 0.0, 1.0)
        valid_ref[pl.ds(s * block, block), :] = jnp.where(position < end, 1.0, 0.0)


def stack_kernel(first_ref, second_ref, *refs):
    out_ref = refs[-1]
    if first_ref.shape == out_ref.shape[1:]:
        out_ref[0], out_ref[1] = first_ref[...], second_ref[...]
    else:
        count = first_ref.shape[0]
        out_ref[:count], out_ref[count:] = first_ref[...], second_ref[...]


def normed_kernel(tok_ref, gain_ref, normed_ref):
    normed_ref[...] = first_norm(tok_ref, gain_ref)


def relay_kernel(bit, forward, flipped, ids_ref, group_ref, other_ref, *refs):
    late = ((ids_ref[SEQ] & bit) != 0) == forward
    mine, other = group_ref[...], other_ref[...]
    if flipped:
        quarter = HALF // 2
        at = (quarter, 0, 3 * quarter, 2 * quarter)
        other = jnp.concatenate([other[:, k : k + quarter] for k in at], axis=1)
    if bit == 1:
        decay, state = jnp.ones_like(mine[:2]), jnp.zeros_like(mine[:2])
    else:
        decay, state = refs[0][0:2, :], refs[0][2:4, :]
    state = jnp.where(late, decay * other[2:] + state, state)
    if refs[-1].shape[0] == 2:
        refs[-1][...] = state
        return
    group_out, before_out = refs[-2:]
    before_out[...] = jnp.concatenate([jnp.where(late, decay * other[:2], decay), state], axis=0)
    first, second = jnp.where(late, other, mine), jnp.where(late, mine, other)
    group_out[...] = jnp.concatenate([first[:2] * second[:2], second[:2] * first[2:] + second[2:]], axis=0)


def gate_shares(f, i):
    most = jnp.maximum(jnp.maximum(-f, -i), 0.0)
    one, low_f, low_i = jnp.exp(-most), jnp.exp(-f - most), jnp.exp(-i - most)
    inverse = 1.0 / ((one + low_i) + (one + low_f))
    return (one + low_i) * inverse, (one + low_f) * inverse, low_f * inverse, low_i * inverse


def first_norm(tok_ref, gain_ref):
    x = inward(tok_ref)
    return (x * unit(x) * gain_ref[...]).astype(bf16)


def unpack(count, ids_ref, slabs, by_device, flat):
    chips = [2 * (ids_ref[X] ^ (k // 2)) + (ids_ref[Y] ^ (k % 2)) for k in range(PLANES)]
    for k, ref in enumerate(slabs):
        lines = ref[pl.ds(ROLES * ROWS, TAIL), :].astype(f32)
        for z in range(ROLES):
            for core in range(2):
                row = z * 2 * PLANES + 2 * chips[k] + core
                by_device[pl.ds(row, 1), :] = lines[z : z + 1, core * ROWS : (core + 1) * ROWS]
    parts = [by_device[pl.ds(k, 8, stride=4), :] for k in range(4)]
    for k in range(3):
        cut = ROWS - (k + 1) * (ROWS - count)
        row = jnp.concatenate([parts[k][:, k * (ROWS - count) : count], parts[k + 1][:, : ROWS - cut]], axis=1)
        flat[pl.ds(k, 8, stride=3), :] = row
    rows = [flat[pl.ds(k, 1), :] for k in range(2 * PLANES)]
    yield jnp.concatenate(rows[:PLANES], axis=1)
    yield jnp.concatenate(rows[PLANES:], axis=1)
    for base in (2 * PLANES, 4 * PLANES):
        for half in range(2):
            at = [base + 2 * chips[k] + (ids_ref[CORE] ^ half) for k in range(PLANES)]
            yield jnp.concatenate([flat[pl.ds(row, 1), :] for row in at], axis=1)


def scan_halves(normed, f_bias, i_bias, rs_ref, held, both_ref, tot_ref, columns, sega_ref, segb_ref, f_ref, i_ref, c_ref):
    for role, ref in enumerate((f_ref, i_ref, c_ref)):
        ref[...] = dot_nt(normed, held[role])
    steps = normed.shape[0] // (2 * SEG)

    def step(j, carry):
        after = []
        for s in range(2):
            at = group(s, steps, j)
            keep, share, _, _ = gate_shares(f_ref[at, :] + f_bias, i_ref[at, :] + i_bias)
            a = keep * rs_ref[at, :]
            b = a * carry[s][1] + share * c_ref[at, :]
            both_ref[0, at, :] = a
            both_ref[1, at, :] = b
            after.append((a * carry[s][0], b))
        return tuple(after)

    start = (jnp.ones((SEG, HALF), f32), jnp.zeros((SEG, HALF), f32))
    ends = lax.fori_loop(0, steps, step, (start, start), unroll=steps)
    for s, (seg_a, seg_b) in enumerate(ends):
        sega_ref[pl.ds(s * SEG, SEG), :] = seg_a
        segb_ref[pl.ds(s * SEG, SEG), :] = seg_b
        tot_a, tot_b = seg_a[0:1], seg_b[0:1]
        for k in range(1, SEG):
            a = seg_a[k : k + 1]
            tot_a, tot_b = a * tot_a, a * tot_b + seg_b[k : k + 1]
        tot_ref[pl.ds(s, 1), columns] = tot_a
        tot_ref[pl.ds(2 + s, 1), columns] = tot_b


def scan_first_kernel(count, ids_ref, tok_ref, rs_ref, *refs):
    slabs, outs, scratch = refs[:PLANES], refs[PLANES:-5], refs[-5:]
    normed_ref, gain_one_ref, gain_two_ref, fo_ref, fp_ref, io_ref, ip_ref, held, both_ref, tot_ref, sega_ref, segb_ref = outs
    f_ref, i_ref, c_ref, by_device, flat = scratch
    gather_roles(slabs, held)
    small = unpack(count, ids_ref, slabs, by_device, flat)
    for ref, value in zip((gain_one_ref, gain_two_ref, fo_ref, fp_ref, io_ref, ip_ref), small, strict=True):
        ref[...] = value
    normed_ref[...] = first_norm(tok_ref, gain_one_ref)
    scan_halves(
        normed_ref[...], fo_ref[...], io_ref[...], rs_ref, held, both_ref, tot_ref, pl.ds(0, HALF),
        sega_ref, segb_ref, f_ref, i_ref, c_ref,
    )


def scan_kernel(first, normed_ref, rs_ref, fb_ref, ib_ref, *refs):
    if not first:
        earlier_ref, *refs = refs
    slabs, (held, both_ref, tot_ref, sega_ref, segb_ref, f_ref, i_ref, c_ref) = refs[:PLANES], refs[-8:]
    gather_roles(slabs, held)
    if not first:
        tot_ref[:, pl.ds(0, HALF)] = earlier_ref[...]
    scan_halves(
        normed_ref[...], fb_ref[...], ib_ref[...], rs_ref, held, both_ref, tot_ref,
        pl.ds(0 if first else HALF, HALF), sega_ref, segb_ref, f_ref, i_ref, c_ref,
    )


def dout_kernel(cot_ref, valid_ref, *refs):
    refs[-1][...] = (inward(cot_ref) * valid_ref[...]).astype(bf16)


def terms_kernel(normed_ref, fb_ref, ib_ref, held, *refs):
    share_ref, df_ref, di_ref, cand_ref, f_ref, i_ref = refs[-6:]
    normed = normed_ref[...]
    for role, ref in enumerate((f_ref, i_ref, cand_ref)):
        ref[...] = dot_nt(normed, held[role])
    f_bias, i_bias = fb_ref[...], ib_ref[...]

    def step(j, carry):
        at = pl.ds(pl.multiple_of(j * 2 * SEG, 2 * SEG), 2 * SEG)
        keep, share, slow_f, slow_i = gate_shares(f_ref[at, :] + f_bias, i_ref[at, :] + i_bias)
        share_ref[at, :] = share
        df_ref[at, :] = keep * slow_f
        di_ref[at, :] = share * slow_i
        return carry

    lax.fori_loop(0, normed.shape[0] // (2 * SEG), step, 0, unroll=4)


def states_kernel(inc_ref, tok_ref, gain_ref, both_o, both_p, sega_o, sega_p, segb_o, segb_p, *refs):
    slabs, refs = refs[: 2 * PLANES], refs[2 * PLANES :]
    states_o, states_p, low_o, low_p, resid_ref, normed_ref, held = refs
    steps = resid_ref.shape[0] // (2 * SEG)
    halves = (
        (both_o, sega_o, segb_o, states_o, low_o, 0),
        (both_p, sega_p, segb_p, states_p, low_p, HALF),
    )
    start = []
    for _, sega, segb, _, _, column in halves:
        for s in range(2):
            seg_a, seg_b = sega[pl.ds(s * SEG, SEG), :], segb[pl.ds(s * SEG, SEG), :]
            at_seg = [inc_ref[pl.ds(s, 1), pl.ds(column, HALF)]]
            for k in range(SEG - 1):
                at_seg.append(seg_a[k : k + 1] * at_seg[-1] + seg_b[k : k + 1])
            start.append(jnp.concatenate(at_seg, axis=0))

    def step(j, carry):
        after = []
        for k, (both, _, _, states, low, _) in enumerate(halves):
            for s in range(2):
                carried, two = carry[2 * k + s], []
                for q in range(2):
                    at = group(s, steps, 2 * j + q)
                    carried = both[0, at, :] * carried
                    two.append(both[1, at, :] + carried)
                    states[at, :] = two[-1]
                low[pair(s, steps, j), :] = jnp.concatenate(two, axis=0).astype(bf16)
                after.append(carried)
        return tuple(after)

    lax.fori_loop(0, steps // 2, step, tuple(start), unroll=4)
    r = inward(tok_ref)
    for q, ref in enumerate(slabs):
        held[0, pl.ds(q * ROWS, ROWS)] = ref[pl.ds(GATES * ROWS, ROWS), :]
    for low, k in zip((low_o, low_p), range(2), strict=True):
        r = r + dot_nn(low[...], held[0, pl.ds(k * HALF, HALF)])
    resid_ref[...] = r
    normed_ref[...] = (r * unit(r) * gain_ref[...]).astype(bf16)


GELU_A = 0.7978845608028654
GELU_B = 0.044715


def mlp_kernel(ids_ref, normed_ref, resid_ref, dout_ref, valid_ref, gain_ref, *refs):
    parts, refs = refs[:4], refs[4:]
    output_ref, dresid_ref, dgain_ref, gown_ref, gpar_ref, held, outer_ref, dnorm_ref = refs

    def bring(at):
        for half in range(2):
            for k in range(ROLES):
                role = z_of(ids_ref, k, ids_ref[CORE] ^ half)
                held[at, half, pl.ds(role, 1)] = parts[2 * half + k // 2][k % 2, at].reshape(1, ROWS, D)

    bring(0)
    outer_ref[...] = jnp.zeros_like(outer_ref)
    dnorm_ref[...] = jnp.zeros_like(dnorm_ref)

    normed, dout = normed_ref[...], dout_ref[...]

    def ahead(i):
        at, low = i // 2, i % 2
        if low == 1 and at + 1 < PLANES:
            bring(at + 1)
        w_up = held[at, :, low].reshape(2 * ROWS, D)
        w_down = held[at, :, low + 2].reshape(2 * ROWS, D)
        return dot_nt(normed, w_up), dot_nt(dout, w_down), w_up, w_down

    now = ahead(0)
    for i in range(2 * PLANES):
        inner, d_act, w_up, w_down = now
        if i + 1 < 2 * PLANES:
            now = ahead(i + 1)
        square = inner * inner
        curve = jnp.tanh(inner * (GELU_A + GELU_A * GELU_B * square))
        half = 0.5 + 0.5 * curve
        activated = (inner * half).astype(bf16)
        slope = half + (half - half * half) * (inner * (2.0 * GELU_A + 6.0 * GELU_A * GELU_B * square))
        d_inner = (slope * d_act).astype(bf16)
        outer_ref[...] += dot_nn(activated, w_down)
        dnorm_ref[...] += dot_nn(d_inner, w_up)
        g_up = dot_tn(d_inner, normed).astype(bf16).reshape(2, ROWS, D)
        g_down = dot_tn(activated, dout).astype(bf16).reshape(2, ROWS, D)
        for k, ref in enumerate((gown_ref, gpar_ref)):
            ref[i // 2, i % 2] = g_up[k]
            ref[i // 2, i % 2 + 2] = g_down[k]
    r = resid_ref[...]
    outward(output_ref, ((r + outer_ref[...]) * valid_ref[...]).astype(bf16))
    dgain_ref[...], d_r = rms_back(r, dnorm_ref[...], gain_ref[...])
    dresid_ref[...] = dout_ref[...].astype(f32) + d_r


def back_kernel(dresid_ref, low_o, low_p, retain_o, retain_p, sega_o, sega_p, held, *refs):
    acc_o, acc_p, tot_ref, segb_o, segb_p, gown_ref, gpar_ref = refs
    steps = dresid_ref.shape[0] // (2 * SEG)
    dmix = dresid_ref[...].astype(bf16)
    for acc, k in zip((acc_o, acc_p), range(2), strict=True):
        acc[...] = dot_nt(dmix, held[0, pl.ds(k * HALF, HALF)])
    halves = ((retain_o, acc_o), (retain_p, acc_p))

    def step(n, carry):
        after = []
        for k, (retain, acc) in enumerate(halves):
            for s in range(2):
                at = group(s, steps, steps - 1 - n)
                back = acc[at, :] + carry[2 * k + s]
                acc[at, :] = back
                after.append(retain[0, at, :] * back)
        return tuple(after)

    ends = lax.fori_loop(0, steps, step, (jnp.zeros((SEG, HALF), f32),) * 4, unroll=8)
    for k, (sega, segb) in enumerate(((sega_o, segb_o), (sega_p, segb_p))):
        for s in range(2):
            emitted = ends[2 * k + s]
            segb[pl.ds(s * SEG, SEG), :] = emitted
            seg_a = sega[pl.ds(s * SEG, SEG), :]
            tot_a, tot_b = seg_a[SEG - 1 :], emitted[SEG - 1 :]
            for q in reversed(range(SEG - 1)):
                a = seg_a[q : q + 1]
                tot_a, tot_b = a * tot_a, a * tot_b + emitted[q : q + 1]
            tot_ref[pl.ds(s, 1), pl.ds(k * HALF, HALF)] = tot_a
            tot_ref[pl.ds(2 + s, 1), pl.ds(k * HALF, HALF)] = tot_b
    for low, ref in ((low_o, gown_ref), (low_p, gpar_ref)):
        ref[...] = dot_tn(low[...], dmix).astype(bf16).reshape(PLANES, 1, ROWS, D)


def gates_kernel(
    column, arr_ref, inc_ref, acc_ref, sega_ref, segb_ref, share_ref, df_ref, di_ref, cand_ref, retain_ref, states_ref,
    rs_ref, normed_ref, order_ref, grad_ref, pf_ref, pi_ref, pc_ref, dfb_ref, dib_ref,
):
    steps = normed_ref.shape[0] // (2 * SEG)
    start, first = [], []
    for s in range(2):
        seg_a, seg_b = sega_ref[pl.ds(s * SEG, SEG), :], segb_ref[pl.ds(s * SEG, SEG), :]
        at_seg = [arr_ref[pl.ds(s, 1), pl.ds(column, HALF)]]
        for k in reversed(range(1, SEG)):
            at_seg.append(seg_a[k : k + 1] * at_seg[-1] + seg_b[k : k + 1])
        start.append(jnp.concatenate(at_seg[::-1], axis=0))
        ends = states_ref[group(s, steps, steps - 1), :]
        first.append(jnp.concatenate([inc_ref[pl.ds(s, 1), pl.ds(column, HALF)], ends[: SEG - 1]], axis=0))

    def step(n, carry):
        *carried, sum_f, sum_i = carry
        m = steps // 2 - 1 - n
        for s in range(2):
            terms = []
            for q in (1, 0):
                j = 2 * m + q
                at = group(s, steps, j)
                back = acc_ref[at, :] + carried[s]
                carried[s] = carried[s] * retain_ref[0, at, :]
                previous = states_ref[group(s, steps, jnp.maximum(j - 1, 0)), :]
                if q == 0:
                    previous = jnp.where(m == 0, first[s], previous)
                both_ways = back * (previous * rs_ref[at, :] - cand_ref[at, :])
                d_f = both_ways * df_ref[at, :]
                d_i = both_ways * di_ref[at, :]
                sum_f = sum_f + d_f
                sum_i = sum_i - d_i
                terms.append((d_f, -d_i, back * share_ref[at, :]))
            for late, early, ref in zip(*terms, (pf_ref, pi_ref, pc_ref), strict=True):
                ref[pair(s, steps, m), :] = jnp.concatenate([early, late], axis=0).astype(bf16)
        return (*carried, sum_f, sum_i)

    nothing = jnp.zeros((SEG, HALF), f32)
    *_, sum_f, sum_i = lax.fori_loop(0, steps // 2, step, (*start, nothing, nothing), unroll=8)
    dfb_ref[...] = jnp.sum(sum_f, axis=0, keepdims=True)
    dib_ref[...] = jnp.sum(sum_i, axis=0, keepdims=True)
    normed = normed_ref[...]
    for role, ref in enumerate((pf_ref, pi_ref, pc_ref)):
        grad_ref[:, role] = dot_tn(ref[...], normed).astype(bf16).reshape(PLANES, ROWS, D)


def input_terms_kernel(ids_ref, tok_ref, dgain_two_ref, dfb_o, dfb_p, dib_o, dib_p, *refs):
    terms, weights, refs = refs[: 2 * GATES], refs[2 * GATES : 2 * GATES + 2], refs[-3:]
    dnorm_ref, small_ref, rows_ref = refs
    d_normed = 0.0
    for role in range(GATES):
        for k in range(2):
            d_normed = d_normed + dot_nn(terms[k * GATES + role][...], weights[k][role])
    dnorm_ref[...] = d_normed
    x = inward(tok_ref)
    d_gain = jnp.sum(d_normed * (x * unit(x)), axis=0, keepdims=True)
    for k in range(PLANES):
        rows_ref[pl.ds(k, 1), :] = d_gain[:, k * ROWS : (k + 1) * ROWS]
        rows_ref[pl.ds(PLANES + k, 1), :] = dgain_two_ref[:, pl.ds(k * ROWS, ROWS)]
        chip = 4 * (ids_ref[X] ^ (k // 2)) + 2 * (ids_ref[Y] ^ (k % 2))
        for core, (fb, ib) in enumerate(((dfb_o, dib_o), (dfb_p, dib_p))):
            row = 2 * PLANES + chip + (ids_ref[CORE] ^ core)
            rows_ref[pl.ds(row, 1), :] = fb[:, pl.ds(k * ROWS, ROWS)]
            rows_ref[pl.ds(row + 2 * PLANES, 1), :] = ib[:, pl.ds(k * ROWS, ROWS)]
    blocks = [rows_ref[pl.ds(k * SEG, SEG), :] for k in range(SMALL_BLOCKS)] + [jnp.zeros((SEG, ROWS), f32)]
    small_ref[...] = jnp.concatenate([jnp.concatenate(blocks, axis=1), jnp.zeros((SEG, D), f32)], axis=0)


def input_kernel(tok_ref, gain_ref, dresid_ref, dnorm_ref, order_ref, dx_ref, done_ref):
    done_ref[...] = jnp.zeros_like(done_ref)
    _, d_x = rms_back(inward(tok_ref), dnorm_ref[...], gain_ref[...])
    outward(dx_ref, (dresid_ref[...] + d_x).astype(bf16))


def mlp_pair_kernel(ids_ref, own_ref, got_ref, out_ref, outgot_ref, *refs):
    core = ids_ref[CORE]
    for k in range(PLANES):
        ref = refs[-2 + k // 2]
        ref[k % 2, pl.ds(0, ROLES)] = (own_ref[k].astype(f32) + got_ref[k].astype(f32)).astype(bf16)
        at = pl.ds(jnp.where(core == 0, 3 - k, k) if k in (1, 2) else k, 1)
        ref[k % 2, pl.ds(ROLES, 1)] = (out_ref[at, 0].astype(f32) + outgot_ref[at, 0].astype(f32)).astype(bf16)


def gate_pair_kernel(own_ref, got_ref, small_ref, small_got, *outs):
    small = (small_ref[...] + small_got[...]).astype(bf16)
    for k, ref in enumerate(outs[-PLANES:]):
        total = (own_ref[k].astype(f32) + got_ref[k].astype(f32)).astype(bf16)
        ref[pl.ds(0, GATES * ROWS), :] = total.reshape(GATES * ROWS, D)
        ref[pl.ds(GATES * ROWS, TAIL), :] = small


def half_sum_kernel(own_ref, got_ref, *refs):
    for k, ref in enumerate(refs[-2:]):
        ref[...] = (own_ref[k].astype(f32) + got_ref[k].astype(f32)).astype(bf16)


def mlp_plane_kernel(ids_ref, own_ref, got_ref, keep_ref, send_ref, out_ref):
    z = ids_ref[Z]
    near_bit = jnp.where(ids_ref[CORE] == 0, 1, 2)

    def total(role):
        at = pl.ds(role, 1)
        return (own_ref[at].astype(f32) + got_ref[at].astype(f32)).astype(bf16).reshape(ROWS, D)

    for k, role in enumerate((z, z ^ near_bit ^ 3)):
        keep_ref[k] = total(role)
        send_ref[k] = total(role ^ near_bit)
    out_ref[...] = total(ROLES)


def mlp_far_kernel(keep_ref, got_ref, *refs):
    stay_ref, send_ref = refs[-2:]
    stay_ref[...] = keep_ref[0].astype(f32) + got_ref[0].astype(f32)
    send_ref[...] = (keep_ref[1].astype(f32) + got_ref[1].astype(f32)).astype(bf16)


def gate_plane_kernel(ids_ref, p0, p1, p2, p3, out_ref, *refs):
    z = ids_ref[Z]
    keep_ref, s1_ref, s2_ref, s3_ref = refs[-4:]

    def total(at):
        terms = [ref[at, :].astype(f32) for ref in (p0, p1, p2, p3)]
        return (terms[0] + terms[1]) + (terms[2] + terms[3])

    def of_role(role):
        at = pl.ds(pl.multiple_of(jnp.minimum(role, GATES - 1) * ROWS, ROWS), ROWS)
        return jnp.where(role == GATES, out_ref[...].astype(f32), total(at))

    small = total(pl.ds(GATES * ROWS, TAIL))
    keep_ref[pl.ds(0, ROWS), :] = of_role(z)
    keep_ref[pl.ds(ROWS, TAIL), :] = small
    for k, ref in enumerate((s1_ref, s2_ref, s3_ref)):
        ref[pl.ds(0, ROWS), :] = of_role(z ^ (k + 1)).astype(bf16)
        ref[pl.ds(ROWS, TAIL), :] = small.astype(bf16)


def joined(at, keep_ref, gots):
    total = keep_ref[at, :]
    for ref in gots:
        total = total + ref[at, :].astype(f32)
    return total


def matrix_step(at, keep_ref, gots, weight_ref, first_ref, second_ref, outs):
    grad_ref, first_out, second_out, dir_ref = outs
    weight = weight_ref[...]
    gradient = joined(at, keep_ref, gots)
    grad_ref[...] = gradient
    first_out[...], second_out[...], direction = moments(
        weight, gradient, first_ref[...], second_ref[...], matrix_decay
    )
    dir_ref[...] = direction
    return weight, direction


def square_rows(value):
    square = jnp.sum((value * value).reshape(-1, SEG, D), axis=0)
    return (square[:, :128] + square[:, 128:256]) + (square[:, 256:384] + square[:, 384:])


def moments_kernel(keep_ref, got_ref, weight_ref, first_ref, second_ref, *outs):
    *outs, wsum_ref, dsum_ref = outs
    weight, direction = matrix_step(
        pl.ds(0, weight_ref.shape[0]), keep_ref, [got_ref], weight_ref, first_ref, second_ref, outs
    )
    wsum_ref[...] = square_rows(weight)
    dsum_ref[...] = square_rows(direction)


def finish_kernel(
    ids_ref, keep_ref, g1_ref, g2_ref, g3_ref, wsum_f, dsum_f,
    mixer_ref, mixer_first, mixer_second, weight_ref, first_ref, second_ref,
    mixer_grad, mixer_first_out, mixer_second_out, mixer_dir, grad_ref, first_out, second_out, dir_ref, squares_ref,
    rows_ref,
):
    gots = (g1_ref, g2_ref, g3_ref)
    mixer_rows = mixer_ref.shape[0]
    mixer_values = matrix_step(
        pl.ds(0, mixer_rows), keep_ref, gots, mixer_ref, mixer_first, mixer_second,
        (mixer_grad, mixer_first_out, mixer_second_out, mixer_dir),
    )
    total = joined(pl.ds(mixer_rows, TAIL), keep_ref, gots)
    rows_ref[...] = jnp.zeros_like(rows_ref)
    for k in range(SMALL_BLOCKS):
        rows_ref[pl.ds(k * SEG, SEG), :] = total[:SEG, k * ROWS : (k + 1) * ROWS]
    weight = weight_ref[...]
    count = weight.shape[1]
    start = ids_ref[DEVICE] * count
    row, lane = start // ROWS, start % ROWS
    two = jnp.concatenate([rows_ref[pl.ds(row, 1), :], rows_ref[pl.ds(row + 1, 1), :]], axis=1)
    two = jnp.broadcast_to(two, (SEG, 2 * ROWS))
    gradient = pltpu.roll(two, (2 * ROWS - lane) % (2 * ROWS), 1)[:1, :count]
    grad_ref[...] = gradient
    first_out[...], second_out[...], direction = moments(weight, gradient, first_ref[...], second_ref[...], 0.0)
    dir_ref[...] = direction
    place = start + lax.broadcasted_iota(jnp.int32, (1, count), 1)
    at = lax.broadcasted_iota(jnp.int32, (1, ROWS), 1)
    bounds = (0, D, 2 * D, 2 * D + H, 2 * D + 2 * H)
    lines = []
    for mixer_value, mlp_sum, value in zip(mixer_values, (wsum_f, dsum_f), (weight, direction), strict=True):
        line = jnp.where(at == ids_ref[MIXER_ROLE], jnp.sum(square_rows(mixer_value), keepdims=True), 0.0)
        line = line + jnp.where(at == ROLES + ids_ref[MLP_ROLE], jnp.sum(mlp_sum[...], keepdims=True), 0.0)
        for k in range(4):
            inside = (place >= bounds[k]) & (place < bounds[k + 1])
            part = jnp.sum(jnp.where(inside, value * value, 0.0), axis=1, keepdims=True)
            line = line + jnp.where(at == ROLES + 2 + k, part, 0.0)
        lines.append(line)
    squares_ref[...] = jnp.concatenate(lines + [jnp.zeros((SEG - 2, ROWS), f32)], axis=0)


def ratio_of(squares_ref, tensor):
    norms = jnp.sqrt(squares_ref[0:2, :])
    ratios = norms[0:1] / (norms[1:2] + 1e-06)
    at = lax.broadcasted_iota(jnp.int32, (1, ROWS), 1)
    return jnp.sum(jnp.where(at == tensor, ratios, 0.0), axis=1, keepdims=True)


def new_weights(ratio, weight_ref, dir_ref, new_ref, copy_ref):
    value = weight_ref[...] - learn_rate * ratio * dir_ref[...]
    new_ref[...] = value
    copy_ref[...] = value.astype(bf16)


def matrix_update_kernel(slot, base, ids_ref, squares_ref, weight_ref, dir_ref, new_ref, copy_ref, done_ref):
    done_ref[...] = jnp.zeros_like(done_ref)
    new_weights(ratio_of(squares_ref, base + ids_ref[slot]), weight_ref, dir_ref, new_ref, copy_ref)


def small_update_kernel(
    ids_ref, squares_ref, weight_ref, dir_ref, order_ref, order2_ref, new_ref, copy_ref, norms_ref, ratios_ref
):
    norms = jnp.sqrt(squares_ref[0:2, :])
    ratios = norms[0:1] / (norms[1:2] + 1e-06)
    norms_ref[...] = norms[:, : norms_ref.shape[1]]
    ratios_ref[...] = ratios[:, : ratios_ref.shape[1]]
    count = weight_ref.shape[1]
    place = ids_ref[DEVICE] * count + lax.broadcasted_iota(jnp.int32, (1, count), 1)
    first, second, third, fourth = (ratio_of(squares_ref, ROLES + 2 + k) for k in range(4))
    ratio = jnp.where(
        place < 2 * D, jnp.where(place < D, first, second), jnp.where(place < 2 * D + H, third, fourth)
    )
    new_weights(ratio, weight_ref, dir_ref, new_ref, copy_ref)


SMEM = pl.BlockSpec(memory_space=pltpu.SMEM)
ANY = pl.BlockSpec(memory_space=pl.ANY)
VMEM = pl.BlockSpec(memory_space=pltpu.VMEM)


def shape(*dims, dtype=f32):
    return jax.ShapeDtypeStruct(dims, dtype)


def near(*dims, dtype=f32):
    return pltpu.VMEM(dims, dtype)


def kept(value):
    return pltpu.with_memory_space_constraint(value, pltpu.VMEM)


def away(value):
    return pltpu.with_memory_space_constraint(value, pltpu.HBM)


def call(kernel, name, out_shape, *args, order=(), far=(), scratch=(), mib=8):
    in_specs = [SMEM if arg.dtype == jnp.int32 else VMEM for arg in args] + [ANY] * (len(far) + len(order))
    return pl.pallas_call(
        kernel,
        in_specs=in_specs,
        out_specs=jax.tree.map(lambda _: VMEM, out_shape),
        out_shape=out_shape,
        scratch_shapes=list(scratch),
        compiler_params=pltpu.CompilerParams(vmem_limit_bytes=mib * 1024 * 1024),
        name=name,
    )(*[arg if arg.dtype == jnp.int32 else kept(arg) for arg in args], *[away(arg) for arg in far], *order)


def exchange_lane(value, second):
    seqs, batches = lax.axis_size("seq"), lax.axis_size("batch")
    pairs = []
    for s in range(seqs):
        for b in range(batches):
            over_x = (b % 2 == 0) != second
            pairs.append((s * batches + b, (s ^ 1) * batches + b if over_x else s * batches + (b ^ 2)))
    return lax.ppermute(value, AXES, pairs)


def exchange_z_lane(value, second):
    seqs, batches = lax.axis_size("seq"), lax.axis_size("batch")
    pairs = []
    for s in range(seqs):
        for b in range(batches):
            bit = 2 if (b % 2 == 0) != second else 4
            pairs.append((s * batches + b, (s ^ bit) * batches + b))
    return lax.ppermute(value, AXES, pairs)


def after(value, *others):
    return lax.optimization_barrier((value, *others))[0]


def over_z(shard):
    return [shard] + [exchange(shard, 2 * k, 0) for k in range(1, 4)]


def z_terms(sends):
    return [exchange(sent, 2 * (k + 1), 0) for k, sent in enumerate(sends)]


def all_sum(value):
    seqs, batches = lax.axis_size("seq"), lax.axis_size("batch")
    bit = 1
    while bit < batches:
        value = value + exchange(value, 0, bit)
        bit *= 2
    bit = 1
    while bit < seqs:
        value = value + exchange(value, bit, 0)
        bit *= 2
    return value


def relay(ids, total, forward, flipped, beside, hold=()):
    group, before, bit = total, [], 1
    joint = near(4, H)
    while bit < lax.axis_size("seq"):
        last = 2 * bit == lax.axis_size("seq")
        other = exchange(group, bit, 0)
        order = beside[bit](group) if bit in beside else []
        got = call(
            functools.partial(relay_kernel, bit, forward, flipped and bit == 1),
            f"relay_{bit}", near(2, H) if last else [joint, joint],
            ids, group, other, *before, *hold, order=order,
        )
        if not last:
            group, before = got[0], [got[1]]
        bit *= 2
    return got


def flip_by(value, axis, bit):
    return jnp.where(bit == 1, jnp.flip(value, axis), value)


def moments(weight, gradient, first_moment, second, decay_rate):
    first_new = first_decay * first_moment + (1.0 - first_decay) * gradient
    second_new = second_decay * second + (1.0 - second_decay) * gradient * gradient
    direction = (
        first_new
        / (1.0 - first_decay**STEP)
        / (jnp.sqrt(second_new / (1.0 - second_decay**STEP)) + moment_eps)
        + decay_rate * weight
    )
    return (first_new, second_new, direction)


def on_device(
    tokens, doc_lengths, cotangent, mixer_weights, mlp_weights, small_params,
    mixer_first, mixer_second, mlp_first, mlp_second, small_first, small_second,
):
    seqs, batches = lax.axis_size("seq"), lax.axis_size("batch")
    seq_at, batch_at = lax.axis_index("seq"), lax.axis_index("batch")
    device = seq_at * batches + batch_at
    streams, block, _ = tokens.shape
    rows = streams * block
    direct = (seqs, batches) == (8, 4)
    if direct:
        z, x, y, c = seq_at // 2, seq_at % 2, batch_at // 2, batch_at % 2
    else:
        z = x = y = c = jnp.zeros((), jnp.int32)
    mixer_role = device * mixer_weights.shape[0] // H
    mlp_role = device * mlp_weights.shape[0] // FF
    ids = jnp.stack([z, x, y, c, seq_at, device, mixer_role, mlp_role]).astype(jnp.int32)

    small_low = small_params.astype(bf16).astype(f32)
    slab = shape(ROLES, ROWS, D, dtype=bf16)
    if direct:
        pair_of = near(2, ROWS, D, dtype=bf16)
        count = small_params.shape[0]
        small_line = jnp.broadcast_to(jnp.pad(small_low, (0, ROWS - count))[None], (SEG, ROWS))
        packed = call(
            pack_kernel, "mixer_pack", near(ROWS + TAIL, D, dtype=bf16),
            ids, mixer_weights, small_line, exchange(small_line, 0, 1),
        )
        mixer_two = call(
            stack_kernel, "mixer_pair", near(2, ROWS + TAIL, D, dtype=bf16), packed, exchange_z_lane(packed, False)
        )
        mixer_far = exchange_z_lane(mixer_two, True)
        mlp_low = after(mlp_weights, packed).astype(bf16)
        mlp_two = call(stack_kernel, "mlp_pair", pair_of, mlp_low, exchange_lane(mlp_low, False))
        mlp_plane = call(stack_kernel, "mlp_plane", slab, mlp_two, exchange_lane(mlp_two, True))
        gate_slab = call(
            slab_kernel, "mixer_slab", shape(ROLES * ROWS + TAIL, D, dtype=bf16),
            ids, mixer_two, mixer_far, order=[mlp_plane], scratch=[pltpu.VMEM((TAIL, D), f32)],
        )
        mixer_own = [gate_slab] + [exchange(gate_slab, *bits) for bits in PLANE_BITS[1:]]
        mlp_plane = after(mlp_plane, gate_slab)
        mlp_early = call(
            stack_kernel, "mlp_early", shape(2, PLANES, ROWS, D, dtype=bf16), mlp_plane, exchange_z_lane(mlp_plane, False)
        )
        mlp_late = exchange_z_lane(mlp_early, True)
    else:
        small_used = lax.all_gather(small_low, AXES, axis=0, tiled=True)

        def gathered(shard):
            full = lax.all_gather(shard.astype(bf16), AXES, axis=0, tiled=True)
            return full.reshape(ROLES, PLANES, 2, ROWS, D)

        full = gathered(mixer_weights)
        mixer_own, mixer_par = [[full[:, p, k].reshape(ROLES * ROWS, D) for p in range(PLANES)] for k in range(2)]
        full = gathered(mlp_weights)
        mlp_parts = [full[roles, :, k] for k in range(2) for roles in (slice(0, 2), slice(2, 4))]

    restart, valid = call(marks_kernel, "marks", [shape(rows, 1), shape(rows, 1)], ids, doc_lengths)

    wide = near(rows, HALF)
    natural = shape(streams, block, D, dtype=bf16)
    low_wide = near(rows, HALF, dtype=bf16)
    low_rows = near(rows, D, dtype=bf16)
    ends = near(2 * SEG, HALF)
    projections = [pltpu.VMEM((rows, HALF), f32)] * 3

    if direct:
        mixer_own = [gate_slab, *after(tuple(mixer_own[1:]), mlp_early, restart, valid)]
        mixer_par = [exchange(part, 0, 1) for part in mixer_own]
    wide_two, gate_weights = near(2, rows, HALF), near(GATES, HALF, D, dtype=bf16)
    if direct:
        normed, gain_one, gain_two, fb_o, fb_p, ib_o, ib_p, weights_o, both_o, tot_o, sega_o, segb_o = call(
            lambda *refs: scan_first_kernel(count, *refs), "scan_own",
            [low_rows] + [near(1, D)] * 2 + [near(1, HALF)] * 4 + [gate_weights, wide_two, near(4, HALF), ends, ends],
            ids, tokens, restart, *mixer_own,
            scratch=projections + [pltpu.VMEM((4 * SEG, ROWS), f32), pltpu.VMEM((3 * SEG, ROWS), f32)],
        )
    else:
        gain_one, gain_two = small_used[:D][None], small_used[D : 2 * D][None]
        biases = small_used[2 * D :].reshape(2, PLANES, 2, ROWS).transpose(0, 2, 1, 3).reshape(4, 1, HALF)
        fb_o, fb_p, ib_o, ib_p = [biases[k] for k in range(4)]
        normed = call(normed_kernel, "first_norm", low_rows, tokens, gain_one)
        weights_o, both_o, tot_o, sega_o, segb_o = call(
            lambda *refs: scan_kernel(True, *refs), "scan_own", [gate_weights, wide_two, near(4, HALF), ends, ends],
            normed, restart, fb_o, ib_o, *mixer_own, scratch=projections,
        )
    weights_p, both_p, tot, sega_p, segb_p = call(
        lambda *refs: scan_kernel(False, *refs), "scan_other", [gate_weights, wide_two, near(4, H), ends, ends],
        normed, restart, fb_p, ib_p, tot_o, *mixer_par, scratch=projections,
    )

    kept_terms = {}

    def terms_own(ready):
        kept_terms["own"] = call(
            terms_kernel, "terms_own", [wide] * 4,
            normed, fb_o, ib_o, weights_o, order=[ready], scratch=projections[:2],
        )
        return [kept_terms["own"][0]]

    def terms_other(ready):
        kept_terms["other"] = call(
            terms_kernel, "terms_other", [wide] * 4,
            normed, fb_p, ib_p, weights_p, order=[ready], scratch=projections[:2],
        )
        return [kept_terms["other"][0]]

    def masked_cotangent(ready):
        kept_terms["d_out"] = call(dout_kernel, "d_out", low_rows, cotangent, valid, order=[ready])
        return [kept_terms["d_out"]]

    incoming = relay(ids, tot, True, direct, {1: terms_own, 2: terms_other, 4: masked_cotangent})
    d_out = kept_terms["d_out"]
    if direct:
        mlp_late = after(mlp_late, incoming)
        mlp_parts = [mlp_early, mlp_late, exchange(mlp_early, 0, 1), exchange(mlp_late, 0, 1)]

    states_o, states_p, low_o, low_p, resid, normed_two, out_weights = call(
        states_kernel, "states",
        [wide, wide, low_wide, low_wide, near(rows, D), low_rows, near(1, H, D, dtype=bf16)],
        incoming, tokens, gain_two, both_o, both_p, sega_o, sega_p, segb_o, segb_p,
        *mixer_own, *mixer_par,
    )

    terms = near(PLANES, ROLES, ROWS, D, dtype=bf16)
    output, d_resid, d_gain_two, mlp_gown, mlp_gpar = call(
        mlp_kernel, "mlp", [natural, near(rows, D), near(1, D), terms, terms],
        ids, normed_two, resid, d_out, valid, gain_two, *mlp_parts, mib=16,
        scratch=[
            pltpu.VMEM((PLANES, 2, ROLES, ROWS, D), bf16), pltpu.VMEM((rows, D), f32), pltpu.VMEM((rows, D), f32),
        ],
    )

    half_terms = near(PLANES, 1, ROWS, D, dtype=bf16)
    back_o, back_p, tot_back, bseg_o, bseg_p, out_gown, out_gpar = call(
        back_kernel, "back_scan", [wide, wide, near(4, H), ends, ends, half_terms, half_terms],
        d_resid, low_o, low_p, both_o, both_p, sega_o, sega_p, out_weights,
    )

    beside = {}
    if direct:
        mlp_got, out_got = exchange(mlp_gpar, 0, 1), exchange(out_gpar, 0, 1)
        two_fives = near(2, ROLES + 1, ROWS, D, dtype=bf16)

        def mlp_pair(ready):
            kept_terms["mlp"] = call(
                mlp_pair_kernel, "mlp_pair_sum", [two_fives] * 2, ids, mlp_gown, mlp_got, out_gown, out_got,
                order=[ready],
            )
            return [kept_terms["mlp"][0]]

        beside = {2: mlp_pair}

    arriving = relay(ids, tot_back, False, direct, beside)
    terms_o, terms_p = kept_terms["own"], kept_terms["other"]
    if direct:
        mlp_keep, mlp_send = kept_terms["mlp"]
        mlp_got = exchange_lane(mlp_send, True)

    def gates_back(column, back, sega, bseg, share, df, di, cand, retain, states, order, name):
        return call(
            lambda *refs: gates_kernel(column, *refs), name,
            [near(PLANES, GATES, ROWS, D, dtype=bf16), low_wide, low_wide, low_wide, near(1, HALF), near(1, HALF)],
            arriving, incoming, back, sega, bseg, share, df, di, cand, retain, states, restart, normed, order=order,
        )

    gate_gpar, pf_p, pi_p, pc_p, dfb_p, dib_p = gates_back(
        HALF, back_p, sega_p, bseg_p, *terms_p, both_p, states_p, [tot_back], "gates_other"
    )
    gate_gown, pf_o, pi_o, pc_o, dfb_o, dib_o = gates_back(
        0, back_o, sega_o, bseg_o, *terms_o, both_o, states_o, [dfb_p], "gates_own"
    )

    order = [dfb_o]
    if direct:
        five = near(ROLES + 1, ROWS, D, dtype=bf16)
        mlp_own_sum, mlp_next = call(
            half_sum_kernel, "mlp_half_sum", [five, five], mlp_keep, mlp_got, order=[dfb_o]
        )
        order = [mlp_own_sum]
    d_normed, small_terms = call(
        input_terms_kernel, "input_terms", [near(rows, D), near(TAIL, D)],
        ids, tokens, d_gain_two, dfb_o, dfb_p, dib_o, dib_p,
        pf_o, pi_o, pc_o, pf_p, pi_p, pc_p, weights_o, weights_p, order=order,
        scratch=[pltpu.VMEM((3 * SEG, ROWS), f32)],
    )

    def input_grad(ready):
        return call(input_kernel, "input_grad", [natural, near(SEG, ROWS)], tokens, gain_one, d_resid, d_normed, order=[ready])

    def with_moments(keep, got, weight, first_moment, second, name):
        count = weight.shape[0]
        return call(
            moments_kernel, name, [shape(count, D)] * 3 + [near(count, D)] + [near(SEG, 128)] * 2,
            keep, got, weight, first_moment, second,
        )

    if direct:
        shard, low_shard = near(ROWS, D), near(ROWS, D, dtype=bf16)
        long, low_long = near(ROWS + TAIL, D), near(ROWS + TAIL, D, dtype=bf16)
        gate_parts = call(
            gate_pair_kernel, "gate_pair_sum", [near(GATES * ROWS + TAIL, D, dtype=bf16)] * PLANES,
            gate_gown, exchange(gate_gpar, 0, 1), small_terms, exchange(small_terms, 0, 1), order=[mlp_own_sum],
        )
        gate_round = [gate_parts[0]] + [
            exchange(part, *bits) for part, bits in zip(gate_parts[1:], PLANE_BITS[1:], strict=True)
        ]
        d_x, x_done = input_grad(gate_parts[0])
        two = near(2, ROWS, D, dtype=bf16)
        mlp_keep, mlp_send, out_sum = call(
            mlp_plane_kernel, "mlp_plane_sum", [two, two, low_shard], ids, mlp_own_sum, exchange_lane(mlp_next, False)
        )
        mlp_stay, mlp_send = call(
            mlp_far_kernel, "mlp_z_sum", [shard, low_shard], mlp_keep, exchange_z_lane(mlp_send, False)
        )
        mlp_done = with_moments(
            mlp_stay, exchange_z_lane(mlp_send, True), mlp_weights, mlp_first, mlp_second, "mlp_moments"
        )
        gate_keep, *gate_sends = call(
            gate_plane_kernel, "gate_plane_sum", [long] + [low_long] * 3, ids, *gate_round, out_sum,
            order=[mlp_done[-1], x_done],
        )
        gate_got = z_terms(gate_sends)
    else:

        def scattered(own, par):
            full_terms = jnp.stack([own, par]).transpose(2, 1, 0, 3, 4).reshape(-1, D)
            return lax.psum_scatter(full_terms, AXES, scatter_dimension=0, tiled=True).astype(f32)

        d_x, _ = input_grad(small_terms)
        mlp_grad = scattered(mlp_gown, mlp_gpar)
        mixer_grad = scattered(
            jnp.concatenate([gate_gown, out_gown], axis=1), jnp.concatenate([gate_gpar, out_gpar], axis=1)
        )
        none = jnp.zeros_like(mlp_grad, dtype=bf16)
        mlp_done = with_moments(mlp_grad, none, mlp_weights, mlp_first, mlp_second, "mlp_moments")
        gate_keep = jnp.concatenate([mixer_grad, lax.psum(small_terms, AXES)], axis=0)
        gate_got = [jnp.zeros_like(gate_keep, dtype=bf16)] * 3
    mlp_grad, mlp_first_new, mlp_second_new, mlp_dir, mlp_wsum, mlp_dsum = mlp_done
    count, mixer_count = small_params.shape[0], mixer_weights.shape[0]
    line, matrix = shape(1, count), shape(mixer_count, D)
    mixer_grad, mixer_first_new, mixer_second_new, mixer_dir, small_grad, small_first_new, small_second_new, small_dir, squares = call(
        finish_kernel, "finish", [matrix] * 3 + [near(mixer_count, D)] + [line] * 3 + [near(1, count), near(SEG, ROWS)],
        ids, gate_keep, *gate_got, mlp_wsum, mlp_dsum, mixer_weights, mixer_first, mixer_second,
        small_params[None], small_first[None], small_second[None], scratch=[pltpu.VMEM((4 * SEG, ROWS), f32)],
    )

    def update(sums, slot, base, weight, direction, name):
        return call(
            lambda *refs: matrix_update_kernel(slot, base, *refs), name,
            [shape(*weight.shape), shape(*weight.shape, dtype=bf16), near(SEG, ROWS)], ids, sums, weight, direction,
        )

    if direct:
        sums = squares
        for bits in ((0, 1), (0, 2), (1, 0)):
            sums = sums + exchange(sums, *bits)
        mixer_new, mixer_copy, mixer_updated = update(sums, MIXER_ROLE, 0, mixer_weights, mixer_dir, "mixer_update")
        sums = after(sums + exchange(sums, 2, 0), mixer_updated)
        mlp_new, mlp_copy, mlp_updated = update(sums, MLP_ROLE, ROLES, mlp_weights, mlp_dir, "mlp_update")
        sums = sums + exchange(sums, 4, 0)
    else:
        sums = all_sum(squares)
        mixer_new, mixer_copy, mixer_updated = update(sums, MIXER_ROLE, 0, mixer_weights, mixer_dir, "mixer_update")
        mlp_new, mlp_copy, mlp_updated = update(sums, MLP_ROLE, ROLES, mlp_weights, mlp_dir, "mlp_update")
    small_new, small_copy, tensor_norms, trust_ratios = call(
        small_update_kernel, "small_update", [line, shape(1, count, dtype=bf16), shape(2, 10), shape(1, 10)],
        ids, sums, small_params[None], small_dir, order=[mixer_updated, mlp_updated],
    )
    return (
        output,
        d_x,
        mixer_grad,
        mlp_grad,
        small_grad[0],
        mixer_first_new,
        mixer_second_new,
        mlp_first_new,
        mlp_second_new,
        small_first_new[0],
        small_second_new[0],
        mixer_new,
        mlp_new,
        small_new[0],
        mixer_copy,
        mlp_copy,
        small_copy[0],
        tensor_norms,
        trust_ratios[0],
    )


def solution(mesh):
    shard = P(("seq", "batch"), None)
    shard_flat = P(("seq", "batch"))
    stream = P("batch", "seq", None)
    return jax.shard_map(
        on_device,
        mesh=mesh,
        in_specs=(
            stream, P("batch", None), stream, shard, shard, shard_flat,
            shard, shard, shard, shard, shard_flat, shard_flat,
        ),
        out_specs=(
            stream, stream, shard, shard, shard_flat, shard, shard, shard, shard, shard_flat, shard_flat,
            shard, shard, shard_flat, shard, shard, shard_flat, P(), P(),
        ),
        check_vma=False,
    )
```

```python
import functools

import jax
import jax.numpy as jnp
from jax import lax
from jax.experimental import pallas as pl
from jax.experimental.pallas import tpu as pltpu
from jax.sharding import PartitionSpec as P

D = 512
H = 1024
FF = 2048
STEP = 5
SEG = 8
ROWS = 128
PLANES = 4
HALF = PLANES * ROWS
GATES = 3
ROLES = 4
TAIL = 16
SMALL_BLOCKS = 3
Z, X, Y, CORE, SEQ, DEVICE, MIXER_ROLE, MLP_ROLE = range(8)

first_decay = 0.5
second_decay = 0.5
learn_rate = 0.25
matrix_decay = 0.01
moment_eps = 1e-06

f32 = jnp.float32
bf16 = jnp.bfloat16
AXES = ("seq", "batch")

PLANE_BITS = ((0, 0), (0, 2), (1, 0), (1, 2))


def dot_nt(a, b):
    return lax.dot_general(a, b, (((1,), (1,)), ((), ())), preferred_element_type=f32)


def dot_nn(a, b):
    return lax.dot_general(a, b, (((1,), (0,)), ((), ())), preferred_element_type=f32)


def dot_tn(a, b):
    return lax.dot_general(a, b, (((0,), (0,)), ((), ())), preferred_element_type=f32)


def exchange(value, seq_bits, batch_bits, targets=None):
    seqs, batches = lax.axis_size("seq"), lax.axis_size("batch")
    pairs = [
        (s * batches + b, (s ^ seq_bits) * batches + (b ^ batch_bits))
        for s in range(seqs)
        for b in range(batches)
        if targets is None or (s ^ seq_bits) in targets
    ]
    return lax.ppermute(value, AXES, pairs)


def unit(x):
    return lax.rsqrt(jnp.mean(x * x, axis=-1, keepdims=True) + 1e-05)


def rms_back(x, d_normed, gain):
    scale = unit(x)
    normal = x * scale
    d_unit = d_normed * gain
    mean = jnp.mean(d_unit * normal, axis=-1, keepdims=True)
    return jnp.sum(d_normed * normal, axis=0, keepdims=True), scale * (d_unit - normal * mean)


def gather_roles(slabs, held):
    for role in range(GATES):
        for q, ref in enumerate(slabs):
            held[role, pl.ds(q * ROWS, ROWS)] = ref[pl.ds(role * ROWS, ROWS), :]


def group(s, steps, j):
    return pl.ds(pl.multiple_of((s * steps + j) * SEG, SEG), SEG)


def pair(s, steps, j):
    return pl.ds(pl.multiple_of((s * steps + 2 * j) * SEG, 2 * SEG), 2 * SEG)


def segment_order(block):
    row = lax.broadcasted_iota(jnp.int32, (block, block), 0)
    position = lax.broadcasted_iota(jnp.int32, (block, block), 1)
    return jnp.where(position == (row % SEG) * (block // SEG) + row // SEG, 1.0, 0.0).astype(bf16)


def inward(ref):
    order = segment_order(ref.shape[1])
    return jnp.concatenate([dot_nn(order, ref[s]) for s in range(2)], axis=0)


def outward(ref, value):
    block = ref.shape[1]
    order = segment_order(block)
    for s in range(2):
        ref[s] = dot_tn(order, value[s * block : (s + 1) * block]).astype(bf16)


def z_of(ids_ref, k, core):
    return ids_ref[Z] ^ (jnp.where(core == 0, k, 3 - k) if k in (1, 2) else k)


def pack_kernel(ids_ref, weights_ref, small_ref, got_ref, out_ref):
    out_ref[pl.ds(0, ROWS), :] = weights_ref[...]
    mine, other = small_ref[...], got_ref[...]
    rest = jnp.zeros((1, ROWS - mine.shape[1]), f32)
    core = ids_ref[CORE]
    lines = [jnp.where(core == 0, mine, other), rest, jnp.where(core == 0, other, mine), rest]
    line = jnp.concatenate(lines + [jnp.zeros((1, D - 2 * ROWS), f32)], axis=1)
    out_ref[pl.ds(ROWS, TAIL), :] = jnp.broadcast_to(line, (TAIL, D)).astype(bf16)


def slab_kernel(ids_ref, early_ref, late_ref, *refs):
    slab_ref, lines = refs[-2:]
    lines[...] = jnp.zeros_like(lines)
    for k in range(ROLES):
        part = (early_ref, late_ref)[k // 2].at[k % 2]
        role = z_of(ids_ref, k, ids_ref[CORE])
        slab_ref[pl.ds(pl.multiple_of(role * ROWS, ROWS), ROWS), :] = part[pl.ds(0, ROWS), :]
        lines[pl.ds(role, 1), :] = part[pl.ds(ROWS, TAIL), :].astype(f32)[0:1]
    slab_ref[pl.ds(ROLES * ROWS, TAIL), :] = lines[...].astype(bf16)


def marks_kernel(ids_ref, lengths_ref, restart_ref, valid_ref):
    block = restart_ref.shape[0] // 2
    row = lax.broadcasted_iota(jnp.int32, (block, 1), 0)
    position = ids_ref[SEQ] * block + (row % SEG) * (block // SEG) + row // SEG
    for s in range(2):
        begins = jnp.zeros((block, 1), jnp.bool_)
        end = 0
        for k in range(lengths_ref.shape[1]):
            begins = begins | (position == end)
            end = end + lengths_ref[s, k]
        begins = begins | (position == end)
        restart_ref[pl.ds(s * block, block), :] = jnp.where(begins, 0.0, 1.0)
        valid_ref[pl.ds(s * block, block), :] = jnp.where(position < end, 1.0, 0.0)


def stack_kernel(first_ref, second_ref, *refs):
    out_ref = refs[-1]
    if first_ref.shape == out_ref.shape[1:]:
        out_ref[0], out_ref[1] = first_ref[...], second_ref[...]
    else:
        count = first_ref.shape[0]
        out_ref[:count], out_ref[count:] = first_ref[...], second_ref[...]


def normed_kernel(tok_ref, gain_ref, normed_ref):
    normed_ref[...] = first_norm(tok_ref, gain_ref)


def relay_kernel(bit, forward, flipped, ids_ref, group_ref, other_ref, *refs):
    late = ((ids_ref[SEQ] & bit) != 0) == forward
    mine, other = group_ref[...], other_ref[...]
    if flipped:
        quarter = HALF // 2
        at = (quarter, 0, 3 * quarter, 2 * quarter)
        other = jnp.concatenate([other[:, k : k + quarter] for k in at], axis=1)
    if bit == 1:
        decay, state = jnp.ones_like(mine[:2]), jnp.zeros_like(mine[:2])
    else:
        decay, state = refs[0][0:2, :], refs[0][2:4, :]
    state = jnp.where(late, decay * other[2:] + state, state)
    if refs[-1].shape[0] == 2:
        refs[-1][...] = state
        return
    group_out, before_out = refs[-2:]
    before_out[...] = jnp.concatenate([jnp.where(late, decay * other[:2], decay), state], axis=0)
    first, second = jnp.where(late, other, mine), jnp.where(late, mine, other)
    group_out[...] = jnp.concatenate([first[:2] * second[:2], second[:2] * first[2:] + second[2:]], axis=0)


def relay_far_kernel(forward, ids_ref, before_ref, *refs):
    terms, state_ref = refs[:ROLES], refs[-1]
    z = ids_ref[Z]
    state = jnp.zeros_like(state_ref)
    for place in range(ROLES - 1):
        source = place if forward else ROLES - 1 - place
        term = terms[0][...]
        for k in range(1, ROLES):
            term = jnp.where((z ^ source) == k, terms[k][...], term)
        earlier = (source < z) if forward else (source > z)
        state = jnp.where(earlier, term[2:] + term[:2] * state, state)
    state_ref[...] = before_ref[2:4, :] + before_ref[0:2, :] * state


def gate_shares(f, i):
    most = jnp.maximum(jnp.maximum(-f, -i), 0.0)
    one, low_f, low_i = jnp.exp(-most), jnp.exp(-f - most), jnp.exp(-i - most)
    inverse = 1.0 / ((one + low_i) + (one + low_f))
    return (one + low_i) * inverse, (one + low_f) * inverse, low_f * inverse, low_i * inverse


def first_norm(tok_ref, gain_ref):
    x = inward(tok_ref)
    return (x * unit(x) * gain_ref[...]).astype(bf16)


def unpack(count, ids_ref, slabs, by_device, flat):
    chips = [2 * (ids_ref[X] ^ (k // 2)) + (ids_ref[Y] ^ (k % 2)) for k in range(PLANES)]
    for k, ref in enumerate(slabs):
        lines = ref[pl.ds(ROLES * ROWS, TAIL), :].astype(f32)
        for z in range(ROLES):
            for core in range(2):
                row = z * 2 * PLANES + 2 * chips[k] + core
                by_device[pl.ds(row, 1), :] = lines[z : z + 1, core * ROWS : (core + 1) * ROWS]
    parts = [by_device[pl.ds(k, 8, stride=4), :] for k in range(4)]
    for k in range(3):
        cut = ROWS - (k + 1) * (ROWS - count)
        row = jnp.concatenate([parts[k][:, k * (ROWS - count) : count], parts[k + 1][:, : ROWS - cut]], axis=1)
        flat[pl.ds(k, 8, stride=3), :] = row
    rows = [flat[pl.ds(k, 1), :] for k in range(2 * PLANES)]
    yield jnp.concatenate(rows[:PLANES], axis=1)
    yield jnp.concatenate(rows[PLANES:], axis=1)
    for base in (2 * PLANES, 4 * PLANES):
        for half in range(2):
            at = [base + 2 * chips[k] + (ids_ref[CORE] ^ half) for k in range(PLANES)]
            yield jnp.concatenate([flat[pl.ds(row, 1), :] for row in at], axis=1)


def scan_halves(normed, f_bias, i_bias, rs_ref, held, both_ref, tot_ref, columns, sega_ref, segb_ref, f_ref, i_ref, c_ref):
    for role, ref in enumerate((f_ref, i_ref, c_ref)):
        ref[...] = dot_nt(normed, held[role])
    steps = normed.shape[0] // (2 * SEG)

    def step(j, carry):
        after = []
        for s in range(2):
            at = group(s, steps, j)
            keep, share, _, _ = gate_shares(f_ref[at, :] + f_bias, i_ref[at, :] + i_bias)
            a = keep * rs_ref[at, :]
            b = a * carry[s][1] + share * c_ref[at, :]
            both_ref[0, at, :] = a
            both_ref[1, at, :] = b
            after.append((a * carry[s][0], b))
        return tuple(after)

    start = (jnp.ones((SEG, HALF), f32), jnp.zeros((SEG, HALF), f32))
    ends = lax.fori_loop(0, steps, step, (start, start), unroll=steps)
    for s, (seg_a, seg_b) in enumerate(ends):
        sega_ref[pl.ds(s * SEG, SEG), :] = seg_a
        segb_ref[pl.ds(s * SEG, SEG), :] = seg_b
        tot_a, tot_b = seg_a[0:1], seg_b[0:1]
        for k in range(1, SEG):
            a = seg_a[k : k + 1]
            tot_a, tot_b = a * tot_a, a * tot_b + seg_b[k : k + 1]
        tot_ref[pl.ds(s, 1), columns] = tot_a
        tot_ref[pl.ds(2 + s, 1), columns] = tot_b


def scan_first_kernel(count, ids_ref, tok_ref, rs_ref, *refs):
    slabs, outs, scratch = refs[:PLANES], refs[PLANES:-5], refs[-5:]
    normed_ref, gain_one_ref, gain_two_ref, fo_ref, fp_ref, io_ref, ip_ref, held, both_ref, tot_ref, sega_ref, segb_ref = outs
    f_ref, i_ref, c_ref, by_device, flat = scratch
    gather_roles(slabs, held)
    small = unpack(count, ids_ref, slabs, by_device, flat)
    for ref, value in zip((gain_one_ref, gain_two_ref, fo_ref, fp_ref, io_ref, ip_ref), small, strict=True):
        ref[...] = value
    normed_ref[...] = first_norm(tok_ref, gain_one_ref)
    scan_halves(
        normed_ref[...], fo_ref[...], io_ref[...], rs_ref, held, both_ref, tot_ref, pl.ds(0, HALF),
        sega_ref, segb_ref, f_ref, i_ref, c_ref,
    )


def scan_kernel(first, normed_ref, rs_ref, fb_ref, ib_ref, *refs):
    if not first:
        earlier_ref, *refs = refs
    slabs, (held, both_ref, tot_ref, sega_ref, segb_ref, f_ref, i_ref, c_ref) = refs[:PLANES], refs[-8:]
    gather_roles(slabs, held)
    if not first:
        tot_ref[:, pl.ds(0, HALF)] = earlier_ref[...]
    scan_halves(
        normed_ref[...], fb_ref[...], ib_ref[...], rs_ref, held, both_ref, tot_ref,
        pl.ds(0 if first else HALF, HALF), sega_ref, segb_ref, f_ref, i_ref, c_ref,
    )


def dout_kernel(cot_ref, valid_ref, *refs):
    refs[-1][...] = (inward(cot_ref) * valid_ref[...]).astype(bf16)


def terms_kernel(normed_ref, fb_ref, ib_ref, held, *refs):
    share_ref, df_ref, di_ref, cand_ref, f_ref, i_ref = refs[-6:]
    normed = normed_ref[...]
    for role, ref in enumerate((f_ref, i_ref, cand_ref)):
        ref[...] = dot_nt(normed, held[role])
    f_bias, i_bias = fb_ref[...], ib_ref[...]

    def step(j, carry):
        at = pl.ds(pl.multiple_of(j * 2 * SEG, 2 * SEG), 2 * SEG)
        keep, share, slow_f, slow_i = gate_shares(f_ref[at, :] + f_bias, i_ref[at, :] + i_bias)
        share_ref[at, :] = share
        df_ref[at, :] = keep * slow_f
        di_ref[at, :] = share * slow_i
        return carry

    lax.fori_loop(0, normed.shape[0] // (2 * SEG), step, 0, unroll=4)


def states_kernel(inc_ref, tok_ref, gain_ref, both_o, both_p, sega_o, sega_p, segb_o, segb_p, *refs):
    slabs, refs = refs[: 2 * PLANES], refs[2 * PLANES :]
    states_o, states_p, low_o, low_p, resid_ref, normed_ref, held = refs
    steps = resid_ref.shape[0] // (2 * SEG)
    halves = (
        (both_o, sega_o, segb_o, states_o, low_o, 0),
        (both_p, sega_p, segb_p, states_p, low_p, HALF),
    )
    start = []
    for _, sega, segb, _, _, column in halves:
        for s in range(2):
            seg_a, seg_b = sega[pl.ds(s * SEG, SEG), :], segb[pl.ds(s * SEG, SEG), :]
            at_seg = [inc_ref[pl.ds(s, 1), pl.ds(column, HALF)]]
            for k in range(SEG - 1):
                at_seg.append(seg_a[k : k + 1] * at_seg[-1] + seg_b[k : k + 1])
            start.append(jnp.concatenate(at_seg, axis=0))

    def step(j, carry):
        after = []
        for k, (both, _, _, states, low, _) in enumerate(halves):
            for s in range(2):
                carried, two = carry[2 * k + s], []
                for q in range(2):
                    at = group(s, steps, 2 * j + q)
                    carried = both[0, at, :] * carried
                    two.append(both[1, at, :] + carried)
                    states[at, :] = two[-1]
                low[pair(s, steps, j), :] = jnp.concatenate(two, axis=0).astype(bf16)
                after.append(carried)
        return tuple(after)

    lax.fori_loop(0, steps // 2, step, tuple(start), unroll=4)
    r = inward(tok_ref)
    for q, ref in enumerate(slabs):
        held[0, pl.ds(q * ROWS, ROWS)] = ref[pl.ds(GATES * ROWS, ROWS), :]
    for low, k in zip((low_o, low_p), range(2), strict=True):
        r = r + dot_nn(low[...], held[0, pl.ds(k * HALF, HALF)])
    resid_ref[...] = r
    normed_ref[...] = (r * unit(r) * gain_ref[...]).astype(bf16)


GELU_A = 0.7978845608028654
GELU_B = 0.044715


def mlp_kernel(ids_ref, normed_ref, resid_ref, dout_ref, valid_ref, gain_ref, *refs):
    parts, refs = refs[:4], refs[4:]
    output_ref, dresid_ref, dgain_ref, gown_ref, gpar_ref, held, outer_ref, dnorm_ref = refs

    def bring(at):
        for half in range(2):
            for k in range(ROLES):
                role = z_of(ids_ref, k, ids_ref[CORE] ^ half)
                held[at, half, pl.ds(role, 1)] = parts[2 * half + k // 2][k % 2, at].reshape(1, ROWS, D)

    bring(0)
    outer_ref[...] = jnp.zeros_like(outer_ref)
    dnorm_ref[...] = jnp.zeros_like(dnorm_ref)

    normed, dout = normed_ref[...], dout_ref[...]

    def ahead(i):
        at, low = i // 2, i % 2
        if low == 1 and at + 1 < PLANES:
            bring(at + 1)
        w_up = held[at, :, low].reshape(2 * ROWS, D)
        w_down = held[at, :, low + 2].reshape(2 * ROWS, D)
        return dot_nt(normed, w_up), dot_nt(dout, w_down), w_up, w_down

    now = ahead(0)
    for i in range(2 * PLANES):
        inner, d_act, w_up, w_down = now
        if i + 1 < 2 * PLANES:
            now = ahead(i + 1)
        square = inner * inner
        curve = jnp.tanh(inner * (GELU_A + GELU_A * GELU_B * square))
        half = 0.5 + 0.5 * curve
        activated = (inner * half).astype(bf16)
        slope = half + (half - half * half) * (inner * (2.0 * GELU_A + 6.0 * GELU_A * GELU_B * square))
        d_inner = (slope * d_act).astype(bf16)
        outer_ref[...] += dot_nn(activated, w_down)
        dnorm_ref[...] += dot_nn(d_inner, w_up)
        g_up = dot_tn(d_inner, normed).astype(bf16).reshape(2, ROWS, D)
        g_down = dot_tn(activated, dout).astype(bf16).reshape(2, ROWS, D)
        for k, ref in enumerate((gown_ref, gpar_ref)):
            ref[i // 2, i % 2] = g_up[k]
            ref[i // 2, i % 2 + 2] = g_down[k]
    r = resid_ref[...]
    outward(output_ref, ((r + outer_ref[...]) * valid_ref[...]).astype(bf16))
    dgain_ref[...], d_r = rms_back(r, dnorm_ref[...], gain_ref[...])
    dresid_ref[...] = dout_ref[...].astype(f32) + d_r


def back_kernel(dresid_ref, low_o, low_p, retain_o, retain_p, sega_o, sega_p, held, *refs):
    acc_o, acc_p, tot_ref, segb_o, segb_p, gown_ref, gpar_ref = refs
    steps = dresid_ref.shape[0] // (2 * SEG)
    dmix = dresid_ref[...].astype(bf16)
    for acc, k in zip((acc_o, acc_p), range(2), strict=True):
        acc[...] = dot_nt(dmix, held[0, pl.ds(k * HALF, HALF)])
    halves = ((retain_o, acc_o), (retain_p, acc_p))

    def step(n, carry):
        after = []
        for k, (retain, acc) in enumerate(halves):
            for s in range(2):
                at = group(s, steps, steps - 1 - n)
                back = acc[at, :] + carry[2 * k + s]
                acc[at, :] = back
                after.append(retain[0, at, :] * back)
        return tuple(after)

    ends = lax.fori_loop(0, steps, step, (jnp.zeros((SEG, HALF), f32),) * 4, unroll=8)
    for k, (sega, segb) in enumerate(((sega_o, segb_o), (sega_p, segb_p))):
        for s in range(2):
            emitted = ends[2 * k + s]
            segb[pl.ds(s * SEG, SEG), :] = emitted
            seg_a = sega[pl.ds(s * SEG, SEG), :]
            tot_a, tot_b = seg_a[SEG - 1 :], emitted[SEG - 1 :]
            for q in reversed(range(SEG - 1)):
                a = seg_a[q : q + 1]
                tot_a, tot_b = a * tot_a, a * tot_b + emitted[q : q + 1]
            tot_ref[pl.ds(s, 1), pl.ds(k * HALF, HALF)] = tot_a
            tot_ref[pl.ds(2 + s, 1), pl.ds(k * HALF, HALF)] = tot_b
    for low, ref in ((low_o, gown_ref), (low_p, gpar_ref)):
        ref[...] = dot_tn(low[...], dmix).astype(bf16).reshape(PLANES, 1, ROWS, D)


def gates_kernel(
    column, arr_ref, inc_ref, acc_ref, sega_ref, segb_ref, share_ref, df_ref, di_ref, cand_ref, retain_ref, states_ref,
    rs_ref, normed_ref, order_ref, grad_ref, pf_ref, pi_ref, pc_ref, dfb_ref, dib_ref,
):
    steps = normed_ref.shape[0] // (2 * SEG)
    start, first = [], []
    for s in range(2):
        seg_a, seg_b = sega_ref[pl.ds(s * SEG, SEG), :], segb_ref[pl.ds(s * SEG, SEG), :]
        at_seg = [arr_ref[pl.ds(s, 1), pl.ds(column, HALF)]]
        for k in reversed(range(1, SEG)):
            at_seg.append(seg_a[k : k + 1] * at_seg[-1] + seg_b[k : k + 1])
        start.append(jnp.concatenate(at_seg[::-1], axis=0))
        ends = states_ref[group(s, steps, steps - 1), :]
        first.append(jnp.concatenate([inc_ref[pl.ds(s, 1), pl.ds(column, HALF)], ends[: SEG - 1]], axis=0))

    def step(n, carry):
        *carried, sum_f, sum_i = carry
        m = steps // 2 - 1 - n
        for s in range(2):
            terms = []
            for q in (1, 0):
                j = 2 * m + q
                at = group(s, steps, j)
                back = acc_ref[at, :] + carried[s]
                carried[s] = carried[s] * retain_ref[0, at, :]
                previous = states_ref[group(s, steps, jnp.maximum(j - 1, 0)), :]
                if q == 0:
                    previous = jnp.where(m == 0, first[s], previous)
                both_ways = back * (previous * rs_ref[at, :] - cand_ref[at, :])
                d_f = both_ways * df_ref[at, :]
                d_i = both_ways * di_ref[at, :]
                sum_f = sum_f + d_f
                sum_i = sum_i - d_i
                terms.append((d_f, -d_i, back * share_ref[at, :]))
            for late, early, ref in zip(*terms, (pf_ref, pi_ref, pc_ref), strict=True):
                ref[pair(s, steps, m), :] = jnp.concatenate([early, late], axis=0).astype(bf16)
        return (*carried, sum_f, sum_i)

    nothing = jnp.zeros((SEG, HALF), f32)
    *_, sum_f, sum_i = lax.fori_loop(0, steps // 2, step, (*start, nothing, nothing), unroll=8)
    dfb_ref[...] = jnp.sum(sum_f, axis=0, keepdims=True)
    dib_ref[...] = jnp.sum(sum_i, axis=0, keepdims=True)
    normed = normed_ref[...]
    for role, ref in enumerate((pf_ref, pi_ref, pc_ref)):
        grad_ref[:, role] = dot_tn(ref[...], normed).astype(bf16).reshape(PLANES, ROWS, D)


def input_terms_kernel(ids_ref, tok_ref, dgain_two_ref, dfb_o, dfb_p, dib_o, dib_p, *refs):
    terms, weights, refs = refs[: 2 * GATES], refs[2 * GATES : 2 * GATES + 2], refs[-3:]
    dnorm_ref, small_ref, rows_ref = refs
    d_normed = 0.0
    for role in range(GATES):
        for k in range(2):
            d_normed = d_normed + dot_nn(terms[k * GATES + role][...], weights[k][role])
    dnorm_ref[...] = d_normed
    x = inward(tok_ref)
    d_gain = jnp.sum(d_normed * (x * unit(x)), axis=0, keepdims=True)
    for k in range(PLANES):
        rows_ref[pl.ds(k, 1), :] = d_gain[:, k * ROWS : (k + 1) * ROWS]
        rows_ref[pl.ds(PLANES + k, 1), :] = dgain_two_ref[:, pl.ds(k * ROWS, ROWS)]
        chip = 4 * (ids_ref[X] ^ (k // 2)) + 2 * (ids_ref[Y] ^ (k % 2))
        for core, (fb, ib) in enumerate(((dfb_o, dib_o), (dfb_p, dib_p))):
            row = 2 * PLANES + chip + (ids_ref[CORE] ^ core)
            rows_ref[pl.ds(row, 1), :] = fb[:, pl.ds(k * ROWS, ROWS)]
            rows_ref[pl.ds(row + 2 * PLANES, 1), :] = ib[:, pl.ds(k * ROWS, ROWS)]
    blocks = [rows_ref[pl.ds(k * SEG, SEG), :] for k in range(SMALL_BLOCKS)] + [jnp.zeros((SEG, ROWS), f32)]
    small_ref[...] = jnp.concatenate([jnp.concatenate(blocks, axis=1), jnp.zeros((SEG, D), f32)], axis=0)


def input_kernel(tok_ref, gain_ref, dresid_ref, dnorm_ref, order_ref, dx_ref, done_ref):
    done_ref[...] = jnp.zeros_like(done_ref)
    _, d_x = rms_back(inward(tok_ref), dnorm_ref[...], gain_ref[...])
    outward(dx_ref, (dresid_ref[...] + d_x).astype(bf16))


def mlp_pair_kernel(ids_ref, own_ref, got_ref, out_ref, outgot_ref, *refs):
    core = ids_ref[CORE]
    for k in range(PLANES):
        ref = refs[-2 + k // 2]
        ref[k % 2, pl.ds(0, ROLES)] = (own_ref[k].astype(f32) + got_ref[k].astype(f32)).astype(bf16)
        at = pl.ds(jnp.where(core == 0, 3 - k, k) if k in (1, 2) else k, 1)
        ref[k % 2, pl.ds(ROLES, 1)] = (out_ref[at, 0].astype(f32) + outgot_ref[at, 0].astype(f32)).astype(bf16)


def gate_pair_kernel(own_ref, got_ref, small_ref, small_got, *outs):
    small = (small_ref[...] + small_got[...]).astype(bf16)
    for k, ref in enumerate(outs[-PLANES:]):
        total = (own_ref[k].astype(f32) + got_ref[k].astype(f32)).astype(bf16)
        ref[pl.ds(0, GATES * ROWS), :] = total.reshape(GATES * ROWS, D)
        ref[pl.ds(GATES * ROWS, TAIL), :] = small


def half_sum_kernel(ids_ref, own_ref, got_ref, *refs):
    keep_ref, send_ref, out_keep, out_send = refs[-4:]
    z = ids_ref[Z]
    near_bit = jnp.where(ids_ref[CORE] == 0, 1, 2)
    for q in range(2):

        def total(role, q=q):
            at = pl.ds(role, 1)
            return (own_ref[q, at].astype(f32) + got_ref[q, at].astype(f32)).astype(bf16).reshape(ROWS, D)

        for k, role in enumerate((z, z ^ near_bit ^ 3)):
            keep_ref[k, q] = total(role)
            send_ref[k, q] = total(role ^ near_bit)
        (out_keep, out_send)[q][...] = total(ROLES)


def mlp_far_kernel(keep_ref, got_ref, *refs):
    stay_ref, send_ref = refs[-2:]
    stay_ref[...] = (keep_ref[0].astype(f32) + got_ref[0].astype(f32)).astype(bf16)
    send_ref[...] = (keep_ref[1].astype(f32) + got_ref[1].astype(f32)).astype(bf16)


def mlp_last_kernel(stay_ref, got_ref, *refs):
    keep_ref, send_ref = refs[-2:]
    keep_ref[...] = stay_ref[0].astype(f32) + got_ref[0].astype(f32)
    send_ref[...] = (stay_ref[1].astype(f32) + got_ref[1].astype(f32)).astype(bf16)


def gate_plane_kernel(ids_ref, p0, p1, p2, p3, out_ref, out_got, *refs):
    z = ids_ref[Z]
    keep_ref, s1_ref, s2_ref, s3_ref = refs[-4:]

    def total(at):
        terms = [ref[at, :].astype(f32) for ref in (p0, p1, p2, p3)]
        return (terms[0] + terms[1]) + (terms[2] + terms[3])

    def of_role(role):
        at = pl.ds(pl.multiple_of(jnp.minimum(role, GATES - 1) * ROWS, ROWS), ROWS)
        return jnp.where(role == GATES, out_ref[...].astype(f32) + out_got[...].astype(f32), total(at))

    small = total(pl.ds(GATES * ROWS, TAIL))
    keep_ref[pl.ds(0, ROWS), :] = of_role(z)
    keep_ref[pl.ds(ROWS, TAIL), :] = small
    for k, ref in enumerate((s1_ref, s2_ref, s3_ref)):
        ref[pl.ds(0, ROWS), :] = of_role(z ^ (k + 1)).astype(bf16)
        ref[pl.ds(ROWS, TAIL), :] = small.astype(bf16)


def joined(at, keep_ref, gots):
    total = keep_ref[at, :]
    for ref in gots:
        total = total + ref[at, :].astype(f32)
    return total


def matrix_step(at, keep_ref, gots, weight_ref, first_ref, second_ref, outs):
    grad_ref, first_out, second_out, dir_ref = outs
    weight = weight_ref[...]
    gradient = joined(at, keep_ref, gots)
    grad_ref[...] = gradient
    first_out[...], second_out[...], direction = moments(
        weight, gradient, first_ref[...], second_ref[...], matrix_decay
    )
    dir_ref[...] = direction
    return weight, direction


def square_rows(value):
    square = jnp.sum((value * value).reshape(-1, SEG, D), axis=0)
    return (square[:, :128] + square[:, 128:256]) + (square[:, 256:384] + square[:, 384:])


def moments_kernel(keep_ref, got_ref, weight_ref, first_ref, second_ref, *outs):
    *outs, wsum_ref, dsum_ref = outs
    weight, direction = matrix_step(
        pl.ds(0, weight_ref.shape[0]), keep_ref, [got_ref], weight_ref, first_ref, second_ref, outs
    )
    wsum_ref[...] = square_rows(weight)
    dsum_ref[...] = square_rows(direction)


def finish_kernel(
    ids_ref, keep_ref, g1_ref, g2_ref, g3_ref, wsum_f, dsum_f,
    mixer_ref, mixer_first, mixer_second, weight_ref, first_ref, second_ref,
    mixer_grad, mixer_first_out, mixer_second_out, mixer_dir, grad_ref, first_out, second_out, dir_ref, squares_ref,
    rows_ref,
):
    gots = (g1_ref, g2_ref, g3_ref)
    mixer_rows = mixer_ref.shape[0]
    mixer_values = matrix_step(
        pl.ds(0, mixer_rows), keep_ref, gots, mixer_ref, mixer_first, mixer_second,
        (mixer_grad, mixer_first_out, mixer_second_out, mixer_dir),
    )
    total = joined(pl.ds(mixer_rows, TAIL), keep_ref, gots)
    rows_ref[...] = jnp.zeros_like(rows_ref)
    for k in range(SMALL_BLOCKS):
        rows_ref[pl.ds(k * SEG, SEG), :] = total[:SEG, k * ROWS : (k + 1) * ROWS]
    weight = weight_ref[...]
    count = weight.shape[1]
    start = ids_ref[DEVICE] * count
    row, lane = start // ROWS, start % ROWS
    two = jnp.concatenate([rows_ref[pl.ds(row, 1), :], rows_ref[pl.ds(row + 1, 1), :]], axis=1)
    two = jnp.broadcast_to(two, (SEG, 2 * ROWS))
    gradient = pltpu.roll(two, (2 * ROWS - lane) % (2 * ROWS), 1)[:1, :count]
    grad_ref[...] = gradient
    first_out[...], second_out[...], direction = moments(weight, gradient, first_ref[...], second_ref[...], 0.0)
    dir_ref[...] = direction
    place = start + lax.broadcasted_iota(jnp.int32, (1, count), 1)
    at = lax.broadcasted_iota(jnp.int32, (1, ROWS), 1)
    bounds = (0, D, 2 * D, 2 * D + H, 2 * D + 2 * H)
    lines = []
    for mixer_value, mlp_sum, value in zip(mixer_values, (wsum_f, dsum_f), (weight, direction), strict=True):
        line = jnp.where(at == ids_ref[MIXER_ROLE], jnp.sum(square_rows(mixer_value), keepdims=True), 0.0)
        line = line + jnp.where(at == ROLES + ids_ref[MLP_ROLE], jnp.sum(mlp_sum[...], keepdims=True), 0.0)
        for k in range(4):
            inside = (place >= bounds[k]) & (place < bounds[k + 1])
            part = jnp.sum(jnp.where(inside, value * value, 0.0), axis=1, keepdims=True)
            line = line + jnp.where(at == ROLES + 2 + k, part, 0.0)
        lines.append(line)
    squares_ref[...] = jnp.concatenate(lines + [jnp.zeros((SEG - 2, ROWS), f32)], axis=0)


def ratio_of(squares_ref, tensor):
    norms = jnp.sqrt(squares_ref[0:2, :])
    ratios = norms[0:1] / (norms[1:2] + 1e-06)
    at = lax.broadcasted_iota(jnp.int32, (1, ROWS), 1)
    return jnp.sum(jnp.where(at == tensor, ratios, 0.0), axis=1, keepdims=True)


def new_weights(ratio, weight_ref, dir_ref, new_ref, copy_ref):
    value = weight_ref[...] - learn_rate * ratio * dir_ref[...]
    new_ref[...] = value
    copy_ref[...] = value.astype(bf16)


def mixer_update_kernel(ids_ref, squares_ref, weight_ref, dir_ref, *refs):
    *ins, new_ref, copy_ref, out0, out1, out2, done_ref = refs
    done_ref[...] = jnp.zeros_like(done_ref)
    new_weights(ratio_of(squares_ref, ids_ref[MIXER_ROLE]), weight_ref, dir_ref, new_ref, copy_ref)
    for ref, out in zip(ins, (out0, out1, out2), strict=True):
        out[...] = ref[...]


def last_update_kernel(
    ids_ref, squares_ref, mlp_ref, mlp_dir, weight_ref, dir_ref, order_ref,
    mlp_new, mlp_copy, new_ref, copy_ref, norms_ref, ratios_ref,
):
    norms = jnp.sqrt(squares_ref[0:2, :])
    ratios = norms[0:1] / (norms[1:2] + 1e-06)
    norms_ref[...] = norms[:, : norms_ref.shape[1]]
    ratios_ref[...] = ratios[:, : ratios_ref.shape[1]]
    new_weights(ratio_of(squares_ref, ROLES + ids_ref[MLP_ROLE]), mlp_ref, mlp_dir, mlp_new, mlp_copy)
    count = weight_ref.shape[1]
    place = ids_ref[DEVICE] * count + lax.broadcasted_iota(jnp.int32, (1, count), 1)
    first, second, third, fourth = (ratio_of(squares_ref, ROLES + 2 + k) for k in range(4))
    ratio = jnp.where(
        place < 2 * D, jnp.where(place < D, first, second), jnp.where(place < 2 * D + H, third, fourth)
    )
    new_weights(ratio, weight_ref, dir_ref, new_ref, copy_ref)


SMEM = pl.BlockSpec(memory_space=pltpu.SMEM)
ANY = pl.BlockSpec(memory_space=pl.ANY)
VMEM = pl.BlockSpec(memory_space=pltpu.VMEM)


def shape(*dims, dtype=f32):
    return jax.ShapeDtypeStruct(dims, dtype)


def near(*dims, dtype=f32):
    return pltpu.VMEM(dims, dtype)


def kept(value):
    return pltpu.with_memory_space_constraint(value, pltpu.VMEM)


def away(value):
    return pltpu.with_memory_space_constraint(value, pltpu.HBM)


def call(kernel, name, out_shape, *args, order=(), far=(), scratch=(), mib=8):
    in_specs = [SMEM if arg.dtype == jnp.int32 else VMEM for arg in args] + [ANY] * (len(far) + len(order))
    return pl.pallas_call(
        kernel,
        in_specs=in_specs,
        out_specs=jax.tree.map(lambda _: VMEM, out_shape),
        out_shape=out_shape,
        scratch_shapes=list(scratch),
        compiler_params=pltpu.CompilerParams(vmem_limit_bytes=mib * 1024 * 1024),
        name=name,
    )(*[arg if arg.dtype == jnp.int32 else kept(arg) for arg in args], *[away(arg) for arg in far], *order)


def exchange_lane(value, second):
    seqs, batches = lax.axis_size("seq"), lax.axis_size("batch")
    pairs = []
    for s in range(seqs):
        for b in range(batches):
            over_x = (b % 2 == 0) != second
            pairs.append((s * batches + b, (s ^ 1) * batches + b if over_x else s * batches + (b ^ 2)))
    return lax.ppermute(value, AXES, pairs)


def exchange_z_lane(value, second):
    seqs, batches = lax.axis_size("seq"), lax.axis_size("batch")
    pairs = []
    for s in range(seqs):
        for b in range(batches):
            bit = 2 if (b % 2 == 0) != second else 4
            pairs.append((s * batches + b, (s ^ bit) * batches + b))
    return lax.ppermute(value, AXES, pairs)


def after(value, *others):
    return lax.optimization_barrier((value, *others))[0]


def over_z(shard):
    return [shard] + [exchange(shard, 2 * k, 0) for k in range(1, 4)]


def z_terms(sends):
    return [exchange(sent, 2 * (k + 1), 0) for k, sent in enumerate(sends)]


def all_sum(value):
    seqs, batches = lax.axis_size("seq"), lax.axis_size("batch")
    bit = 1
    while bit < batches:
        value = value + exchange(value, 0, bit)
        bit *= 2
    bit = 1
    while bit < seqs:
        value = value + exchange(value, bit, 0)
        bit *= 2
    return value


def relay(ids, total, forward, flipped, beside, hold=()):
    group, before, bit = total, [], 1
    joint = near(4, H)
    if flipped:
        other = exchange(group, 1, 0)
        order = beside[1](group) if 1 in beside else []
        pair, before = call(
            functools.partial(relay_kernel, 1, forward, True), "relay_near", [joint, joint], ids, group, other, order=order
        )
        others = [exchange(pair, 2 * k, 0) for k in range(1, ROLES)]
        order = beside[2](pair) if 2 in beside else []
        return call(
            functools.partial(relay_far_kernel, forward), "relay_far", near(2, H), ids, before, pair, *others, order=order
        )
    while bit < lax.axis_size("seq"):
        last = 2 * bit == lax.axis_size("seq")
        other = exchange(group, bit, 0)
        order = beside[bit](group) if bit in beside else []
        got = call(
            functools.partial(relay_kernel, bit, forward, flipped and bit == 1),
            f"relay_{bit}", near(2, H) if last else [joint, joint],
            ids, group, other, *before, *hold, order=order,
        )
        if not last:
            group, before = got[0], [got[1]]
        bit *= 2
    return got


def flip_by(value, axis, bit):
    return jnp.where(bit == 1, jnp.flip(value, axis), value)


def moments(weight, gradient, first_moment, second, decay_rate):
    first_new = first_decay * first_moment + (1.0 - first_decay) * gradient
    second_new = second_decay * second + (1.0 - second_decay) * gradient * gradient
    direction = (
        first_new
        / (1.0 - first_decay**STEP)
        / (jnp.sqrt(second_new / (1.0 - second_decay**STEP)) + moment_eps)
        + decay_rate * weight
    )
    return (first_new, second_new, direction)


def on_device(
    tokens, doc_lengths, cotangent, mixer_weights, mlp_weights, small_params,
    mixer_first, mixer_second, mlp_first, mlp_second, small_first, small_second,
):
    seqs, batches = lax.axis_size("seq"), lax.axis_size("batch")
    seq_at, batch_at = lax.axis_index("seq"), lax.axis_index("batch")
    device = seq_at * batches + batch_at
    streams, block, _ = tokens.shape
    rows = streams * block
    direct = (seqs, batches) == (8, 4)
    if direct:
        z, x, y, c = seq_at // 2, seq_at % 2, batch_at // 2, batch_at % 2
    else:
        z = x = y = c = jnp.zeros((), jnp.int32)
    mixer_role = device * mixer_weights.shape[0] // H
    mlp_role = device * mlp_weights.shape[0] // FF
    ids = jnp.stack([z, x, y, c, seq_at, device, mixer_role, mlp_role]).astype(jnp.int32)

    slab = shape(ROLES, ROWS, D, dtype=bf16)
    if direct:
        pair_of = near(2, ROWS, D, dtype=bf16)
        count = small_params.shape[0]
        packed = call(
            pack_kernel, "mixer_pack", near(ROWS + TAIL, D, dtype=bf16),
            ids, mixer_weights.astype(bf16), small_params[None], exchange(small_params, 0, 1)[None],
        )
        mixer_two = call(
            stack_kernel, "mixer_pair", near(2, ROWS + TAIL, D, dtype=bf16), packed, exchange_z_lane(packed, False)
        )
        mixer_far = exchange_z_lane(mixer_two, True)
        mlp_low = after(mlp_weights, packed).astype(bf16)
        mlp_two = call(stack_kernel, "mlp_pair", pair_of, mlp_low, exchange_lane(mlp_low, False))
        mlp_plane = call(stack_kernel, "mlp_plane", slab, mlp_two, exchange_lane(mlp_two, True))
        gate_slab = call(
            slab_kernel, "mixer_slab", shape(ROLES * ROWS + TAIL, D, dtype=bf16),
            ids, mixer_two, mixer_far, order=[mlp_plane], scratch=[pltpu.VMEM((TAIL, D), f32)],
        )
        mixer_own = [gate_slab] + [exchange(gate_slab, *bits) for bits in PLANE_BITS[1:]]
        mlp_plane = after(mlp_plane, gate_slab)
        mlp_early = call(
            stack_kernel, "mlp_early", shape(2, PLANES, ROWS, D, dtype=bf16), mlp_plane, exchange_z_lane(mlp_plane, False)
        )
        mlp_late = exchange_z_lane(mlp_early, True)
    else:
        small_used = lax.all_gather(small_params.astype(bf16).astype(f32), AXES, axis=0, tiled=True)

        def gathered(shard):
            full = lax.all_gather(shard.astype(bf16), AXES, axis=0, tiled=True)
            return full.reshape(ROLES, PLANES, 2, ROWS, D)

        full = gathered(mixer_weights)
        mixer_own, mixer_par = [[full[:, p, k].reshape(ROLES * ROWS, D) for p in range(PLANES)] for k in range(2)]
        full = gathered(mlp_weights)
        mlp_parts = [full[roles, :, k] for k in range(2) for roles in (slice(0, 2), slice(2, 4))]

    restart, valid = call(marks_kernel, "marks", [shape(rows, 1), shape(rows, 1)], ids, doc_lengths)

    wide = near(rows, HALF)
    natural = shape(streams, block, D, dtype=bf16)
    low_wide = near(rows, HALF, dtype=bf16)
    low_rows = near(rows, D, dtype=bf16)
    ends = near(2 * SEG, HALF)
    projections = [pltpu.VMEM((rows, HALF), f32)] * 3

    if direct:
        mixer_own = [gate_slab, *after(tuple(mixer_own[1:]), mlp_early, restart, valid)]
        mixer_par = [exchange(part, 0, 1) for part in mixer_own]
    wide_two, gate_weights = near(2, rows, HALF), near(GATES, HALF, D, dtype=bf16)
    if direct:
        normed, gain_one, gain_two, fb_o, fb_p, ib_o, ib_p, weights_o, both_o, tot_o, sega_o, segb_o = call(
            lambda *refs: scan_first_kernel(count, *refs), "scan_own",
            [low_rows] + [near(1, D)] * 2 + [near(1, HALF)] * 4 + [gate_weights, wide_two, near(4, HALF), ends, ends],
            ids, tokens, restart, *mixer_own,
            scratch=projections + [pltpu.VMEM((4 * SEG, ROWS), f32), pltpu.VMEM((3 * SEG, ROWS), f32)],
        )
    else:
        gain_one, gain_two = small_used[:D][None], small_used[D : 2 * D][None]
        biases = small_used[2 * D :].reshape(2, PLANES, 2, ROWS).transpose(0, 2, 1, 3).reshape(4, 1, HALF)
        fb_o, fb_p, ib_o, ib_p = [biases[k] for k in range(4)]
        normed = call(normed_kernel, "first_norm", low_rows, tokens, gain_one)
        weights_o, both_o, tot_o, sega_o, segb_o = call(
            lambda *refs: scan_kernel(True, *refs), "scan_own", [gate_weights, wide_two, near(4, HALF), ends, ends],
            normed, restart, fb_o, ib_o, *mixer_own, scratch=projections,
        )
    weights_p, both_p, tot, sega_p, segb_p = call(
        lambda *refs: scan_kernel(False, *refs), "scan_other", [gate_weights, wide_two, near(4, H), ends, ends],
        normed, restart, fb_p, ib_p, tot_o, *mixer_par, scratch=projections,
    )

    kept_terms = {}

    def terms_own(ready):
        kept_terms["own"] = call(
            terms_kernel, "terms_own", [wide] * 4,
            normed, fb_o, ib_o, weights_o, order=[ready], scratch=projections[:2],
        )
        return [kept_terms["own"][0]]

    def terms_other(ready):
        kept_terms["other"] = call(
            terms_kernel, "terms_other", [wide] * 4,
            normed, fb_p, ib_p, weights_p, order=[ready], scratch=projections[:2],
        )
        return [kept_terms["other"][0]]

    def masked_cotangent(ready):
        kept_terms["d_out"] = call(dout_kernel, "d_out", low_rows, cotangent, valid, order=[ready])
        return [kept_terms["d_out"]]

    def terms_both(ready):
        order = terms_other(ready)
        return order + (masked_cotangent(ready) if direct else [])

    incoming = relay(ids, tot, True, direct, {1: terms_own, 2: terms_both, 4: masked_cotangent})
    d_out = kept_terms["d_out"]
    if direct:
        mlp_late = after(mlp_late, incoming)
        mlp_parts = [mlp_early, mlp_late, exchange(mlp_early, 0, 1), exchange(mlp_late, 0, 1)]

    states_o, states_p, low_o, low_p, resid, normed_two, out_weights = call(
        states_kernel, "states",
        [wide, wide, low_wide, low_wide, near(rows, D), low_rows, near(1, H, D, dtype=bf16)],
        incoming, tokens, gain_two, both_o, both_p, sega_o, sega_p, segb_o, segb_p,
        *mixer_own, *mixer_par,
    )

    terms = near(PLANES, ROLES, ROWS, D, dtype=bf16)
    output, d_resid, d_gain_two, mlp_gown, mlp_gpar = call(
        mlp_kernel, "mlp", [natural, near(rows, D), near(1, D), terms, terms],
        ids, normed_two, resid, d_out, valid, gain_two, *mlp_parts, mib=16,
        scratch=[
            pltpu.VMEM((PLANES, 2, ROLES, ROWS, D), bf16), pltpu.VMEM((rows, D), f32), pltpu.VMEM((rows, D), f32),
        ],
    )

    half_terms = near(PLANES, 1, ROWS, D, dtype=bf16)
    back_o, back_p, tot_back, bseg_o, bseg_p, out_gown, out_gpar = call(
        back_kernel, "back_scan", [wide, wide, near(4, H), ends, ends, half_terms, half_terms],
        d_resid, low_o, low_p, both_o, both_p, sega_o, sega_p, out_weights,
    )

    beside = {}
    if direct:
        mlp_got, out_got = exchange(mlp_gpar, 0, 1), exchange(out_gpar, 0, 1)
        two_fives = near(2, ROLES + 1, ROWS, D, dtype=bf16)

        def mlp_pair(ready):
            kept_terms["mlp"] = call(
                mlp_pair_kernel, "mlp_pair_sum", [two_fives] * 2, ids, mlp_gown, mlp_got, out_gown, out_got,
                order=[ready],
            )
            return [kept_terms["mlp"][0]]

        beside = {2: mlp_pair}

    arriving = relay(ids, tot_back, False, direct, beside)
    terms_o, terms_p = kept_terms["own"], kept_terms["other"]
    if direct:
        mlp_keep, mlp_send = kept_terms["mlp"]
        mlp_got = exchange_lane(mlp_send, True)

    def gates_back(column, back, sega, bseg, share, df, di, cand, retain, states, order, name):
        return call(
            lambda *refs: gates_kernel(column, *refs), name,
            [near(PLANES, GATES, ROWS, D, dtype=bf16), low_wide, low_wide, low_wide, near(1, HALF), near(1, HALF)],
            arriving, incoming, back, sega, bseg, share, df, di, cand, retain, states, restart, normed, order=order,
        )

    gate_gpar, pf_p, pi_p, pc_p, dfb_p, dib_p = gates_back(
        HALF, back_p, sega_p, bseg_p, *terms_p, both_p, states_p, [tot_back], "gates_other"
    )
    gate_gown, pf_o, pi_o, pc_o, dfb_o, dib_o = gates_back(
        0, back_o, sega_o, bseg_o, *terms_o, both_o, states_o, [dfb_p], "gates_own"
    )

    d_normed, small_terms = call(
        input_terms_kernel, "input_terms", [near(rows, D), near(TAIL, D)],
        ids, tokens, d_gain_two, dfb_o, dfb_p, dib_o, dib_p,
        pf_o, pi_o, pc_o, pf_p, pi_p, pc_p, weights_o, weights_p, order=[dfb_o],
        scratch=[pltpu.VMEM((3 * SEG, ROWS), f32)],
    )

    def input_grad(ready):
        return call(input_kernel, "input_grad", [natural, near(SEG, ROWS)], tokens, gain_one, d_resid, d_normed, order=[ready])

    def with_moments(keep, got, weight, first_moment, second, name):
        count = weight.shape[0]
        return call(
            moments_kernel, name, [shape(count, D)] * 3 + [near(count, D)] + [near(SEG, 128)] * 2,
            keep, got, weight, first_moment, second,
        )

    if direct:
        shard, low_shard = near(ROWS, D), near(ROWS, D, dtype=bf16)
        long, low_long = near(ROWS + TAIL, D), near(ROWS + TAIL, D, dtype=bf16)
        quarter, low_shard = near(2, 2, ROWS, D, dtype=bf16), near(ROWS, D, dtype=bf16)
        mlp_keep, mlp_send, out_keep, out_send = call(
            half_sum_kernel, "mlp_half_sum", [quarter, quarter, low_shard, low_shard], ids, mlp_keep, mlp_got,
            order=[small_terms],
        )
        gate_parts = call(
            gate_pair_kernel, "gate_pair_sum", [near(GATES * ROWS + TAIL, D, dtype=bf16)] * PLANES,
            gate_gown, exchange(gate_gpar, 0, 1), small_terms, exchange(small_terms, 0, 1), order=[out_keep],
        )
        gate_round = [gate_parts[0]] + [
            exchange(part, *bits) for part, bits in zip(gate_parts[1:], PLANE_BITS[1:], strict=True)
        ]
        d_x, x_done = input_grad(gate_parts[0])
        out_got = exchange_lane(out_send, False)
        two = near(2, ROWS, D, dtype=bf16)
        mlp_stay, mlp_send = call(
            mlp_far_kernel, "mlp_z_sum", [two, two], mlp_keep, exchange_z_lane(mlp_send, False)
        )
        mlp_stay, mlp_send = call(
            mlp_last_kernel, "mlp_z_last", [shard, low_shard], mlp_stay, exchange_z_lane(mlp_send, True)
        )
        mlp_done = with_moments(
            mlp_stay, exchange_lane(mlp_send, False), mlp_weights, mlp_first, mlp_second, "mlp_moments"
        )
        gate_keep, *gate_sends = call(
            gate_plane_kernel, "gate_plane_sum", [long] + [low_long] * 3, ids, *gate_round, out_keep, out_got,
            order=[x_done],
        )
        gate_got = z_terms(gate_sends)
    else:

        def scattered(own, par):
            full_terms = jnp.stack([own, par]).transpose(2, 1, 0, 3, 4).reshape(-1, D)
            return lax.psum_scatter(full_terms, AXES, scatter_dimension=0, tiled=True).astype(f32)

        d_x, _ = input_grad(small_terms)
        mlp_grad = scattered(mlp_gown, mlp_gpar)
        mixer_grad = scattered(
            jnp.concatenate([gate_gown, out_gown], axis=1), jnp.concatenate([gate_gpar, out_gpar], axis=1)
        )
        none = jnp.zeros_like(mlp_grad, dtype=bf16)
        mlp_done = with_moments(mlp_grad, none, mlp_weights, mlp_first, mlp_second, "mlp_moments")
        gate_keep = jnp.concatenate([mixer_grad, lax.psum(small_terms, AXES)], axis=0)
        gate_got = [jnp.zeros_like(gate_keep, dtype=bf16)] * 3
    mlp_grad, mlp_first_new, mlp_second_new, mlp_dir, mlp_wsum, mlp_dsum = mlp_done
    count, mixer_count = small_params.shape[0], mixer_weights.shape[0]
    line, matrix = shape(1, count), shape(mixer_count, D)
    mixer_grad, mixer_first_new, mixer_second_new, mixer_dir, small_grad, small_first_new, small_second_new, small_dir, squares = call(
        finish_kernel, "finish", [near(mixer_count, D)] * 4 + [line] * 3 + [near(1, count), near(SEG, ROWS)],
        ids, gate_keep, *gate_got, mlp_wsum, mlp_dsum, mixer_weights, mixer_first, mixer_second,
        small_params[None], small_first[None], small_second[None], scratch=[pltpu.VMEM((4 * SEG, ROWS), f32)],
    )

    def mixer_update(sums):
        matrix = shape(mixer_count, D)
        return call(
            mixer_update_kernel, "mixer_update", [matrix, shape(mixer_count, D, dtype=bf16)] + [matrix] * 3 + [near(SEG, ROWS)],
            ids, sums, mixer_weights, mixer_dir, mixer_grad, mixer_first_new, mixer_second_new,
        )

    if direct:
        sums = squares + exchange(squares, 0, 1)
        over_y, over_x, over_both = (exchange(sums, *bits) for bits in PLANE_BITS[1:])
        sums = (sums + over_y) + (over_x + over_both)
        stored = mixer_update(sums)
        near_z, far_z, both_z = (exchange(sums, 2 * k, 0) for k in range(1, ROLES))
        sums = (sums + near_z) + (far_z + both_z)
    else:
        sums = all_sum(squares)
        stored = mixer_update(sums)
    mixer_new, mixer_copy, mixer_grad, mixer_first_new, mixer_second_new, mixer_updated = stored
    matrix, low_line = shape(*mlp_weights.shape), shape(1, count, dtype=bf16)
    mlp_new, mlp_copy, small_new, small_copy, tensor_norms, trust_ratios = call(
        last_update_kernel, "last_update",
        [matrix, shape(*mlp_weights.shape, dtype=bf16), line, low_line, shape(2, 10), shape(1, 10)],
        ids, sums, mlp_weights, mlp_dir, small_params[None], small_dir, order=[mixer_updated],
    )
    return (
        output,
        d_x,
        mixer_grad,
        mlp_grad,
        small_grad[0],
        mixer_first_new,
        mixer_second_new,
        mlp_first_new,
        mlp_second_new,
        small_first_new[0],
        small_second_new[0],
        mixer_new,
        mlp_new,
        small_new[0],
        mixer_copy,
        mlp_copy,
        small_copy[0],
        tensor_norms,
        trust_ratios[0],
    )


def solution(mesh):
    shard = P(("seq", "batch"), None)
    shard_flat = P(("seq", "batch"))
    stream = P("batch", "seq", None)
    return jax.shard_map(
        on_device,
        mesh=mesh,
        in_specs=(
            stream, P("batch", None), stream, shard, shard, shard_flat,
            shard, shard, shard, shard, shard_flat, shard_flat,
        ),
        out_specs=(
            stream, stream, shard, shard, shard_flat, shard, shard, shard, shard, shard_flat, shard_flat,
            shard, shard, shard_flat, shard, shard, shard_flat, P(), P(),
        ),
        check_vma=False,
    )
```

```python
import functools

import jax
import jax.numpy as jnp
from jax import lax
from jax.experimental import pallas as pl
from jax.experimental.pallas import tpu as pltpu
from jax.sharding import PartitionSpec as P

D = 512
H = 1024
FF = 2048
STEP = 5
SEG = 8
ROWS = 128
PLANES = 4
HALF = PLANES * ROWS
GATES = 3
ROLES = 4
TAIL = 16
SMALL_BLOCKS = 3
Z, X, Y, CORE, SEQ, DEVICE, MIXER_ROLE, MLP_ROLE = range(8)

first_decay = 0.5
second_decay = 0.5
learn_rate = 0.25
matrix_decay = 0.01
moment_eps = 1e-06

f32 = jnp.float32
bf16 = jnp.bfloat16
AXES = ("seq", "batch")

PLANE_BITS = ((0, 0), (0, 2), (1, 0), (1, 2))


def dot_nt(a, b):
    return lax.dot_general(a, b, (((1,), (1,)), ((), ())), preferred_element_type=f32)


def dot_nn(a, b):
    return lax.dot_general(a, b, (((1,), (0,)), ((), ())), preferred_element_type=f32)


def dot_tn(a, b):
    return lax.dot_general(a, b, (((0,), (0,)), ((), ())), preferred_element_type=f32)


def exchange(value, seq_bits, batch_bits, targets=None):
    seqs, batches = lax.axis_size("seq"), lax.axis_size("batch")
    pairs = [
        (s * batches + b, (s ^ seq_bits) * batches + (b ^ batch_bits))
        for s in range(seqs)
        for b in range(batches)
        if targets is None or (s ^ seq_bits) in targets
    ]
    return lax.ppermute(value, AXES, pairs)


def unit(x):
    return lax.rsqrt(jnp.mean(x * x, axis=-1, keepdims=True) + 1e-05)


def rms_back(x, d_normed, gain):
    scale = unit(x)
    normal = x * scale
    d_unit = d_normed * gain
    mean = jnp.mean(d_unit * normal, axis=-1, keepdims=True)
    return jnp.sum(d_normed * normal, axis=0, keepdims=True), scale * (d_unit - normal * mean)


def gather_roles(slabs, held):
    for role in range(GATES):
        for q, ref in enumerate(slabs):
            held[role, pl.ds(q * ROWS, ROWS)] = ref[pl.ds(role * ROWS, ROWS), :]


def group(s, steps, j):
    return pl.ds(pl.multiple_of((s * steps + j) * SEG, SEG), SEG)


def pair(s, steps, j):
    return pl.ds(pl.multiple_of((s * steps + 2 * j) * SEG, 2 * SEG), 2 * SEG)


def segment_order(block):
    row = lax.broadcasted_iota(jnp.int32, (block, block), 0)
    position = lax.broadcasted_iota(jnp.int32, (block, block), 1)
    return jnp.where(position == (row % SEG) * (block // SEG) + row // SEG, 1.0, 0.0).astype(bf16)


def inward(ref):
    order = segment_order(ref.shape[1])
    return jnp.concatenate([dot_nn(order, ref[s]) for s in range(2)], axis=0)


def outward(ref, value):
    block = ref.shape[1]
    order = segment_order(block)
    for s in range(2):
        ref[s] = dot_tn(order, value[s * block : (s + 1) * block]).astype(bf16)


def z_of(ids_ref, k, core):
    return ids_ref[Z] ^ (jnp.where(core == 0, k, 3 - k) if k in (1, 2) else k)


def pack_kernel(ids_ref, weights_ref, small_ref, got_ref, out_ref):
    out_ref[pl.ds(0, ROWS), :] = weights_ref[...]
    mine, other = small_ref[...], got_ref[...]
    rest = jnp.zeros((1, ROWS - mine.shape[1]), f32)
    core = ids_ref[CORE]
    lines = [jnp.where(core == 0, mine, other), rest, jnp.where(core == 0, other, mine), rest]
    line = jnp.concatenate(lines + [jnp.zeros((1, D - 2 * ROWS), f32)], axis=1)
    out_ref[pl.ds(ROWS, TAIL), :] = jnp.broadcast_to(line, (TAIL, D)).astype(bf16)


def slab_kernel(ids_ref, early_ref, late_ref, *refs):
    slab_ref, lines = refs[-2:]
    lines[...] = jnp.zeros_like(lines)
    for k in range(ROLES):
        part = (early_ref, late_ref)[k // 2].at[k % 2]
        role = z_of(ids_ref, k, ids_ref[CORE])
        slab_ref[pl.ds(pl.multiple_of(role * ROWS, ROWS), ROWS), :] = part[pl.ds(0, ROWS), :]
        lines[pl.ds(role, 1), :] = part[pl.ds(ROWS, TAIL), :].astype(f32)[0:1]
    slab_ref[pl.ds(ROLES * ROWS, TAIL), :] = lines[...].astype(bf16)


def marks_kernel(ids_ref, lengths_ref, restart_ref, valid_ref):
    block = restart_ref.shape[0] // 2
    row = lax.broadcasted_iota(jnp.int32, (block, 1), 0)
    position = ids_ref[SEQ] * block + (row % SEG) * (block // SEG) + row // SEG
    for s in range(2):
        begins = jnp.zeros((block, 1), jnp.bool_)
        end = 0
        for k in range(lengths_ref.shape[1]):
            begins = begins | (position == end)
            end = end + lengths_ref[s, k]
        begins = begins | (position == end)
        restart_ref[pl.ds(s * block, block), :] = jnp.where(begins, 0.0, 1.0)
        valid_ref[pl.ds(s * block, block), :] = jnp.where(position < end, 1.0, 0.0)


def stack_kernel(first_ref, second_ref, *refs):
    out_ref = refs[-1]
    if first_ref.shape == out_ref.shape[1:]:
        out_ref[0], out_ref[1] = first_ref[...], second_ref[...]
    else:
        count = first_ref.shape[0]
        out_ref[:count], out_ref[count:] = first_ref[...], second_ref[...]


def normed_kernel(tok_ref, gain_ref, normed_ref):
    normed_ref[...] = first_norm(tok_ref, gain_ref)


def relay_kernel(bit, forward, flipped, ids_ref, group_ref, other_ref, *refs):
    late = ((ids_ref[SEQ] & bit) != 0) == forward
    mine, other = group_ref[...], other_ref[...]
    if flipped:
        quarter = HALF // 2
        at = (quarter, 0, 3 * quarter, 2 * quarter)
        other = jnp.concatenate([other[:, k : k + quarter] for k in at], axis=1)
    if bit == 1:
        decay, state = jnp.ones_like(mine[:2]), jnp.zeros_like(mine[:2])
    else:
        decay, state = refs[0][0:2, :], refs[0][2:4, :]
    state = jnp.where(late, decay * other[2:] + state, state)
    if refs[-1].shape[0] == 2:
        refs[-1][...] = state
        return
    group_out, before_out = refs[-2:]
    before_out[...] = jnp.concatenate([jnp.where(late, decay * other[:2], decay), state], axis=0)
    first, second = jnp.where(late, other, mine), jnp.where(late, mine, other)
    group_out[...] = jnp.concatenate([first[:2] * second[:2], second[:2] * first[2:] + second[2:]], axis=0)


def relay_far_kernel(forward, ids_ref, before_ref, *refs):
    terms, state_ref = refs[:ROLES], refs[-1]
    z = ids_ref[Z]
    state = jnp.zeros_like(state_ref)
    for place in range(ROLES - 1):
        source = place if forward else ROLES - 1 - place
        term = terms[0][...]
        for k in range(1, ROLES):
            term = jnp.where((z ^ source) == k, terms[k][...], term)
        earlier = (source < z) if forward else (source > z)
        state = jnp.where(earlier, term[2:] + term[:2] * state, state)
    state_ref[...] = before_ref[2:4, :] + before_ref[0:2, :] * state


def gate_shares(f, i):
    most = jnp.maximum(jnp.maximum(-f, -i), 0.0)
    one, low_f, low_i = jnp.exp(-most), jnp.exp(-f - most), jnp.exp(-i - most)
    inverse = 1.0 / ((one + low_i) + (one + low_f))
    return (one + low_i) * inverse, (one + low_f) * inverse, low_f * inverse, low_i * inverse


def first_norm(tok_ref, gain_ref):
    x = inward(tok_ref)
    return (x * unit(x) * gain_ref[...]).astype(bf16)


def unpack(count, ids_ref, slabs, by_device, flat):
    chips = [2 * (ids_ref[X] ^ (k // 2)) + (ids_ref[Y] ^ (k % 2)) for k in range(PLANES)]
    for k, ref in enumerate(slabs):
        lines = ref[pl.ds(ROLES * ROWS, TAIL), :].astype(f32)
        for z in range(ROLES):
            for core in range(2):
                row = z * 2 * PLANES + 2 * chips[k] + core
                by_device[pl.ds(row, 1), :] = lines[z : z + 1, core * ROWS : (core + 1) * ROWS]
    parts = [by_device[pl.ds(k, 8, stride=4), :] for k in range(4)]
    for k in range(3):
        cut = ROWS - (k + 1) * (ROWS - count)
        row = jnp.concatenate([parts[k][:, k * (ROWS - count) : count], parts[k + 1][:, : ROWS - cut]], axis=1)
        flat[pl.ds(k, 8, stride=3), :] = row
    rows = [flat[pl.ds(k, 1), :] for k in range(2 * PLANES)]
    yield jnp.concatenate(rows[:PLANES], axis=1)
    yield jnp.concatenate(rows[PLANES:], axis=1)
    for base in (2 * PLANES, 4 * PLANES):
        for half in range(2):
            at = [base + 2 * chips[k] + (ids_ref[CORE] ^ half) for k in range(PLANES)]
            yield jnp.concatenate([flat[pl.ds(row, 1), :] for row in at], axis=1)


def scan_halves(normed, f_bias, i_bias, rs_ref, held, both_ref, tot_ref, columns, sega_ref, segb_ref, f_ref, i_ref, c_ref):
    for role, ref in enumerate((f_ref, i_ref, c_ref)):
        ref[...] = dot_nt(normed, held[role])
    steps = normed.shape[0] // (2 * SEG)

    def step(j, carry):
        after = []
        for s in range(2):
            at = group(s, steps, j)
            keep, share, _, _ = gate_shares(f_ref[at, :] + f_bias, i_ref[at, :] + i_bias)
            a = keep * rs_ref[at, :]
            b = a * carry[s][1] + share * c_ref[at, :]
            both_ref[0, at, :] = a
            both_ref[1, at, :] = b
            after.append((a * carry[s][0], b))
        return tuple(after)

    start = (jnp.ones((SEG, HALF), f32), jnp.zeros((SEG, HALF), f32))
    ends = lax.fori_loop(0, steps, step, (start, start), unroll=steps)
    for s, (seg_a, seg_b) in enumerate(ends):
        sega_ref[pl.ds(s * SEG, SEG), :] = seg_a
        segb_ref[pl.ds(s * SEG, SEG), :] = seg_b
        tot_a, tot_b = seg_a[0:1], seg_b[0:1]
        for k in range(1, SEG):
            a = seg_a[k : k + 1]
            tot_a, tot_b = a * tot_a, a * tot_b + seg_b[k : k + 1]
        tot_ref[pl.ds(s, 1), columns] = tot_a
        tot_ref[pl.ds(2 + s, 1), columns] = tot_b


def scan_first_kernel(count, ids_ref, tok_ref, rs_ref, *refs):
    slabs, outs, scratch = refs[:PLANES], refs[PLANES:-5], refs[-5:]
    normed_ref, gain_one_ref, gain_two_ref, fo_ref, fp_ref, io_ref, ip_ref, held, both_ref, tot_ref, sega_ref, segb_ref = outs
    f_ref, i_ref, c_ref, by_device, flat = scratch
    gather_roles(slabs, held)
    small = unpack(count, ids_ref, slabs, by_device, flat)
    for ref, value in zip((gain_one_ref, gain_two_ref, fo_ref, fp_ref, io_ref, ip_ref), small, strict=True):
        ref[...] = value
    normed_ref[...] = first_norm(tok_ref, gain_one_ref)
    scan_halves(
        normed_ref[...], fo_ref[...], io_ref[...], rs_ref, held, both_ref, tot_ref, pl.ds(0, HALF),
        sega_ref, segb_ref, f_ref, i_ref, c_ref,
    )


def scan_kernel(first, normed_ref, rs_ref, fb_ref, ib_ref, *refs):
    if not first:
        earlier_ref, *refs = refs
    slabs, (held, both_ref, tot_ref, sega_ref, segb_ref, f_ref, i_ref, c_ref) = refs[:PLANES], refs[-8:]
    gather_roles(slabs, held)
    if not first:
        tot_ref[:, pl.ds(0, HALF)] = earlier_ref[...]
    scan_halves(
        normed_ref[...], fb_ref[...], ib_ref[...], rs_ref, held, both_ref, tot_ref,
        pl.ds(0 if first else HALF, HALF), sega_ref, segb_ref, f_ref, i_ref, c_ref,
    )


def dout_kernel(cot_ref, valid_ref, *refs):
    refs[-1][...] = (inward(cot_ref) * valid_ref[...]).astype(bf16)


def terms_kernel(normed_ref, fb_ref, ib_ref, held, *refs):
    share_ref, df_ref, di_ref, cand_ref, f_ref, i_ref = refs[-6:]
    normed = normed_ref[...]
    for role, ref in enumerate((f_ref, i_ref, cand_ref)):
        ref[...] = dot_nt(normed, held[role])
    f_bias, i_bias = fb_ref[...], ib_ref[...]

    def step(j, carry):
        at = pl.ds(pl.multiple_of(j * 2 * SEG, 2 * SEG), 2 * SEG)
        keep, share, slow_f, slow_i = gate_shares(f_ref[at, :] + f_bias, i_ref[at, :] + i_bias)
        share_ref[at, :] = share
        df_ref[at, :] = keep * slow_f
        di_ref[at, :] = share * slow_i
        return carry

    lax.fori_loop(0, normed.shape[0] // (2 * SEG), step, 0, unroll=8)


def states_kernel(inc_ref, tok_ref, gain_ref, both_o, both_p, sega_o, sega_p, segb_o, segb_p, *refs):
    slabs, refs = refs[: 2 * PLANES], refs[2 * PLANES :]
    states_o, states_p, low_o, low_p, resid_ref, normed_ref, held = refs
    steps = resid_ref.shape[0] // (2 * SEG)
    halves = (
        (both_o, sega_o, segb_o, states_o, low_o, 0),
        (both_p, sega_p, segb_p, states_p, low_p, HALF),
    )
    start = []
    for _, sega, segb, _, _, column in halves:
        for s in range(2):
            seg_a, seg_b = sega[pl.ds(s * SEG, SEG), :], segb[pl.ds(s * SEG, SEG), :]
            at_seg = [inc_ref[pl.ds(s, 1), pl.ds(column, HALF)]]
            for k in range(SEG - 1):
                at_seg.append(seg_a[k : k + 1] * at_seg[-1] + seg_b[k : k + 1])
            start.append(jnp.concatenate(at_seg, axis=0))

    def step(j, carry):
        after = []
        for k, (both, _, _, states, low, _) in enumerate(halves):
            for s in range(2):
                carried, two = carry[2 * k + s], []
                for q in range(2):
                    at = group(s, steps, 2 * j + q)
                    carried = both[0, at, :] * carried
                    two.append(both[1, at, :] + carried)
                    states[at, :] = two[-1]
                low[pair(s, steps, j), :] = jnp.concatenate(two, axis=0).astype(bf16)
                after.append(carried)
        return tuple(after)

    lax.fori_loop(0, steps // 2, step, tuple(start), unroll=steps // 2)
    r = inward(tok_ref)
    for q, ref in enumerate(slabs):
        held[0, pl.ds(q * ROWS, ROWS)] = ref[pl.ds(GATES * ROWS, ROWS), :]
    for low, k in zip((low_o, low_p), range(2), strict=True):
        r = r + dot_nn(low[...], held[0, pl.ds(k * HALF, HALF)])
    resid_ref[...] = r
    normed_ref[...] = (r * unit(r) * gain_ref[...]).astype(bf16)


GELU_A = 0.7978845608028654
GELU_B = 0.044715


def mlp_kernel(ids_ref, normed_ref, resid_ref, dout_ref, gain_ref, *refs):
    parts, refs = refs[:4], refs[4:]
    dresid_ref, dgain_ref, gown_ref, gpar_ref, act_ref, held, dnorm_ref = refs

    def bring(at):
        for half in range(2):
            for k in range(ROLES):
                role = z_of(ids_ref, k, ids_ref[CORE] ^ half)
                held[at, half, pl.ds(role, 1)] = parts[2 * half + k // 2][k % 2, at].reshape(1, ROWS, D)

    bring(0)
    dnorm_ref[...] = jnp.zeros_like(dnorm_ref)

    normed, dout = normed_ref[...], dout_ref[...]

    def ahead(i):
        at, low = i // 2, i % 2
        if low == 1 and at + 1 < PLANES:
            bring(at + 1)
        w_up = held[at, :, low].reshape(2 * ROWS, D)
        w_down = held[at, :, low + 2].reshape(2 * ROWS, D)
        return dot_nt(normed, w_up), dot_nt(dout, w_down), w_up, w_down

    now = ahead(0)
    for i in range(2 * PLANES):
        inner, d_act, w_up, w_down = now
        if i + 1 < 2 * PLANES:
            now = ahead(i + 1)
        square = inner * inner
        curve = jnp.tanh(inner * (GELU_A + GELU_A * GELU_B * square))
        half = 0.5 + 0.5 * curve
        activated = (inner * half).astype(bf16)
        slope = half + (half - half * half) * (inner * (2.0 * GELU_A + 6.0 * GELU_A * GELU_B * square))
        d_inner = (slope * d_act).astype(bf16)
        act_ref[i] = activated
        dnorm_ref[...] += dot_nn(d_inner, w_up)
        g_up = dot_tn(d_inner, normed).astype(bf16).reshape(2, ROWS, D)
        g_down = dot_tn(activated, dout).astype(bf16).reshape(2, ROWS, D)
        for k, ref in enumerate((gown_ref, gpar_ref)):
            ref[i // 2, i % 2] = g_up[k]
            ref[i // 2, i % 2 + 2] = g_down[k]
    r = resid_ref[...]
    dgain_ref[...], d_r = rms_back(r, dnorm_ref[...], gain_ref[...])
    dresid_ref[...] = dout_ref[...].astype(f32) + d_r


def back_kernel(dresid_ref, low_o, low_p, retain_o, retain_p, sega_o, sega_p, held, *refs):
    acc_o, acc_p, tot_ref, segb_o, segb_p, gown_ref, gpar_ref = refs
    steps = dresid_ref.shape[0] // (2 * SEG)
    dmix = dresid_ref[...].astype(bf16)
    for acc, k in zip((acc_o, acc_p), range(2), strict=True):
        acc[...] = dot_nt(dmix, held[0, pl.ds(k * HALF, HALF)])
    halves = ((retain_o, acc_o), (retain_p, acc_p))

    def step(n, carry):
        after = []
        for k, (retain, acc) in enumerate(halves):
            for s in range(2):
                at = group(s, steps, steps - 1 - n)
                back = acc[at, :] + carry[2 * k + s]
                acc[at, :] = back
                after.append(retain[0, at, :] * back)
        return tuple(after)

    ends = lax.fori_loop(0, steps, step, (jnp.zeros((SEG, HALF), f32),) * 4, unroll=steps)
    for k, (sega, segb) in enumerate(((sega_o, segb_o), (sega_p, segb_p))):
        for s in range(2):
            emitted = ends[2 * k + s]
            segb[pl.ds(s * SEG, SEG), :] = emitted
            seg_a = sega[pl.ds(s * SEG, SEG), :]
            tot_a, tot_b = seg_a[SEG - 1 :], emitted[SEG - 1 :]
            for q in reversed(range(SEG - 1)):
                a = seg_a[q : q + 1]
                tot_a, tot_b = a * tot_a, a * tot_b + emitted[q : q + 1]
            tot_ref[pl.ds(s, 1), pl.ds(k * HALF, HALF)] = tot_a
            tot_ref[pl.ds(2 + s, 1), pl.ds(k * HALF, HALF)] = tot_b
    for low, ref in ((low_o, gown_ref), (low_p, gpar_ref)):
        ref[...] = dot_tn(low[...], dmix).astype(bf16).reshape(PLANES, 1, ROWS, D)


def gates_kernel(
    column, arr_ref, inc_ref, acc_ref, sega_ref, segb_ref, share_ref, df_ref, di_ref, cand_ref, retain_ref, states_ref,
    rs_ref, normed_ref, order_ref, grad_ref, pf_ref, pi_ref, pc_ref, dfb_ref, dib_ref,
):
    steps = normed_ref.shape[0] // (2 * SEG)
    start, first = [], []
    for s in range(2):
        seg_a, seg_b = sega_ref[pl.ds(s * SEG, SEG), :], segb_ref[pl.ds(s * SEG, SEG), :]
        at_seg = [arr_ref[pl.ds(s, 1), pl.ds(column, HALF)]]
        for k in reversed(range(1, SEG)):
            at_seg.append(seg_a[k : k + 1] * at_seg[-1] + seg_b[k : k + 1])
        start.append(jnp.concatenate(at_seg[::-1], axis=0))
        ends = states_ref[group(s, steps, steps - 1), :]
        first.append(jnp.concatenate([inc_ref[pl.ds(s, 1), pl.ds(column, HALF)], ends[: SEG - 1]], axis=0))

    def step(n, carry):
        *carried, sum_f, sum_i = carry
        m = steps // 2 - 1 - n
        for s in range(2):
            terms = []
            for q in (1, 0):
                j = 2 * m + q
                at = group(s, steps, j)
                back = acc_ref[at, :] + carried[s]
                carried[s] = carried[s] * retain_ref[0, at, :]
                previous = states_ref[group(s, steps, jnp.maximum(j - 1, 0)), :]
                if q == 0:
                    previous = jnp.where(m == 0, first[s], previous)
                both_ways = back * (previous * rs_ref[at, :] - cand_ref[at, :])
                d_f = both_ways * df_ref[at, :]
                d_i = both_ways * di_ref[at, :]
                sum_f = sum_f + d_f
                sum_i = sum_i - d_i
                terms.append((d_f, -d_i, back * share_ref[at, :]))
            for late, early, ref in zip(*terms, (pf_ref, pi_ref, pc_ref), strict=True):
                ref[pair(s, steps, m), :] = jnp.concatenate([early, late], axis=0).astype(bf16)
        return (*carried, sum_f, sum_i)

    nothing = jnp.zeros((SEG, HALF), f32)
    *_, sum_f, sum_i = lax.fori_loop(0, steps // 2, step, (*start, nothing, nothing), unroll=steps // 2)
    dfb_ref[...] = jnp.sum(sum_f, axis=0, keepdims=True)
    dib_ref[...] = jnp.sum(sum_i, axis=0, keepdims=True)
    normed = normed_ref[...]
    for role, ref in enumerate((pf_ref, pi_ref, pc_ref)):
        grad_ref[:, role] = dot_tn(ref[...], normed).astype(bf16).reshape(PLANES, ROWS, D)


def input_terms_kernel(ids_ref, tok_ref, dgain_two_ref, dfb_o, dfb_p, dib_o, dib_p, *refs):
    terms, weights, refs = refs[: 2 * GATES], refs[2 * GATES : 2 * GATES + 2], refs[-3:]
    dnorm_ref, small_ref, rows_ref = refs
    d_normed = 0.0
    for role in range(GATES):
        for k in range(2):
            d_normed = d_normed + dot_nn(terms[k * GATES + role][...], weights[k][role])
    dnorm_ref[...] = d_normed
    x = inward(tok_ref)
    d_gain = jnp.sum(d_normed * (x * unit(x)), axis=0, keepdims=True)
    for k in range(PLANES):
        rows_ref[pl.ds(k, 1), :] = d_gain[:, k * ROWS : (k + 1) * ROWS]
        rows_ref[pl.ds(PLANES + k, 1), :] = dgain_two_ref[:, pl.ds(k * ROWS, ROWS)]
        chip = 4 * (ids_ref[X] ^ (k // 2)) + 2 * (ids_ref[Y] ^ (k % 2))
        for core, (fb, ib) in enumerate(((dfb_o, dib_o), (dfb_p, dib_p))):
            row = 2 * PLANES + chip + (ids_ref[CORE] ^ core)
            rows_ref[pl.ds(row, 1), :] = fb[:, pl.ds(k * ROWS, ROWS)]
            rows_ref[pl.ds(row + 2 * PLANES, 1), :] = ib[:, pl.ds(k * ROWS, ROWS)]
    blocks = [rows_ref[pl.ds(k * SEG, SEG), :] for k in range(SMALL_BLOCKS)] + [jnp.zeros((SEG, ROWS), f32)]
    small_ref[...] = jnp.concatenate([jnp.concatenate(blocks, axis=1), jnp.zeros((SEG, D), f32)], axis=0)


def outputs_kernel(tok_ref, gain_ref, dresid_ref, dnorm_ref, resid_ref, valid_ref, act_ref, held, order_ref, dx_ref, output_ref, done_ref):
    done_ref[...] = jnp.zeros_like(done_ref)
    _, d_x = rms_back(inward(tok_ref), dnorm_ref[...], gain_ref[...])
    outward(dx_ref, (dresid_ref[...] + d_x).astype(bf16))
    total = resid_ref[...]
    for i in range(2 * PLANES):
        total = total + dot_nn(act_ref[i], held[i // 2, :, i % 2 + 2].reshape(2 * ROWS, D))
    outward(output_ref, (total * valid_ref[...]).astype(bf16))


def out_place(core, k):
    return jnp.where(core == 0, 3 - k, k) if k in (1, 2) else k


def mlp_pair_kernel(ids_ref, own_ref, got_ref, out_ref, outgot_ref, *refs):
    for q in range(2):
        ref = refs[-1].at[q]
        ref[pl.ds(0, ROLES)] = (own_ref[2 + q].astype(f32) + got_ref[2 + q].astype(f32)).astype(bf16)
        at = pl.ds(out_place(ids_ref[CORE], 2 + q), 1)
        ref[pl.ds(ROLES, 1)] = (out_ref[at, 0].astype(f32) + outgot_ref[at, 0].astype(f32)).astype(bf16)


def gate_pair_kernel(own_ref, got_ref, small_ref, small_got, *outs):
    small = (small_ref[...] + small_got[...]).astype(bf16)
    for k, ref in enumerate(outs[-PLANES:]):
        total = (own_ref[k].astype(f32) + got_ref[k].astype(f32)).astype(bf16)
        ref[pl.ds(0, GATES * ROWS), :] = total.reshape(GATES * ROWS, D)
        ref[pl.ds(GATES * ROWS, TAIL), :] = small


def half_sum_kernel(ids_ref, own_ref, pair_ref, out_ref, outpair_ref, got_ref, *refs):
    keep_ref, send_ref, out_keep, out_send = refs[-4:]
    z = ids_ref[Z]
    near_bit = jnp.where(ids_ref[CORE] == 0, 1, 2)
    for q in range(2):

        def total(role, q=q):
            at = pl.ds(role, 1)
            terms = own_ref[q, at].astype(f32) + pair_ref[q, at].astype(f32)
            return (terms + got_ref[q, at].astype(f32)).astype(bf16).reshape(ROWS, D)

        for k, role in enumerate((z, z ^ near_bit ^ 3)):
            keep_ref[k, q] = total(role)
            send_ref[k, q] = total(role ^ near_bit)
        at = pl.ds(out_place(ids_ref[CORE], q), 1)
        terms = out_ref[at, 0].astype(f32) + outpair_ref[at, 0].astype(f32)
        (out_keep, out_send)[q][...] = (terms + got_ref[q, pl.ds(ROLES, 1)].astype(f32)).astype(bf16).reshape(ROWS, D)


def mlp_far_kernel(keep_ref, got_ref, *refs):
    stay_ref, send_ref = refs[-2:]
    stay_ref[...] = (keep_ref[0].astype(f32) + got_ref[0].astype(f32)).astype(bf16)
    send_ref[...] = (keep_ref[1].astype(f32) + got_ref[1].astype(f32)).astype(bf16)


def mlp_last_kernel(stay_ref, got_ref, *refs):
    keep_ref, send_ref = refs[-2:]
    keep_ref[...] = stay_ref[0].astype(f32) + got_ref[0].astype(f32)
    send_ref[...] = (stay_ref[1].astype(f32) + got_ref[1].astype(f32)).astype(bf16)


def gate_plane_kernel(ids_ref, p0, p1, p2, p3, out_ref, out_got, *refs):
    z = ids_ref[Z]
    keep_ref, s1_ref, s2_ref, s3_ref = refs[-4:]

    def total(at):
        terms = [ref[at, :].astype(f32) for ref in (p0, p1, p2, p3)]
        return (terms[0] + terms[1]) + (terms[2] + terms[3])

    def of_role(role):
        at = pl.ds(pl.multiple_of(jnp.minimum(role, GATES - 1) * ROWS, ROWS), ROWS)
        return jnp.where(role == GATES, out_ref[...].astype(f32) + out_got[...].astype(f32), total(at))

    small = total(pl.ds(GATES * ROWS, TAIL))
    keep_ref[pl.ds(0, ROWS), :] = of_role(z)
    keep_ref[pl.ds(ROWS, TAIL), :] = small
    for k, ref in enumerate((s1_ref, s2_ref, s3_ref)):
        ref[pl.ds(0, ROWS), :] = of_role(z ^ (k + 1)).astype(bf16)
        ref[pl.ds(ROWS, TAIL), :] = small.astype(bf16)


def joined(at, keep_ref, gots):
    total = keep_ref[at, :]
    for ref in gots:
        total = total + ref[at, :].astype(f32)
    return total


def matrix_step(at, keep_ref, gots, weight_ref, first_ref, second_ref, outs):
    grad_ref, first_out, second_out, dir_ref = outs
    weight = weight_ref[...]
    gradient = joined(at, keep_ref, gots)
    grad_ref[...] = gradient
    first_out[...], second_out[...], direction = moments(
        weight, gradient, first_ref[...], second_ref[...], matrix_decay
    )
    dir_ref[...] = direction
    return weight, direction


def square_rows(value):
    square = jnp.sum((value * value).reshape(-1, SEG, D), axis=0)
    return (square[:, :128] + square[:, 128:256]) + (square[:, 256:384] + square[:, 384:])


def moments_kernel(keep_ref, got_ref, weight_ref, first_ref, second_ref, *outs):
    *outs, wsum_ref, dsum_ref = outs
    weight, direction = matrix_step(
        pl.ds(0, weight_ref.shape[0]), keep_ref, [got_ref], weight_ref, first_ref, second_ref, outs
    )
    wsum_ref[...] = square_rows(weight)
    dsum_ref[...] = square_rows(direction)


def finish_kernel(
    ids_ref, keep_ref, g1_ref, g2_ref, g3_ref, wsum_f, dsum_f,
    mixer_ref, mixer_first, mixer_second, weight_ref, first_ref, second_ref,
    mixer_grad, mixer_first_out, mixer_second_out, mixer_dir, grad_ref, first_out, second_out, dir_ref, squares_ref,
    rows_ref,
):
    gots = (g1_ref, g2_ref, g3_ref)
    mixer_rows = mixer_ref.shape[0]
    mixer_values = matrix_step(
        pl.ds(0, mixer_rows), keep_ref, gots, mixer_ref, mixer_first, mixer_second,
        (mixer_grad, mixer_first_out, mixer_second_out, mixer_dir),
    )
    total = joined(pl.ds(mixer_rows, TAIL), keep_ref, gots)
    rows_ref[...] = jnp.zeros_like(rows_ref)
    for k in range(SMALL_BLOCKS):
        rows_ref[pl.ds(k * SEG, SEG), :] = total[:SEG, k * ROWS : (k + 1) * ROWS]
    weight = weight_ref[...]
    count = weight.shape[1]
    start = ids_ref[DEVICE] * count
    row, lane = start // ROWS, start % ROWS
    two = jnp.concatenate([rows_ref[pl.ds(row, 1), :], rows_ref[pl.ds(row + 1, 1), :]], axis=1)
    two = jnp.broadcast_to(two, (SEG, 2 * ROWS))
    gradient = pltpu.roll(two, (2 * ROWS - lane) % (2 * ROWS), 1)[:1, :count]
    grad_ref[...] = gradient
    first_out[...], second_out[...], direction = moments(weight, gradient, first_ref[...], second_ref[...], 0.0)
    dir_ref[...] = direction
    place = start + lax.broadcasted_iota(jnp.int32, (1, count), 1)
    at = lax.broadcasted_iota(jnp.int32, (1, ROWS), 1)
    bounds = (0, D, 2 * D, 2 * D + H, 2 * D + 2 * H)
    lines = []
    for mixer_value, mlp_sum, value in zip(mixer_values, (wsum_f, dsum_f), (weight, direction), strict=True):
        line = jnp.where(at == ids_ref[MIXER_ROLE], jnp.sum(square_rows(mixer_value), keepdims=True), 0.0)
        line = line + jnp.where(at == ROLES + ids_ref[MLP_ROLE], jnp.sum(mlp_sum[...], keepdims=True), 0.0)
        for k in range(4):
            inside = (place >= bounds[k]) & (place < bounds[k + 1])
            part = jnp.sum(jnp.where(inside, value * value, 0.0), axis=1, keepdims=True)
            line = line + jnp.where(at == ROLES + 2 + k, part, 0.0)
        lines.append(line)
    squares_ref[...] = jnp.concatenate(lines + [jnp.zeros((SEG - 2, ROWS), f32)], axis=0)


def ratio_of(squares_ref, tensor):
    norms = jnp.sqrt(squares_ref[0:2, :])
    ratios = norms[0:1] / (norms[1:2] + 1e-06)
    at = lax.broadcasted_iota(jnp.int32, (1, ROWS), 1)
    return jnp.sum(jnp.where(at == tensor, ratios, 0.0), axis=1, keepdims=True)


def new_weights(ratio, weight_ref, dir_ref, new_ref, copy_ref):
    value = weight_ref[...] - learn_rate * ratio * dir_ref[...]
    new_ref[...] = value
    copy_ref[...] = value.astype(bf16)


def mixer_update_kernel(ids_ref, squares_ref, weight_ref, dir_ref, *refs):
    *ins, new_ref, copy_ref, out0, out1, out2, done_ref = refs
    done_ref[...] = jnp.zeros_like(done_ref)
    new_weights(ratio_of(squares_ref, ids_ref[MIXER_ROLE]), weight_ref, dir_ref, new_ref, copy_ref)
    for ref, out in zip(ins, (out0, out1, out2), strict=True):
        out[...] = ref[...]


def last_update_kernel(
    ids_ref, squares_ref, mlp_ref, mlp_dir, weight_ref, dir_ref, order_ref,
    mlp_new, mlp_copy, new_ref, copy_ref, norms_ref, ratios_ref,
):
    norms = jnp.sqrt(squares_ref[0:2, :])
    ratios = norms[0:1] / (norms[1:2] + 1e-06)
    norms_ref[...] = norms[:, : norms_ref.shape[1]]
    ratios_ref[...] = ratios[:, : ratios_ref.shape[1]]
    new_weights(ratio_of(squares_ref, ROLES + ids_ref[MLP_ROLE]), mlp_ref, mlp_dir, mlp_new, mlp_copy)
    count = weight_ref.shape[1]
    place = ids_ref[DEVICE] * count + lax.broadcasted_iota(jnp.int32, (1, count), 1)
    first, second, third, fourth = (ratio_of(squares_ref, ROLES + 2 + k) for k in range(4))
    ratio = jnp.where(
        place < 2 * D, jnp.where(place < D, first, second), jnp.where(place < 2 * D + H, third, fourth)
    )
    new_weights(ratio, weight_ref, dir_ref, new_ref, copy_ref)


SMEM = pl.BlockSpec(memory_space=pltpu.SMEM)
ANY = pl.BlockSpec(memory_space=pl.ANY)
VMEM = pl.BlockSpec(memory_space=pltpu.VMEM)


def shape(*dims, dtype=f32):
    return jax.ShapeDtypeStruct(dims, dtype)


def near(*dims, dtype=f32):
    return pltpu.VMEM(dims, dtype)


def kept(value):
    return pltpu.with_memory_space_constraint(value, pltpu.VMEM)


def away(value):
    return pltpu.with_memory_space_constraint(value, pltpu.HBM)


def call(kernel, name, out_shape, *args, order=(), far=(), scratch=(), mib=8):
    in_specs = [SMEM if arg.dtype == jnp.int32 else VMEM for arg in args] + [ANY] * (len(far) + len(order))
    return pl.pallas_call(
        kernel,
        in_specs=in_specs,
        out_specs=jax.tree.map(lambda _: VMEM, out_shape),
        out_shape=out_shape,
        scratch_shapes=list(scratch),
        compiler_params=pltpu.CompilerParams(vmem_limit_bytes=mib * 1024 * 1024),
        name=name,
    )(*[arg if arg.dtype == jnp.int32 else kept(arg) for arg in args], *[away(arg) for arg in far], *order)


def exchange_lane(value, second):
    seqs, batches = lax.axis_size("seq"), lax.axis_size("batch")
    pairs = []
    for s in range(seqs):
        for b in range(batches):
            over_x = (b % 2 == 0) != second
            pairs.append((s * batches + b, (s ^ 1) * batches + b if over_x else s * batches + (b ^ 2)))
    return lax.ppermute(value, AXES, pairs)


def exchange_z_lane(value, second):
    seqs, batches = lax.axis_size("seq"), lax.axis_size("batch")
    pairs = []
    for s in range(seqs):
        for b in range(batches):
            bit = 2 if (b % 2 == 0) != second else 4
            pairs.append((s * batches + b, (s ^ bit) * batches + b))
    return lax.ppermute(value, AXES, pairs)


def after(value, *others):
    return lax.optimization_barrier((value, *others))[0]


def over_z(shard):
    return [shard] + [exchange(shard, 2 * k, 0) for k in range(1, 4)]


def z_terms(sends):
    return [exchange(sent, 2 * (k + 1), 0) for k, sent in enumerate(sends)]


def all_sum(value):
    seqs, batches = lax.axis_size("seq"), lax.axis_size("batch")
    bit = 1
    while bit < batches:
        value = value + exchange(value, 0, bit)
        bit *= 2
    bit = 1
    while bit < seqs:
        value = value + exchange(value, bit, 0)
        bit *= 2
    return value


def relay(ids, total, forward, flipped, beside, hold=()):
    group, before, bit = total, [], 1
    joint = near(4, H)
    if flipped:
        other = exchange(group, 1, 0)
        order = beside[1](group) if 1 in beside else []
        pair, before = call(
            functools.partial(relay_kernel, 1, forward, True), "relay_near", [joint, joint], ids, group, other, order=order
        )
        others = [exchange(pair, 2 * k, 0) for k in range(1, ROLES)]
        order = beside[2](pair) if 2 in beside else []
        return call(
            functools.partial(relay_far_kernel, forward), "relay_far", near(2, H), ids, before, pair, *others, order=order
        )
    while bit < lax.axis_size("seq"):
        last = 2 * bit == lax.axis_size("seq")
        other = exchange(group, bit, 0)
        order = beside[bit](group) if bit in beside else []
        got = call(
            functools.partial(relay_kernel, bit, forward, flipped and bit == 1),
            f"relay_{bit}", near(2, H) if last else [joint, joint],
            ids, group, other, *before, *hold, order=order,
        )
        if not last:
            group, before = got[0], [got[1]]
        bit *= 2
    return got


def flip_by(value, axis, bit):
    return jnp.where(bit == 1, jnp.flip(value, axis), value)


def moments(weight, gradient, first_moment, second, decay_rate):
    first_new = first_decay * first_moment + (1.0 - first_decay) * gradient
    second_new = second_decay * second + (1.0 - second_decay) * gradient * gradient
    direction = (
        first_new
        / (1.0 - first_decay**STEP)
        / (jnp.sqrt(second_new / (1.0 - second_decay**STEP)) + moment_eps)
        + decay_rate * weight
    )
    return (first_new, second_new, direction)


def on_device(
    tokens, doc_lengths, cotangent, mixer_weights, mlp_weights, small_params,
    mixer_first, mixer_second, mlp_first, mlp_second, small_first, small_second,
):
    seqs, batches = lax.axis_size("seq"), lax.axis_size("batch")
    seq_at, batch_at = lax.axis_index("seq"), lax.axis_index("batch")
    device = seq_at * batches + batch_at
    streams, block, _ = tokens.shape
    rows = streams * block
    direct = (seqs, batches) == (8, 4)
    if direct:
        z, x, y, c = seq_at // 2, seq_at % 2, batch_at // 2, batch_at % 2
    else:
        z = x = y = c = jnp.zeros((), jnp.int32)
    mixer_role = device * mixer_weights.shape[0] // H
    mlp_role = device * mlp_weights.shape[0] // FF
    ids = jnp.stack([z, x, y, c, seq_at, device, mixer_role, mlp_role]).astype(jnp.int32)

    slab = shape(ROLES, ROWS, D, dtype=bf16)
    if direct:
        pair_of = near(2, ROWS, D, dtype=bf16)
        count = small_params.shape[0]
        packed = call(
            pack_kernel, "mixer_pack", near(ROWS + TAIL, D, dtype=bf16),
            ids, mixer_weights.astype(bf16), small_params[None], exchange(small_params, 0, 1)[None],
        )
        mixer_two = call(
            stack_kernel, "mixer_pair", near(2, ROWS + TAIL, D, dtype=bf16), packed, exchange_z_lane(packed, False)
        )
        mixer_far = exchange_z_lane(mixer_two, True)
        mlp_low = after(mlp_weights, packed).astype(bf16)
        mlp_two = call(stack_kernel, "mlp_pair", pair_of, mlp_low, exchange_lane(mlp_low, False))
        mlp_plane = call(stack_kernel, "mlp_plane", slab, mlp_two, exchange_lane(mlp_two, True))
        gate_slab = call(
            slab_kernel, "mixer_slab", shape(ROLES * ROWS + TAIL, D, dtype=bf16),
            ids, mixer_two, mixer_far, order=[mlp_plane], scratch=[pltpu.VMEM((TAIL, D), f32)],
        )
        mixer_own = [gate_slab] + [exchange(gate_slab, *bits) for bits in PLANE_BITS[1:]]
        mlp_plane = after(mlp_plane, gate_slab)
        mlp_early = call(
            stack_kernel, "mlp_early", shape(2, PLANES, ROWS, D, dtype=bf16), mlp_plane, exchange_z_lane(mlp_plane, False)
        )
        mlp_late = exchange_z_lane(mlp_early, True)
    else:
        small_used = lax.all_gather(small_params.astype(bf16).astype(f32), AXES, axis=0, tiled=True)

        def gathered(shard):
            full = lax.all_gather(shard.astype(bf16), AXES, axis=0, tiled=True)
            return full.reshape(ROLES, PLANES, 2, ROWS, D)

        full = gathered(mixer_weights)
        mixer_own, mixer_par = [[full[:, p, k].reshape(ROLES * ROWS, D) for p in range(PLANES)] for k in range(2)]
        full = gathered(mlp_weights)
        mlp_parts = [full[roles, :, k] for k in range(2) for roles in (slice(0, 2), slice(2, 4))]

    restart, valid = call(marks_kernel, "marks", [shape(rows, 1), shape(rows, 1)], ids, doc_lengths)
    d_out = call(dout_kernel, "d_out", near(rows, D, dtype=bf16), cotangent, valid)

    wide = near(rows, HALF)
    natural = shape(streams, block, D, dtype=bf16)
    low_wide = near(rows, HALF, dtype=bf16)
    low_rows = near(rows, D, dtype=bf16)
    ends = near(2 * SEG, HALF)
    projections = [pltpu.VMEM((rows, HALF), f32)] * 3

    if direct:
        mixer_own = [gate_slab, *after(tuple(mixer_own[1:]), mlp_early, restart, d_out)]
        mixer_par = [exchange(part, 0, 1) for part in mixer_own]
    wide_two, gate_weights = near(2, rows, HALF), near(GATES, HALF, D, dtype=bf16)
    if direct:
        normed, gain_one, gain_two, fb_o, fb_p, ib_o, ib_p, weights_o, both_o, tot_o, sega_o, segb_o = call(
            lambda *refs: scan_first_kernel(count, *refs), "scan_own",
            [low_rows] + [near(1, D)] * 2 + [near(1, HALF)] * 4 + [gate_weights, wide_two, near(4, HALF), ends, ends],
            ids, tokens, restart, *mixer_own,
            scratch=projections + [pltpu.VMEM((4 * SEG, ROWS), f32), pltpu.VMEM((3 * SEG, ROWS), f32)],
        )
    else:
        gain_one, gain_two = small_used[:D][None], small_used[D : 2 * D][None]
        biases = small_used[2 * D :].reshape(2, PLANES, 2, ROWS).transpose(0, 2, 1, 3).reshape(4, 1, HALF)
        fb_o, fb_p, ib_o, ib_p = [biases[k] for k in range(4)]
        normed = call(normed_kernel, "first_norm", low_rows, tokens, gain_one)
        weights_o, both_o, tot_o, sega_o, segb_o = call(
            lambda *refs: scan_kernel(True, *refs), "scan_own", [gate_weights, wide_two, near(4, HALF), ends, ends],
            normed, restart, fb_o, ib_o, *mixer_own, scratch=projections,
        )
    weights_p, both_p, tot, sega_p, segb_p = call(
        lambda *refs: scan_kernel(False, *refs), "scan_other", [gate_weights, wide_two, near(4, H), ends, ends],
        normed, restart, fb_p, ib_p, tot_o, *mixer_par, scratch=projections,
    )

    kept_terms = {}

    def terms_own(ready):
        kept_terms["own"] = call(
            terms_kernel, "terms_own", [wide] * 4,
            normed, fb_o, ib_o, weights_o, order=[ready], scratch=projections[:2],
        )
        return [kept_terms["own"][0]]

    def terms_other(ready):
        kept_terms["other"] = call(
            terms_kernel, "terms_other", [wide] * 4,
            normed, fb_p, ib_p, weights_p, order=[ready], scratch=projections[:2],
        )
        return [kept_terms["other"][0]]

    incoming = relay(ids, tot, True, direct, {1: terms_own, 2: terms_other})
    if direct:
        mlp_late = after(mlp_late, incoming)
        mlp_parts = [mlp_early, mlp_late, exchange(mlp_early, 0, 1), exchange(mlp_late, 0, 1)]

    states_o, states_p, low_o, low_p, resid, normed_two, out_weights = call(
        states_kernel, "states",
        [wide, wide, low_wide, low_wide, near(rows, D), low_rows, near(1, H, D, dtype=bf16)],
        incoming, tokens, gain_two, both_o, both_p, sega_o, sega_p, segb_o, segb_p,
        *mixer_own, *mixer_par,
    )

    terms = near(PLANES, ROLES, ROWS, D, dtype=bf16)
    d_resid, d_gain_two, mlp_gown, mlp_gpar, mlp_act, mlp_held = call(
        mlp_kernel, "mlp",
        [
            near(rows, D), near(1, D), terms, terms, near(2 * PLANES, rows, 2 * ROWS, dtype=bf16),
            near(PLANES, 2, ROLES, ROWS, D, dtype=bf16),
        ],
        ids, normed_two, resid, d_out, gain_two, *mlp_parts, mib=16, scratch=[pltpu.VMEM((rows, D), f32)],
    )

    half_terms = near(PLANES, 1, ROWS, D, dtype=bf16)
    back_o, back_p, tot_back, bseg_o, bseg_p, out_gown, out_gpar = call(
        back_kernel, "back_scan", [wide, wide, near(4, H), ends, ends, half_terms, half_terms],
        d_resid, low_o, low_p, both_o, both_p, sega_o, sega_p, out_weights,
    )

    beside = {}
    if direct:
        mlp_got, out_got = exchange(mlp_gpar, 0, 1), exchange(out_gpar, 0, 1)
        two_fives = near(2, ROLES + 1, ROWS, D, dtype=bf16)

        def mlp_pair(ready):
            kept_terms["mlp"] = call(
                mlp_pair_kernel, "mlp_pair_sum", two_fives, ids, mlp_gown, mlp_got, out_gown, out_got,
                order=[ready],
            )
            return [kept_terms["mlp"]]

        beside = {2: mlp_pair}

    arriving = relay(ids, tot_back, False, direct, beside)
    terms_o, terms_p = kept_terms["own"], kept_terms["other"]
    if direct:
        mlp_round = exchange_lane(kept_terms["mlp"], True)

    def gates_back(column, back, sega, bseg, share, df, di, cand, retain, states, order, name):
        return call(
            lambda *refs: gates_kernel(column, *refs), name,
            [near(PLANES, GATES, ROWS, D, dtype=bf16), low_wide, low_wide, low_wide, near(1, HALF), near(1, HALF)],
            arriving, incoming, back, sega, bseg, share, df, di, cand, retain, states, restart, normed, order=order,
        )

    gate_gpar, pf_p, pi_p, pc_p, dfb_p, dib_p = gates_back(
        HALF, back_p, sega_p, bseg_p, *terms_p, both_p, states_p, [tot_back], "gates_other"
    )
    gate_gown, pf_o, pi_o, pc_o, dfb_o, dib_o = gates_back(
        0, back_o, sega_o, bseg_o, *terms_o, both_o, states_o, [dfb_p], "gates_own"
    )

    d_normed, small_terms = call(
        input_terms_kernel, "input_terms", [near(rows, D), near(TAIL, D)],
        ids, tokens, d_gain_two, dfb_o, dfb_p, dib_o, dib_p,
        pf_o, pi_o, pc_o, pf_p, pi_p, pc_p, weights_o, weights_p, order=[dfb_o],
        scratch=[pltpu.VMEM((3 * SEG, ROWS), f32)],
    )

    def token_outputs(ready):
        return call(
            outputs_kernel, "outputs", [natural, natural, near(SEG, ROWS)],
            tokens, gain_one, d_resid, d_normed, resid, valid, mlp_act, mlp_held, order=[ready],
        )

    def with_moments(keep, got, weight, first_moment, second, name):
        count = weight.shape[0]
        return call(
            moments_kernel, name, [shape(count, D)] * 3 + [near(count, D)] + [near(SEG, 128)] * 2,
            keep, got, weight, first_moment, second,
        )

    if direct:
        shard, low_shard = near(ROWS, D), near(ROWS, D, dtype=bf16)
        long, low_long = near(ROWS + TAIL, D), near(ROWS + TAIL, D, dtype=bf16)
        quarter, low_shard = near(2, 2, ROWS, D, dtype=bf16), near(ROWS, D, dtype=bf16)
        small_got = exchange(small_terms, 0, 1)
        mlp_keep, mlp_send, out_keep, out_send = call(
            half_sum_kernel, "mlp_half_sum", [quarter, quarter, low_shard, low_shard], ids,
            mlp_gown, mlp_got, out_gown, out_got, mlp_round, order=[small_got],
        )
        gate_parts = call(
            gate_pair_kernel, "gate_pair_sum", [near(GATES * ROWS + TAIL, D, dtype=bf16)] * PLANES,
            gate_gown, exchange(gate_gpar, 0, 1), small_terms, small_got, order=[out_keep],
        )
        gate_round = [gate_parts[0]] + [
            exchange(part, *bits) for part, bits in zip(gate_parts[1:], PLANE_BITS[1:], strict=True)
        ]
        d_x, output, x_done = token_outputs(gate_parts[0])
        out_got = exchange_lane(out_send, False)
        two = near(2, ROWS, D, dtype=bf16)
        mlp_stay, mlp_send = call(
            mlp_far_kernel, "mlp_z_sum", [two, two], mlp_keep, exchange_z_lane(mlp_send, False)
        )
        mlp_stay, mlp_send = call(
            mlp_last_kernel, "mlp_z_last", [shard, low_shard], mlp_stay, exchange_z_lane(mlp_send, True)
        )
        mlp_done = with_moments(
            mlp_stay, exchange_lane(mlp_send, False), mlp_weights, mlp_first, mlp_second, "mlp_moments"
        )
        gate_keep, *gate_sends = call(
            gate_plane_kernel, "gate_plane_sum", [long] + [low_long] * 3, ids, *gate_round, out_keep, out_got,
            order=[x_done],
        )
        gate_got = z_terms(gate_sends)
    else:

        def scattered(own, par):
            full_terms = jnp.stack([own, par]).transpose(2, 1, 0, 3, 4).reshape(-1, D)
            return lax.psum_scatter(full_terms, AXES, scatter_dimension=0, tiled=True).astype(f32)

        d_x, output, _ = token_outputs(small_terms)
        mlp_grad = scattered(mlp_gown, mlp_gpar)
        mixer_grad = scattered(
            jnp.concatenate([gate_gown, out_gown], axis=1), jnp.concatenate([gate_gpar, out_gpar], axis=1)
        )
        none = jnp.zeros_like(mlp_grad, dtype=bf16)
        mlp_done = with_moments(mlp_grad, none, mlp_weights, mlp_first, mlp_second, "mlp_moments")
        gate_keep = jnp.concatenate([mixer_grad, lax.psum(small_terms, AXES)], axis=0)
        gate_got = [jnp.zeros_like(gate_keep, dtype=bf16)] * 3
    mlp_grad, mlp_first_new, mlp_second_new, mlp_dir, mlp_wsum, mlp_dsum = mlp_done
    count, mixer_count = small_params.shape[0], mixer_weights.shape[0]
    line, matrix = shape(1, count), shape(mixer_count, D)
    mixer_grad, mixer_first_new, mixer_second_new, mixer_dir, small_grad, small_first_new, small_second_new, small_dir, squares = call(
        finish_kernel, "finish", [near(mixer_count, D)] * 4 + [line] * 3 + [near(1, count), near(SEG, ROWS)],
        ids, gate_keep, *gate_got, mlp_wsum, mlp_dsum, mixer_weights, mixer_first, mixer_second,
        small_params[None], small_first[None], small_second[None], scratch=[pltpu.VMEM((4 * SEG, ROWS), f32)],
    )

    def mixer_update(sums):
        matrix = shape(mixer_count, D)
        return call(
            mixer_update_kernel, "mixer_update", [matrix, shape(mixer_count, D, dtype=bf16)] + [matrix] * 3 + [near(SEG, ROWS)],
            ids, sums, mixer_weights, mixer_dir, mixer_grad, mixer_first_new, mixer_second_new,
        )

    if direct:
        sums = squares + exchange(squares, 0, 1)
        over_y, over_x, over_both = (exchange(sums, *bits) for bits in PLANE_BITS[1:])
        sums = (sums + over_y) + (over_x + over_both)
        stored = mixer_update(sums)
        near_z, far_z, both_z = (exchange(sums, 2 * k, 0) for k in range(1, ROLES))
        sums = (sums + near_z) + (far_z + both_z)
    else:
        sums = all_sum(squares)
        stored = mixer_update(sums)
    mixer_new, mixer_copy, mixer_grad, mixer_first_new, mixer_second_new, mixer_updated = stored
    matrix, low_line = shape(*mlp_weights.shape), shape(1, count, dtype=bf16)
    mlp_new, mlp_copy, small_new, small_copy, tensor_norms, trust_ratios = call(
        last_update_kernel, "last_update",
        [matrix, shape(*mlp_weights.shape, dtype=bf16), line, low_line, shape(2, 10), shape(1, 10)],
        ids, sums, mlp_weights, mlp_dir, small_params[None], small_dir, order=[mixer_updated],
    )
    return (
        output,
        d_x,
        mixer_grad,
        mlp_grad,
        small_grad[0],
        mixer_first_new,
        mixer_second_new,
        mlp_first_new,
        mlp_second_new,
        small_first_new[0],
        small_second_new[0],
        mixer_new,
        mlp_new,
        small_new[0],
        mixer_copy,
        mlp_copy,
        small_copy[0],
        tensor_norms,
        trust_ratios[0],
    )


def solution(mesh):
    shard = P(("seq", "batch"), None)
    shard_flat = P(("seq", "batch"))
    stream = P("batch", "seq", None)
    return jax.shard_map(
        on_device,
        mesh=mesh,
        in_specs=(
            stream, P("batch", None), stream, shard, shard, shard_flat,
            shard, shard, shard, shard, shard_flat, shard_flat,
        ),
        out_specs=(
            stream, stream, shard, shard, shard_flat, shard, shard, shard, shard, shard_flat, shard_flat,
            shard, shard, shard_flat, shard, shard, shard_flat, P(), P(),
        ),
        check_vma=False,
    )
```

```python
import functools

import jax
import jax.numpy as jnp
from jax import lax
from jax.experimental import pallas as pl
from jax.experimental.pallas import tpu as pltpu
from jax.sharding import PartitionSpec as P

D = 512
H = 1024
FF = 2048
STEP = 5
SEG = 8
ROWS = 128
PLANES = 4
HALF = PLANES * ROWS
GATES = 3
ROLES = 4
TAIL = 16
SMALL_BLOCKS = 3
Z, X, Y, CORE, SEQ, DEVICE, MIXER_ROLE, MLP_ROLE = range(8)

first_decay = 0.5
second_decay = 0.5
learn_rate = 0.25
matrix_decay = 0.01
moment_eps = 1e-06

f32 = jnp.float32
bf16 = jnp.bfloat16
AXES = ("seq", "batch")

PLANE_BITS = ((0, 0), (0, 2), (1, 0), (1, 2))


def dot_nt(a, b):
    return lax.dot_general(a, b, (((1,), (1,)), ((), ())), preferred_element_type=f32)


def dot_nn(a, b):
    return lax.dot_general(a, b, (((1,), (0,)), ((), ())), preferred_element_type=f32)


def dot_tn(a, b):
    return lax.dot_general(a, b, (((0,), (0,)), ((), ())), preferred_element_type=f32)


def exchange(value, seq_bits, batch_bits, targets=None):
    seqs, batches = lax.axis_size("seq"), lax.axis_size("batch")
    pairs = [
        (s * batches + b, (s ^ seq_bits) * batches + (b ^ batch_bits))
        for s in range(seqs)
        for b in range(batches)
        if targets is None or (s ^ seq_bits) in targets
    ]
    return lax.ppermute(value, AXES, pairs)


def unit(x):
    return lax.rsqrt(jnp.mean(x * x, axis=-1, keepdims=True) + 1e-05)


def rms_back(x, d_normed, gain):
    scale = unit(x)
    normal = x * scale
    d_unit = d_normed * gain
    mean = jnp.mean(d_unit * normal, axis=-1, keepdims=True)
    return jnp.sum(d_normed * normal, axis=0, keepdims=True), scale * (d_unit - normal * mean)


def gather_roles(slabs, held):
    for role in range(GATES):
        for q, ref in enumerate(slabs):
            held[role, pl.ds(q * ROWS, ROWS)] = ref[pl.ds(role * ROWS, ROWS), :]


def group(s, steps, j):
    return pl.ds(pl.multiple_of((s * steps + j) * SEG, SEG), SEG)


def pair(s, steps, j):
    return pl.ds(pl.multiple_of((s * steps + 2 * j) * SEG, 2 * SEG), 2 * SEG)


def segment_order(block):
    row = lax.broadcasted_iota(jnp.int32, (block, block), 0)
    position = lax.broadcasted_iota(jnp.int32, (block, block), 1)
    return jnp.where(position == (row % SEG) * (block // SEG) + row // SEG, 1.0, 0.0).astype(bf16)


def inward(ref):
    order = segment_order(ref.shape[1])
    return jnp.concatenate([dot_nn(order, ref[s]) for s in range(2)], axis=0)


def outward(ref, value):
    block = ref.shape[1]
    order = segment_order(block)
    for s in range(2):
        ref[s] = dot_tn(order, value[s * block : (s + 1) * block]).astype(bf16)


def z_of(ids_ref, k, core):
    return ids_ref[Z] ^ (jnp.where(core == 0, k, 3 - k) if k in (1, 2) else k)


def pack_kernel(ids_ref, weights_ref, got_ref, small_ref, out_ref, held, sem):
    copy = pltpu.make_async_copy(small_ref, held, sem)
    copy.start()
    out_ref[pl.ds(0, ROWS), :] = weights_ref[...]
    copy.wait()
    mine, other = held[...], got_ref[...]
    rest = jnp.zeros((1, ROWS - mine.shape[1]), f32)
    core = ids_ref[CORE]
    lines = [jnp.where(core == 0, mine, other), rest, jnp.where(core == 0, other, mine), rest]
    line = jnp.concatenate(lines + [jnp.zeros((1, D - 2 * ROWS), f32)], axis=1)
    out_ref[pl.ds(ROWS, TAIL), :] = jnp.broadcast_to(line, (TAIL, D)).astype(bf16)


def slab_kernel(ids_ref, early_ref, late_ref, *refs):
    slab_ref, lines = refs[-2:]
    lines[...] = jnp.zeros_like(lines)
    for k in range(ROLES):
        part = (early_ref, late_ref)[k // 2].at[k % 2]
        role = z_of(ids_ref, k, ids_ref[CORE])
        slab_ref[pl.ds(pl.multiple_of(role * ROWS, ROWS), ROWS), :] = part[pl.ds(0, ROWS), :]
        lines[pl.ds(role, 1), :] = part[pl.ds(ROWS, TAIL), :].astype(f32)[0:1]
    slab_ref[pl.ds(ROLES * ROWS, TAIL), :] = lines[...].astype(bf16)


def marks_kernel(ids_ref, lengths_ref, restart_ref, valid_ref):
    block = restart_ref.shape[0] // 2
    row = lax.broadcasted_iota(jnp.int32, (block, 1), 0)
    position = ids_ref[SEQ] * block + (row % SEG) * (block // SEG) + row // SEG
    for s in range(2):
        begins = jnp.zeros((block, 1), jnp.bool_)
        end = 0
        for k in range(lengths_ref.shape[1]):
            begins = begins | (position == end)
            end = end + lengths_ref[s, k]
        begins = begins | (position == end)
        restart_ref[pl.ds(s * block, block), :] = jnp.where(begins, 0.0, 1.0)
        valid_ref[pl.ds(s * block, block), :] = jnp.where(position < end, 1.0, 0.0)


def stack_kernel(first_ref, second_ref, *refs):
    out_ref = refs[-1]
    if first_ref.shape == out_ref.shape[1:]:
        out_ref[0], out_ref[1] = first_ref[...], second_ref[...]
    else:
        count = first_ref.shape[0]
        out_ref[:count], out_ref[count:] = first_ref[...], second_ref[...]


def normed_kernel(tok_ref, gain_ref, normed_ref):
    normed_ref[...] = first_norm(tok_ref, gain_ref)


def relay_kernel(bit, forward, flipped, ids_ref, group_ref, other_ref, *refs):
    late = ((ids_ref[SEQ] & bit) != 0) == forward
    mine, other = group_ref[...], other_ref[...]
    if flipped:
        quarter = HALF // 2
        at = (quarter, 0, 3 * quarter, 2 * quarter)
        other = jnp.concatenate([other[:, k : k + quarter] for k in at], axis=1)
    if bit == 1:
        decay, state = jnp.ones_like(mine[:2]), jnp.zeros_like(mine[:2])
    else:
        decay, state = refs[0][0:2, :], refs[0][2:4, :]
    state = jnp.where(late, decay * other[2:] + state, state)
    if refs[-1].shape[0] == 2:
        refs[-1][...] = state
        return
    group_out, before_out = refs[-2:]
    before_out[...] = jnp.concatenate([jnp.where(late, decay * other[:2], decay), state], axis=0)
    first, second = jnp.where(late, other, mine), jnp.where(late, mine, other)
    group_out[...] = jnp.concatenate([first[:2] * second[:2], second[:2] * first[2:] + second[2:]], axis=0)


def relay_far_kernel(forward, ids_ref, before_ref, *refs):
    terms, state_ref = refs[:ROLES], refs[-1]
    z = ids_ref[Z]
    state = jnp.zeros_like(state_ref)
    for place in range(ROLES - 1):
        source = place if forward else ROLES - 1 - place
        term = terms[0][...]
        for k in range(1, ROLES):
            term = jnp.where((z ^ source) == k, terms[k][...], term)
        earlier = (source < z) if forward else (source > z)
        state = jnp.where(earlier, term[2:] + term[:2] * state, state)
    state_ref[...] = before_ref[2:4, :] + before_ref[0:2, :] * state


def gate_shares(f, i):
    most = jnp.maximum(jnp.maximum(-f, -i), 0.0)
    one, low_f, low_i = jnp.exp(-most), jnp.exp(-f - most), jnp.exp(-i - most)
    inverse = 1.0 / ((one + low_i) + (one + low_f))
    return (one + low_i) * inverse, (one + low_f) * inverse, low_f * inverse, low_i * inverse


def first_norm(tok_ref, gain_ref):
    x = inward(tok_ref)
    return (x * unit(x) * gain_ref[...]).astype(bf16)


def unpack(count, ids_ref, slabs, by_device, flat):
    chips = [2 * (ids_ref[X] ^ (k // 2)) + (ids_ref[Y] ^ (k % 2)) for k in range(PLANES)]
    for k, ref in enumerate(slabs):
        lines = ref[pl.ds(ROLES * ROWS, TAIL), :].astype(f32)
        for z in range(ROLES):
            for core in range(2):
                row = z * 2 * PLANES + 2 * chips[k] + core
                by_device[pl.ds(row, 1), :] = lines[z : z + 1, core * ROWS : (core + 1) * ROWS]
    parts = [by_device[pl.ds(k, 8, stride=4), :] for k in range(4)]
    for k in range(3):
        cut = ROWS - (k + 1) * (ROWS - count)
        row = jnp.concatenate([parts[k][:, k * (ROWS - count) : count], parts[k + 1][:, : ROWS - cut]], axis=1)
        flat[pl.ds(k, 8, stride=3), :] = row
    rows = [flat[pl.ds(k, 1), :] for k in range(2 * PLANES)]
    yield jnp.concatenate(rows[:PLANES], axis=1)
    yield jnp.concatenate(rows[PLANES:], axis=1)
    for base in (2 * PLANES, 4 * PLANES):
        for half in range(2):
            at = [base + 2 * chips[k] + (ids_ref[CORE] ^ half) for k in range(PLANES)]
            yield jnp.concatenate([flat[pl.ds(row, 1), :] for row in at], axis=1)


def scan_halves(normed, f_bias, i_bias, rs_ref, held, both_ref, tot_ref, columns, sega_ref, segb_ref, f_ref, i_ref, c_ref):
    for role, ref in enumerate((f_ref, i_ref, c_ref)):
        ref[...] = dot_nt(normed, held[role])
    steps = normed.shape[0] // (2 * SEG)

    def step(j, carry):
        after = []
        for s in range(2):
            at = group(s, steps, j)
            keep, share, _, _ = gate_shares(f_ref[at, :] + f_bias, i_ref[at, :] + i_bias)
            a = keep * rs_ref[at, :]
            b = a * carry[s][1] + share * c_ref[at, :]
            both_ref[0, at, :] = a
            both_ref[1, at, :] = b
            after.append((a * carry[s][0], b))
        return tuple(after)

    start = (jnp.ones((SEG, HALF), f32), jnp.zeros((SEG, HALF), f32))
    ends = lax.fori_loop(0, steps, step, (start, start), unroll=steps)
    for s, (seg_a, seg_b) in enumerate(ends):
        sega_ref[pl.ds(s * SEG, SEG), :] = seg_a
        segb_ref[pl.ds(s * SEG, SEG), :] = seg_b
        tot_a, tot_b = seg_a[0:1], seg_b[0:1]
        for k in range(1, SEG):
            a = seg_a[k : k + 1]
            tot_a, tot_b = a * tot_a, a * tot_b + seg_b[k : k + 1]
        tot_ref[pl.ds(s, 1), columns] = tot_a
        tot_ref[pl.ds(2 + s, 1), columns] = tot_b


def scan_first_kernel(count, ids_ref, tok_ref, rs_ref, *refs):
    slabs, outs, scratch = refs[:PLANES], refs[PLANES:-5], refs[-5:]
    normed_ref, gain_one_ref, gain_two_ref, fo_ref, fp_ref, io_ref, ip_ref, held, both_ref, tot_ref, sega_ref, segb_ref = outs
    f_ref, i_ref, c_ref, by_device, flat = scratch
    gather_roles(slabs, held)
    small = unpack(count, ids_ref, slabs, by_device, flat)
    for ref, value in zip((gain_one_ref, gain_two_ref, fo_ref, fp_ref, io_ref, ip_ref), small, strict=True):
        ref[...] = value
    normed_ref[...] = first_norm(tok_ref, gain_one_ref)
    scan_halves(
        normed_ref[...], fo_ref[...], io_ref[...], rs_ref, held, both_ref, tot_ref, pl.ds(0, HALF),
        sega_ref, segb_ref, f_ref, i_ref, c_ref,
    )


def scan_kernel(first, normed_ref, rs_ref, fb_ref, ib_ref, *refs):
    if not first:
        earlier_ref, *refs = refs
    slabs, (held, both_ref, tot_ref, sega_ref, segb_ref, f_ref, i_ref, c_ref) = refs[:PLANES], refs[-8:]
    gather_roles(slabs, held)
    if not first:
        tot_ref[:, pl.ds(0, HALF)] = earlier_ref[...]
    scan_halves(
        normed_ref[...], fb_ref[...], ib_ref[...], rs_ref, held, both_ref, tot_ref,
        pl.ds(0 if first else HALF, HALF), sega_ref, segb_ref, f_ref, i_ref, c_ref,
    )


def dout_kernel(cot_ref, valid_ref, *refs):
    refs[-1][...] = (inward(cot_ref) * valid_ref[...]).astype(bf16)


def terms_kernel(normed_ref, fb_ref, ib_ref, held, *refs):
    share_ref, df_ref, di_ref, cand_ref, f_ref, i_ref = refs[-6:]
    normed = normed_ref[...]
    for role, ref in enumerate((f_ref, i_ref, cand_ref)):
        ref[...] = dot_nt(normed, held[role])
    f_bias, i_bias = fb_ref[...], ib_ref[...]

    def step(j, carry):
        at = pl.ds(pl.multiple_of(j * 2 * SEG, 2 * SEG), 2 * SEG)
        keep, share, slow_f, slow_i = gate_shares(f_ref[at, :] + f_bias, i_ref[at, :] + i_bias)
        share_ref[at, :] = share
        df_ref[at, :] = keep * slow_f
        di_ref[at, :] = share * slow_i
        return carry

    lax.fori_loop(0, normed.shape[0] // (2 * SEG), step, 0, unroll=8)


def states_kernel(inc_ref, tok_ref, gain_ref, both_o, both_p, sega_o, sega_p, segb_o, segb_p, *refs):
    slabs, refs = refs[: 2 * PLANES], refs[2 * PLANES :]
    states_o, states_p, low_o, low_p, resid_ref, normed_ref, held = refs
    steps = resid_ref.shape[0] // (2 * SEG)
    halves = (
        (both_o, sega_o, segb_o, states_o, low_o, 0),
        (both_p, sega_p, segb_p, states_p, low_p, HALF),
    )
    start = []
    for _, sega, segb, _, _, column in halves:
        for s in range(2):
            seg_a, seg_b = sega[pl.ds(s * SEG, SEG), :], segb[pl.ds(s * SEG, SEG), :]
            at_seg = [inc_ref[pl.ds(s, 1), pl.ds(column, HALF)]]
            for k in range(SEG - 1):
                at_seg.append(seg_a[k : k + 1] * at_seg[-1] + seg_b[k : k + 1])
            start.append(jnp.concatenate(at_seg, axis=0))

    def step(j, carry):
        after = []
        for k, (both, _, _, states, low, _) in enumerate(halves):
            for s in range(2):
                carried, two = carry[2 * k + s], []
                for q in range(2):
                    at = group(s, steps, 2 * j + q)
                    carried = both[0, at, :] * carried
                    two.append(both[1, at, :] + carried)
                    states[at, :] = two[-1]
                low[pair(s, steps, j), :] = jnp.concatenate(two, axis=0).astype(bf16)
                after.append(carried)
        return tuple(after)

    lax.fori_loop(0, steps // 2, step, tuple(start), unroll=steps // 2)
    r = inward(tok_ref)
    for q, ref in enumerate(slabs):
        held[0, pl.ds(q * ROWS, ROWS)] = ref[pl.ds(GATES * ROWS, ROWS), :]
    for low, k in zip((low_o, low_p), range(2), strict=True):
        r = r + dot_nn(low[...], held[0, pl.ds(k * HALF, HALF)])
    resid_ref[...] = r
    normed_ref[...] = (r * unit(r) * gain_ref[...]).astype(bf16)


GELU_A = 0.7978845608028654
GELU_B = 0.044715


def mlp_kernel(ids_ref, normed_ref, resid_ref, dout_ref, gain_ref, *refs):
    parts, refs = refs[:4], refs[4:]
    dresid_ref, dgain_ref, gown_ref, gnear_ref, gfar_ref, act_ref, held, dnorm_ref = refs

    def bring(at):
        for half in range(2):
            for k in range(ROLES):
                role = z_of(ids_ref, k, ids_ref[CORE] ^ half)
                held[at, half, pl.ds(role, 1)] = parts[2 * half + k // 2][k % 2, at].reshape(1, ROWS, D)

    bring(0)
    dnorm_ref[...] = jnp.zeros_like(dnorm_ref)

    normed, dout = normed_ref[...], dout_ref[...]

    def ahead(i):
        at, low = i // 2, i % 2
        if low == 1 and at + 1 < PLANES:
            bring(at + 1)
        w_up = held[at, :, low].reshape(2 * ROWS, D)
        w_down = held[at, :, low + 2].reshape(2 * ROWS, D)
        return dot_nt(normed, w_up), dot_nt(dout, w_down), w_up, w_down

    now = ahead(0)
    for i in range(2 * PLANES):
        inner, d_act, w_up, w_down = now
        if i + 1 < 2 * PLANES:
            now = ahead(i + 1)
        square = inner * inner
        curve = jnp.tanh(inner * (GELU_A + GELU_A * GELU_B * square))
        half = 0.5 + 0.5 * curve
        activated = (inner * half).astype(bf16)
        slope = half + (half - half * half) * (inner * (2.0 * GELU_A + 6.0 * GELU_A * GELU_B * square))
        d_inner = (slope * d_act).astype(bf16)
        act_ref[i] = activated
        dnorm_ref[...] += dot_nn(d_inner, w_up)
        g_up = dot_tn(d_inner, normed).astype(bf16).reshape(2, ROWS, D)
        g_down = dot_tn(activated, dout).astype(bf16).reshape(2, ROWS, D)
        q = i // 2
        for k, ref in enumerate((gown_ref.at[q], (gnear_ref, gfar_ref)[q // 2].at[q % 2])):
            ref[i % 2] = g_up[k]
            ref[i % 2 + 2] = g_down[k]
    r = resid_ref[...]
    dgain_ref[...], d_r = rms_back(r, dnorm_ref[...], gain_ref[...])
    dresid_ref[...] = dout_ref[...].astype(f32) + d_r


def back_kernel(dresid_ref, low_o, low_p, retain_o, retain_p, sega_o, sega_p, held, *refs):
    acc_o, acc_p, tot_ref, segb_o, segb_p, gown_ref, gpar_ref = refs
    steps = dresid_ref.shape[0] // (2 * SEG)
    dmix = dresid_ref[...].astype(bf16)
    for acc, k in zip((acc_o, acc_p), range(2), strict=True):
        acc[...] = dot_nt(dmix, held[0, pl.ds(k * HALF, HALF)])
    halves = ((retain_o, acc_o), (retain_p, acc_p))

    def step(n, carry):
        after = []
        for k, (retain, acc) in enumerate(halves):
            for s in range(2):
                at = group(s, steps, steps - 1 - n)
                back = acc[at, :] + carry[2 * k + s]
                acc[at, :] = back
                after.append(retain[0, at, :] * back)
        return tuple(after)

    ends = lax.fori_loop(0, steps, step, (jnp.zeros((SEG, HALF), f32),) * 4, unroll=steps)
    for k, (sega, segb) in enumerate(((sega_o, segb_o), (sega_p, segb_p))):
        for s in range(2):
            emitted = ends[2 * k + s]
            segb[pl.ds(s * SEG, SEG), :] = emitted
            seg_a = sega[pl.ds(s * SEG, SEG), :]
            tot_a, tot_b = seg_a[SEG - 1 :], emitted[SEG - 1 :]
            for q in reversed(range(SEG - 1)):
                a = seg_a[q : q + 1]
                tot_a, tot_b = a * tot_a, a * tot_b + emitted[q : q + 1]
            tot_ref[pl.ds(s, 1), pl.ds(k * HALF, HALF)] = tot_a
            tot_ref[pl.ds(2 + s, 1), pl.ds(k * HALF, HALF)] = tot_b
    for low, ref in ((low_o, gown_ref), (low_p, gpar_ref)):
        ref[...] = dot_tn(low[...], dmix).astype(bf16).reshape(PLANES, 1, ROWS, D)


def gates_kernel(
    column, arr_ref, inc_ref, acc_ref, sega_ref, segb_ref, share_ref, df_ref, di_ref, cand_ref, retain_ref, states_ref,
    rs_ref, normed_ref, order_ref, grad_ref, pf_ref, pi_ref, pc_ref, dfb_ref, dib_ref,
):
    steps = normed_ref.shape[0] // (2 * SEG)
    start, first = [], []
    for s in range(2):
        seg_a, seg_b = sega_ref[pl.ds(s * SEG, SEG), :], segb_ref[pl.ds(s * SEG, SEG), :]
        at_seg = [arr_ref[pl.ds(s, 1), pl.ds(column, HALF)]]
        for k in reversed(range(1, SEG)):
            at_seg.append(seg_a[k : k + 1] * at_seg[-1] + seg_b[k : k + 1])
        start.append(jnp.concatenate(at_seg[::-1], axis=0))
        ends = states_ref[group(s, steps, steps - 1), :]
        first.append(jnp.concatenate([inc_ref[pl.ds(s, 1), pl.ds(column, HALF)], ends[: SEG - 1]], axis=0))

    def step(n, carry):
        *carried, sum_f, sum_i = carry
        m = steps // 2 - 1 - n
        for s in range(2):
            terms = []
            for q in (1, 0):
                j = 2 * m + q
                at = group(s, steps, j)
                back = acc_ref[at, :] + carried[s]
                carried[s] = carried[s] * retain_ref[0, at, :]
                previous = states_ref[group(s, steps, jnp.maximum(j - 1, 0)), :]
                if q == 0:
                    previous = jnp.where(m == 0, first[s], previous)
                both_ways = back * (previous * rs_ref[at, :] - cand_ref[at, :])
                d_f = both_ways * df_ref[at, :]
                d_i = both_ways * di_ref[at, :]
                sum_f = sum_f + d_f
                sum_i = sum_i - d_i
                terms.append((d_f, -d_i, back * share_ref[at, :]))
            for late, early, ref in zip(*terms, (pf_ref, pi_ref, pc_ref), strict=True):
                ref[pair(s, steps, m), :] = jnp.concatenate([early, late], axis=0).astype(bf16)
        return (*carried, sum_f, sum_i)

    nothing = jnp.zeros((SEG, HALF), f32)
    *_, sum_f, sum_i = lax.fori_loop(0, steps // 2, step, (*start, nothing, nothing), unroll=steps // 2)
    dfb_ref[...] = jnp.sum(sum_f, axis=0, keepdims=True)
    dib_ref[...] = jnp.sum(sum_i, axis=0, keepdims=True)
    normed = normed_ref[...]
    for role, ref in enumerate((pf_ref, pi_ref, pc_ref)):
        grad_ref[:, role] = dot_tn(ref[...], normed).astype(bf16).reshape(PLANES, ROWS, D)


def input_terms_kernel(ids_ref, tok_ref, dgain_two_ref, dfb_o, dfb_p, dib_o, dib_p, *refs):
    terms, weights, refs = refs[: 2 * GATES], refs[2 * GATES : 2 * GATES + 2], refs[-3:]
    dnorm_ref, small_ref, rows_ref = refs
    d_normed = 0.0
    for role in range(GATES):
        for k in range(2):
            d_normed = d_normed + dot_nn(terms[k * GATES + role][...], weights[k][role])
    dnorm_ref[...] = d_normed
    x = inward(tok_ref)
    d_gain = jnp.sum(d_normed * (x * unit(x)), axis=0, keepdims=True)
    for k in range(PLANES):
        rows_ref[pl.ds(k, 1), :] = d_gain[:, k * ROWS : (k + 1) * ROWS]
        rows_ref[pl.ds(PLANES + k, 1), :] = dgain_two_ref[:, pl.ds(k * ROWS, ROWS)]
        chip = 4 * (ids_ref[X] ^ (k // 2)) + 2 * (ids_ref[Y] ^ (k % 2))
        for core, (fb, ib) in enumerate(((dfb_o, dib_o), (dfb_p, dib_p))):
            row = 2 * PLANES + chip + (ids_ref[CORE] ^ core)
            rows_ref[pl.ds(row, 1), :] = fb[:, pl.ds(k * ROWS, ROWS)]
            rows_ref[pl.ds(row + 2 * PLANES, 1), :] = ib[:, pl.ds(k * ROWS, ROWS)]
    blocks = [rows_ref[pl.ds(k * SEG, SEG), :] for k in range(SMALL_BLOCKS)] + [jnp.zeros((SEG, ROWS), f32)]
    small_ref[...] = jnp.concatenate([jnp.concatenate(blocks, axis=1), jnp.zeros((SEG, D), f32)], axis=0)


def outputs_kernel(tok_ref, gain_ref, dresid_ref, dnorm_ref, resid_ref, valid_ref, act_ref, held, order_ref, dx_ref, output_ref, done_ref):
    done_ref[...] = jnp.zeros_like(done_ref)
    _, d_x = rms_back(inward(tok_ref), dnorm_ref[...], gain_ref[...])
    outward(dx_ref, (dresid_ref[...] + d_x).astype(bf16))
    total = resid_ref[...]
    for i in range(2 * PLANES):
        total = total + dot_nn(act_ref[i], held[i // 2, :, i % 2 + 2].reshape(2 * ROWS, D))
    outward(output_ref, (total * valid_ref[...]).astype(bf16))


def out_place(core, k):
    return jnp.where(core == 0, 3 - k, k) if k in (1, 2) else k


def mlp_pair_kernel(ids_ref, own_ref, got_ref, out_ref, outgot_ref, *refs):
    for q in range(2):
        ref = refs[-1].at[q]
        ref[pl.ds(0, ROLES)] = (own_ref[2 + q].astype(f32) + got_ref[q].astype(f32)).astype(bf16)
        at = pl.ds(out_place(ids_ref[CORE], 2 + q), 1)
        ref[pl.ds(ROLES, 1)] = (out_ref[at, 0].astype(f32) + outgot_ref[at, 0].astype(f32)).astype(bf16)


def gate_pair_kernel(own_ref, got_ref, small_ref, small_got, *outs):
    small = (small_ref[...] + small_got[...]).astype(bf16)
    for k, ref in enumerate(outs[-PLANES:]):
        total = (own_ref[k].astype(f32) + got_ref[k].astype(f32)).astype(bf16)
        ref[pl.ds(0, GATES * ROWS), :] = total.reshape(GATES * ROWS, D)
        ref[pl.ds(GATES * ROWS, TAIL), :] = small


def half_sum_kernel(ids_ref, own_ref, pair_ref, out_ref, outpair_ref, got_ref, *refs):
    keep_ref, send_ref, out_keep, out_send = refs[-4:]
    z = ids_ref[Z]
    near_bit = jnp.where(ids_ref[CORE] == 0, 1, 2)
    for q in range(2):

        def total(role, q=q):
            at = pl.ds(role, 1)
            terms = own_ref[q, at].astype(f32) + pair_ref[q, at].astype(f32)
            return (terms + got_ref[q, at].astype(f32)).astype(bf16).reshape(ROWS, D)

        for k, role in enumerate((z, z ^ near_bit ^ 3)):
            keep_ref[k, q] = total(role)
            send_ref[k, q] = total(role ^ near_bit)
        at = pl.ds(out_place(ids_ref[CORE], q), 1)
        terms = out_ref[at, 0].astype(f32) + outpair_ref[at, 0].astype(f32)
        (out_keep, out_send)[q][...] = (terms + got_ref[q, pl.ds(ROLES, 1)].astype(f32)).astype(bf16).reshape(ROWS, D)


def mlp_far_kernel(keep_ref, got_ref, *refs):
    stay_ref, send_ref = refs[-2:]
    stay_ref[...] = (keep_ref[0].astype(f32) + got_ref[0].astype(f32)).astype(bf16)
    send_ref[...] = (keep_ref[1].astype(f32) + got_ref[1].astype(f32)).astype(bf16)


def mlp_last_kernel(stay_ref, got_ref, *refs):
    keep_ref, send_ref = refs[-2:]
    keep_ref[...] = stay_ref[0].astype(f32) + got_ref[0].astype(f32)
    send_ref[...] = (stay_ref[1].astype(f32) + got_ref[1].astype(f32)).astype(bf16)


def gate_plane_kernel(ids_ref, p0, p1, p2, p3, out_ref, out_got, *refs):
    z = ids_ref[Z]
    keep_ref, s1_ref, s2_ref, s3_ref = refs[-4:]

    def total(at):
        terms = [ref[at, :].astype(f32) for ref in (p0, p1, p2, p3)]
        return (terms[0] + terms[1]) + (terms[2] + terms[3])

    def of_role(role):
        at = pl.ds(pl.multiple_of(jnp.minimum(role, GATES - 1) * ROWS, ROWS), ROWS)
        return jnp.where(role == GATES, out_ref[...].astype(f32) + out_got[...].astype(f32), total(at))

    small = total(pl.ds(GATES * ROWS, TAIL))
    keep_ref[pl.ds(0, ROWS), :] = of_role(z)
    keep_ref[pl.ds(ROWS, TAIL), :] = small
    for k, ref in enumerate((s1_ref, s2_ref, s3_ref)):
        ref[pl.ds(0, ROWS), :] = of_role(z ^ (k + 1)).astype(bf16)
        ref[pl.ds(ROWS, TAIL), :] = small.astype(bf16)


def joined(at, keep_ref, gots):
    total = keep_ref[at, :]
    for ref in gots:
        total = total + ref[at, :].astype(f32)
    return total


def matrix_step(at, keep_ref, gots, weight_ref, first_ref, second_ref, outs):
    grad_ref, first_out, second_out, dir_ref = outs
    weight = weight_ref[...]
    gradient = joined(at, keep_ref, gots)
    grad_ref[...] = gradient
    first_out[...], second_out[...], direction = moments(
        weight, gradient, first_ref[...], second_ref[...], matrix_decay
    )
    dir_ref[...] = direction
    return weight, direction


def square_rows(value):
    square = jnp.sum((value * value).reshape(-1, SEG, D), axis=0)
    return (square[:, :128] + square[:, 128:256]) + (square[:, 256:384] + square[:, 384:])


def moments_kernel(keep_ref, got_ref, weight_ref, first_ref, second_ref, *outs):
    *outs, wsum_ref, dsum_ref = outs
    weight, direction = matrix_step(
        pl.ds(0, weight_ref.shape[0]), keep_ref, [got_ref], weight_ref, first_ref, second_ref, outs
    )
    wsum_ref[...] = square_rows(weight)
    dsum_ref[...] = square_rows(direction)


def finish_kernel(
    ids_ref, keep_ref, g1_ref, g2_ref, g3_ref, wsum_f, dsum_f,
    mixer_ref, mixer_first, mixer_second, weight_ref, first_ref, second_ref,
    mixer_grad, mixer_first_out, mixer_second_out, mixer_dir, grad_ref, first_out, second_out, dir_ref, squares_ref,
    rows_ref,
):
    gots = (g1_ref, g2_ref, g3_ref)
    mixer_rows = mixer_ref.shape[0]
    mixer_values = matrix_step(
        pl.ds(0, mixer_rows), keep_ref, gots, mixer_ref, mixer_first, mixer_second,
        (mixer_grad, mixer_first_out, mixer_second_out, mixer_dir),
    )
    total = joined(pl.ds(mixer_rows, TAIL), keep_ref, gots)
    rows_ref[...] = jnp.zeros_like(rows_ref)
    for k in range(SMALL_BLOCKS):
        rows_ref[pl.ds(k * SEG, SEG), :] = total[:SEG, k * ROWS : (k + 1) * ROWS]
    weight = weight_ref[...]
    count = weight.shape[1]
    start = ids_ref[DEVICE] * count
    row, lane = start // ROWS, start % ROWS
    two = jnp.concatenate([rows_ref[pl.ds(row, 1), :], rows_ref[pl.ds(row + 1, 1), :]], axis=1)
    two = jnp.broadcast_to(two, (SEG, 2 * ROWS))
    gradient = pltpu.roll(two, (2 * ROWS - lane) % (2 * ROWS), 1)[:1, :count]
    grad_ref[...] = gradient
    first_out[...], second_out[...], direction = moments(weight, gradient, first_ref[...], second_ref[...], 0.0)
    dir_ref[...] = direction
    place = start + lax.broadcasted_iota(jnp.int32, (1, count), 1)
    at = lax.broadcasted_iota(jnp.int32, (1, ROWS), 1)
    bounds = (0, D, 2 * D, 2 * D + H, 2 * D + 2 * H)
    lines = []
    for mixer_value, mlp_sum, value in zip(mixer_values, (wsum_f, dsum_f), (weight, direction), strict=True):
        line = jnp.where(at == ids_ref[MIXER_ROLE], jnp.sum(square_rows(mixer_value), keepdims=True), 0.0)
        line = line + jnp.where(at == ROLES + ids_ref[MLP_ROLE], jnp.sum(mlp_sum[...], keepdims=True), 0.0)
        for k in range(4):
            inside = (place >= bounds[k]) & (place < bounds[k + 1])
            part = jnp.sum(jnp.where(inside, value * value, 0.0), axis=1, keepdims=True)
            line = line + jnp.where(at == ROLES + 2 + k, part, 0.0)
        lines.append(line)
    squares_ref[...] = jnp.concatenate(lines + [jnp.zeros((SEG - 2, ROWS), f32)], axis=0)


def ratio_of(squares_ref, tensor):
    norms = jnp.sqrt(squares_ref[0:2, :])
    ratios = norms[0:1] / (norms[1:2] + 1e-06)
    at = lax.broadcasted_iota(jnp.int32, (1, ROWS), 1)
    return jnp.sum(jnp.where(at == tensor, ratios, 0.0), axis=1, keepdims=True)


def new_weights(ratio, weight_ref, dir_ref, new_ref, copy_ref):
    value = weight_ref[...] - learn_rate * ratio * dir_ref[...]
    new_ref[...] = value
    copy_ref[...] = value.astype(bf16)


def mixer_update_kernel(ids_ref, squares_ref, weight_ref, dir_ref, *refs):
    ins, (new_ref, copy_ref, *outs, done_ref) = refs[:6], refs[6:]
    done_ref[...] = jnp.zeros_like(done_ref)
    new_weights(ratio_of(squares_ref, ids_ref[MIXER_ROLE]), weight_ref, dir_ref, new_ref, copy_ref)
    for ref, out in zip(ins, outs, strict=True):
        out[...] = ref[...]


def last_update_kernel(
    ids_ref, squares_ref, mlp_ref, mlp_dir, weight_ref, dir_ref, order_ref,
    mlp_new, mlp_copy, new_ref, copy_ref, norms_ref, ratios_ref,
):
    norms = jnp.sqrt(squares_ref[0:2, :])
    ratios = norms[0:1] / (norms[1:2] + 1e-06)
    norms_ref[...] = norms[:, : norms_ref.shape[1]]
    ratios_ref[...] = ratios[:, : ratios_ref.shape[1]]
    new_weights(ratio_of(squares_ref, ROLES + ids_ref[MLP_ROLE]), mlp_ref, mlp_dir, mlp_new, mlp_copy)
    count = weight_ref.shape[1]
    place = ids_ref[DEVICE] * count + lax.broadcasted_iota(jnp.int32, (1, count), 1)
    first, second, third, fourth = (ratio_of(squares_ref, ROLES + 2 + k) for k in range(4))
    ratio = jnp.where(
        place < 2 * D, jnp.where(place < D, first, second), jnp.where(place < 2 * D + H, third, fourth)
    )
    new_weights(ratio, weight_ref, dir_ref, new_ref, copy_ref)


SMEM = pl.BlockSpec(memory_space=pltpu.SMEM)
ANY = pl.BlockSpec(memory_space=pl.ANY)
VMEM = pl.BlockSpec(memory_space=pltpu.VMEM)


def shape(*dims, dtype=f32):
    return jax.ShapeDtypeStruct(dims, dtype)


def near(*dims, dtype=f32):
    return pltpu.VMEM(dims, dtype)


def kept(value):
    return pltpu.with_memory_space_constraint(value, pltpu.VMEM)


def away(value):
    return pltpu.with_memory_space_constraint(value, pltpu.HBM)


def call(kernel, name, out_shape, *args, order=(), far=(), scratch=(), mib=8):
    in_specs = [SMEM if arg.dtype == jnp.int32 else VMEM for arg in args] + [ANY] * (len(far) + len(order))
    return pl.pallas_call(
        kernel,
        in_specs=in_specs,
        out_specs=jax.tree.map(lambda _: VMEM, out_shape),
        out_shape=out_shape,
        scratch_shapes=list(scratch),
        compiler_params=pltpu.CompilerParams(vmem_limit_bytes=mib * 1024 * 1024),
        name=name,
    )(*[arg if arg.dtype == jnp.int32 else kept(arg) for arg in args], *[away(arg) for arg in far], *order)


def exchange_lane(value, second):
    seqs, batches = lax.axis_size("seq"), lax.axis_size("batch")
    pairs = []
    for s in range(seqs):
        for b in range(batches):
            over_x = (b % 2 == 0) != second
            pairs.append((s * batches + b, (s ^ 1) * batches + b if over_x else s * batches + (b ^ 2)))
    return lax.ppermute(value, AXES, pairs)


def exchange_z_lane(value, second):
    seqs, batches = lax.axis_size("seq"), lax.axis_size("batch")
    pairs = []
    for s in range(seqs):
        for b in range(batches):
            bit = 2 if (b % 2 == 0) != second else 4
            pairs.append((s * batches + b, (s ^ bit) * batches + b))
    return lax.ppermute(value, AXES, pairs)


def after(value, *others):
    return lax.optimization_barrier((value, *others))[0]


def over_z(shard):
    return [shard] + [exchange(shard, 2 * k, 0) for k in range(1, 4)]


def z_terms(sends):
    return [exchange(sent, 2 * (k + 1), 0) for k, sent in enumerate(sends)]


def all_sum(value):
    seqs, batches = lax.axis_size("seq"), lax.axis_size("batch")
    bit = 1
    while bit < batches:
        value = value + exchange(value, 0, bit)
        bit *= 2
    bit = 1
    while bit < seqs:
        value = value + exchange(value, bit, 0)
        bit *= 2
    return value


def relay(ids, total, forward, flipped, beside, hold=()):
    group, before, bit = total, [], 1
    joint = near(4, H)
    if flipped:
        other = exchange(group, 1, 0)
        order = beside[1](group) if 1 in beside else []
        pair, before = call(
            functools.partial(relay_kernel, 1, forward, True), "relay_near", [joint, joint], ids, group, other, order=order
        )
        others = [exchange(pair, 2 * k, 0) for k in range(1, ROLES)]
        order = beside[2](pair) if 2 in beside else []
        return call(
            functools.partial(relay_far_kernel, forward), "relay_far", near(2, H), ids, before, pair, *others, order=order
        )
    while bit < lax.axis_size("seq"):
        last = 2 * bit == lax.axis_size("seq")
        other = exchange(group, bit, 0)
        order = beside[bit](group) if bit in beside else []
        got = call(
            functools.partial(relay_kernel, bit, forward, flipped and bit == 1),
            f"relay_{bit}", near(2, H) if last else [joint, joint],
            ids, group, other, *before, *hold, order=order,
        )
        if not last:
            group, before = got[0], [got[1]]
        bit *= 2
    return got


def flip_by(value, axis, bit):
    return jnp.where(bit == 1, jnp.flip(value, axis), value)


def moments(weight, gradient, first_moment, second, decay_rate):
    first_new = first_decay * first_moment + (1.0 - first_decay) * gradient
    second_new = second_decay * second + (1.0 - second_decay) * gradient * gradient
    direction = (
        first_new
        / (1.0 - first_decay**STEP)
        / (jnp.sqrt(second_new / (1.0 - second_decay**STEP)) + moment_eps)
        + decay_rate * weight
    )
    return (first_new, second_new, direction)


def on_device(
    tokens, doc_lengths, cotangent, mixer_weights, mlp_weights, small_params,
    mixer_first, mixer_second, mlp_first, mlp_second, small_first, small_second,
):
    seqs, batches = lax.axis_size("seq"), lax.axis_size("batch")
    seq_at, batch_at = lax.axis_index("seq"), lax.axis_index("batch")
    device = seq_at * batches + batch_at
    streams, block, _ = tokens.shape
    rows = streams * block
    direct = (seqs, batches) == (8, 4)
    if direct:
        z, x, y, c = seq_at // 2, seq_at % 2, batch_at // 2, batch_at % 2
    else:
        z = x = y = c = jnp.zeros((), jnp.int32)
    mixer_role = device * mixer_weights.shape[0] // H
    mlp_role = device * mlp_weights.shape[0] // FF
    ids = jnp.stack([z, x, y, c, seq_at, device, mixer_role, mlp_role]).astype(jnp.int32)

    slab = shape(ROLES, ROWS, D, dtype=bf16)
    if direct:
        pair_of = near(2, ROWS, D, dtype=bf16)
        count = small_params.shape[0]
        packed = call(
            pack_kernel, "mixer_pack", near(ROWS + TAIL, D, dtype=bf16),
            ids, mixer_weights.astype(bf16), exchange(small_params, 0, 1)[None], far=[small_params[None]],
            scratch=[pltpu.VMEM((1, count), f32), pltpu.SemaphoreType.DMA(())],
        )
        mixer_two = call(
            stack_kernel, "mixer_pair", near(2, ROWS + TAIL, D, dtype=bf16), packed, exchange_z_lane(packed, False)
        )
        mixer_far = exchange_z_lane(mixer_two, True)
        mlp_low = after(mlp_weights, packed).astype(bf16)
        mlp_two = call(stack_kernel, "mlp_pair", pair_of, mlp_low, exchange_lane(mlp_low, False))
        mlp_plane = call(stack_kernel, "mlp_plane", slab, mlp_two, exchange_lane(mlp_two, True))
        gate_slab = call(
            slab_kernel, "mixer_slab", shape(ROLES * ROWS + TAIL, D, dtype=bf16),
            ids, mixer_two, mixer_far, order=[mlp_plane], scratch=[pltpu.VMEM((TAIL, D), f32)],
        )
        mixer_own = [gate_slab] + [exchange(gate_slab, *bits) for bits in PLANE_BITS[1:]]
        mlp_plane = after(mlp_plane, gate_slab)
        mlp_early = call(
            stack_kernel, "mlp_early", shape(2, PLANES, ROWS, D, dtype=bf16), mlp_plane, exchange_z_lane(mlp_plane, False)
        )
        mlp_late = exchange_z_lane(mlp_early, True)
    else:
        small_used = lax.all_gather(small_params.astype(bf16), AXES, axis=0, tiled=True).astype(f32)

        def gathered(shard):
            full = lax.all_gather(shard.astype(bf16), AXES, axis=0, tiled=True)
            return full.reshape(ROLES, PLANES, 2, ROWS, D)

        full = gathered(mixer_weights)
        mixer_own, mixer_par = [[full[:, p, k].reshape(ROLES * ROWS, D) for p in range(PLANES)] for k in range(2)]
        full = gathered(mlp_weights)
        orders = (jnp.array([0, 1, 2, 3]), jnp.array([0, 2, 1, 3]))
        mlp_parts = [full[orders[k], :, k][at] for k in range(2) for at in (slice(0, 2), slice(2, 4))]

    restart, valid = call(marks_kernel, "marks", [shape(rows, 1), shape(rows, 1)], ids, doc_lengths)
    d_out = call(dout_kernel, "d_out", near(rows, D, dtype=bf16), cotangent, valid)

    wide = near(rows, HALF)
    natural = shape(streams, block, D, dtype=bf16)
    low_wide = near(rows, HALF, dtype=bf16)
    low_rows = near(rows, D, dtype=bf16)
    ends = near(2 * SEG, HALF)
    projections = [pltpu.VMEM((rows, HALF), f32)] * 3

    if direct:
        mixer_own = [gate_slab, *after(tuple(mixer_own[1:]), mlp_early, restart, d_out)]
        mixer_par = [exchange(part, 0, 1) for part in mixer_own]
    wide_two, gate_weights = near(2, rows, HALF), near(GATES, HALF, D, dtype=bf16)
    if direct:
        normed, gain_one, gain_two, fb_o, fb_p, ib_o, ib_p, weights_o, both_o, tot_o, sega_o, segb_o = call(
            lambda *refs: scan_first_kernel(count, *refs), "scan_own",
            [low_rows] + [near(1, D)] * 2 + [near(1, HALF)] * 4 + [gate_weights, wide_two, near(4, HALF), ends, ends],
            ids, tokens, restart, *mixer_own,
            scratch=projections + [pltpu.VMEM((4 * SEG, ROWS), f32), pltpu.VMEM((3 * SEG, ROWS), f32)],
        )
    else:
        gain_one, gain_two = small_used[:D][None], small_used[D : 2 * D][None]
        biases = small_used[2 * D :].reshape(2, PLANES, 2, ROWS).transpose(0, 2, 1, 3).reshape(4, 1, HALF)
        fb_o, fb_p, ib_o, ib_p = [biases[k] for k in range(4)]
        normed = call(normed_kernel, "first_norm", low_rows, tokens, gain_one)
        weights_o, both_o, tot_o, sega_o, segb_o = call(
            lambda *refs: scan_kernel(True, *refs), "scan_own", [gate_weights, wide_two, near(4, HALF), ends, ends],
            normed, restart, fb_o, ib_o, *mixer_own, scratch=projections,
        )
    weights_p, both_p, tot, sega_p, segb_p = call(
        lambda *refs: scan_kernel(False, *refs), "scan_other", [gate_weights, wide_two, near(4, H), ends, ends],
        normed, restart, fb_p, ib_p, tot_o, *mixer_par, scratch=projections,
    )

    kept_terms = {}

    def terms_own(ready):
        kept_terms["own"] = call(
            terms_kernel, "terms_own", [wide] * 4,
            normed, fb_o, ib_o, weights_o, order=[ready], scratch=projections[:2],
        )
        return [kept_terms["own"][0]]

    def terms_other(ready):
        kept_terms["other"] = call(
            terms_kernel, "terms_other", [wide] * 4,
            normed, fb_p, ib_p, weights_p, order=[ready], scratch=projections[:2],
        )
        return [kept_terms["other"][0]]

    incoming = relay(ids, tot, True, direct, {1: terms_own, 2: terms_other})
    if direct:
        mlp_late = after(mlp_late, incoming)
        mlp_parts = [mlp_early, mlp_late, exchange(mlp_early, 0, 1), exchange(mlp_late, 0, 1)]

    states_o, states_p, low_o, low_p, resid, normed_two, out_weights = call(
        states_kernel, "states",
        [wide, wide, low_wide, low_wide, near(rows, D), low_rows, near(1, H, D, dtype=bf16)],
        incoming, tokens, gain_two, both_o, both_p, sega_o, sega_p, segb_o, segb_p,
        *mixer_own, *mixer_par,
    )

    terms, half_terms_two = near(PLANES, ROLES, ROWS, D, dtype=bf16), near(2, ROLES, ROWS, D, dtype=bf16)
    d_resid, d_gain_two, mlp_gown, mlp_gnear, mlp_gfar, mlp_act, mlp_held = call(
        mlp_kernel, "mlp",
        [
            near(rows, D), near(1, D), terms, half_terms_two, half_terms_two, near(2 * PLANES, rows, 2 * ROWS, dtype=bf16),
            near(PLANES, 2, ROLES, ROWS, D, dtype=bf16),
        ],
        ids, normed_two, resid, d_out, gain_two, *mlp_parts, mib=16, scratch=[pltpu.VMEM((rows, D), f32)],
    )

    half_terms = near(PLANES, 1, ROWS, D, dtype=bf16)
    back_o, back_p, tot_back, bseg_o, bseg_p, out_gown, out_gpar = call(
        back_kernel, "back_scan", [wide, wide, near(4, H), ends, ends, half_terms, half_terms],
        d_resid, low_o, low_p, both_o, both_p, sega_o, sega_p, out_weights,
    )

    beside = {}
    if direct:
        mlp_got_far, out_got = exchange(mlp_gfar, 0, 1), exchange(out_gpar, 0, 1)
        mlp_got = exchange(after(mlp_gnear, tot_back), 0, 1)
        two_fives = near(2, ROLES + 1, ROWS, D, dtype=bf16)

        def mlp_pair(ready):
            kept_terms["mlp"] = call(
                mlp_pair_kernel, "mlp_pair_sum", two_fives, ids, mlp_gown, mlp_got_far, out_gown, out_got,
                order=[ready],
            )
            return [kept_terms["mlp"]]

        def mark_pair(ready):
            kept_terms["pair"] = ready
            return []

        beside = {1: mlp_pair, 2: mark_pair}

    arriving = relay(ids, tot_back, False, direct, beside)
    terms_o, terms_p = kept_terms["own"], kept_terms["other"]
    if direct:
        mlp_round = exchange_lane(after(kept_terms["mlp"], kept_terms["pair"]), True)

    def gates_back(column, back, sega, bseg, share, df, di, cand, retain, states, order, name):
        return call(
            lambda *refs: gates_kernel(column, *refs), name,
            [near(PLANES, GATES, ROWS, D, dtype=bf16), low_wide, low_wide, low_wide, near(1, HALF), near(1, HALF)],
            arriving, incoming, back, sega, bseg, share, df, di, cand, retain, states, restart, normed, order=order,
        )

    gate_gpar, pf_p, pi_p, pc_p, dfb_p, dib_p = gates_back(
        HALF, back_p, sega_p, bseg_p, *terms_p, both_p, states_p, [tot_back], "gates_other"
    )
    gate_gown, pf_o, pi_o, pc_o, dfb_o, dib_o = gates_back(
        0, back_o, sega_o, bseg_o, *terms_o, both_o, states_o, [dfb_p], "gates_own"
    )

    d_normed, small_terms = call(
        input_terms_kernel, "input_terms", [near(rows, D), near(TAIL, D)],
        ids, tokens, d_gain_two, dfb_o, dfb_p, dib_o, dib_p,
        pf_o, pi_o, pc_o, pf_p, pi_p, pc_p, weights_o, weights_p, order=[dfb_o],
        scratch=[pltpu.VMEM((3 * SEG, ROWS), f32)],
    )

    def token_outputs(ready):
        return call(
            outputs_kernel, "outputs", [natural, natural, near(SEG, ROWS)],
            tokens, gain_one, d_resid, d_normed, resid, valid, mlp_act, mlp_held, order=[ready],
        )

    def with_moments(keep, got, weight, first_moment, second, name):
        count = weight.shape[0]
        return call(
            moments_kernel, name, [shape(count, D)] * 3 + [near(count, D)] + [near(SEG, 128)] * 2,
            keep, got, weight, first_moment, second,
        )

    if direct:
        shard, low_shard = near(ROWS, D), near(ROWS, D, dtype=bf16)
        long, low_long = near(ROWS + TAIL, D), near(ROWS + TAIL, D, dtype=bf16)
        quarter, low_shard = near(2, 2, ROWS, D, dtype=bf16), near(ROWS, D, dtype=bf16)
        small_got = exchange(small_terms, 0, 1)
        mlp_keep, mlp_send, out_keep, out_send = call(
            half_sum_kernel, "mlp_half_sum", [quarter, quarter, low_shard, low_shard], ids,
            mlp_gown, mlp_got, out_gown, out_got, mlp_round, order=[small_got],
        )
        gate_parts = call(
            gate_pair_kernel, "gate_pair_sum", [near(GATES * ROWS + TAIL, D, dtype=bf16)] * PLANES,
            gate_gown, exchange(gate_gpar, 0, 1), small_terms, small_got, order=[out_keep],
        )
        gate_round = [gate_parts[0]] + [
            exchange(part, *bits) for part, bits in zip(gate_parts[1:], PLANE_BITS[1:], strict=True)
        ]
        d_x, output, x_done = token_outputs(gate_parts[0])
        out_got = exchange_lane(out_send, False)
        two = near(2, ROWS, D, dtype=bf16)
        mlp_stay, mlp_send = call(
            mlp_far_kernel, "mlp_z_sum", [two, two], mlp_keep, exchange_z_lane(mlp_send, False)
        )
        mlp_stay, mlp_send = call(
            mlp_last_kernel, "mlp_z_last", [shard, low_shard], mlp_stay, exchange_z_lane(mlp_send, True)
        )
        mlp_done = with_moments(
            mlp_stay, exchange_lane(mlp_send, False), mlp_weights, mlp_first, mlp_second, "mlp_moments"
        )
        gate_keep, *gate_sends = call(
            gate_plane_kernel, "gate_plane_sum", [long] + [low_long] * 3, ids, *gate_round, out_keep, out_got,
            order=[x_done],
        )
        gate_got = z_terms(gate_sends)
    else:

        def scattered(own, par):
            full_terms = jnp.stack([own, par]).transpose(2, 1, 0, 3, 4).reshape(-1, D)
            return lax.psum_scatter(full_terms.astype(f32), AXES, scatter_dimension=0, tiled=True)

        d_x, output, _ = token_outputs(small_terms)
        mlp_grad = scattered(mlp_gown, jnp.concatenate([mlp_gnear, mlp_gfar], axis=0))
        mixer_grad = scattered(
            jnp.concatenate([gate_gown, out_gown], axis=1), jnp.concatenate([gate_gpar, out_gpar], axis=1)
        )
        none = jnp.zeros_like(mlp_grad, dtype=bf16)
        mlp_done = with_moments(mlp_grad, none, mlp_weights, mlp_first, mlp_second, "mlp_moments")
        gate_keep = jnp.concatenate([mixer_grad, lax.psum(small_terms, AXES)], axis=0)
        gate_got = [jnp.zeros_like(gate_keep, dtype=bf16)] * 3
    mlp_grad, mlp_first_new, mlp_second_new, mlp_dir, mlp_wsum, mlp_dsum = mlp_done
    count, mixer_count = small_params.shape[0], mixer_weights.shape[0]
    line, matrix = shape(1, count), shape(mixer_count, D)
    mixer_grad, mixer_first_new, mixer_second_new, mixer_dir, small_grad, small_first_new, small_second_new, small_dir, squares = call(
        finish_kernel, "finish", [near(mixer_count, D)] * 4 + [near(1, count)] * 4 + [near(SEG, ROWS)],
        ids, gate_keep, *gate_got, mlp_wsum, mlp_dsum, mixer_weights, mixer_first, mixer_second,
        small_params[None], small_first[None], small_second[None], scratch=[pltpu.VMEM((4 * SEG, ROWS), f32)],
    )

    def mixer_update(sums):
        matrix = shape(mixer_count, D)
        return call(
            mixer_update_kernel, "mixer_update", [matrix, shape(mixer_count, D, dtype=bf16)] + [matrix] * 3 + [line] * 3 + [near(SEG, ROWS)],
            ids, sums, mixer_weights, mixer_dir, mixer_grad, mixer_first_new, mixer_second_new,
            small_grad, small_first_new, small_second_new,
        )

    if direct:
        sums = squares + exchange(squares, 0, 1)
        over_y, over_x, over_both = (exchange(sums, *bits) for bits in PLANE_BITS[1:])
        sums = (sums + over_y) + (over_x + over_both)
        stored = mixer_update(sums)
        near_z, far_z, both_z = (exchange(sums, 2 * k, 0) for k in range(1, ROLES))
        sums = (sums + near_z) + (far_z + both_z)
    else:
        sums = all_sum(squares)
        stored = mixer_update(sums)
    mixer_new, mixer_copy, mixer_grad, mixer_first_new, mixer_second_new, *stored = stored
    small_grad, small_first_new, small_second_new, mixer_updated = stored
    matrix, low_line = shape(*mlp_weights.shape), shape(1, count, dtype=bf16)
    mlp_new, mlp_copy, small_new, small_copy, tensor_norms, trust_ratios = call(
        last_update_kernel, "last_update",
        [matrix, shape(*mlp_weights.shape, dtype=bf16), line, low_line, shape(2, 10), shape(1, 10)],
        ids, sums, mlp_weights, mlp_dir, small_params[None], small_dir, order=[mixer_updated],
    )
    return (
        output,
        d_x,
        mixer_grad,
        mlp_grad,
        small_grad[0],
        mixer_first_new,
        mixer_second_new,
        mlp_first_new,
        mlp_second_new,
        small_first_new[0],
        small_second_new[0],
        mixer_new,
        mlp_new,
        small_new[0],
        mixer_copy,
        mlp_copy,
        small_copy[0],
        tensor_norms,
        trust_ratios[0],
    )


def solution(mesh):
    shard = P(("seq", "batch"), None)
    shard_flat = P(("seq", "batch"))
    stream = P("batch", "seq", None)
    return jax.shard_map(
        on_device,
        mesh=mesh,
        in_specs=(
            stream, P("batch", None), stream, shard, shard, shard_flat,
            shard, shard, shard, shard, shard_flat, shard_flat,
        ),
        out_specs=(
            stream, stream, shard, shard, shard_flat, shard, shard, shard, shard, shard_flat, shard_flat,
            shard, shard, shard_flat, shard, shard, shard_flat, P(), P(),
        ),
        check_vma=False,
    )
```

```python
import functools

import jax
import jax.numpy as jnp
from jax import lax
from jax.experimental import pallas as pl
from jax.experimental.pallas import tpu as pltpu
from jax.sharding import PartitionSpec as P

D = 512
H = 1024
FF = 2048
STEP = 5
SEG = 8
ROWS = 128
PLANES = 4
HALF = PLANES * ROWS
GATES = 3
ROLES = 4
TAIL = 16
SMALL_BLOCKS = 3
Z, X, Y, CORE, SEQ, DEVICE, MIXER_ROLE, MLP_ROLE = range(8)

first_decay = 0.5
second_decay = 0.5
learn_rate = 0.25
matrix_decay = 0.01
moment_eps = 1e-06

f32 = jnp.float32
bf16 = jnp.bfloat16
AXES = ("seq", "batch")

PLANE_BITS = ((0, 0), (0, 2), (1, 0), (1, 2))


def dot_nt(a, b):
    return lax.dot_general(a, b, (((1,), (1,)), ((), ())), preferred_element_type=f32)


def dot_nn(a, b):
    return lax.dot_general(a, b, (((1,), (0,)), ((), ())), preferred_element_type=f32)


def dot_tn(a, b):
    return lax.dot_general(a, b, (((0,), (0,)), ((), ())), preferred_element_type=f32)


def exchange(value, seq_bits, batch_bits, targets=None):
    seqs, batches = lax.axis_size("seq"), lax.axis_size("batch")
    pairs = [
        (s * batches + b, (s ^ seq_bits) * batches + (b ^ batch_bits))
        for s in range(seqs)
        for b in range(batches)
        if targets is None or (s ^ seq_bits) in targets
    ]
    return lax.ppermute(value, AXES, pairs)


def unit(x):
    return lax.rsqrt(jnp.mean(x * x, axis=-1, keepdims=True) + 1e-05)


def rms_back(x, d_normed, gain):
    scale = unit(x)
    normal = x * scale
    d_unit = d_normed * gain
    mean = jnp.mean(d_unit * normal, axis=-1, keepdims=True)
    return jnp.sum(d_normed * normal, axis=0, keepdims=True), scale * (d_unit - normal * mean)


def gather_roles(slabs, held):
    for role in range(GATES):
        for q, ref in enumerate(slabs):
            held[role, pl.ds(q * ROWS, ROWS)] = ref[pl.ds(role * ROWS, ROWS), :]


def group(s, steps, j):
    return pl.ds(pl.multiple_of((s * steps + j) * SEG, SEG), SEG)


def pair(s, steps, j):
    return pl.ds(pl.multiple_of((s * steps + 2 * j) * SEG, 2 * SEG), 2 * SEG)


def segment_order(block):
    row = lax.broadcasted_iota(jnp.int32, (block, block), 0)
    position = lax.broadcasted_iota(jnp.int32, (block, block), 1)
    return jnp.where(position == (row % SEG) * (block // SEG) + row // SEG, 1.0, 0.0).astype(bf16)


def inward(ref):
    order = segment_order(ref.shape[1])
    return jnp.concatenate([dot_nn(order, ref[s]) for s in range(2)], axis=0)


def outward(ref, value):
    block = ref.shape[1]
    order = segment_order(block)
    for s in range(2):
        ref[s] = dot_tn(order, value[s * block : (s + 1) * block]).astype(bf16)


def z_of(ids_ref, k, core):
    return ids_ref[Z] ^ (jnp.where(core == 0, k, 3 - k) if k in (1, 2) else k)


def pack_kernel(ids_ref, weights_ref, got_ref, small_ref, out_ref, held, sem):
    copy = pltpu.make_async_copy(small_ref, held, sem)
    copy.start()
    out_ref[pl.ds(0, ROWS), :] = weights_ref[...]
    copy.wait()
    mine, other = held[...], got_ref[...]
    rest = jnp.zeros((1, ROWS - mine.shape[1]), f32)
    core = ids_ref[CORE]
    lines = [jnp.where(core == 0, mine, other), rest, jnp.where(core == 0, other, mine), rest]
    line = jnp.concatenate(lines + [jnp.zeros((1, D - 2 * ROWS), f32)], axis=1)
    out_ref[pl.ds(ROWS, TAIL), :] = jnp.broadcast_to(line, (TAIL, D)).astype(bf16)


def slab_kernel(ids_ref, early_ref, late_ref, *refs):
    slab_ref, lines = refs[-2:]
    lines[...] = jnp.zeros_like(lines)
    for k in range(ROLES):
        part = (early_ref, late_ref)[k // 2].at[k % 2]
        role = z_of(ids_ref, k, ids_ref[CORE])
        slab_ref[pl.ds(pl.multiple_of(role * ROWS, ROWS), ROWS), :] = part[pl.ds(0, ROWS), :]
        lines[pl.ds(role, 1), :] = part[pl.ds(ROWS, TAIL), :].astype(f32)[0:1]
    slab_ref[pl.ds(ROLES * ROWS, TAIL), :] = lines[...].astype(bf16)


def marks_kernel(ids_ref, lengths_ref, restart_ref, valid_ref):
    block = restart_ref.shape[0] // 2
    row = lax.broadcasted_iota(jnp.int32, (block, 1), 0)
    position = ids_ref[SEQ] * block + (row % SEG) * (block // SEG) + row // SEG
    for s in range(2):
        begins = jnp.zeros((block, 1), jnp.bool_)
        end = 0
        for k in range(lengths_ref.shape[1]):
            begins = begins | (position == end)
            end = end + lengths_ref[s, k]
        begins = begins | (position == end)
        restart_ref[pl.ds(s * block, block), :] = jnp.where(begins, 0.0, 1.0)
        valid_ref[pl.ds(s * block, block), :] = jnp.where(position < end, 1.0, 0.0)


def stack_kernel(first_ref, second_ref, *refs):
    out_ref = refs[-1]
    if first_ref.shape == out_ref.shape[1:]:
        out_ref[0], out_ref[1] = first_ref[...], second_ref[...]
    else:
        count = first_ref.shape[0]
        out_ref[:count], out_ref[count:] = first_ref[...], second_ref[...]


def normed_kernel(tok_ref, gain_ref, normed_ref):
    normed_ref[...] = first_norm(tok_ref, gain_ref)


def relay_kernel(bit, forward, flipped, ids_ref, group_ref, other_ref, *refs):
    late = ((ids_ref[SEQ] & bit) != 0) == forward
    mine, other = group_ref[...], other_ref[...]
    if flipped:
        quarter = HALF // 2
        at = (quarter, 0, 3 * quarter, 2 * quarter)
        other = jnp.concatenate([other[:, k : k + quarter] for k in at], axis=1)
    if bit == 1:
        decay, state = jnp.ones_like(mine[:2]), jnp.zeros_like(mine[:2])
    else:
        decay, state = refs[0][0:2, :], refs[0][2:4, :]
    state = jnp.where(late, decay * other[2:] + state, state)
    if refs[-1].shape[0] == 2:
        refs[-1][...] = state
        return
    group_out, before_out = refs[-2:]
    before_out[...] = jnp.concatenate([jnp.where(late, decay * other[:2], decay), state], axis=0)
    first, second = jnp.where(late, other, mine), jnp.where(late, mine, other)
    group_out[...] = jnp.concatenate([first[:2] * second[:2], second[:2] * first[2:] + second[2:]], axis=0)


def relay_far_kernel(forward, ids_ref, before_ref, *refs):
    terms, state_ref = refs[:ROLES], refs[-1]
    z = ids_ref[Z]
    state = jnp.zeros_like(state_ref)
    for place in range(ROLES - 1):
        source = place if forward else ROLES - 1 - place
        term = terms[0][...]
        for k in range(1, ROLES):
            term = jnp.where((z ^ source) == k, terms[k][...], term)
        earlier = (source < z) if forward else (source > z)
        state = jnp.where(earlier, term[2:] + term[:2] * state, state)
    state_ref[...] = before_ref[2:4, :] + before_ref[0:2, :] * state


def gate_shares(f, i):
    most = jnp.maximum(jnp.maximum(-f, -i), 0.0)
    one, low_f, low_i = jnp.exp(-most), jnp.exp(-f - most), jnp.exp(-i - most)
    inverse = 1.0 / ((one + low_i) + (one + low_f))
    return (one + low_i) * inverse, (one + low_f) * inverse, low_f * inverse, low_i * inverse


def first_norm(tok_ref, gain_ref):
    x = inward(tok_ref)
    return (x * unit(x) * gain_ref[...]).astype(bf16)


def unpack(count, ids_ref, slabs, by_device, flat):
    chips = [2 * (ids_ref[X] ^ (k // 2)) + (ids_ref[Y] ^ (k % 2)) for k in range(PLANES)]
    for k, ref in enumerate(slabs):
        lines = ref[pl.ds(ROLES * ROWS, TAIL), :].astype(f32)
        for z in range(ROLES):
            for core in range(2):
                row = z * 2 * PLANES + 2 * chips[k] + core
                by_device[pl.ds(row, 1), :] = lines[z : z + 1, core * ROWS : (core + 1) * ROWS]
    parts = [by_device[pl.ds(k, 8, stride=4), :] for k in range(4)]
    for k in range(3):
        cut = ROWS - (k + 1) * (ROWS - count)
        row = jnp.concatenate([parts[k][:, k * (ROWS - count) : count], parts[k + 1][:, : ROWS - cut]], axis=1)
        flat[pl.ds(k, 8, stride=3), :] = row
    rows = [flat[pl.ds(k, 1), :] for k in range(2 * PLANES)]
    yield jnp.concatenate(rows[:PLANES], axis=1)
    yield jnp.concatenate(rows[PLANES:], axis=1)
    for base in (2 * PLANES, 4 * PLANES):
        for half in range(2):
            at = [base + 2 * chips[k] + (ids_ref[CORE] ^ half) for k in range(PLANES)]
            yield jnp.concatenate([flat[pl.ds(row, 1), :] for row in at], axis=1)


def scan_halves(normed, f_bias, i_bias, rs_ref, held, both_ref, tot_ref, columns, sega_ref, segb_ref, f_ref, i_ref, c_ref):
    for role, ref in enumerate((f_ref, i_ref, c_ref)):
        ref[...] = dot_nt(normed, held[role])
    steps = normed.shape[0] // (2 * SEG)

    def step(j, carry):
        after = []
        for s in range(2):
            at = group(s, steps, j)
            keep, share, _, _ = gate_shares(f_ref[at, :] + f_bias, i_ref[at, :] + i_bias)
            a = keep * rs_ref[at, :]
            b = a * carry[s][1] + share * c_ref[at, :]
            both_ref[0, at, :] = a
            both_ref[1, at, :] = b
            after.append((a * carry[s][0], b))
        return tuple(after)

    start = (jnp.ones((SEG, HALF), f32), jnp.zeros((SEG, HALF), f32))
    ends = lax.fori_loop(0, steps, step, (start, start), unroll=steps)
    for s, (seg_a, seg_b) in enumerate(ends):
        sega_ref[pl.ds(s * SEG, SEG), :] = seg_a
        segb_ref[pl.ds(s * SEG, SEG), :] = seg_b
        tot_a, tot_b = seg_a[0:1], seg_b[0:1]
        for k in range(1, SEG):
            a = seg_a[k : k + 1]
            tot_a, tot_b = a * tot_a, a * tot_b + seg_b[k : k + 1]
        tot_ref[pl.ds(s, 1), columns] = tot_a
        tot_ref[pl.ds(2 + s, 1), columns] = tot_b


def scan_first_kernel(count, ids_ref, tok_ref, rs_ref, *refs):
    slabs, outs, scratch = refs[:PLANES], refs[PLANES:-5], refs[-5:]
    normed_ref, gain_one_ref, gain_two_ref, fo_ref, fp_ref, io_ref, ip_ref, held, both_ref, tot_ref, sega_ref, segb_ref = outs
    f_ref, i_ref, c_ref, by_device, flat = scratch
    gather_roles(slabs, held)
    small = unpack(count, ids_ref, slabs, by_device, flat)
    for ref, value in zip((gain_one_ref, gain_two_ref, fo_ref, fp_ref, io_ref, ip_ref), small, strict=True):
        ref[...] = value
    normed_ref[...] = first_norm(tok_ref, gain_one_ref)
    scan_halves(
        normed_ref[...], fo_ref[...], io_ref[...], rs_ref, held, both_ref, tot_ref, pl.ds(0, HALF),
        sega_ref, segb_ref, f_ref, i_ref, c_ref,
    )


def scan_kernel(first, normed_ref, rs_ref, fb_ref, ib_ref, *refs):
    if not first:
        earlier_ref, *refs = refs
    slabs, (held, both_ref, tot_ref, sega_ref, segb_ref, f_ref, i_ref, c_ref) = refs[:PLANES], refs[-8:]
    gather_roles(slabs, held)
    if not first:
        tot_ref[:, pl.ds(0, HALF)] = earlier_ref[...]
    scan_halves(
        normed_ref[...], fb_ref[...], ib_ref[...], rs_ref, held, both_ref, tot_ref,
        pl.ds(0 if first else HALF, HALF), sega_ref, segb_ref, f_ref, i_ref, c_ref,
    )


def dout_kernel(cot_ref, valid_ref, *refs):
    refs[-1][...] = (inward(cot_ref) * valid_ref[...]).astype(bf16)


def terms_kernel(normed_ref, fb_ref, ib_ref, held, *refs):
    share_ref, df_ref, di_ref, cand_ref, f_ref, i_ref = refs[-6:]
    normed = normed_ref[...]
    for role, ref in enumerate((f_ref, i_ref, cand_ref)):
        ref[...] = dot_nt(normed, held[role])
    f_bias, i_bias = fb_ref[...], ib_ref[...]

    def step(j, carry):
        at = pl.ds(pl.multiple_of(j * 2 * SEG, 2 * SEG), 2 * SEG)
        keep, share, slow_f, slow_i = gate_shares(f_ref[at, :] + f_bias, i_ref[at, :] + i_bias)
        share_ref[at, :] = share
        df_ref[at, :] = keep * slow_f
        di_ref[at, :] = share * slow_i
        return carry

    lax.fori_loop(0, normed.shape[0] // (2 * SEG), step, 0, unroll=8)


def states_kernel(inc_ref, tok_ref, gain_ref, both_o, both_p, sega_o, sega_p, segb_o, segb_p, *refs):
    slabs, refs = refs[: 2 * PLANES], refs[2 * PLANES :]
    states_o, states_p, low_o, low_p, resid_ref, normed_ref, held = refs
    steps = resid_ref.shape[0] // (2 * SEG)
    halves = (
        (both_o, sega_o, segb_o, states_o, low_o, 0),
        (both_p, sega_p, segb_p, states_p, low_p, HALF),
    )
    start = []
    for _, sega, segb, _, _, column in halves:
        for s in range(2):
            seg_a, seg_b = sega[pl.ds(s * SEG, SEG), :], segb[pl.ds(s * SEG, SEG), :]
            at_seg = [inc_ref[pl.ds(s, 1), pl.ds(column, HALF)]]
            for k in range(SEG - 1):
                at_seg.append(seg_a[k : k + 1] * at_seg[-1] + seg_b[k : k + 1])
            start.append(jnp.concatenate(at_seg, axis=0))

    def step(j, carry):
        after = []
        for k, (both, _, _, states, low, _) in enumerate(halves):
            for s in range(2):
                carried, two = carry[2 * k + s], []
                for q in range(2):
                    at = group(s, steps, 2 * j + q)
                    carried = both[0, at, :] * carried
                    two.append(both[1, at, :] + carried)
                    states[at, :] = two[-1]
                low[pair(s, steps, j), :] = jnp.concatenate(two, axis=0).astype(bf16)
                after.append(carried)
        return tuple(after)

    lax.fori_loop(0, steps // 2, step, tuple(start), unroll=steps // 2)
    r = inward(tok_ref)
    for q, ref in enumerate(slabs):
        held[0, pl.ds(q * ROWS, ROWS)] = ref[pl.ds(GATES * ROWS, ROWS), :]
    for low, k in zip((low_o, low_p), range(2), strict=True):
        r = r + dot_nn(low[...], held[0, pl.ds(k * HALF, HALF)])
    resid_ref[...] = r
    normed_ref[...] = (r * unit(r) * gain_ref[...]).astype(bf16)


GELU_A = 0.7978845608028654
GELU_B = 0.044715


def mlp_kernel(ids_ref, normed_ref, resid_ref, dout_ref, gain_ref, *refs):
    parts, refs = refs[:4], refs[4:]
    dresid_ref, dgain_ref, gown_ref, gnear_ref, gfar_ref, act_ref, held, dnorm_ref = refs

    def bring(at):
        for half in range(2):
            for k in range(ROLES):
                role = z_of(ids_ref, k, ids_ref[CORE] ^ half)
                held[at, half, pl.ds(role, 1)] = parts[2 * half + k // 2][k % 2, at].reshape(1, ROWS, D)

    bring(0)
    dnorm_ref[...] = jnp.zeros_like(dnorm_ref)

    normed, dout = normed_ref[...], dout_ref[...]

    def ahead(i):
        at, low = i // 2, i % 2
        if low == 1 and at + 1 < PLANES:
            bring(at + 1)
        w_up = held[at, :, low].reshape(2 * ROWS, D)
        w_down = held[at, :, low + 2].reshape(2 * ROWS, D)
        return dot_nt(normed, w_up), dot_nt(dout, w_down), w_up, w_down

    now = ahead(0)
    for i in range(2 * PLANES):
        inner, d_act, w_up, w_down = now
        if i + 1 < 2 * PLANES:
            now = ahead(i + 1)
        square = inner * inner
        curve = jnp.tanh(inner * (GELU_A + GELU_A * GELU_B * square))
        half = 0.5 + 0.5 * curve
        activated = (inner * half).astype(bf16)
        slope = half + (half - half * half) * (inner * (2.0 * GELU_A + 6.0 * GELU_A * GELU_B * square))
        d_inner = (slope * d_act).astype(bf16)
        act_ref[i] = activated
        dnorm_ref[...] += dot_nn(d_inner, w_up)
        g_up = dot_tn(d_inner, normed).astype(bf16).reshape(2, ROWS, D)
        g_down = dot_tn(activated, dout).astype(bf16).reshape(2, ROWS, D)
        q = i // 2
        for k, ref in enumerate((gown_ref.at[q], (gnear_ref, gfar_ref)[q // 2].at[q % 2])):
            ref[i % 2] = g_up[k]
            ref[i % 2 + 2] = g_down[k]
    r = resid_ref[...]
    dgain_ref[...], d_r = rms_back(r, dnorm_ref[...], gain_ref[...])
    dresid_ref[...] = dout_ref[...].astype(f32) + d_r


def back_kernel(dresid_ref, low_o, low_p, retain_o, retain_p, sega_o, sega_p, held, *refs):
    acc_o, acc_p, tot_ref, segb_o, segb_p, gown_ref, gpar_ref = refs
    steps = dresid_ref.shape[0] // (2 * SEG)
    dmix = dresid_ref[...].astype(bf16)
    for acc, k in zip((acc_o, acc_p), range(2), strict=True):
        acc[...] = dot_nt(dmix, held[0, pl.ds(k * HALF, HALF)])
    halves = ((retain_o, acc_o), (retain_p, acc_p))

    def step(n, carry):
        after = []
        for k, (retain, acc) in enumerate(halves):
            for s in range(2):
                at = group(s, steps, steps - 1 - n)
                back = acc[at, :] + carry[2 * k + s]
                acc[at, :] = back
                after.append(retain[0, at, :] * back)
        return tuple(after)

    ends = lax.fori_loop(0, steps, step, (jnp.zeros((SEG, HALF), f32),) * 4, unroll=steps)
    for k, (sega, segb) in enumerate(((sega_o, segb_o), (sega_p, segb_p))):
        for s in range(2):
            emitted = ends[2 * k + s]
            segb[pl.ds(s * SEG, SEG), :] = emitted
            seg_a = sega[pl.ds(s * SEG, SEG), :]
            tot_a, tot_b = seg_a[SEG - 1 :], emitted[SEG - 1 :]
            for q in reversed(range(SEG - 1)):
                a = seg_a[q : q + 1]
                tot_a, tot_b = a * tot_a, a * tot_b + emitted[q : q + 1]
            tot_ref[pl.ds(s, 1), pl.ds(k * HALF, HALF)] = tot_a
            tot_ref[pl.ds(2 + s, 1), pl.ds(k * HALF, HALF)] = tot_b
    for low, ref in ((low_o, gown_ref), (low_p, gpar_ref)):
        ref[...] = dot_tn(low[...], dmix).astype(bf16).reshape(PLANES, 1, ROWS, D)


def gates_kernel(
    column, arr_ref, inc_ref, acc_ref, sega_ref, segb_ref, share_ref, df_ref, di_ref, cand_ref, retain_ref, states_ref,
    rs_ref, normed_ref, order_ref, grad_ref, pf_ref, pi_ref, pc_ref, dfb_ref, dib_ref,
):
    steps = normed_ref.shape[0] // (2 * SEG)
    start, first = [], []
    for s in range(2):
        seg_a, seg_b = sega_ref[pl.ds(s * SEG, SEG), :], segb_ref[pl.ds(s * SEG, SEG), :]
        at_seg = [arr_ref[pl.ds(s, 1), pl.ds(column, HALF)]]
        for k in reversed(range(1, SEG)):
            at_seg.append(seg_a[k : k + 1] * at_seg[-1] + seg_b[k : k + 1])
        start.append(jnp.concatenate(at_seg[::-1], axis=0))
        ends = states_ref[group(s, steps, steps - 1), :]
        first.append(jnp.concatenate([inc_ref[pl.ds(s, 1), pl.ds(column, HALF)], ends[: SEG - 1]], axis=0))

    def step(n, carry):
        *carried, sum_f, sum_i = carry
        m = steps // 2 - 1 - n
        for s in range(2):
            terms = []
            for q in (1, 0):
                j = 2 * m + q
                at = group(s, steps, j)
                back = acc_ref[at, :] + carried[s]
                carried[s] = carried[s] * retain_ref[0, at, :]
                previous = states_ref[group(s, steps, jnp.maximum(j - 1, 0)), :]
                if q == 0:
                    previous = jnp.where(m == 0, first[s], previous)
                both_ways = back * (previous * rs_ref[at, :] - cand_ref[at, :])
                d_f = both_ways * df_ref[at, :]
                d_i = both_ways * di_ref[at, :]
                sum_f = sum_f + d_f
                sum_i = sum_i - d_i
                terms.append((d_f, -d_i, back * share_ref[at, :]))
            for late, early, ref in zip(*terms, (pf_ref, pi_ref, pc_ref), strict=True):
                ref[pair(s, steps, m), :] = jnp.concatenate([early, late], axis=0).astype(bf16)
        return (*carried, sum_f, sum_i)

    nothing = jnp.zeros((SEG, HALF), f32)
    *_, sum_f, sum_i = lax.fori_loop(0, steps // 2, step, (*start, nothing, nothing), unroll=steps // 2)
    dfb_ref[...] = jnp.sum(sum_f, axis=0, keepdims=True)
    dib_ref[...] = jnp.sum(sum_i, axis=0, keepdims=True)
    normed = normed_ref[...]
    for role, ref in enumerate((pf_ref, pi_ref, pc_ref)):
        grad_ref[:, role] = dot_tn(ref[...], normed).astype(bf16).reshape(PLANES, ROWS, D)


def input_terms_kernel(ids_ref, tok_ref, dgain_two_ref, dfb_o, dfb_p, dib_o, dib_p, *refs):
    terms, weights, refs = refs[: 2 * GATES], refs[2 * GATES : 2 * GATES + 2], refs[-3:]
    dnorm_ref, small_ref, rows_ref = refs
    d_normed = 0.0
    for role in range(GATES):
        for k in range(2):
            d_normed = d_normed + dot_nn(terms[k * GATES + role][...], weights[k][role])
    dnorm_ref[...] = d_normed
    x = inward(tok_ref)
    d_gain = jnp.sum(d_normed * (x * unit(x)), axis=0, keepdims=True)
    for k in range(PLANES):
        rows_ref[pl.ds(k, 1), :] = d_gain[:, k * ROWS : (k + 1) * ROWS]
        rows_ref[pl.ds(PLANES + k, 1), :] = dgain_two_ref[:, pl.ds(k * ROWS, ROWS)]
        chip = 4 * (ids_ref[X] ^ (k // 2)) + 2 * (ids_ref[Y] ^ (k % 2))
        for core, (fb, ib) in enumerate(((dfb_o, dib_o), (dfb_p, dib_p))):
            row = 2 * PLANES + chip + (ids_ref[CORE] ^ core)
            rows_ref[pl.ds(row, 1), :] = fb[:, pl.ds(k * ROWS, ROWS)]
            rows_ref[pl.ds(row + 2 * PLANES, 1), :] = ib[:, pl.ds(k * ROWS, ROWS)]
    blocks = [rows_ref[pl.ds(k * SEG, SEG), :] for k in range(SMALL_BLOCKS)] + [jnp.zeros((SEG, ROWS), f32)]
    small_ref[...] = jnp.concatenate([jnp.concatenate(blocks, axis=1), jnp.zeros((SEG, D), f32)], axis=0)


def outputs_kernel(tok_ref, gain_ref, dresid_ref, dnorm_ref, resid_ref, valid_ref, act_ref, held, order_ref, dx_ref, output_ref, done_ref):
    done_ref[...] = jnp.zeros_like(done_ref)
    _, d_x = rms_back(inward(tok_ref), dnorm_ref[...], gain_ref[...])
    outward(dx_ref, (dresid_ref[...] + d_x).astype(bf16))
    total = resid_ref[...]
    for i in range(2 * PLANES):
        total = total + dot_nn(act_ref[i], held[i // 2, :, i % 2 + 2].reshape(2 * ROWS, D))
    outward(output_ref, (total * valid_ref[...]).astype(bf16))


def out_place(core, k):
    return jnp.where(core == 0, 3 - k, k) if k in (1, 2) else k


def mlp_pair_kernel(ids_ref, own_ref, got_ref, out_ref, outgot_ref, *refs):
    for q in range(2):
        ref = refs[-1].at[q]
        ref[pl.ds(0, ROLES)] = (own_ref[2 + q].astype(f32) + got_ref[q].astype(f32)).astype(bf16)
        at = pl.ds(out_place(ids_ref[CORE], 2 + q), 1)
        ref[pl.ds(ROLES, 1)] = (out_ref[at, 0].astype(f32) + outgot_ref[at, 0].astype(f32)).astype(bf16)


def gate_pair_kernel(own_ref, got_ref, small_ref, small_got, *outs):
    small = (small_ref[...] + small_got[...]).astype(bf16)
    for k, ref in enumerate(outs[-PLANES:]):
        total = (own_ref[k].astype(f32) + got_ref[k].astype(f32)).astype(bf16)
        ref[pl.ds(0, GATES * ROWS), :] = total.reshape(GATES * ROWS, D)
        ref[pl.ds(GATES * ROWS, TAIL), :] = small


def half_sum_kernel(ids_ref, own_ref, pair_ref, out_ref, outpair_ref, got_ref, *refs):
    keep_ref, send_ref, out_keep, out_send = refs[-4:]
    z = ids_ref[Z]
    near_bit = jnp.where(ids_ref[CORE] == 0, 1, 2)
    for q in range(2):

        def total(role, q=q):
            at = pl.ds(role, 1)
            terms = own_ref[q, at].astype(f32) + pair_ref[q, at].astype(f32)
            return (terms + got_ref[q, at].astype(f32)).astype(bf16).reshape(ROWS, D)

        for k, role in enumerate((z, z ^ near_bit ^ 3)):
            keep_ref[k, q] = total(role)
            send_ref[k, q] = total(role ^ near_bit)
        at = pl.ds(out_place(ids_ref[CORE], q), 1)
        terms = out_ref[at, 0].astype(f32) + outpair_ref[at, 0].astype(f32)
        (out_keep, out_send)[q][...] = (terms + got_ref[q, pl.ds(ROLES, 1)].astype(f32)).astype(bf16).reshape(ROWS, D)


def mlp_far_kernel(keep_ref, got_ref, *refs):
    stay_ref, send_ref = refs[-2:]
    stay_ref[...] = (keep_ref[0].astype(f32) + got_ref[0].astype(f32)).astype(bf16)
    send_ref[...] = (keep_ref[1].astype(f32) + got_ref[1].astype(f32)).astype(bf16)


def mlp_last_kernel(stay_ref, got_ref, *refs):
    keep_ref, send_ref = refs[-2:]
    keep_ref[...] = stay_ref[0].astype(f32) + got_ref[0].astype(f32)
    send_ref[...] = (stay_ref[1].astype(f32) + got_ref[1].astype(f32)).astype(bf16)


def gate_plane_kernel(ids_ref, p0, p1, p2, p3, out_ref, out_got, *refs):
    z = ids_ref[Z]
    keep_ref, s1_ref, s2_ref, s3_ref = refs[-4:]

    def total(at):
        terms = [ref[at, :].astype(f32) for ref in (p0, p1, p2, p3)]
        return (terms[0] + terms[1]) + (terms[2] + terms[3])

    def of_role(role):
        at = pl.ds(pl.multiple_of(jnp.minimum(role, GATES - 1) * ROWS, ROWS), ROWS)
        return jnp.where(role == GATES, out_ref[...].astype(f32) + out_got[...].astype(f32), total(at))

    small = total(pl.ds(GATES * ROWS, TAIL))
    keep_ref[pl.ds(0, ROWS), :] = of_role(z)
    keep_ref[pl.ds(ROWS, TAIL), :] = small
    for k, ref in enumerate((s1_ref, s2_ref, s3_ref)):
        ref[pl.ds(0, ROWS), :] = of_role(z ^ (k + 1)).astype(bf16)
        ref[pl.ds(ROWS, TAIL), :] = small.astype(bf16)


def joined(at, keep_ref, gots):
    total = keep_ref[at, :]
    for ref in gots:
        total = total + ref[at, :].astype(f32)
    return total


def matrix_step(at, keep_ref, gots, weight_ref, first_ref, second_ref, outs):
    grad_ref, first_out, second_out, dir_ref = outs
    weight = weight_ref[...]
    gradient = joined(at, keep_ref, gots)
    grad_ref[...] = gradient
    first_out[...], second_out[...], direction = moments(
        weight, gradient, first_ref[...], second_ref[...], matrix_decay
    )
    dir_ref[...] = direction
    return weight, direction


def square_rows(value):
    square = jnp.sum((value * value).reshape(-1, SEG, D), axis=0)
    return (square[:, :128] + square[:, 128:256]) + (square[:, 256:384] + square[:, 384:])


def moments_kernel(keep_ref, got_ref, weight_ref, first_ref, second_ref, *outs):
    *outs, wsum_ref, dsum_ref = outs
    weight, direction = matrix_step(
        pl.ds(0, weight_ref.shape[0]), keep_ref, [got_ref], weight_ref, first_ref, second_ref, outs
    )
    wsum_ref[...] = square_rows(weight)
    dsum_ref[...] = square_rows(direction)


def finish_kernel(
    ids_ref, keep_ref, g1_ref, g2_ref, g3_ref, wsum_f, dsum_f,
    mixer_ref, mixer_first, mixer_second, weight_ref, first_ref, second_ref,
    mixer_grad, mixer_first_out, mixer_second_out, mixer_dir, grad_ref, first_out, second_out, dir_ref, squares_ref,
    rows_ref,
):
    gots = (g1_ref, g2_ref, g3_ref)
    mixer_rows = mixer_ref.shape[0]
    mixer_values = matrix_step(
        pl.ds(0, mixer_rows), keep_ref, gots, mixer_ref, mixer_first, mixer_second,
        (mixer_grad, mixer_first_out, mixer_second_out, mixer_dir),
    )
    total = joined(pl.ds(mixer_rows, TAIL), keep_ref, gots)
    rows_ref[...] = jnp.zeros_like(rows_ref)
    for k in range(SMALL_BLOCKS):
        rows_ref[pl.ds(k * SEG, SEG), :] = total[:SEG, k * ROWS : (k + 1) * ROWS]
    weight = weight_ref[...]
    count = weight.shape[1]
    start = ids_ref[DEVICE] * count
    row, lane = start // ROWS, start % ROWS
    two = jnp.concatenate([rows_ref[pl.ds(row, 1), :], rows_ref[pl.ds(row + 1, 1), :]], axis=1)
    two = jnp.broadcast_to(two, (SEG, 2 * ROWS))
    gradient = pltpu.roll(two, (2 * ROWS - lane) % (2 * ROWS), 1)[:1, :count]
    grad_ref[...] = gradient
    first_out[...], second_out[...], direction = moments(weight, gradient, first_ref[...], second_ref[...], 0.0)
    dir_ref[...] = direction
    place = start + lax.broadcasted_iota(jnp.int32, (1, count), 1)
    at = lax.broadcasted_iota(jnp.int32, (1, ROWS), 1)
    bounds = (0, D, 2 * D, 2 * D + H, 2 * D + 2 * H)
    lines = []
    for mixer_value, mlp_sum, value in zip(mixer_values, (wsum_f, dsum_f), (weight, direction), strict=True):
        line = jnp.where(at == ids_ref[MIXER_ROLE], jnp.sum(square_rows(mixer_value), keepdims=True), 0.0)
        line = line + jnp.where(at == ROLES + ids_ref[MLP_ROLE], jnp.sum(mlp_sum[...], keepdims=True), 0.0)
        for k in range(4):
            inside = (place >= bounds[k]) & (place < bounds[k + 1])
            part = jnp.sum(jnp.where(inside, value * value, 0.0), axis=1, keepdims=True)
            line = line + jnp.where(at == ROLES + 2 + k, part, 0.0)
        lines.append(line)
    squares_ref[...] = jnp.concatenate(lines + [jnp.zeros((SEG - 2, ROWS), f32)], axis=0)


def ratio_of(squares_ref, tensor):
    norms = jnp.sqrt(squares_ref[0:2, :])
    ratios = norms[0:1] / (norms[1:2] + 1e-06)
    at = lax.broadcasted_iota(jnp.int32, (1, ROWS), 1)
    return jnp.sum(jnp.where(at == tensor, ratios, 0.0), axis=1, keepdims=True)


def new_weights(ratio, weight_ref, dir_ref, new_ref, copy_ref):
    value = weight_ref[...] - learn_rate * ratio * dir_ref[...]
    new_ref[...] = value
    copy_ref[...] = value.astype(bf16)


def mixer_update_kernel(ids_ref, squares_ref, weight_ref, dir_ref, *refs):
    ins, (new_ref, copy_ref, *outs, done_ref) = refs[:6], refs[6:]
    done_ref[...] = jnp.zeros_like(done_ref)
    new_weights(ratio_of(squares_ref, ids_ref[MIXER_ROLE]), weight_ref, dir_ref, new_ref, copy_ref)
    for ref, out in zip(ins, outs, strict=True):
        out[...] = ref[...]


def last_update_kernel(
    ids_ref, squares_ref, mlp_ref, mlp_dir, weight_ref, dir_ref, order_ref,
    mlp_new, mlp_copy, new_ref, copy_ref, norms_ref, ratios_ref,
):
    norms = jnp.sqrt(squares_ref[0:2, :])
    ratios = norms[0:1] / (norms[1:2] + 1e-06)
    norms_ref[...] = norms[:, : norms_ref.shape[1]]
    ratios_ref[...] = ratios[:, : ratios_ref.shape[1]]
    new_weights(ratio_of(squares_ref, ROLES + ids_ref[MLP_ROLE]), mlp_ref, mlp_dir, mlp_new, mlp_copy)
    count = weight_ref.shape[1]
    place = ids_ref[DEVICE] * count + lax.broadcasted_iota(jnp.int32, (1, count), 1)
    first, second, third, fourth = (ratio_of(squares_ref, ROLES + 2 + k) for k in range(4))
    ratio = jnp.where(
        place < 2 * D, jnp.where(place < D, first, second), jnp.where(place < 2 * D + H, third, fourth)
    )
    new_weights(ratio, weight_ref, dir_ref, new_ref, copy_ref)


SMEM = pl.BlockSpec(memory_space=pltpu.SMEM)
ANY = pl.BlockSpec(memory_space=pl.ANY)
VMEM = pl.BlockSpec(memory_space=pltpu.VMEM)


def shape(*dims, dtype=f32):
    return jax.ShapeDtypeStruct(dims, dtype)


def near(*dims, dtype=f32):
    return pltpu.VMEM(dims, dtype)


def kept(value):
    return pltpu.with_memory_space_constraint(value, pltpu.VMEM)


def away(value):
    return pltpu.with_memory_space_constraint(value, pltpu.HBM)


def call(kernel, name, out_shape, *args, order=(), far=(), scratch=(), mib=8):
    in_specs = [SMEM if arg.dtype == jnp.int32 else VMEM for arg in args] + [ANY] * (len(far) + len(order))
    return pl.pallas_call(
        kernel,
        in_specs=in_specs,
        out_specs=jax.tree.map(lambda _: VMEM, out_shape),
        out_shape=out_shape,
        scratch_shapes=list(scratch),
        compiler_params=pltpu.CompilerParams(vmem_limit_bytes=mib * 1024 * 1024),
        name=name,
    )(*[arg if arg.dtype == jnp.int32 else kept(arg) for arg in args], *[away(arg) for arg in far], *order)


def exchange_lane(value, second):
    seqs, batches = lax.axis_size("seq"), lax.axis_size("batch")
    pairs = []
    for s in range(seqs):
        for b in range(batches):
            over_x = (b % 2 == 0) != second
            pairs.append((s * batches + b, (s ^ 1) * batches + b if over_x else s * batches + (b ^ 2)))
    return lax.ppermute(value, AXES, pairs)


def exchange_z_lane(value, second):
    seqs, batches = lax.axis_size("seq"), lax.axis_size("batch")
    pairs = []
    for s in range(seqs):
        for b in range(batches):
            bit = 2 if (b % 2 == 0) != second else 4
            pairs.append((s * batches + b, (s ^ bit) * batches + b))
    return lax.ppermute(value, AXES, pairs)


def after(value, *others):
    return lax.optimization_barrier((value, *others))[0]


def over_z(shard):
    return [shard] + [exchange(shard, 2 * k, 0) for k in range(1, 4)]


def z_terms(sends):
    return [exchange(sent, 2 * (k + 1), 0) for k, sent in enumerate(sends)]


def all_sum(value):
    seqs, batches = lax.axis_size("seq"), lax.axis_size("batch")
    bit = 1
    while bit < batches:
        value = value + exchange(value, 0, bit)
        bit *= 2
    bit = 1
    while bit < seqs:
        value = value + exchange(value, bit, 0)
        bit *= 2
    return value


def relay(ids, total, forward, flipped, beside, hold=()):
    group, before, bit = total, [], 1
    joint = near(4, H)
    if flipped:
        other = exchange(group, 1, 0)
        order = beside[1](group) if 1 in beside else []
        pair, before = call(
            functools.partial(relay_kernel, 1, forward, True), "relay_near", [joint, joint], ids, group, other, order=order
        )
        others = [exchange(pair, 2 * k, 0) for k in range(1, ROLES)]
        order = beside[2](pair) if 2 in beside else []
        return call(
            functools.partial(relay_far_kernel, forward), "relay_far", near(2, H), ids, before, pair, *others, order=order
        )
    while bit < lax.axis_size("seq"):
        last = 2 * bit == lax.axis_size("seq")
        other = exchange(group, bit, 0)
        order = beside[bit](group) if bit in beside else []
        got = call(
            functools.partial(relay_kernel, bit, forward, flipped and bit == 1),
            f"relay_{bit}", near(2, H) if last else [joint, joint],
            ids, group, other, *before, *hold, order=order,
        )
        if not last:
            group, before = got[0], [got[1]]
        bit *= 2
    return got


def flip_by(value, axis, bit):
    return jnp.where(bit == 1, jnp.flip(value, axis), value)


def moments(weight, gradient, first_moment, second, decay_rate):
    first_new = first_decay * first_moment + (1.0 - first_decay) * gradient
    second_new = second_decay * second + (1.0 - second_decay) * gradient * gradient
    direction = (
        first_new
        / (1.0 - first_decay**STEP)
        / (jnp.sqrt(second_new / (1.0 - second_decay**STEP)) + moment_eps)
        + decay_rate * weight
    )
    return (first_new, second_new, direction)


def on_device(
    tokens, doc_lengths, cotangent, mixer_weights, mlp_weights, small_params,
    mixer_first, mixer_second, mlp_first, mlp_second, small_first, small_second,
):
    seqs, batches = lax.axis_size("seq"), lax.axis_size("batch")
    seq_at, batch_at = lax.axis_index("seq"), lax.axis_index("batch")
    device = seq_at * batches + batch_at
    streams, block, _ = tokens.shape
    rows = streams * block
    direct = (seqs, batches) == (8, 4)
    if direct:
        z, x, y, c = seq_at // 2, seq_at % 2, batch_at // 2, batch_at % 2
    else:
        z = x = y = c = jnp.zeros((), jnp.int32)
    mixer_role = device * mixer_weights.shape[0] // H
    mlp_role = device * mlp_weights.shape[0] // FF
    ids = jnp.stack([z, x, y, c, seq_at, device, mixer_role, mlp_role]).astype(jnp.int32)

    slab = shape(ROLES, ROWS, D, dtype=bf16)
    if direct:
        pair_of = near(2, ROWS, D, dtype=bf16)
        count = small_params.shape[0]
        packed = call(
            pack_kernel, "mixer_pack", near(ROWS + TAIL, D, dtype=bf16),
            ids, mixer_weights.astype(bf16), exchange(small_params, 0, 1)[None], far=[small_params[None]],
            scratch=[pltpu.VMEM((1, count), f32), pltpu.SemaphoreType.DMA(())],
        )
        mixer_two = call(
            stack_kernel, "mixer_pair", near(2, ROWS + TAIL, D, dtype=bf16), packed, exchange_z_lane(packed, False)
        )
        mixer_far = exchange_z_lane(mixer_two, True)
        mlp_low = after(mlp_weights, packed).astype(bf16)
        mlp_two = call(stack_kernel, "mlp_pair", pair_of, mlp_low, exchange_lane(mlp_low, False))
        mlp_plane = call(stack_kernel, "mlp_plane", slab, mlp_two, exchange_lane(mlp_two, True))
        gate_slab = call(
            slab_kernel, "mixer_slab", shape(ROLES * ROWS + TAIL, D, dtype=bf16),
            ids, mixer_two, mixer_far, order=[mlp_plane], scratch=[pltpu.VMEM((TAIL, D), f32)],
        )
        mixer_own = [gate_slab] + [exchange(gate_slab, *bits) for bits in PLANE_BITS[1:]]
        mlp_plane = after(mlp_plane, gate_slab)
        mlp_early = call(
            stack_kernel, "mlp_early", shape(2, PLANES, ROWS, D, dtype=bf16), mlp_plane, exchange_z_lane(mlp_plane, False)
        )
        mlp_late = exchange_z_lane(mlp_early, True)
    else:
        small_used = lax.all_gather(small_params.astype(bf16), AXES, axis=0, tiled=True).astype(f32)

        def gathered(shard):
            full = lax.all_gather(shard.astype(bf16), AXES, axis=0, tiled=True)
            return full.reshape(ROLES, PLANES, 2, ROWS, D)

        full = gathered(mixer_weights)
        mixer_own, mixer_par = [[full[:, p, k].reshape(ROLES * ROWS, D) for p in range(PLANES)] for k in range(2)]
        full = gathered(mlp_weights)
        orders = (jnp.array([0, 1, 2, 3]), jnp.array([0, 2, 1, 3]))
        mlp_parts = [full[orders[k], :, k][at] for k in range(2) for at in (slice(0, 2), slice(2, 4))]

    restart, valid = call(marks_kernel, "marks", [shape(rows, 1), shape(rows, 1)], ids, doc_lengths)
    d_out = call(dout_kernel, "d_out", near(rows, D, dtype=bf16), cotangent, valid)

    wide = near(rows, HALF)
    natural = shape(streams, block, D, dtype=bf16)
    low_wide = near(rows, HALF, dtype=bf16)
    low_rows = near(rows, D, dtype=bf16)
    ends = near(2 * SEG, HALF)
    projections = [pltpu.VMEM((rows, HALF), f32)] * 3

    if direct:
        mixer_own = [gate_slab, *after(tuple(mixer_own[1:]), mlp_early, restart, d_out)]
        mixer_par = [exchange(part, 0, 1) for part in mixer_own]
    wide_two, gate_weights = near(2, rows, HALF), near(GATES, HALF, D, dtype=bf16)
    if direct:
        normed, gain_one, gain_two, fb_o, fb_p, ib_o, ib_p, weights_o, both_o, tot_o, sega_o, segb_o = call(
            lambda *refs: scan_first_kernel(count, *refs), "scan_own",
            [low_rows] + [near(1, D)] * 2 + [near(1, HALF)] * 4 + [gate_weights, wide_two, near(4, HALF), ends, ends],
            ids, tokens, restart, *mixer_own,
            scratch=projections + [pltpu.VMEM((4 * SEG, ROWS), f32), pltpu.VMEM((3 * SEG, ROWS), f32)],
        )
    else:
        gain_one, gain_two = small_used[:D][None], small_used[D : 2 * D][None]
        biases = small_used[2 * D :].reshape(2, PLANES, 2, ROWS).transpose(0, 2, 1, 3).reshape(4, 1, HALF)
        fb_o, fb_p, ib_o, ib_p = [biases[k] for k in range(4)]
        normed = call(normed_kernel, "first_norm", low_rows, tokens, gain_one)
        weights_o, both_o, tot_o, sega_o, segb_o = call(
            lambda *refs: scan_kernel(True, *refs), "scan_own", [gate_weights, wide_two, near(4, HALF), ends, ends],
            normed, restart, fb_o, ib_o, *mixer_own, scratch=projections,
        )
    weights_p, both_p, tot, sega_p, segb_p = call(
        lambda *refs: scan_kernel(False, *refs), "scan_other", [gate_weights, wide_two, near(4, H), ends, ends],
        normed, restart, fb_p, ib_p, tot_o, *mixer_par, scratch=projections,
    )

    kept_terms = {}

    def terms_own(ready):
        kept_terms["own"] = call(
            terms_kernel, "terms_own", [wide] * 4,
            normed, fb_o, ib_o, weights_o, order=[ready], scratch=projections[:2],
        )
        return [kept_terms["own"][0]]

    def terms_other(ready):
        kept_terms["other"] = call(
            terms_kernel, "terms_other", [wide] * 4,
            normed, fb_p, ib_p, weights_p, order=[ready], scratch=projections[:2],
        )
        return [kept_terms["other"][0]]

    incoming = relay(ids, tot, True, direct, {1: terms_own, 2: terms_other})
    if direct:
        mlp_late = after(mlp_late, incoming)
        mlp_parts = [mlp_early, mlp_late, exchange(mlp_early, 0, 1), exchange(mlp_late, 0, 1)]

    states_o, states_p, low_o, low_p, resid, normed_two, out_weights = call(
        states_kernel, "states",
        [wide, wide, low_wide, low_wide, near(rows, D), low_rows, near(1, H, D, dtype=bf16)],
        incoming, tokens, gain_two, both_o, both_p, sega_o, sega_p, segb_o, segb_p,
        *mixer_own, *mixer_par,
    )

    terms, half_terms_two = near(PLANES, ROLES, ROWS, D, dtype=bf16), near(2, ROLES, ROWS, D, dtype=bf16)
    d_resid, d_gain_two, mlp_gown, mlp_gnear, mlp_gfar, mlp_act, mlp_held = call(
        mlp_kernel, "mlp",
        [
            near(rows, D), near(1, D), terms, half_terms_two, half_terms_two, near(2 * PLANES, rows, 2 * ROWS, dtype=bf16),
            near(PLANES, 2, ROLES, ROWS, D, dtype=bf16),
        ],
        ids, normed_two, resid, d_out, gain_two, *mlp_parts, mib=16, scratch=[pltpu.VMEM((rows, D), f32)],
    )

    half_terms = near(PLANES, 1, ROWS, D, dtype=bf16)
    back_o, back_p, tot_back, bseg_o, bseg_p, out_gown, out_gpar = call(
        back_kernel, "back_scan", [wide, wide, near(4, H), ends, ends, half_terms, half_terms],
        d_resid, low_o, low_p, both_o, both_p, sega_o, sega_p, out_weights,
    )

    beside = {}
    if direct:
        mlp_got_far, out_got = exchange(mlp_gfar, 0, 1), exchange(out_gpar, 0, 1)
        mlp_got = exchange(after(mlp_gnear, tot_back), 0, 1)
        two_fives = near(2, ROLES + 1, ROWS, D, dtype=bf16)

        def mlp_pair(ready):
            kept_terms["mlp"] = call(
                mlp_pair_kernel, "mlp_pair_sum", two_fives, ids, mlp_gown, mlp_got_far, out_gown, out_got,
                order=[ready],
            )
            return [kept_terms["mlp"]]

        def mark_pair(ready):
            kept_terms["pair"] = ready
            return []

        beside = {1: mlp_pair, 2: mark_pair}

    arriving = relay(ids, tot_back, False, direct, beside)
    terms_o, terms_p = kept_terms["own"], kept_terms["other"]
    if direct:
        mlp_round = exchange_lane(after(kept_terms["mlp"], kept_terms["pair"]), True)

    def gates_back(column, back, sega, bseg, share, df, di, cand, retain, states, order, name):
        return call(
            lambda *refs: gates_kernel(column, *refs), name,
            [near(PLANES, GATES, ROWS, D, dtype=bf16), low_wide, low_wide, low_wide, near(1, HALF), near(1, HALF)],
            arriving, incoming, back, sega, bseg, share, df, di, cand, retain, states, restart, normed, order=order,
        )

    gate_gpar, pf_p, pi_p, pc_p, dfb_p, dib_p = gates_back(
        HALF, back_p, sega_p, bseg_p, *terms_p, both_p, states_p, [tot_back], "gates_other"
    )
    gate_gown, pf_o, pi_o, pc_o, dfb_o, dib_o = gates_back(
        0, back_o, sega_o, bseg_o, *terms_o, both_o, states_o, [dfb_p], "gates_own"
    )

    d_normed, small_terms = call(
        input_terms_kernel, "input_terms", [near(rows, D), near(TAIL, D)],
        ids, tokens, d_gain_two, dfb_o, dfb_p, dib_o, dib_p,
        pf_o, pi_o, pc_o, pf_p, pi_p, pc_p, weights_o, weights_p, order=[dfb_o],
        scratch=[pltpu.VMEM((3 * SEG, ROWS), f32)],
    )

    def token_outputs(ready):
        return call(
            outputs_kernel, "outputs", [natural, natural, near(SEG, ROWS)],
            tokens, gain_one, d_resid, d_normed, resid, valid, mlp_act, mlp_held, order=[ready],
        )

    def with_moments(keep, got, weight, first_moment, second, name):
        count = weight.shape[0]
        return call(
            moments_kernel, name, [shape(count, D)] * 3 + [near(count, D)] + [near(SEG, 128)] * 2,
            keep, got, weight, first_moment, second,
        )

    if direct:
        shard, low_shard = near(ROWS, D), near(ROWS, D, dtype=bf16)
        long, low_long = near(ROWS + TAIL, D), near(ROWS + TAIL, D, dtype=bf16)
        quarter, low_shard = near(2, 2, ROWS, D, dtype=bf16), near(ROWS, D, dtype=bf16)
        small_got = exchange(small_terms, 0, 1)
        mlp_keep, mlp_send, out_keep, out_send = call(
            half_sum_kernel, "mlp_half_sum", [quarter, quarter, low_shard, low_shard], ids,
            mlp_gown, mlp_got, out_gown, out_got, mlp_round, order=[small_got],
        )
        gate_parts = call(
            gate_pair_kernel, "gate_pair_sum", [near(GATES * ROWS + TAIL, D, dtype=bf16)] * PLANES,
            gate_gown, exchange(gate_gpar, 0, 1), small_terms, small_got, order=[out_keep],
        )
        over_both, over_x, over_y = (exchange(gate_parts[k], *PLANE_BITS[k]) for k in (3, 2, 1))
        gate_round = [gate_parts[0], over_y, over_x, over_both]
        d_x, output, x_done = token_outputs(gate_parts[0])
        out_got = exchange_lane(out_send, False)
        two = near(2, ROWS, D, dtype=bf16)
        mlp_stay, mlp_send = call(
            mlp_far_kernel, "mlp_z_sum", [two, two], mlp_keep, exchange_z_lane(mlp_send, False)
        )
        mlp_stay, mlp_send = call(
            mlp_last_kernel, "mlp_z_last", [shard, low_shard], mlp_stay, exchange_z_lane(mlp_send, True)
        )
        mlp_done = with_moments(
            mlp_stay, exchange_lane(mlp_send, False), mlp_weights, mlp_first, mlp_second, "mlp_moments"
        )
        gate_keep, *gate_sends = call(
            gate_plane_kernel, "gate_plane_sum", [long] + [low_long] * 3, ids, *gate_round, out_keep, out_got,
            order=[x_done],
        )
        gate_got = z_terms(gate_sends)
    else:

        def scattered(own, par):
            full_terms = jnp.stack([own, par]).transpose(2, 1, 0, 3, 4).reshape(-1, D)
            return lax.psum_scatter(full_terms.astype(f32), AXES, scatter_dimension=0, tiled=True)

        d_x, output, _ = token_outputs(small_terms)
        mlp_grad = scattered(mlp_gown, jnp.concatenate([mlp_gnear, mlp_gfar], axis=0))
        mixer_grad = scattered(
            jnp.concatenate([gate_gown, out_gown], axis=1), jnp.concatenate([gate_gpar, out_gpar], axis=1)
        )
        none = jnp.zeros_like(mlp_grad, dtype=bf16)
        mlp_done = with_moments(mlp_grad, none, mlp_weights, mlp_first, mlp_second, "mlp_moments")
        gate_keep = jnp.concatenate([mixer_grad, lax.psum(small_terms, AXES)], axis=0)
        gate_got = [jnp.zeros_like(gate_keep, dtype=bf16)] * 3
    mlp_grad, mlp_first_new, mlp_second_new, mlp_dir, mlp_wsum, mlp_dsum = mlp_done
    count, mixer_count = small_params.shape[0], mixer_weights.shape[0]
    line, matrix = shape(1, count), shape(mixer_count, D)
    mixer_grad, mixer_first_new, mixer_second_new, mixer_dir, small_grad, small_first_new, small_second_new, small_dir, squares = call(
        finish_kernel, "finish", [near(mixer_count, D)] * 4 + [near(1, count)] * 4 + [near(SEG, ROWS)],
        ids, gate_keep, *gate_got, mlp_wsum, mlp_dsum, mixer_weights, mixer_first, mixer_second,
        small_params[None], small_first[None], small_second[None], scratch=[pltpu.VMEM((4 * SEG, ROWS), f32)],
    )

    def mixer_update(sums):
        matrix = shape(mixer_count, D)
        return call(
            mixer_update_kernel, "mixer_update", [matrix, shape(mixer_count, D, dtype=bf16)] + [matrix] * 3 + [line] * 3 + [near(SEG, ROWS)],
            ids, sums, mixer_weights, mixer_dir, mixer_grad, mixer_first_new, mixer_second_new,
            small_grad, small_first_new, small_second_new,
        )

    if direct:
        sums = squares + exchange(squares, 0, 1)
        over_y, over_x, over_both = (exchange(sums, *bits) for bits in PLANE_BITS[1:])
        sums = (sums + over_y) + (over_x + over_both)
        stored = mixer_update(sums)
        near_z, far_z, both_z = (exchange(sums, 2 * k, 0) for k in range(1, ROLES))
        sums = (sums + near_z) + (far_z + both_z)
    else:
        sums = all_sum(squares)
        stored = mixer_update(sums)
    mixer_new, mixer_copy, mixer_grad, mixer_first_new, mixer_second_new, *stored = stored
    small_grad, small_first_new, small_second_new, mixer_updated = stored
    matrix, low_line = shape(*mlp_weights.shape), shape(1, count, dtype=bf16)
    mlp_new, mlp_copy, small_new, small_copy, tensor_norms, trust_ratios = call(
        last_update_kernel, "last_update",
        [matrix, shape(*mlp_weights.shape, dtype=bf16), line, low_line, shape(2, 10), shape(1, 10)],
        ids, sums, mlp_weights, mlp_dir, small_params[None], small_dir, order=[mixer_updated],
    )
    return (
        output,
        d_x,
        mixer_grad,
        mlp_grad,
        small_grad[0],
        mixer_first_new,
        mixer_second_new,
        mlp_first_new,
        mlp_second_new,
        small_first_new[0],
        small_second_new[0],
        mixer_new,
        mlp_new,
        small_new[0],
        mixer_copy,
        mlp_copy,
        small_copy[0],
        tensor_norms,
        trust_ratios[0],
    )


def solution(mesh):
    shard = P(("seq", "batch"), None)
    shard_flat = P(("seq", "batch"))
    stream = P("batch", "seq", None)
    return jax.shard_map(
        on_device,
        mesh=mesh,
        in_specs=(
            stream, P("batch", None), stream, shard, shard, shard_flat,
            shard, shard, shard, shard, shard_flat, shard_flat,
        ),
        out_specs=(
            stream, stream, shard, shard, shard_flat, shard, shard, shard, shard, shard_flat, shard_flat,
            shard, shard, shard_flat, shard, shard, shard_flat, P(), P(),
        ),
        check_vma=False,
    )
```
